32 devices in a mesh: ep: 8 (over y, x, core), tp: 4 (over z).
Axes of the slice: x: 2, y: 2, z: 4, core: 2. Of those that a mesh axis runs over, the one named last changes fastest.
Arguments:
- inputs: bfloat16 [4096, 2048], P('ep'), may hold values from -6 to 6
- gain_attn: float32 [2048], replicated, may hold values from 0.5 to 1.5
- w_query: bfloat16 [2048, 3072], P(None, 'tp'), may hold values from -0.125 to 0.125
- w_latent: bfloat16 [2048, 576], replicated, may hold values from -0.125 to 0.125
- gain_latent: float32 [512], replicated, may hold values from 0.5 to 1.5
- w_latent_up: bfloat16 [512, 4096], P(None, 'tp'), may hold values from -0.25 to 0.25
- w_output: bfloat16 [2048, 2048], P('tp'), may hold values from -0.5 to 0.5
- gain_ffn: float32 [2048], replicated, may hold values from 0.5 to 1.5
- w_router: float32 [2048, 8], replicated, may hold values from -0.0625 to 0.0625
- w_shared_in: bfloat16 [2, 2048, 2816], P(None, None, 'tp'), may hold values from -0.125 to 0.125
- w_shared_out: bfloat16 [2816, 2048], P('tp'), may hold values from -0.109375 to 0.109375
- w_expert_in: bfloat16 [8, 2, 2048, 1408], P('ep', None, None, 'tp'), may hold values from -0.125 to 0.125
- w_expert_out: bfloat16 [8, 1408, 2048], P('ep', 'tp'), may hold values from -0.21875 to 0.21875
- expert_ids: int32 [4096, 6], P('ep'), may hold values from 0 to 7, as said below
- slot_ids: int32 [4096, 6], P('ep'), may hold values from 0 to 432, as said below
- cotangent: bfloat16 [4096, 2048], P('ep'), may hold values from -6 to 6
Outputs:
- block_out: bfloat16 [4096, 2048], P('ep')
- grad_inputs: bfloat16 [4096, 2048], P('ep')
- grad_gain_attn: float32 [2048], P(('ep', 'tp'))
- grad_query: float32 [2048, 3072], P('ep', 'tp')
- grad_latent: float32 [2048, 576], P(('ep', 'tp'))
- grad_gain_latent: float32 [512], P(('ep', 'tp'))
- grad_latent_up: float32 [512, 4096], P('ep', 'tp')
- grad_output: float32 [2048, 2048], P('tp', 'ep')
- grad_gain_ffn: float32 [2048], P(('ep', 'tp'))
- grad_router: float32 [2048, 8], P(('ep', 'tp'))
- grad_shared_in: float32 [2, 2048, 2816], P(None, 'ep', 'tp')
- grad_shared_out: float32 [2816, 2048], P('tp', 'ep')
- grad_expert_in: float32 [8, 2, 2048, 1408], P('ep', None, None, 'tp')
- grad_expert_out: float32 [8, 1408, 2048], P('ep', 'tp')
The draws below stay inside these ranges and needn't reach their ends.
Inputs may be any that keep to these rules, and one draw needn't show every extreme that they name: `expert_ids`: each row names 6 different experts; in the 512 rows of each index of ep, some expert is named by more than 432 rows. `slot_ids`: within the 512 rows of one index of ep, the pairs naming one expert are numbered 0, 1, 2, ... in the order of rows and then k; numbers 432 and beyond are replaced by 432, which marks a dropped pair.
All inputs are finite; a program needn't handle non-finite values.
Results may differ from the reference program's by a relative error of at most 0.02.
Values may be sent and summed in bfloat16 or wider, within the bound.
A program may use at most 320 MiB of HBM per device.

```python
import math
import jax
import jax.numpy as jnp
from jax import lax

D = 2048
HEADS = 16
NOPE = 128
ROPE = 64
VDIM = 128
KV_RANK = 512
HE = 1408
TOPK = 6
LENGTH = 512
BLOCK = 256
SHARED_H = 2816
EXPERTS = 8
TOKENS = 4096
CAP = 432


def route_table(key):
    score_key, hot_key, offset_key, bias_key = jax.random.split(key, 4)
    blocks = TOKENS // LENGTH
    scores = jax.random.randint(score_key, (TOKENS, EXPERTS), 0, 4096)
    block_bias = jax.random.randint(bias_key, (blocks, EXPERTS), 0, 2048)
    hot_expert = jax.random.randint(hot_key, (blocks,), 0, EXPERTS)
    offset_draw = jax.random.randint(offset_key, (blocks,), 0, LENGTH)
    position = jnp.arange(TOKENS) % LENGTH
    block_of = jnp.arange(TOKENS) // LENGTH
    forced = (position + offset_draw[block_of]) % LENGTH < min(LENGTH, CAP + LENGTH // 8)
    columns = jnp.arange(EXPERTS)
    boost_value = jnp.where(forced[:, None] & (columns[None, :] == hot_expert[block_of][:, None]), 8192, 0)
    ranking = (scores + block_bias[block_of] + boost_value) * EXPERTS + columns[None, :]
    chosen_ids = lax.top_k(ranking, TOPK)[1].astype(jnp.int32)
    picked_onehot = (chosen_ids[:, :, None] == columns[None, None, :]).astype(jnp.int32).reshape(blocks, LENGTH * TOPK, EXPERTS)
    before = jnp.cumsum(picked_onehot, axis=1) - picked_onehot
    slot_number = jnp.sum(before * picked_onehot, axis=-1).reshape(TOKENS, TOPK)
    slot_number = jnp.where(slot_number < CAP, slot_number, CAP)
    return (chosen_ids, slot_number.astype(jnp.int32))


def draw_expert_ids(key, part):
    return route_table(key)[0]


def draw_slot_ids(key, part):
    return route_table(key)[1]


def spiked(values, own_key, source, target, parts, factor):
    owner, partner = [(jnp.arange(values.shape[dim]) // (values.shape[dim] // parts)).reshape([-1 if axis == dim else 1 for axis in range(values.ndim)]) for dim in (source, target)]
    chosen = jax.random.permutation(own_key, parts)[partner]
    strong = (owner == chosen) | (owner == (partner + parts // 2) % parts)
    return jnp.where(strong, factor * values, values)


def block_levels(rng, extent, cuts, least, top_value):
    gain = 1.0
    for dim, shards_of in cuts:
        heights = jax.random.uniform(jax.random.fold_in(jax.random.fold_in(rng, 6), dim), (shards_of,), jnp.float32, least / len(cuts), top_value / len(cuts))
        gain = gain * jnp.repeat(jnp.exp(heights), extent[dim] // shards_of).reshape((-1,) + (1,) * (len(extent) - 1 - dim))
    return gain


def bell_draw(stream_key, dims, deviation, most, shards=(), kind=jnp.bfloat16):
    entries = jax.random.normal(stream_key, dims, jnp.float32) * deviation
    if len(shards) > 0:
        entries = block_levels(stream_key, dims, shards, -0.22, 0.18) * entries
    return jnp.clip(entries, min=-most, max=most).astype(kind)


def gaussian_with(stream_key, dims, width, limit, cuts, heavy, kind=jnp.bfloat16):
    array = width * jax.random.normal(stream_key, dims, jnp.float32)
    if cuts:
        array = array * block_levels(stream_key, dims, cuts, -0.22, 0.18)
    return jnp.clip(spiked(array, jax.random.fold_in(stream_key, 3), *heavy), -limit, limit).astype(kind)


def setup_inputs(seed: int = 0) -> dict:
    key_of = jax.random.split(jax.random.key(seed), 17)
    inputs = gaussian_with(key_of[0], (TOKENS, D), 1.0, 6.0, ((0, 8),), (0, 1, 8, 2.0))
    gain_attn = jnp.clip(1.0 + 0.1 * jax.random.normal(key_of[1], (D,), jnp.float32), 0.5, 1.5)
    w_query = bell_draw(key_of[2], (D, HEADS * (NOPE + ROPE)), D ** -0.5, 0.125, ((1, 4),))
    w_latent = bell_draw(key_of[3], (D, KV_RANK + ROPE), D ** -0.5, 0.125)
    gain_latent = jnp.clip(1.0 + 0.1 * jax.random.normal(key_of[4], (KV_RANK,), jnp.float32), 0.5, 1.5)
    w_latent_up = bell_draw(key_of[5], (KV_RANK, HEADS * (NOPE + VDIM)), KV_RANK ** -0.5, 0.25, ((1, 4),))
    w_output = bell_draw(key_of[6], (HEADS * VDIM, D), (HEADS * VDIM // 16) ** -0.5, 0.5, ((0, 4),))
    gain_ffn = jnp.clip(1.0 + 0.1 * jax.random.normal(key_of[7], (D,), jnp.float32), 0.5, 1.5)
    w_router = bell_draw(key_of[8], (D, EXPERTS), (4 * D) ** -0.5, 0.0625, (), jnp.float32)
    w_shared_in = bell_draw(key_of[9], (2, D, SHARED_H), D ** -0.5, 0.125, ((2, 4),))
    w_shared_out = bell_draw(key_of[10], (SHARED_H, D), SHARED_H ** -0.5, 0.109375, ((0, 4),))
    w_expert_in = bell_draw(key_of[11], (EXPERTS, 2, D, HE), D ** -0.5, 0.125, ((0, 8), (3, 4)))
    w_expert_out = bell_draw(key_of[12], (EXPERTS, HE, D), (max(1, HE * TOPK * TOPK // (EXPERTS * EXPERTS))) ** -0.5, 0.21875, ((0, 8), (1, 4)))
    expert_ids = draw_expert_ids(jax.random.fold_in(key_of[16], 71), 0)
    slot_ids = draw_slot_ids(jax.random.fold_in(key_of[16], 71), 0)
    cotangent = gaussian_with(key_of[15], (TOKENS, D), 1.0, 6.0, ((0, 8),), (0, 1, 8, 2.0))
    return {"inputs": inputs, "gain_attn": gain_attn, "w_query": w_query, "w_latent": w_latent, "gain_latent": gain_latent, "w_latent_up": w_latent_up, "w_output": w_output, "gain_ffn": gain_ffn, "w_router": w_router, "w_shared_in": w_shared_in, "w_shared_out": w_shared_out, "w_expert_in": w_expert_in, "w_expert_out": w_expert_out, "expert_ids": expert_ids, "slot_ids": slot_ids, "cotangent": cotangent}


EPSILON = 1e-06
HIGHEST = lax.Precision.HIGHEST

@jax.custom_vjp
def low(v):
    return lax.optimization_barrier(v.astype(jnp.bfloat16)).astype(jnp.float32)

@jax.custom_vjp
def low_back(v):
    return v

def low_keep(v):
    return (low(v), None)

def low_pass(kept, grad):
    return (grad,)

def back_keep(v):
    return (v, None)

def back_low(kept, grad):
    return (low(grad),)
low.defvjp(low_keep, low_pass)
low_back.defvjp(back_keep, back_low)

def matmul(left, right):
    return jnp.dot(left, right, precision=HIGHEST, preferred_element_type=jnp.float32)

def rms_norm(vector, gain_vec):
    return vector * lax.rsqrt(lax.optimization_barrier(jnp.mean(vector * vector, axis=-1, keepdims=True)) + EPSILON) * gain_vec

def angles(length, rope_width):
    half_width = rope_width // 2
    position = jnp.arange(length, dtype=jnp.float32)
    inverse = jnp.exp(jnp.arange(half_width, dtype=jnp.float32) * (-math.log(10000.0) / half_width))
    angle_table = position[:, None] * inverse[None, :]
    return (jnp.cos(angle_table), jnp.sin(angle_table))

def rotate(values, cosine, sine_table):
    half_width = values.shape[-1] // 2
    front_part = values[..., :half_width]
    second = values[..., half_width:]
    return jnp.concatenate([front_part * cosine - second * sine_table, second * cosine + front_part * sine_table], axis=-1)

def silu(gate_val):
    return gate_val * jax.nn.sigmoid(gate_val)

def attend(pieces):
    query_rot, key_nope, key_rope, values = pieces
    score_scale = (NOPE + ROPE) ** (-0.5)
    nope_scores = jnp.einsum('qhd,khd->hqk', query_rot[..., :NOPE], key_nope, precision=HIGHEST)
    rope_scores = jnp.einsum('qhr,kr->hqk', query_rot[..., NOPE:], key_rope, precision=HIGHEST)
    scores = low_back((nope_scores + rope_scores) * score_scale)
    block_ids = jnp.arange(LENGTH) // BLOCK
    allowed = block_ids[None, :] <= block_ids[:, None]
    scores = jnp.where(allowed[None], scores, -1e+30)
    row_peak = lax.optimization_barrier(jnp.max(scores, axis=-1, keepdims=True))
    exp_scores = jnp.exp(scores - row_peak)
    attn_probs = low(exp_scores / lax.optimization_barrier(jnp.sum(exp_scores, axis=-1, keepdims=True)))
    return jnp.einsum('hqk,khd->qhd', attn_probs, values, precision=HIGHEST)

def forward(inputs, gain_attn, w_query, w_latent, gain_latent, w_latent_up, w_output, gain_ffn, w_router, w_shared_in, w_shared_out, w_expert_in, w_expert_out, expert_ids, slot_ids):
    sequences = TOKENS // LENGTH
    cosine, sine_table = angles(LENGTH, ROPE)
    cos_all = jnp.tile(cosine, (sequences, 1))
    sin_all = jnp.tile(sine_table, (sequences, 1))
    hidden_attn = low(rms_norm(inputs, gain_attn))
    query_raw = low_back(matmul(hidden_attn, w_query)).reshape(TOKENS, HEADS, NOPE + ROPE)
    query_rot = low(jnp.concatenate([query_raw[..., :NOPE], rotate(query_raw[..., NOPE:], cos_all[:, None], sin_all[:, None])], axis=-1))
    latent = low_back(matmul(hidden_attn, w_latent))
    latent_in = low(rms_norm(latent[:, :KV_RANK], gain_latent))
    key_rope = low(rotate(latent[:, KV_RANK:], cos_all, sin_all))
    key_value = low(low_back(matmul(latent_in, w_latent_up))).reshape(TOKENS, HEADS, NOPE + VDIM)
    pieces = (query_rot.reshape(sequences, LENGTH, HEADS, NOPE + ROPE), key_value[..., :NOPE].reshape(sequences, LENGTH, HEADS, NOPE), key_rope.reshape(sequences, LENGTH, ROPE), key_value[..., NOPE:].reshape(sequences, LENGTH, HEADS, VDIM))
    attended = lax.map(jax.checkpoint(attend), pieces).reshape(TOKENS, HEADS * VDIM)
    attended = low(low_back(attended))
    middle = inputs + low_back(matmul(attended, w_output))
    hidden_ffn = low(rms_norm(middle, gain_ffn))
    logits = matmul(hidden_ffn, w_router)
    row_peak = lax.optimization_barrier(jnp.max(logits, axis=-1, keepdims=True))
    exp_logits = jnp.exp(logits - row_peak)
    router_probs = exp_logits / lax.optimization_barrier(jnp.sum(exp_logits, axis=-1, keepdims=True))
    pair_gate = jnp.take_along_axis(router_probs, expert_ids, axis=1)
    token_index = jnp.arange(TOKENS, dtype=jnp.int32)
    block_of = token_index // LENGTH
    kept_pair = slot_ids < CAP
    place = jnp.where(kept_pair, (expert_ids * sequences + block_of[:, None]) * CAP + slot_ids, EXPERTS * sequences * CAP).astype(jnp.int32)
    owner_row = jnp.full((EXPERTS * sequences * CAP,), TOKENS, jnp.int32).at[place.reshape(-1)].set(jnp.repeat(token_index, TOPK), mode='drop')
    buffer = jnp.take(hidden_ffn, owner_row, axis=0, mode='fill', fill_value=0.0).reshape(EXPERTS, sequences * CAP, D)
    gate_up = low_back(jnp.einsum('end,egdh->engh', buffer, w_expert_in, precision=HIGHEST))
    activated = low(silu(gate_up[:, :, 0]) * gate_up[:, :, 1])
    expert_result = low_back(jnp.einsum('enh,ehd->end', activated, w_expert_out, precision=HIGHEST)).reshape(-1, D)
    picked_rows = jnp.take(expert_result, place, axis=0, mode='fill', fill_value=0.0)
    routed = lax.optimization_barrier(jnp.sum(pair_gate[..., None] * picked_rows, axis=1))
    shared_gate = low_back(matmul(hidden_ffn, w_shared_in[0]))
    shared_up = low_back(matmul(hidden_ffn, w_shared_in[1]))
    shared_act = low(silu(shared_gate) * shared_up)
    shared_result = low_back(matmul(shared_act, w_shared_out))
    return middle + shared_result + routed

def reference(inputs, gain_attn, w_query, w_latent, gain_latent, w_latent_up, w_output, gain_ffn, w_router, w_shared_in, w_shared_out, w_expert_in, w_expert_out, expert_ids, slot_ids, cotangent):
    floats = [array_in.astype(jnp.float32) for array_in in (inputs, gain_attn, w_query, w_latent, gain_latent, w_latent_up, w_output, gain_ffn, w_router, w_shared_in, w_shared_out, w_expert_in, w_expert_out)]

    def wrapped(*pieces):
        return forward(*pieces, expert_ids, slot_ids)
    result, pullback = jax.vjp(wrapped, *floats)
    gradients = pullback(cotangent.astype(jnp.float32))
    return (result.astype(jnp.bfloat16), gradients[0].astype(jnp.bfloat16), gradients[1], gradients[2], gradients[3], gradients[4], gradients[5], gradients[6], gradients[7], gradients[8], gradients[9], gradients[10], gradients[11], gradients[12])
```

```python
import math

import jax
import jax.numpy as jnp
from jax import lax
from jax.sharding import PartitionSpec as P

NOPE = 128
ROPE = 64
VDIM = 128
KV_RANK = 512
TOPK = 6
BLOCK = 256


EPSILON = 1e-06
HIGHEST = lax.Precision.HIGHEST


def angles(length, rope_width):
    half_width = rope_width // 2
    position = jnp.arange(length, dtype=jnp.float32)
    inverse = jnp.exp(jnp.arange(half_width, dtype=jnp.float32) * (-math.log(10000.0) / half_width))
    angle_table = position[:, None] * inverse[None, :]
    return (jnp.cos(angle_table), jnp.sin(angle_table))


def rotate(values, cosine, sine_table):
    half_width = values.shape[-1] // 2
    front_part = values[..., :half_width]
    second = values[..., half_width:]
    return jnp.concatenate(
        [front_part * cosine - second * sine_table, second * cosine + front_part * sine_table],
        axis=-1,
    )


def silu_parts(gate_val):
    sigmoid_val = jax.nn.sigmoid(gate_val)
    return (gate_val * sigmoid_val, sigmoid_val * (1.0 + gate_val * (1.0 - sigmoid_val)))


def norm_back(grad_norm, gain_vec, normed, inverse):
    scaled = grad_norm * gain_vec
    return inverse * (scaled - normed * jnp.mean(scaled * normed, axis=-1, keepdims=True))


def attention_scores(query_rot, key_nope, key_rope, score_scale, allowed):
    nope_scores = jnp.einsum(
        "qhd,khd->hqk", query_rot[..., :NOPE], key_nope, preferred_element_type=jnp.float32
    )
    rope_scores = jnp.einsum(
        "qhr,kr->hqk", query_rot[..., NOPE:], key_rope, preferred_element_type=jnp.float32
    )
    return jnp.where(allowed[None], (nope_scores + rope_scores) * score_scale, -1e30)


def expert_forward(received, w_expert_in, w_expert_out, sources):
    sectioned = received.reshape(sources, -1, received.shape[1], received.shape[2])
    gate_up = jnp.einsum(
        "secd,egdh->secgh", sectioned, w_expert_in, preferred_element_type=jnp.float32
    )
    gate_val, gate_slope = silu_parts(gate_up[..., 0, :])
    activated = (gate_val * gate_up[..., 1, :]).astype(jnp.bfloat16)
    produced = jnp.einsum(
        "sech,ehd->secd", activated, w_expert_out, preferred_element_type=jnp.float32
    )
    return (sectioned, gate_up, activated, produced.reshape(received.shape))


def body_slots(
    inputs,
    gain_attn,
    w_query,
    w_latent,
    gain_latent,
    w_latent_up,
    w_output,
    gain_ffn,
    w_router,
    w_shared_in,
    w_shared_out,
    w_expert_in,
    w_expert_out,
    expert_ids,
    slot_ids,
    cotangent,
):
    tokens, model_width = inputs.shape
    tp_count = lax.axis_size("tp")
    tp_index = lax.axis_index("tp")
    heads_here = w_output.shape[0] // VDIM
    experts = w_router.shape[1]
    local_experts = w_expert_in.shape[0]
    sources = experts // local_experts
    capacity = (9 * tokens * TOPK + 64 * experts - 1) // (64 * experts) * 8
    qk_width = NOPE + ROPE
    score_scale = qk_width ** (-0.5)
    rows_part = tokens // tp_count
    row_start = tp_index * rows_part
    resid = inputs.astype(jnp.float32)
    inv_first = lax.rsqrt(jnp.mean(resid * resid, axis=-1, keepdims=True) + EPSILON)
    normed_first = resid * inv_first
    hidden_attn = (normed_first * gain_attn).astype(jnp.bfloat16)
    cosine, sine_table = angles(tokens, ROPE)
    query_raw = jnp.dot(hidden_attn, w_query, preferred_element_type=jnp.float32).reshape(
        tokens, heads_here, qk_width
    )
    query_rot = jnp.concatenate(
        [
            query_raw[..., :NOPE],
            rotate(query_raw[..., NOPE:], cosine[:, None], sine_table[:, None]),
        ],
        axis=-1,
    ).astype(jnp.bfloat16)
    latent = jnp.dot(hidden_attn, w_latent, preferred_element_type=jnp.float32)
    compressed = latent[:, :KV_RANK]
    inv_latent = lax.rsqrt(jnp.mean(compressed * compressed, axis=-1, keepdims=True) + EPSILON)
    normed_latent = compressed * inv_latent
    latent_in = (normed_latent * gain_latent).astype(jnp.bfloat16)
    key_rope = rotate(latent[:, KV_RANK:], cosine, sine_table).astype(jnp.bfloat16)
    key_value = (
        jnp.dot(latent_in, w_latent_up, preferred_element_type=jnp.float32)
        .astype(jnp.bfloat16)
        .reshape(tokens, heads_here, NOPE + VDIM)
    )
    key_nope = key_value[..., :NOPE]
    values = key_value[..., NOPE:]
    block_ids = jnp.arange(tokens) // BLOCK
    allowed = block_ids[None, :] <= block_ids[:, None]
    scores = attention_scores(query_rot, key_nope, key_rope, score_scale, allowed)
    row_peak = jnp.max(scores, axis=-1, keepdims=True)
    exp_scores = jnp.exp(scores - row_peak)
    totals = jnp.sum(exp_scores, axis=-1, keepdims=True)
    attn_probs = exp_scores / totals
    log_total = row_peak + jnp.log(totals)
    attended = (
        jnp.einsum(
            "hqk,khd->qhd",
            attn_probs.astype(jnp.bfloat16),
            values,
            preferred_element_type=jnp.float32,
        )
        .astype(jnp.bfloat16)
        .reshape(tokens, heads_here * VDIM)
    )
    attn_full = lax.psum(
        jnp.dot(attended, w_output, preferred_element_type=jnp.float32).astype(jnp.bfloat16), "tp"
    ).astype(jnp.float32)
    middle = resid + attn_full
    inv_second = lax.rsqrt(jnp.mean(middle * middle, axis=-1, keepdims=True) + EPSILON)
    normed_second = middle * inv_second
    hidden_ffn = (normed_second * gain_ffn).astype(jnp.bfloat16)
    hidden_wide = hidden_ffn.astype(jnp.float32)
    logits = jnp.dot(hidden_wide, w_router, precision=HIGHEST, preferred_element_type=jnp.float32)
    logit_peak = jnp.max(logits, axis=-1, keepdims=True)
    exp_logits = jnp.exp(logits - logit_peak)
    router_probs = exp_logits / jnp.sum(exp_logits, axis=-1, keepdims=True)
    route_onehot = (
        expert_ids[:, :, None] == jnp.arange(experts, dtype=jnp.int32)[None, None, :]
    ).astype(jnp.float32)
    pair_gate = jnp.sum(route_onehot * router_probs[:, None, :], axis=-1)
    kept_pair = slot_ids < capacity
    flat_index = jnp.where(kept_pair, expert_ids * capacity + slot_ids, experts * capacity)
    row_numbers = jnp.broadcast_to(jnp.arange(tokens, dtype=jnp.int32)[:, None], (tokens, TOPK))
    owner_row = (
        jnp.full((experts * capacity,), tokens, jnp.int32)
        .at[flat_index.reshape(-1)]
        .set(row_numbers.reshape(-1), mode="drop")
    )
    outgoing = jnp.take(hidden_ffn, owner_row, axis=0, mode="fill", fill_value=0).reshape(
        experts, capacity, model_width
    )
    received = lax.all_to_all(outgoing, "ep", split_axis=0, concat_axis=0, tiled=True)
    sectioned, gate_up, activated, produced = expert_forward(
        received, w_expert_in, w_expert_out, sources
    )
    returned = lax.all_to_all(
        produced.astype(jnp.bfloat16), "ep", split_axis=0, concat_axis=0, tiled=True
    ).astype(produced.dtype)
    out_grad = cotangent.astype(jnp.float32)
    back_rows = returned.reshape(-1, model_width)
    combined = jnp.zeros((tokens, model_width), jnp.float32)
    gate_cols = []
    for pick_index in range(TOPK):
        taken_rows = jnp.take(
            back_rows, flat_index[:, pick_index], axis=0, mode="fill", fill_value=0.0
        )
        combined = combined + pair_gate[:, pick_index : pick_index + 1] * taken_rows
        gate_cols.append(jnp.sum(out_grad * taken_rows, axis=-1))
    gate_grad = jnp.stack(gate_cols, axis=1)
    shared_gate = jnp.dot(hidden_ffn, w_shared_in[0], preferred_element_type=jnp.float32)
    shared_up = jnp.dot(hidden_ffn, w_shared_in[1], preferred_element_type=jnp.float32)
    shared_val, shared_slope = silu_parts(shared_gate)
    shared_act = (shared_val * shared_up).astype(jnp.bfloat16)
    branch_part = jnp.dot(shared_act, w_shared_out, preferred_element_type=jnp.float32) + combined
    ffn_full = lax.psum(branch_part.astype(jnp.bfloat16), "tp").astype(jnp.float32)
    block_out = (middle + ffn_full).astype(jnp.bfloat16)
    slot_gate = (
        jnp.zeros((experts * capacity,), jnp.float32)
        .at[flat_index.reshape(-1)]
        .set(pair_gate.reshape(-1), mode="drop")
    )
    gathered_grad = jnp.take(cotangent, owner_row, axis=0, mode="fill", fill_value=0)
    slot_grad = (
        (slot_gate[:, None] * gathered_grad.astype(jnp.float32))
        .astype(jnp.bfloat16)
        .reshape(experts, capacity, model_width)
    )
    grad_arrived = lax.all_to_all(slot_grad, "ep", split_axis=0, concat_axis=0, tiled=True).reshape(
        sectioned.shape
    )
    act_grad = jnp.einsum(
        "secd,ehd->sech", grad_arrived, w_expert_out, preferred_element_type=jnp.float32
    )
    gate_val, gate_slope = silu_parts(gate_up[..., 0, :])
    up_val = gate_up[..., 1, :]
    gu_grad = jnp.stack([act_grad * up_val * gate_slope, act_grad * gate_val], axis=-2).astype(
        jnp.bfloat16
    )
    grad_expert_out = jnp.einsum(
        "sech,secd->ehd", activated, grad_arrived, preferred_element_type=jnp.float32
    )
    grad_expert_in = jnp.einsum(
        "secd,secgh->egdh", sectioned, gu_grad, preferred_element_type=jnp.float32
    )
    rows_grad = jnp.einsum(
        "secgh,egdh->secd", gu_grad, w_expert_in, preferred_element_type=jnp.float32
    ).reshape(received.shape)
    returned_grad = (
        lax.all_to_all(
            rows_grad.astype(jnp.bfloat16), "ep", split_axis=0, concat_axis=0, tiled=True
        )
        .astype(rows_grad.dtype)
        .reshape(-1, model_width)
    )
    routed_grad = jnp.zeros((tokens, model_width), jnp.float32)
    for pick_index in range(TOPK):
        routed_grad = routed_grad + jnp.take(
            returned_grad, flat_index[:, pick_index], axis=0, mode="fill", fill_value=0.0
        )
    shared_act_grad = jnp.einsum(
        "td,fd->tf", cotangent, w_shared_out, preferred_element_type=jnp.float32
    )
    shared_gate_grad = (shared_act_grad * shared_up * shared_slope).astype(jnp.bfloat16)
    shared_up_grad = (shared_act_grad * shared_val).astype(jnp.bfloat16)
    shared_out_grad = jnp.einsum(
        "tf,td->fd", shared_act, cotangent, preferred_element_type=jnp.float32
    )
    shared_in_grad = jnp.stack(
        [
            jnp.einsum(
                "td,tf->df", hidden_ffn, shared_gate_grad, preferred_element_type=jnp.float32
            ),
            jnp.einsum("td,tf->df", hidden_ffn, shared_up_grad, preferred_element_type=jnp.float32),
        ],
        axis=0,
    )
    shared_back = jnp.einsum(
        "tf,df->td", shared_gate_grad, w_shared_in[0], preferred_element_type=jnp.float32
    ) + jnp.einsum("tf,df->td", shared_up_grad, w_shared_in[1], preferred_element_type=jnp.float32)
    prob_grad = jnp.sum(route_onehot * gate_grad[:, :, None], axis=1)
    logit_grad = router_probs * (
        prob_grad - jnp.sum(router_probs * prob_grad, axis=-1, keepdims=True)
    )
    router_back = jnp.einsum(
        "te,de->td", logit_grad, w_router, precision=HIGHEST, preferred_element_type=jnp.float32
    )
    router_grad = jnp.einsum(
        "td,te->de", hidden_wide, logit_grad, precision=HIGHEST, preferred_element_type=jnp.float32
    )
    ffn_grad = lax.psum(
        (shared_back + routed_grad + router_back).astype(jnp.bfloat16), "tp"
    ).astype(jnp.float32)
    middle_grad = out_grad + norm_back(ffn_grad, gain_ffn, normed_second, inv_second)
    gain_ffn_grad = jnp.sum(
        lax.dynamic_slice_in_dim(ffn_grad * normed_second, row_start, rows_part, 0), axis=0
    )
    branch_grad = middle_grad.astype(jnp.bfloat16)
    output_w_grad = jnp.einsum(
        "tf,td->fd", attended, branch_grad, preferred_element_type=jnp.float32
    )
    attended_grad = (
        jnp.einsum("td,fd->tf", branch_grad, w_output, preferred_element_type=jnp.float32)
        .astype(jnp.bfloat16)
        .reshape(tokens, heads_here, VDIM)
    )
    scores_again = attention_scores(query_rot, key_nope, key_rope, score_scale, allowed)
    probs_again = jnp.exp(scores_again - log_total)
    values_grad = jnp.einsum(
        "hqk,qhd->khd",
        probs_again.astype(jnp.bfloat16),
        attended_grad,
        preferred_element_type=jnp.float32,
    )
    prob_part = jnp.einsum(
        "qhd,khd->hqk", attended_grad, values, preferred_element_type=jnp.float32
    )
    score_grad = (
        probs_again * (prob_part - jnp.sum(probs_again * prob_part, axis=-1, keepdims=True))
    ).astype(jnp.bfloat16)
    query_nope_grad = (
        jnp.einsum("hqk,khd->qhd", score_grad, key_nope, preferred_element_type=jnp.float32)
        * score_scale
    )
    query_rope_grad = (
        jnp.einsum("hqk,kr->qhr", score_grad, key_rope, preferred_element_type=jnp.float32)
        * score_scale
    )
    key_nope_grad = (
        jnp.einsum(
            "hqk,qhd->khd", score_grad, query_rot[..., :NOPE], preferred_element_type=jnp.float32
        )
        * score_scale
    )
    key_rope_grad = (
        jnp.einsum(
            "hqk,qhr->kr", score_grad, query_rot[..., NOPE:], preferred_element_type=jnp.float32
        )
        * score_scale
    )
    kv_grad = (
        jnp.concatenate([key_nope_grad, values_grad], axis=-1)
        .astype(jnp.bfloat16)
        .reshape(tokens, heads_here * (NOPE + VDIM))
    )
    latent_up_grad = jnp.einsum("tr,tf->rf", latent_in, kv_grad, preferred_element_type=jnp.float32)
    latent_in_grad = jnp.einsum(
        "tf,rf->tr", kv_grad, w_latent_up, preferred_element_type=jnp.float32
    )
    gain_latent_grad = jnp.sum(latent_in_grad * normed_latent, axis=0)
    latent_grad_part = jnp.concatenate(
        [
            norm_back(latent_in_grad, gain_latent, normed_latent, inv_latent),
            rotate(key_rope_grad, cosine, -sine_table),
        ],
        axis=-1,
    )
    query_grad = (
        jnp.concatenate(
            [query_nope_grad, rotate(query_rope_grad, cosine[:, None], -sine_table[:, None])],
            axis=-1,
        )
        .astype(jnp.bfloat16)
        .reshape(tokens, heads_here * qk_width)
    )
    query_w_grad = jnp.einsum(
        "td,tf->df", hidden_attn, query_grad, preferred_element_type=jnp.float32
    )
    hidden_part = jnp.einsum("tf,df->td", query_grad, w_query, preferred_element_type=jnp.float32)
    hidden_sum, latent_sum = (
        lax.psum(hidden_part.astype(jnp.bfloat16), "tp").astype(jnp.float32),
        lax.psum(latent_grad_part.astype(jnp.bfloat16), "tp").astype(jnp.float32),
    )
    latent_low = latent_sum.astype(jnp.bfloat16)
    attn_in_grad = hidden_sum + jnp.einsum(
        "tf,df->td", latent_low, w_latent, preferred_element_type=jnp.float32
    )
    latent_w_grad = jnp.einsum(
        "td,tf->df",
        lax.dynamic_slice_in_dim(hidden_attn, row_start, rows_part, 0),
        lax.dynamic_slice_in_dim(latent_low, row_start, rows_part, 0),
        preferred_element_type=jnp.float32,
    )
    gain_attn_grad = jnp.sum(
        lax.dynamic_slice_in_dim(attn_in_grad * normed_first, row_start, rows_part, 0), axis=0
    )
    grad_inputs = (
        middle_grad + norm_back(attn_in_grad, gain_attn, normed_first, inv_first)
    ).astype(jnp.bfloat16)
    grad_query, grad_latent_up, grad_output, grad_shared_in, grad_shared_out = (
        lax.psum_scatter(
            query_w_grad.astype(jnp.bfloat16), "ep", scatter_dimension=0, tiled=True
        ).astype(jnp.float32),
        lax.psum_scatter(
            latent_up_grad.astype(jnp.bfloat16), "ep", scatter_dimension=0, tiled=True
        ).astype(jnp.float32),
        lax.psum_scatter(
            output_w_grad.astype(jnp.bfloat16), "ep", scatter_dimension=1, tiled=True
        ).astype(jnp.float32),
        lax.psum_scatter(
            shared_in_grad.astype(jnp.bfloat16), "ep", scatter_dimension=1, tiled=True
        ).astype(jnp.float32),
        lax.psum_scatter(
            shared_out_grad.astype(jnp.bfloat16), "ep", scatter_dimension=1, tiled=True
        ).astype(jnp.float32),
    )
    grad_latent, grad_gain_latent, grad_gain_attn, grad_gain_ffn, grad_router = (
        lax.psum_scatter(latent_w_grad, ("ep", "tp"), scatter_dimension=0, tiled=True),
        lax.psum_scatter(gain_latent_grad, ("ep", "tp"), scatter_dimension=0, tiled=True),
        lax.psum_scatter(gain_attn_grad, ("ep", "tp"), scatter_dimension=0, tiled=True),
        lax.psum_scatter(gain_ffn_grad, ("ep", "tp"), scatter_dimension=0, tiled=True),
        lax.psum_scatter(router_grad, ("ep", "tp"), scatter_dimension=0, tiled=True),
    )
    return (
        block_out,
        grad_inputs,
        grad_gain_attn,
        grad_query,
        grad_latent,
        grad_gain_latent,
        grad_latent_up,
        grad_output,
        grad_gain_ffn,
        grad_router,
        grad_shared_in,
        grad_shared_out,
        grad_expert_in,
        grad_expert_out,
    )


def padded_hidden(routed, shared):
    return -(-(routed + shared + 24) // 128) * 128


def split_wide(values):
    high = values.astype(jnp.bfloat16)
    rest = values - high.astype(jnp.float32)
    mid = rest.astype(jnp.bfloat16)
    low = (rest - mid.astype(jnp.float32)).astype(jnp.bfloat16)
    return (high, mid, low)


def body_dense(
    inputs,
    gain_attn,
    w_query,
    w_latent,
    gain_latent,
    w_latent_up,
    w_output,
    gain_ffn,
    w_router,
    w_shared_in,
    w_shared_out,
    w_expert_in,
    w_expert_out,
    expert_ids,
    slot_ids,
    cotangent,
):
    f32, bf16 = jnp.float32, jnp.bfloat16
    tokens, model_width = inputs.shape
    ep_count, tp_count = lax.axis_size("ep"), lax.axis_size("tp")
    ep_index, tp_index = lax.axis_index("ep"), lax.axis_index("tp")
    heads_here = w_output.shape[0] // VDIM
    experts = w_router.shape[1]
    capacity = (9 * tokens * TOPK + 64 * experts - 1) // (64 * experts) * 8
    qk_width = NOPE + ROPE
    score_scale = qk_width ** (-0.5)
    rows_part = tokens // tp_count
    row_start = tp_index * rows_part
    every = ("ep", "tp")

    expert_range = jnp.arange(experts, dtype=jnp.int32)
    kept = jnp.any(
        (expert_ids[:, :, None] == expert_range) & (slot_ids < capacity)[:, :, None], axis=1
    ).astype(f32)
    kept_here = lax.all_to_all(kept, "ep", split_axis=1, concat_axis=0, tiled=True)
    cot_all = lax.all_gather(cotangent, "ep", tiled=True)

    routed = w_expert_in.shape[3]
    shared = w_shared_in.shape[2] // ep_count
    hidden = padded_hidden(routed, shared)
    shared_start = ep_index * shared
    shared_in = lax.dynamic_slice_in_dim(w_shared_in, shared_start, shared, 2)
    shared_out = lax.dynamic_slice_in_dim(w_shared_out, shared_start, shared, 0)
    router_parts = jnp.concatenate(split_wide(w_router), axis=1)
    fill = hidden - routed - shared
    w_in = jnp.concatenate(
        [
            w_expert_in[0, 0],
            shared_in[0],
            jnp.pad(router_parts, ((0, 0), (0, fill - router_parts.shape[1]))),
            w_expert_in[0, 1],
            shared_in[1],
            jnp.zeros((model_width, fill), bf16),
        ],
        axis=1,
    )
    w_out = jnp.concatenate(
        [w_expert_out[0], shared_out, jnp.zeros((fill, model_width), bf16)], axis=0
    )

    resid = inputs.astype(f32)
    inv_first = lax.rsqrt(jnp.mean(resid * resid, axis=-1, keepdims=True) + EPSILON)
    normed_first = resid * inv_first
    hidden_attn = (normed_first * gain_attn).astype(bf16)
    cosine, sine_table = angles(tokens, ROPE)
    query_raw = jnp.dot(hidden_attn, w_query, preferred_element_type=f32).reshape(
        tokens, heads_here, qk_width
    )
    query_rot = jnp.concatenate(
        [
            query_raw[..., :NOPE],
            rotate(query_raw[..., NOPE:], cosine[:, None], sine_table[:, None]),
        ],
        axis=-1,
    ).astype(bf16)
    latent = jnp.dot(hidden_attn, w_latent, preferred_element_type=f32)
    compressed = latent[:, :KV_RANK]
    inv_latent = lax.rsqrt(jnp.mean(compressed * compressed, axis=-1, keepdims=True) + EPSILON)
    normed_latent = compressed * inv_latent
    latent_in = (normed_latent * gain_latent).astype(bf16)
    key_rope = rotate(latent[:, KV_RANK:], cosine, sine_table).astype(bf16)
    key_value = (
        jnp.dot(latent_in, w_latent_up, preferred_element_type=f32)
        .astype(bf16)
        .reshape(tokens, heads_here, NOPE + VDIM)
    )
    key_nope = key_value[..., :NOPE]
    values = key_value[..., NOPE:]
    block_ids = jnp.arange(tokens) // BLOCK
    allowed = block_ids[None, :] <= block_ids[:, None]
    scores = attention_scores(query_rot, key_nope, key_rope, score_scale, allowed)
    row_peak = jnp.max(scores, axis=-1, keepdims=True)
    exp_scores = jnp.exp(scores - row_peak)
    totals = jnp.sum(exp_scores, axis=-1, keepdims=True)
    attn_probs = exp_scores / totals
    log_total = row_peak + jnp.log(totals)
    attended = (
        jnp.einsum("hqk,khd->qhd", attn_probs.astype(bf16), values, preferred_element_type=f32)
        .astype(bf16)
        .reshape(tokens, heads_here * VDIM)
    )
    attn_part = jnp.dot(attended, w_output, preferred_element_type=f32).astype(bf16)

    attn_rows = lax.psum_scatter(attn_part, "tp", scatter_dimension=0, tiled=True).astype(f32)
    resid_rows = lax.dynamic_slice_in_dim(resid, row_start, rows_part, 0)
    cot_rows = lax.dynamic_slice_in_dim(cotangent, row_start, rows_part, 0).astype(f32)
    middle = resid_rows + attn_rows
    inv_second = lax.rsqrt(jnp.mean(middle * middle, axis=-1, keepdims=True) + EPSILON)
    normed_second = middle * inv_second
    hidden_rows = (normed_second * gain_ffn).astype(bf16)
    hidden_all = lax.all_gather(hidden_rows, every, tiled=True)

    gate_up = jnp.dot(hidden_all, w_in, preferred_element_type=f32)
    gate_val, up_val = gate_up[:, :hidden], gate_up[:, hidden:]
    base = routed + shared
    logits = (
        gate_val[:, base : base + experts]
        + gate_val[:, base + experts : base + 2 * experts]
        + gate_val[:, base + 2 * experts : base + 3 * experts]
    )
    exp_logits = jnp.exp(logits - jnp.max(logits, axis=-1, keepdims=True))
    router_probs = exp_logits / jnp.sum(exp_logits, axis=-1, keepdims=True)
    here = (expert_range == ep_index).astype(f32)[None]
    prob_here = jnp.sum(router_probs * here, axis=-1, keepdims=True)
    unit_index = jnp.arange(hidden)[None]
    is_routed = unit_index < routed
    unit_gate = jnp.where(is_routed, prob_here * kept_here, 1.0)
    silu_val, silu_slope = silu_parts(gate_val)
    activated = silu_val * up_val
    gated = (activated * unit_gate).astype(bf16)
    out_part = jnp.dot(gated, w_out, preferred_element_type=f32).astype(bf16)
    act_grad = jnp.einsum("td,fd->tf", cot_all, w_out, preferred_element_type=f32)
    pair_grad = (
        jnp.sum(jnp.where(is_routed, activated * act_grad, 0.0), axis=-1, keepdims=True) * kept_here
    )
    logit_grad = pair_grad * prob_here * (here - router_probs)
    act_grad = act_grad * unit_gate
    gate_grad = (act_grad * up_val * silu_slope).astype(bf16)
    up_grad = (act_grad * silu_val).astype(bf16)
    rows_grad = (
        jnp.einsum("tf,df->td", gate_grad, w_in[:, :hidden], preferred_element_type=f32)
        + jnp.einsum("tf,df->td", up_grad, w_in[:, hidden:], preferred_element_type=f32)
        + jnp.einsum(
            "te,de->td", logit_grad, w_router, precision=HIGHEST, preferred_element_type=f32
        )
    ).astype(bf16)
    out_grad_w = jnp.einsum("tf,td->fd", gated, cot_all, preferred_element_type=f32)
    in_grad_gate = jnp.einsum("td,tf->df", hidden_all, gate_grad, preferred_element_type=f32)
    in_grad_up = jnp.einsum("td,tf->df", hidden_all, up_grad, preferred_element_type=f32)
    router_grad = jnp.einsum(
        "td,te->de",
        hidden_all.astype(f32),
        logit_grad,
        precision=HIGHEST,
        preferred_element_type=f32,
    )
    grad_expert_in = jnp.stack([in_grad_gate[:, :routed], in_grad_up[:, :routed]])[None]
    grad_expert_out = out_grad_w[None, :routed]
    shared_in_part = jnp.stack([in_grad_gate[:, routed:base], in_grad_up[:, routed:base]])
    grad_shared_in = lax.all_to_all(
        shared_in_part.astype(bf16), "ep", split_axis=1, concat_axis=2, tiled=True
    ).astype(f32)
    grad_shared_out = lax.all_to_all(
        out_grad_w[routed:base].astype(bf16), "ep", split_axis=1, concat_axis=0, tiled=True
    ).astype(f32)

    def sum_rows(part):
        plane = lax.psum_scatter(part, "ep", scatter_dimension=0, tiled=True)
        return lax.psum_scatter(plane, "tp", scatter_dimension=0, tiled=True).astype(f32)

    ffn_grad = sum_rows(rows_grad)
    ffn_rows = sum_rows(out_part)
    block_out = lax.all_gather((middle + ffn_rows).astype(bf16), "tp", tiled=True)
    middle_grad = cot_rows + norm_back(ffn_grad, gain_ffn, normed_second, inv_second)
    gain_ffn_grad = jnp.sum(ffn_grad * normed_second, axis=0)
    branch_grad = lax.all_gather(middle_grad.astype(bf16), "tp", tiled=True)

    output_w_grad = jnp.einsum("tf,td->fd", attended, branch_grad, preferred_element_type=f32)
    attended_grad = (
        jnp.einsum("td,fd->tf", branch_grad, w_output, preferred_element_type=f32)
        .astype(bf16)
        .reshape(tokens, heads_here, VDIM)
    )
    scores_again = attention_scores(query_rot, key_nope, key_rope, score_scale, allowed)
    probs_again = jnp.exp(scores_again - log_total)
    values_grad = jnp.einsum(
        "hqk,qhd->khd", probs_again.astype(bf16), attended_grad, preferred_element_type=f32
    )
    prob_part = jnp.einsum("qhd,khd->hqk", attended_grad, values, preferred_element_type=f32)
    score_grad = (
        probs_again * (prob_part - jnp.sum(probs_again * prob_part, axis=-1, keepdims=True))
    ).astype(bf16)
    query_nope_grad = (
        jnp.einsum("hqk,khd->qhd", score_grad, key_nope, preferred_element_type=f32) * score_scale
    )
    query_rope_grad = (
        jnp.einsum("hqk,kr->qhr", score_grad, key_rope, preferred_element_type=f32) * score_scale
    )
    key_nope_grad = (
        jnp.einsum("hqk,qhd->khd", score_grad, query_rot[..., :NOPE], preferred_element_type=f32)
        * score_scale
    )
    key_rope_grad = (
        jnp.einsum("hqk,qhr->kr", score_grad, query_rot[..., NOPE:], preferred_element_type=f32)
        * score_scale
    )
    kv_grad = (
        jnp.concatenate([key_nope_grad, values_grad], axis=-1)
        .astype(bf16)
        .reshape(tokens, heads_here * (NOPE + VDIM))
    )
    latent_up_grad = jnp.einsum("tr,tf->rf", latent_in, kv_grad, preferred_element_type=f32)
    latent_in_grad = jnp.einsum("tf,rf->tr", kv_grad, w_latent_up, preferred_element_type=f32)
    gain_latent_grad = jnp.sum(latent_in_grad * normed_latent, axis=0)
    latent_grad_part = jnp.concatenate(
        [
            norm_back(latent_in_grad, gain_latent, normed_latent, inv_latent),
            rotate(key_rope_grad, cosine, -sine_table),
        ],
        axis=-1,
    ).astype(bf16)
    query_grad = (
        jnp.concatenate(
            [query_nope_grad, rotate(query_rope_grad, cosine[:, None], -sine_table[:, None])],
            axis=-1,
        )
        .astype(bf16)
        .reshape(tokens, heads_here * qk_width)
    )
    query_w_grad = jnp.einsum("td,tf->df", hidden_attn, query_grad, preferred_element_type=f32)
    hidden_part = (
        jnp.einsum("tf,df->td", query_grad, w_query, preferred_element_type=f32)
        + jnp.einsum("tf,df->td", latent_grad_part, w_latent, preferred_element_type=f32)
    ).astype(bf16)
    attn_in_grad = lax.psum_scatter(hidden_part, "tp", scatter_dimension=0, tiled=True).astype(f32)
    latent_w_grad = jnp.einsum(
        "td,tf->df", hidden_attn, latent_grad_part, preferred_element_type=f32
    )
    normed_rows = lax.dynamic_slice_in_dim(normed_first, row_start, rows_part, 0)
    inv_rows = lax.dynamic_slice_in_dim(inv_first, row_start, rows_part, 0)
    gain_attn_grad = jnp.sum(attn_in_grad * normed_rows, axis=0)
    grad_inputs = lax.all_gather(
        (middle_grad + norm_back(attn_in_grad, gain_attn, normed_rows, inv_rows)).astype(bf16),
        "tp",
        tiled=True,
    )
    grad_query, grad_latent_up, grad_output = (
        lax.psum_scatter(
            query_w_grad.astype(bf16), "ep", scatter_dimension=0, tiled=True
        ).astype(f32),
        lax.psum_scatter(
            latent_up_grad.astype(bf16), "ep", scatter_dimension=0, tiled=True
        ).astype(f32),
        lax.psum_scatter(
            output_w_grad.astype(bf16), "ep", scatter_dimension=1, tiled=True
        ).astype(f32),
    )

    def sum_all(part):
        plane = lax.psum_scatter(part, "ep", scatter_dimension=0, tiled=True)
        return lax.psum_scatter(plane, "tp", scatter_dimension=0, tiled=True)

    grad_latent, grad_gain_latent, grad_gain_attn, grad_gain_ffn, grad_router = (
        sum_all(latent_w_grad),
        sum_all(gain_latent_grad),
        sum_all(gain_attn_grad),
        sum_all(gain_ffn_grad),
        sum_all(router_grad),
    )
    return (
        block_out,
        grad_inputs,
        grad_gain_attn,
        grad_query,
        grad_latent,
        grad_gain_latent,
        grad_latent_up,
        grad_output,
        grad_gain_ffn,
        grad_router,
        grad_shared_in,
        grad_shared_out,
        grad_expert_in,
        grad_expert_out,
    )


def solution(mesh):
    body = body_dense if mesh.shape["ep"] == 8 else body_slots
    placed = (
        P("ep", None),
        P(),
        P(None, "tp"),
        P(),
        P(),
        P(None, "tp"),
        P("tp", None),
        P(),
        P(),
        P(None, None, "tp"),
        P("tp", None),
        P("ep", None, None, "tp"),
        P("ep", "tp", None),
        P("ep", None),
        P("ep", None),
        P("ep", None),
    )
    return jax.shard_map(
        body,
        mesh=mesh,
        in_specs=placed,
        out_specs=(
            P("ep", None),
            P("ep", None),
            P(("ep", "tp")),
            P("ep", "tp"),
            P(("ep", "tp"), None),
            P(("ep", "tp")),
            P("ep", "tp"),
            P("tp", "ep"),
            P(("ep", "tp")),
            P(("ep", "tp"), None),
            P(None, "ep", "tp"),
            P("tp", "ep"),
            P("ep", None, None, "tp"),
            P("ep", "tp", None),
        ),
        check_vma=False,
    )
```

```python
import functools
import math

import jax
import jax.numpy as jnp
from jax import lax
from jax.experimental import pallas as pl
from jax.experimental.pallas import tpu as pltpu
from jax.sharding import PartitionSpec as P

NOPE = 128
ROPE = 64
VDIM = 128
KV_RANK = 512
TOPK = 6
BLOCK = 256


EPSILON = 1e-06
HIGHEST = lax.Precision.HIGHEST


def angles(length, rope_width):
    half_width = rope_width // 2
    position = jnp.arange(length, dtype=jnp.float32)
    inverse = jnp.exp(jnp.arange(half_width, dtype=jnp.float32) * (-math.log(10000.0) / half_width))
    angle_table = position[:, None] * inverse[None, :]
    return (jnp.cos(angle_table), jnp.sin(angle_table))


def rotate(values, cosine, sine_table):
    half_width = values.shape[-1] // 2
    front_part = values[..., :half_width]
    second = values[..., half_width:]
    return jnp.concatenate(
        [front_part * cosine - second * sine_table, second * cosine + front_part * sine_table],
        axis=-1,
    )


def silu_parts(gate_val):
    sigmoid_val = jax.nn.sigmoid(gate_val)
    return (gate_val * sigmoid_val, sigmoid_val * (1.0 + gate_val * (1.0 - sigmoid_val)))


def norm_back(grad_norm, gain_vec, normed, inverse):
    scaled = grad_norm * gain_vec
    return inverse * (scaled - normed * jnp.mean(scaled * normed, axis=-1, keepdims=True))


def attention_scores(query_rot, key_nope, key_rope, score_scale, allowed):
    nope_scores = jnp.einsum(
        "qhd,khd->hqk", query_rot[..., :NOPE], key_nope, preferred_element_type=jnp.float32
    )
    rope_scores = jnp.einsum(
        "qhr,kr->hqk", query_rot[..., NOPE:], key_rope, preferred_element_type=jnp.float32
    )
    return jnp.where(allowed[None], (nope_scores + rope_scores) * score_scale, -1e30)


def expert_forward(received, w_expert_in, w_expert_out, sources):
    sectioned = received.reshape(sources, -1, received.shape[1], received.shape[2])
    gate_up = jnp.einsum(
        "secd,egdh->secgh", sectioned, w_expert_in, preferred_element_type=jnp.float32
    )
    gate_val, gate_slope = silu_parts(gate_up[..., 0, :])
    activated = (gate_val * gate_up[..., 1, :]).astype(jnp.bfloat16)
    produced = jnp.einsum(
        "sech,ehd->secd", activated, w_expert_out, preferred_element_type=jnp.float32
    )
    return (sectioned, gate_up, activated, produced.reshape(received.shape))


def body_slots(
    inputs,
    gain_attn,
    w_query,
    w_latent,
    gain_latent,
    w_latent_up,
    w_output,
    gain_ffn,
    w_router,
    w_shared_in,
    w_shared_out,
    w_expert_in,
    w_expert_out,
    expert_ids,
    slot_ids,
    cotangent,
):
    tokens, model_width = inputs.shape
    tp_count = lax.axis_size("tp")
    tp_index = lax.axis_index("tp")
    heads_here = w_output.shape[0] // VDIM
    experts = w_router.shape[1]
    local_experts = w_expert_in.shape[0]
    sources = experts // local_experts
    capacity = (9 * tokens * TOPK + 64 * experts - 1) // (64 * experts) * 8
    qk_width = NOPE + ROPE
    score_scale = qk_width ** (-0.5)
    rows_part = tokens // tp_count
    row_start = tp_index * rows_part
    resid = inputs.astype(jnp.float32)
    inv_first = lax.rsqrt(jnp.mean(resid * resid, axis=-1, keepdims=True) + EPSILON)
    normed_first = resid * inv_first
    hidden_attn = (normed_first * gain_attn).astype(jnp.bfloat16)
    cosine, sine_table = angles(tokens, ROPE)
    query_raw = jnp.dot(hidden_attn, w_query, preferred_element_type=jnp.float32).reshape(
        tokens, heads_here, qk_width
    )
    query_rot = jnp.concatenate(
        [
            query_raw[..., :NOPE],
            rotate(query_raw[..., NOPE:], cosine[:, None], sine_table[:, None]),
        ],
        axis=-1,
    ).astype(jnp.bfloat16)
    latent = jnp.dot(hidden_attn, w_latent, preferred_element_type=jnp.float32)
    compressed = latent[:, :KV_RANK]
    inv_latent = lax.rsqrt(jnp.mean(compressed * compressed, axis=-1, keepdims=True) + EPSILON)
    normed_latent = compressed * inv_latent
    latent_in = (normed_latent * gain_latent).astype(jnp.bfloat16)
    key_rope = rotate(latent[:, KV_RANK:], cosine, sine_table).astype(jnp.bfloat16)
    key_value = (
        jnp.dot(latent_in, w_latent_up, preferred_element_type=jnp.float32)
        .astype(jnp.bfloat16)
        .reshape(tokens, heads_here, NOPE + VDIM)
    )
    key_nope = key_value[..., :NOPE]
    values = key_value[..., NOPE:]
    block_ids = jnp.arange(tokens) // BLOCK
    allowed = block_ids[None, :] <= block_ids[:, None]
    scores = attention_scores(query_rot, key_nope, key_rope, score_scale, allowed)
    row_peak = jnp.max(scores, axis=-1, keepdims=True)
    exp_scores = jnp.exp(scores - row_peak)
    totals = jnp.sum(exp_scores, axis=-1, keepdims=True)
    attn_probs = exp_scores / totals
    log_total = row_peak + jnp.log(totals)
    attended = (
        jnp.einsum(
            "hqk,khd->qhd",
            attn_probs.astype(jnp.bfloat16),
            values,
            preferred_element_type=jnp.float32,
        )
        .astype(jnp.bfloat16)
        .reshape(tokens, heads_here * VDIM)
    )
    attn_full = lax.psum(
        jnp.dot(attended, w_output, preferred_element_type=jnp.float32).astype(jnp.bfloat16), "tp"
    ).astype(jnp.float32)
    middle = resid + attn_full
    inv_second = lax.rsqrt(jnp.mean(middle * middle, axis=-1, keepdims=True) + EPSILON)
    normed_second = middle * inv_second
    hidden_ffn = (normed_second * gain_ffn).astype(jnp.bfloat16)
    hidden_wide = hidden_ffn.astype(jnp.float32)
    logits = jnp.dot(hidden_wide, w_router, precision=HIGHEST, preferred_element_type=jnp.float32)
    logit_peak = jnp.max(logits, axis=-1, keepdims=True)
    exp_logits = jnp.exp(logits - logit_peak)
    router_probs = exp_logits / jnp.sum(exp_logits, axis=-1, keepdims=True)
    route_onehot = (
        expert_ids[:, :, None] == jnp.arange(experts, dtype=jnp.int32)[None, None, :]
    ).astype(jnp.float32)
    pair_gate = jnp.sum(route_onehot * router_probs[:, None, :], axis=-1)
    kept_pair = slot_ids < capacity
    flat_index = jnp.where(kept_pair, expert_ids * capacity + slot_ids, experts * capacity)
    row_numbers = jnp.broadcast_to(jnp.arange(tokens, dtype=jnp.int32)[:, None], (tokens, TOPK))
    owner_row = (
        jnp.full((experts * capacity,), tokens, jnp.int32)
        .at[flat_index.reshape(-1)]
        .set(row_numbers.reshape(-1), mode="drop")
    )
    outgoing = jnp.take(hidden_ffn, owner_row, axis=0, mode="fill", fill_value=0).reshape(
        experts, capacity, model_width
    )
    received = lax.all_to_all(outgoing, "ep", split_axis=0, concat_axis=0, tiled=True)
    sectioned, gate_up, activated, produced = expert_forward(
        received, w_expert_in, w_expert_out, sources
    )
    returned = lax.all_to_all(
        produced.astype(jnp.bfloat16), "ep", split_axis=0, concat_axis=0, tiled=True
    ).astype(produced.dtype)
    out_grad = cotangent.astype(jnp.float32)
    back_rows = returned.reshape(-1, model_width)
    combined = jnp.zeros((tokens, model_width), jnp.float32)
    gate_cols = []
    for pick_index in range(TOPK):
        taken_rows = jnp.take(
            back_rows, flat_index[:, pick_index], axis=0, mode="fill", fill_value=0.0
        )
        combined = combined + pair_gate[:, pick_index : pick_index + 1] * taken_rows
        gate_cols.append(jnp.sum(out_grad * taken_rows, axis=-1))
    gate_grad = jnp.stack(gate_cols, axis=1)
    shared_gate = jnp.dot(hidden_ffn, w_shared_in[0], preferred_element_type=jnp.float32)
    shared_up = jnp.dot(hidden_ffn, w_shared_in[1], preferred_element_type=jnp.float32)
    shared_val, shared_slope = silu_parts(shared_gate)
    shared_act = (shared_val * shared_up).astype(jnp.bfloat16)
    branch_part = jnp.dot(shared_act, w_shared_out, preferred_element_type=jnp.float32) + combined
    ffn_full = lax.psum(branch_part.astype(jnp.bfloat16), "tp").astype(jnp.float32)
    block_out = (middle + ffn_full).astype(jnp.bfloat16)
    slot_gate = (
        jnp.zeros((experts * capacity,), jnp.float32)
        .at[flat_index.reshape(-1)]
        .set(pair_gate.reshape(-1), mode="drop")
    )
    gathered_grad = jnp.take(cotangent, owner_row, axis=0, mode="fill", fill_value=0)
    slot_grad = (
        (slot_gate[:, None] * gathered_grad.astype(jnp.float32))
        .astype(jnp.bfloat16)
        .reshape(experts, capacity, model_width)
    )
    grad_arrived = lax.all_to_all(slot_grad, "ep", split_axis=0, concat_axis=0, tiled=True).reshape(
        sectioned.shape
    )
    act_grad = jnp.einsum(
        "secd,ehd->sech", grad_arrived, w_expert_out, preferred_element_type=jnp.float32
    )
    gate_val, gate_slope = silu_parts(gate_up[..., 0, :])
    up_val = gate_up[..., 1, :]
    gu_grad = jnp.stack([act_grad * up_val * gate_slope, act_grad * gate_val], axis=-2).astype(
        jnp.bfloat16
    )
    grad_expert_out = jnp.einsum(
        "sech,secd->ehd", activated, grad_arrived, preferred_element_type=jnp.float32
    )
    grad_expert_in = jnp.einsum(
        "secd,secgh->egdh", sectioned, gu_grad, preferred_element_type=jnp.float32
    )
    rows_grad = jnp.einsum(
        "secgh,egdh->secd", gu_grad, w_expert_in, preferred_element_type=jnp.float32
    ).reshape(received.shape)
    returned_grad = (
        lax.all_to_all(
            rows_grad.astype(jnp.bfloat16), "ep", split_axis=0, concat_axis=0, tiled=True
        )
        .astype(rows_grad.dtype)
        .reshape(-1, model_width)
    )
    routed_grad = jnp.zeros((tokens, model_width), jnp.float32)
    for pick_index in range(TOPK):
        routed_grad = routed_grad + jnp.take(
            returned_grad, flat_index[:, pick_index], axis=0, mode="fill", fill_value=0.0
        )
    shared_act_grad = jnp.einsum(
        "td,fd->tf", cotangent, w_shared_out, preferred_element_type=jnp.float32
    )
    shared_gate_grad = (shared_act_grad * shared_up * shared_slope).astype(jnp.bfloat16)
    shared_up_grad = (shared_act_grad * shared_val).astype(jnp.bfloat16)
    shared_out_grad = jnp.einsum(
        "tf,td->fd", shared_act, cotangent, preferred_element_type=jnp.float32
    )
    shared_in_grad = jnp.stack(
        [
            jnp.einsum(
                "td,tf->df", hidden_ffn, shared_gate_grad, preferred_element_type=jnp.float32
            ),
            jnp.einsum("td,tf->df", hidden_ffn, shared_up_grad, preferred_element_type=jnp.float32),
        ],
        axis=0,
    )
    shared_back = jnp.einsum(
        "tf,df->td", shared_gate_grad, w_shared_in[0], preferred_element_type=jnp.float32
    ) + jnp.einsum("tf,df->td", shared_up_grad, w_shared_in[1], preferred_element_type=jnp.float32)
    prob_grad = jnp.sum(route_onehot * gate_grad[:, :, None], axis=1)
    logit_grad = router_probs * (
        prob_grad - jnp.sum(router_probs * prob_grad, axis=-1, keepdims=True)
    )
    router_back = jnp.einsum(
        "te,de->td", logit_grad, w_router, precision=HIGHEST, preferred_element_type=jnp.float32
    )
    router_grad = jnp.einsum(
        "td,te->de", hidden_wide, logit_grad, precision=HIGHEST, preferred_element_type=jnp.float32
    )
    ffn_grad = lax.psum(
        (shared_back + routed_grad + router_back).astype(jnp.bfloat16), "tp"
    ).astype(jnp.float32)
    middle_grad = out_grad + norm_back(ffn_grad, gain_ffn, normed_second, inv_second)
    gain_ffn_grad = jnp.sum(
        lax.dynamic_slice_in_dim(ffn_grad * normed_second, row_start, rows_part, 0), axis=0
    )
    branch_grad = middle_grad.astype(jnp.bfloat16)
    output_w_grad = jnp.einsum(
        "tf,td->fd", attended, branch_grad, preferred_element_type=jnp.float32
    )
    attended_grad = (
        jnp.einsum("td,fd->tf", branch_grad, w_output, preferred_element_type=jnp.float32)
        .astype(jnp.bfloat16)
        .reshape(tokens, heads_here, VDIM)
    )
    scores_again = attention_scores(query_rot, key_nope, key_rope, score_scale, allowed)
    probs_again = jnp.exp(scores_again - log_total)
    values_grad = jnp.einsum(
        "hqk,qhd->khd",
        probs_again.astype(jnp.bfloat16),
        attended_grad,
        preferred_element_type=jnp.float32,
    )
    prob_part = jnp.einsum(
        "qhd,khd->hqk", attended_grad, values, preferred_element_type=jnp.float32
    )
    score_grad = (
        probs_again * (prob_part - jnp.sum(probs_again * prob_part, axis=-1, keepdims=True))
    ).astype(jnp.bfloat16)
    query_nope_grad = (
        jnp.einsum("hqk,khd->qhd", score_grad, key_nope, preferred_element_type=jnp.float32)
        * score_scale
    )
    query_rope_grad = (
        jnp.einsum("hqk,kr->qhr", score_grad, key_rope, preferred_element_type=jnp.float32)
        * score_scale
    )
    key_nope_grad = (
        jnp.einsum(
            "hqk,qhd->khd", score_grad, query_rot[..., :NOPE], preferred_element_type=jnp.float32
        )
        * score_scale
    )
    key_rope_grad = (
        jnp.einsum(
            "hqk,qhr->kr", score_grad, query_rot[..., NOPE:], preferred_element_type=jnp.float32
        )
        * score_scale
    )
    kv_grad = (
        jnp.concatenate([key_nope_grad, values_grad], axis=-1)
        .astype(jnp.bfloat16)
        .reshape(tokens, heads_here * (NOPE + VDIM))
    )
    latent_up_grad = jnp.einsum("tr,tf->rf", latent_in, kv_grad, preferred_element_type=jnp.float32)
    latent_in_grad = jnp.einsum(
        "tf,rf->tr", kv_grad, w_latent_up, preferred_element_type=jnp.float32
    )
    gain_latent_grad = jnp.sum(latent_in_grad * normed_latent, axis=0)
    latent_grad_part = jnp.concatenate(
        [
            norm_back(latent_in_grad, gain_latent, normed_latent, inv_latent),
            rotate(key_rope_grad, cosine, -sine_table),
        ],
        axis=-1,
    )
    query_grad = (
        jnp.concatenate(
            [query_nope_grad, rotate(query_rope_grad, cosine[:, None], -sine_table[:, None])],
            axis=-1,
        )
        .astype(jnp.bfloat16)
        .reshape(tokens, heads_here * qk_width)
    )
    query_w_grad = jnp.einsum(
        "td,tf->df", hidden_attn, query_grad, preferred_element_type=jnp.float32
    )
    hidden_part = jnp.einsum("tf,df->td", query_grad, w_query, preferred_element_type=jnp.float32)
    hidden_sum, latent_sum = (
        lax.psum(hidden_part.astype(jnp.bfloat16), "tp").astype(jnp.float32),
        lax.psum(latent_grad_part.astype(jnp.bfloat16), "tp").astype(jnp.float32),
    )
    latent_low = latent_sum.astype(jnp.bfloat16)
    attn_in_grad = hidden_sum + jnp.einsum(
        "tf,df->td", latent_low, w_latent, preferred_element_type=jnp.float32
    )
    latent_w_grad = jnp.einsum(
        "td,tf->df",
        lax.dynamic_slice_in_dim(hidden_attn, row_start, rows_part, 0),
        lax.dynamic_slice_in_dim(latent_low, row_start, rows_part, 0),
        preferred_element_type=jnp.float32,
    )
    gain_attn_grad = jnp.sum(
        lax.dynamic_slice_in_dim(attn_in_grad * normed_first, row_start, rows_part, 0), axis=0
    )
    grad_inputs = (
        middle_grad + norm_back(attn_in_grad, gain_attn, normed_first, inv_first)
    ).astype(jnp.bfloat16)
    grad_query, grad_latent_up, grad_output, grad_shared_in, grad_shared_out = (
        lax.psum_scatter(
            query_w_grad.astype(jnp.bfloat16), "ep", scatter_dimension=0, tiled=True
        ).astype(jnp.float32),
        lax.psum_scatter(
            latent_up_grad.astype(jnp.bfloat16), "ep", scatter_dimension=0, tiled=True
        ).astype(jnp.float32),
        lax.psum_scatter(
            output_w_grad.astype(jnp.bfloat16), "ep", scatter_dimension=1, tiled=True
        ).astype(jnp.float32),
        lax.psum_scatter(
            shared_in_grad.astype(jnp.bfloat16), "ep", scatter_dimension=1, tiled=True
        ).astype(jnp.float32),
        lax.psum_scatter(
            shared_out_grad.astype(jnp.bfloat16), "ep", scatter_dimension=1, tiled=True
        ).astype(jnp.float32),
    )
    grad_latent, grad_gain_latent, grad_gain_attn, grad_gain_ffn, grad_router = (
        lax.psum_scatter(latent_w_grad, ("ep", "tp"), scatter_dimension=0, tiled=True),
        lax.psum_scatter(gain_latent_grad, ("ep", "tp"), scatter_dimension=0, tiled=True),
        lax.psum_scatter(gain_attn_grad, ("ep", "tp"), scatter_dimension=0, tiled=True),
        lax.psum_scatter(gain_ffn_grad, ("ep", "tp"), scatter_dimension=0, tiled=True),
        lax.psum_scatter(router_grad, ("ep", "tp"), scatter_dimension=0, tiled=True),
    )
    return (
        block_out,
        grad_inputs,
        grad_gain_attn,
        grad_query,
        grad_latent,
        grad_gain_latent,
        grad_latent_up,
        grad_output,
        grad_gain_ffn,
        grad_router,
        grad_shared_in,
        grad_shared_out,
        grad_expert_in,
        grad_expert_out,
    )


MESH = pl.DeviceIdType.MESH


def plane_partners(ep):
    flip = lambda bit: ep + bit - 2 * bit * (lax.rem(lax.div(ep, bit), 2))
    return flip(1), flip(2), flip(4), flip


def greet(devices):
    barrier = pltpu.get_barrier_semaphore()
    for ep, tp in devices:
        pl.semaphore_signal(barrier, inc=1, device_id=(ep, tp), device_id_type=MESH)
    pl.semaphore_wait(barrier, len(devices))


def remote(src, dst, send, recv, device):
    return pltpu.make_async_remote_copy(
        src_ref=src, dst_ref=dst, send_sem=send, recv_sem=recv, device_id=device, device_id_type=MESH
    )


def line_order(tp):
    pick = lambda a, b, c, d: jnp.where(tp == 0, a, jnp.where(tp == 1, b, jnp.where(tp == 2, c, d)))
    return (tp, pick(1, 0, 3, 2), pick(2, 2, 1, 1), pick(3, 3, 0, 0))


def gather_kernel(rows, depth, own_ref, all_ref, local_sem, zsend, zrecv, psend, precv):
    ep, tp = lax.axis_index("ep"), lax.axis_index("tp")
    pair, xn, yn, flip = plane_partners(ep)
    parity = lax.rem(ep, 2)
    passed = jnp.where(parity == 0, xn, yn)
    onward = jnp.where(parity == 0, yn, xn)
    diag = xn + yn - ep
    twin = lambda b: b + pair - ep
    up, down = jnp.minimum(tp + 1, depth - 1), jnp.maximum(tp - 1, 0)
    barrier = pltpu.get_barrier_semaphore()
    for to in (pair, xn, yn):
        pl.semaphore_signal(barrier, inc=1, device_id=(to, tp), device_id_type=MESH)

    @pl.when(tp > 0)
    def _():
        pl.semaphore_signal(barrier, inc=1, device_id=(ep, down), device_id_type=MESH)

    @pl.when(tp < depth - 1)
    def _():
        pl.semaphore_signal(barrier, inc=1, device_id=(ep, up), device_id_type=MESH)

    pl.semaphore_wait(barrier, jnp.where((tp > 0) & (tp < depth - 1), 5, 4))
    local = pltpu.make_async_copy(own_ref, all_ref.at[ep, tp], local_sem)
    local.start()
    order = line_order(tp)

    def unit(block, chunk):
        return all_ref.at[block, chunk]

    def along(src, chunk, way, to):
        return remote(src, unit(ep, chunk), zsend.at[chunk, way], zrecv.at[chunk], (ep, to))

    def plane(src, block, chunk, slot, to):
        return remote(src, unit(block, chunk), psend.at[chunk, slot], precv.at[chunk, slot], (to, tp))

    def goes_up(chunk):
        return (chunk <= tp) & (tp < depth - 1)

    def goes_down(chunk):
        return (chunk >= tp) & (tp > 0)

    for k in range(depth + 1):
        if k < depth:
            chunk = order[k]
            src = own_ref if k == 0 else unit(ep, chunk)
            if k > 0:
                along(src, chunk, 0, up).wait_recv()

            @pl.when(goes_up(chunk))
            def _():
                along(src, chunk, 0, up).start()

            @pl.when(goes_down(chunk))
            def _():
                along(src, chunk, 1, down).start()

            plane(src, ep, chunk, 1, xn).start()
            plane(src, ep, chunk, 2, yn).start()
            plane(src, ep, chunk, 0, pair).start()
        if k > 0:
            chunk = order[k - 1]
            plane(unit(xn, chunk), xn, chunk, 1, xn).wait_recv()
            plane(unit(yn, chunk), yn, chunk, 2, yn).wait_recv()
            plane(unit(passed, chunk), passed, chunk, 3, onward).start()
            plane(unit(xn, chunk), xn, chunk, 4, pair).start()
            plane(unit(yn, chunk), yn, chunk, 5, pair).start()
        if k > 1:
            chunk = order[k - 2]
            plane(unit(diag, chunk), diag, chunk, 3, onward).wait_recv()
            plane(unit(diag, chunk), diag, chunk, 6, pair).start()
    chunk = order[depth - 1]
    plane(unit(diag, chunk), diag, chunk, 3, onward).wait_recv()
    plane(unit(diag, chunk), diag, chunk, 6, pair).start()
    for k in range(depth):
        chunk = order[k]
        for slot, block in ((0, pair), (4, twin(xn)), (5, twin(yn)), (6, twin(diag))):
            plane(unit(block, chunk), block, chunk, slot, pair).wait_recv()
    local.wait()
    for k in range(depth):
        chunk = order[k]

        @pl.when(goes_up(chunk))
        def _():
            along(own_ref, chunk, 0, up).wait_send()

        @pl.when(goes_down(chunk))
        def _():
            along(own_ref, chunk, 1, down).wait_send()

        for slot in range(7):
            plane(own_ref, ep, chunk, slot, pair).wait_send()


def gather_all(own, blocks, depth, cid):
    rows, width = own.shape
    out = pl.pallas_call(
        functools.partial(gather_kernel, rows, depth),
        out_shape=jax.ShapeDtypeStruct((blocks, depth, rows, width), own.dtype),
        in_specs=[pl.BlockSpec(memory_space=pltpu.VMEM)],
        out_specs=pl.BlockSpec(memory_space=pl.ANY),
        scratch_shapes=[
            pltpu.SemaphoreType.DMA,
            pltpu.SemaphoreType.DMA((depth, 2)),
            pltpu.SemaphoreType.DMA((depth,)),
            pltpu.SemaphoreType.DMA((depth, 7)),
            pltpu.SemaphoreType.DMA((depth, 7)),
        ],
        compiler_params=pltpu.CompilerParams(collective_id=cid, has_side_effects=True, vmem_limit_bytes=56 << 20),
    )(own)
    return out.reshape(blocks * depth * rows, width)


def sum_kernel(rows, depth, part_ref, out_ref, mine, got_pair, got_first, got_second, got_z, keep,
               mine_sem, ps, pr, fs, fr, ss, sr, zs, zr):
    f32 = jnp.float32
    ep, tp = lax.axis_index("ep"), lax.axis_index("tp")
    pair, xn, yn, flip = plane_partners(ep)
    parity = lax.rem(ep, 2)
    first = jnp.where(parity == 0, xn, yn)
    second = jnp.where(parity == 0, yn, xn)
    diag = xn + yn - ep
    other = lambda b: b + pair - ep
    blocks = (first, diag, ep, second)
    greet([(pair, tp), (xn, tp), (yn, tp)] + [(ep, lax.rem(tp + k, depth)) for k in range(1, depth)])
    steps = [(k + 1) % depth for k in range(depth)]

    def chunk_of(i):
        return lax.rem(tp + steps[i], depth)

    def pair_copy(i, slot):
        return remote(part_ref.at[other(blocks[slot]), chunk_of(i)], got_pair.at[i, pslot(slot)], ps.at[i, slot], pr.at[i, pslot(slot)], (pair, tp))

    def pslot(slot):
        return {0: 3, 1: 1, 2: 2, 3: 0}[slot]

    def pair_wait(i, slot):
        return remote(part_ref.at[ep, chunk_of(i)], got_pair.at[i, slot], ps.at[i, slot], pr.at[i, slot], (pair, tp))

    def mine_copy(i, slot):
        return pltpu.make_async_copy(part_ref.at[blocks[slot], chunk_of(i)], mine.at[i, slot], mine_sem.at[i, slot])

    def first_copy(i, slot):
        return remote(mine.at[i, slot], got_first.at[i, slot], fs.at[i, slot], fr.at[i, slot], (first, tp))

    def second_copy(i):
        return remote(mine.at[i, 3], got_second.at[i], ss.at[i], sr.at[i], (second, tp))

    def z_copy(i):
        k = steps[i]
        return remote(mine.at[i, 2], got_z.at[k - 1], zs.at[k - 1], zr.at[k - 1], (ep, lax.rem(tp + k, depth)))

    def add(dst, a, b):
        def body(r, _):
            sl = pl.ds(pl.multiple_of(r * 16, 16), 16)
            dst[sl, :] = (a[sl, :].astype(f32) + b[sl, :].astype(f32)).astype(dst.dtype)
            return 0
        lax.fori_loop(0, rows // 16, body, 0)

    for i in range(depth):
        for slot in (3, 1, 2, 0):
            pair_copy(i, slot).start()
        for slot in range(4):
            mine_copy(i, slot).start()

    def stage_a(i):
        for slot in range(4):
            mine_copy(i, slot).wait()
            pair_wait(i, slot).wait_recv()
            add(mine.at[i, slot], mine.at[i, slot], got_pair.at[i, slot])
            if slot < 2:
                first_copy(i, slot).start()

    def stage_b(i):
        first_copy(i, 1).wait_recv()
        add(mine.at[i, 3], mine.at[i, 3], got_first.at[i, 1])
        second_copy(i).start()
        first_copy(i, 0).wait_recv()
        add(mine.at[i, 2], mine.at[i, 2], got_first.at[i, 0])

    def stage_c(i):
        second_copy(i).wait_recv()
        if i < depth - 1:
            add(mine.at[i, 2], mine.at[i, 2], got_second.at[i])
            z_copy(i).start()
        else:
            add(keep, mine.at[i, 2], got_second.at[i])

    for t in range(depth + 2):
        if t < depth:
            stage_a(t)
        if 0 <= t - 1 < depth:
            stage_b(t - 1)
        if 0 <= t - 2 < depth:
            stage_c(t - 2)
    for i in range(depth - 1):
        z_copy(i).wait_recv()

    def total(r, _):
        sl = pl.ds(pl.multiple_of(r * 16, 16), 16)
        v = keep[sl, :]
        for k in range(depth - 1):
            v = v + got_z[k, sl, :].astype(f32)
        out_ref[sl, :] = v
        return 0

    lax.fori_loop(0, rows // 16, total, 0)
    for i in range(depth):
        for slot in range(4):
            pair_copy(i, slot).wait_send()
        for slot in range(2):
            first_copy(i, slot).wait_send()
        second_copy(i).wait_send()
        if i < depth - 1:
            z_copy(i).wait_send()


def sum_all_rows(part, blocks, depth, cid):
    width = part.shape[-1]
    rows = part.shape[0] // (blocks * depth)
    bf, f32 = part.dtype, jnp.float32
    D = pltpu.SemaphoreType.DMA
    return pl.pallas_call(
        functools.partial(sum_kernel, rows, depth),
        out_shape=jax.ShapeDtypeStruct((rows, width), f32),
        in_specs=[pl.BlockSpec(memory_space=pl.ANY)],
        out_specs=pl.BlockSpec(memory_space=pltpu.VMEM),
        scratch_shapes=[
            pltpu.VMEM((depth, 4, rows, width), bf),
            pltpu.VMEM((depth, 4, rows, width), bf),
            pltpu.VMEM((depth, 2, rows, width), bf),
            pltpu.VMEM((depth, rows, width), bf),
            pltpu.VMEM((depth - 1, rows, width), bf),
            pltpu.VMEM((rows, width), f32),
            D((depth, 4)), D((depth, 4)), D((depth, 4)), D((depth, 2)), D((depth, 2)), D((depth,)), D((depth,)),
            D((depth - 1,)), D((depth - 1,)),
        ],
        compiler_params=pltpu.CompilerParams(collective_id=cid, has_side_effects=True, vmem_limit_bytes=56 << 20),
    )(part.reshape(blocks, depth, rows, width))


def padded_hidden(routed, shared):
    return -(-(routed + shared + 24) // 128) * 128


def split_wide(values):
    high = values.astype(jnp.bfloat16)
    rest = values - high.astype(jnp.float32)
    mid = rest.astype(jnp.bfloat16)
    low = (rest - mid.astype(jnp.float32)).astype(jnp.bfloat16)
    return (high, mid, low)


def body_dense(
    inputs,
    gain_attn,
    w_query,
    w_latent,
    gain_latent,
    w_latent_up,
    w_output,
    gain_ffn,
    w_router,
    w_shared_in,
    w_shared_out,
    w_expert_in,
    w_expert_out,
    expert_ids,
    slot_ids,
    cotangent,
):
    f32, bf16 = jnp.float32, jnp.bfloat16
    tokens, model_width = inputs.shape
    ep_count, tp_count = lax.axis_size("ep"), lax.axis_size("tp")
    ep_index, tp_index = lax.axis_index("ep"), lax.axis_index("tp")
    heads_here = w_output.shape[0] // VDIM
    experts = w_router.shape[1]
    capacity = (9 * tokens * TOPK + 64 * experts - 1) // (64 * experts) * 8
    qk_width = NOPE + ROPE
    score_scale = qk_width ** (-0.5)
    rows_part = tokens // tp_count
    row_start = tp_index * rows_part

    expert_range = jnp.arange(experts, dtype=jnp.int32)
    kept = jnp.any(
        (expert_ids[:, :, None] == expert_range) & (slot_ids < capacity)[:, :, None], axis=1
    ).astype(f32)
    kept_here = lax.all_to_all(kept, "ep", split_axis=1, concat_axis=0, tiled=True)
    cot_all = lax.all_gather(cotangent, "ep", tiled=True)

    routed = w_expert_in.shape[3]
    shared = w_shared_in.shape[2] // ep_count
    hidden = padded_hidden(routed, shared)
    shared_start = ep_index * shared
    shared_in = lax.dynamic_slice_in_dim(w_shared_in, shared_start, shared, 2)
    shared_out = lax.dynamic_slice_in_dim(w_shared_out, shared_start, shared, 0)
    router_parts = jnp.concatenate(split_wide(w_router), axis=1)
    fill = hidden - routed - shared
    w_in = jnp.concatenate(
        [
            w_expert_in[0, 0],
            shared_in[0],
            jnp.pad(router_parts, ((0, 0), (0, fill - router_parts.shape[1]))),
            w_expert_in[0, 1],
            shared_in[1],
            jnp.zeros((model_width, fill), bf16),
        ],
        axis=1,
    )
    w_out = jnp.concatenate(
        [w_expert_out[0], shared_out, jnp.zeros((fill, model_width), bf16)], axis=0
    )

    resid = inputs.astype(f32)
    inv_first = lax.rsqrt(jnp.mean(resid * resid, axis=-1, keepdims=True) + EPSILON)
    normed_first = resid * inv_first
    hidden_attn = (normed_first * gain_attn).astype(bf16)
    cosine, sine_table = angles(tokens, ROPE)
    query_raw = jnp.dot(hidden_attn, w_query, preferred_element_type=f32).reshape(
        tokens, heads_here, qk_width
    )
    query_rot = jnp.concatenate(
        [
            query_raw[..., :NOPE],
            rotate(query_raw[..., NOPE:], cosine[:, None], sine_table[:, None]),
        ],
        axis=-1,
    ).astype(bf16)
    latent = jnp.dot(hidden_attn, w_latent, preferred_element_type=f32)
    compressed = latent[:, :KV_RANK]
    inv_latent = lax.rsqrt(jnp.mean(compressed * compressed, axis=-1, keepdims=True) + EPSILON)
    normed_latent = compressed * inv_latent
    latent_in = (normed_latent * gain_latent).astype(bf16)
    key_rope = rotate(latent[:, KV_RANK:], cosine, sine_table).astype(bf16)
    key_value = (
        jnp.dot(latent_in, w_latent_up, preferred_element_type=f32)
        .astype(bf16)
        .reshape(tokens, heads_here, NOPE + VDIM)
    )
    key_nope = key_value[..., :NOPE]
    values = key_value[..., NOPE:]
    block_ids = jnp.arange(tokens) // BLOCK
    allowed = block_ids[None, :] <= block_ids[:, None]
    scores = attention_scores(query_rot, key_nope, key_rope, score_scale, allowed)
    row_peak = jnp.max(scores, axis=-1, keepdims=True)
    exp_scores = jnp.exp(scores - row_peak)
    totals = jnp.sum(exp_scores, axis=-1, keepdims=True)
    attn_probs = exp_scores / totals
    log_total = row_peak + jnp.log(totals)
    attended = (
        jnp.einsum("hqk,khd->qhd", attn_probs.astype(bf16), values, preferred_element_type=f32)
        .astype(bf16)
        .reshape(tokens, heads_here * VDIM)
    )
    attn_part = jnp.dot(attended, w_output, preferred_element_type=f32).astype(bf16)

    attn_rows = lax.psum_scatter(attn_part, "tp", scatter_dimension=0, tiled=True).astype(f32)
    resid_rows = lax.dynamic_slice_in_dim(resid, row_start, rows_part, 0)
    cot_rows = lax.dynamic_slice_in_dim(cotangent, row_start, rows_part, 0).astype(f32)
    middle = resid_rows + attn_rows
    inv_second = lax.rsqrt(jnp.mean(middle * middle, axis=-1, keepdims=True) + EPSILON)
    normed_second = middle * inv_second
    hidden_rows = (normed_second * gain_ffn).astype(bf16)
    hidden_all = gather_all(hidden_rows, ep_count, tp_count, 0)

    gate_up = jnp.dot(hidden_all, w_in, preferred_element_type=f32)
    gate_val, up_val = gate_up[:, :hidden], gate_up[:, hidden:]
    base = routed + shared
    logits = (
        gate_val[:, base : base + experts]
        + gate_val[:, base + experts : base + 2 * experts]
        + gate_val[:, base + 2 * experts : base + 3 * experts]
    )
    exp_logits = jnp.exp(logits - jnp.max(logits, axis=-1, keepdims=True))
    router_probs = exp_logits / jnp.sum(exp_logits, axis=-1, keepdims=True)
    here = (expert_range == ep_index).astype(f32)[None]
    prob_here = jnp.sum(router_probs * here, axis=-1, keepdims=True)
    unit_index = jnp.arange(hidden)[None]
    is_routed = unit_index < routed
    unit_gate = jnp.where(is_routed, prob_here * kept_here, 1.0)
    silu_val, silu_slope = silu_parts(gate_val)
    activated = silu_val * up_val
    gated = (activated * unit_gate).astype(bf16)
    out_part = jnp.dot(gated, w_out, preferred_element_type=f32).astype(bf16)
    act_grad = jnp.einsum("td,fd->tf", cot_all, w_out, preferred_element_type=f32)
    pair_grad = (
        jnp.sum(jnp.where(is_routed, activated * act_grad, 0.0), axis=-1, keepdims=True) * kept_here
    )
    logit_grad = pair_grad * prob_here * (here - router_probs)
    act_grad = act_grad * unit_gate
    gate_grad = (act_grad * up_val * silu_slope).astype(bf16)
    up_grad = (act_grad * silu_val).astype(bf16)
    rows_grad = (
        jnp.einsum("tf,df->td", gate_grad, w_in[:, :hidden], preferred_element_type=f32)
        + jnp.einsum("tf,df->td", up_grad, w_in[:, hidden:], preferred_element_type=f32)
        + jnp.einsum(
            "te,de->td", logit_grad, w_router, precision=HIGHEST, preferred_element_type=f32
        )
    ).astype(bf16)
    out_grad_w = jnp.einsum("tf,td->fd", gated, cot_all, preferred_element_type=f32)
    in_grad_gate = jnp.einsum("td,tf->df", hidden_all, gate_grad, preferred_element_type=f32)
    in_grad_up = jnp.einsum("td,tf->df", hidden_all, up_grad, preferred_element_type=f32)
    router_grad = jnp.einsum(
        "td,te->de",
        hidden_all.astype(f32),
        logit_grad,
        precision=HIGHEST,
        preferred_element_type=f32,
    )
    grad_expert_in = jnp.stack([in_grad_gate[:, :routed], in_grad_up[:, :routed]])[None]
    grad_expert_out = out_grad_w[None, :routed]
    shared_in_part = jnp.stack([in_grad_gate[:, routed:base], in_grad_up[:, routed:base]])
    grad_shared_in = lax.all_to_all(
        shared_in_part.astype(bf16), "ep", split_axis=1, concat_axis=2, tiled=True
    ).astype(f32)
    grad_shared_out = lax.all_to_all(
        out_grad_w[routed:base].astype(bf16), "ep", split_axis=1, concat_axis=0, tiled=True
    ).astype(f32)

    def sum_rows(part):
        plane = lax.psum_scatter(part, "ep", scatter_dimension=0, tiled=True)
        return lax.psum_scatter(plane, "tp", scatter_dimension=0, tiled=True).astype(f32)

    ffn_grad = sum_all_rows(rows_grad, ep_count, tp_count, 1)
    ffn_rows = sum_rows(out_part)
    block_out = lax.all_gather((middle + ffn_rows).astype(bf16), "tp", tiled=True)
    middle_grad = cot_rows + norm_back(ffn_grad, gain_ffn, normed_second, inv_second)
    gain_ffn_grad = jnp.sum(ffn_grad * normed_second, axis=0)
    branch_grad = lax.all_gather(middle_grad.astype(bf16), "tp", tiled=True)

    output_w_grad = jnp.einsum("tf,td->fd", attended, branch_grad, preferred_element_type=f32)
    attended_grad = (
        jnp.einsum("td,fd->tf", branch_grad, w_output, preferred_element_type=f32)
        .astype(bf16)
        .reshape(tokens, heads_here, VDIM)
    )
    scores_again = attention_scores(query_rot, key_nope, key_rope, score_scale, allowed)
    probs_again = jnp.exp(scores_again - log_total)
    values_grad = jnp.einsum(
        "hqk,qhd->khd", probs_again.astype(bf16), attended_grad, preferred_element_type=f32
    )
    prob_part = jnp.einsum("qhd,khd->hqk", attended_grad, values, preferred_element_type=f32)
    score_grad = (
        probs_again * (prob_part - jnp.sum(probs_again * prob_part, axis=-1, keepdims=True))
    ).astype(bf16)
    query_nope_grad = (
        jnp.einsum("hqk,khd->qhd", score_grad, key_nope, preferred_element_type=f32) * score_scale
    )
    query_rope_grad = (
        jnp.einsum("hqk,kr->qhr", score_grad, key_rope, preferred_element_type=f32) * score_scale
    )
    key_nope_grad = (
        jnp.einsum("hqk,qhd->khd", score_grad, query_rot[..., :NOPE], preferred_element_type=f32)
        * score_scale
    )
    key_rope_grad = (
        jnp.einsum("hqk,qhr->kr", score_grad, query_rot[..., NOPE:], preferred_element_type=f32)
        * score_scale
    )
    kv_grad = (
        jnp.concatenate([key_nope_grad, values_grad], axis=-1)
        .astype(bf16)
        .reshape(tokens, heads_here * (NOPE + VDIM))
    )
    latent_up_grad = jnp.einsum("tr,tf->rf", latent_in, kv_grad, preferred_element_type=f32)
    latent_in_grad = jnp.einsum("tf,rf->tr", kv_grad, w_latent_up, preferred_element_type=f32)
    gain_latent_grad = jnp.sum(latent_in_grad * normed_latent, axis=0)
    latent_grad_part = jnp.concatenate(
        [
            norm_back(latent_in_grad, gain_latent, normed_latent, inv_latent),
            rotate(key_rope_grad, cosine, -sine_table),
        ],
        axis=-1,
    ).astype(bf16)
    query_grad = (
        jnp.concatenate(
            [query_nope_grad, rotate(query_rope_grad, cosine[:, None], -sine_table[:, None])],
            axis=-1,
        )
        .astype(bf16)
        .reshape(tokens, heads_here * qk_width)
    )
    query_w_grad = jnp.einsum("td,tf->df", hidden_attn, query_grad, preferred_element_type=f32)
    hidden_part = (
        jnp.einsum("tf,df->td", query_grad, w_query, preferred_element_type=f32)
        + jnp.einsum("tf,df->td", latent_grad_part, w_latent, preferred_element_type=f32)
    ).astype(bf16)
    attn_in_grad = lax.psum_scatter(hidden_part, "tp", scatter_dimension=0, tiled=True).astype(f32)
    latent_w_grad = jnp.einsum(
        "td,tf->df", hidden_attn, latent_grad_part, preferred_element_type=f32
    )
    normed_rows = lax.dynamic_slice_in_dim(normed_first, row_start, rows_part, 0)
    inv_rows = lax.dynamic_slice_in_dim(inv_first, row_start, rows_part, 0)
    gain_attn_grad = jnp.sum(attn_in_grad * normed_rows, axis=0)
    grad_inputs = lax.all_gather(
        (middle_grad + norm_back(attn_in_grad, gain_attn, normed_rows, inv_rows)).astype(bf16),
        "tp",
        tiled=True,
    )
    grad_query, grad_latent_up, grad_output = (
        lax.psum_scatter(
            query_w_grad.astype(bf16), "ep", scatter_dimension=0, tiled=True
        ).astype(f32),
        lax.psum_scatter(
            latent_up_grad.astype(bf16), "ep", scatter_dimension=0, tiled=True
        ).astype(f32),
        lax.psum_scatter(
            output_w_grad.astype(bf16), "ep", scatter_dimension=1, tiled=True
        ).astype(f32),
    )

    def sum_all(part):
        plane = lax.psum_scatter(part, "ep", scatter_dimension=0, tiled=True)
        return lax.psum_scatter(plane, "tp", scatter_dimension=0, tiled=True)

    grad_latent, grad_gain_latent, grad_gain_attn, grad_gain_ffn, grad_router = (
        sum_all(latent_w_grad),
        sum_all(gain_latent_grad),
        sum_all(gain_attn_grad),
        sum_all(gain_ffn_grad),
        sum_all(router_grad),
    )
    return (
        block_out,
        grad_inputs,
        grad_gain_attn,
        grad_query,
        grad_latent,
        grad_gain_latent,
        grad_latent_up,
        grad_output,
        grad_gain_ffn,
        grad_router,
        grad_shared_in,
        grad_shared_out,
        grad_expert_in,
        grad_expert_out,
    )


def solution(mesh):
    near = mesh.shape["ep"] == 8 and mesh.shape["tp"] == 4
    body = body_dense if near else body_slots
    placed = (
        P("ep", None),
        P(),
        P(None, "tp"),
        P(),
        P(),
        P(None, "tp"),
        P("tp", None),
        P(),
        P(),
        P(None, None, "tp"),
        P("tp", None),
        P("ep", None, None, "tp"),
        P("ep", "tp", None),
        P("ep", None),
        P("ep", None),
        P("ep", None),
    )
    return jax.shard_map(
        body,
        mesh=mesh,
        in_specs=placed,
        out_specs=(
            P("ep", None),
            P("ep", None),
            P(("ep", "tp")),
            P("ep", "tp"),
            P(("ep", "tp"), None),
            P(("ep", "tp")),
            P("ep", "tp"),
            P("tp", "ep"),
            P(("ep", "tp")),
            P(("ep", "tp"), None),
            P(None, "ep", "tp"),
            P("tp", "ep"),
            P("ep", None, None, "tp"),
            P("ep", "tp", None),
        ),
        check_vma=False,
    )
```

```python
import functools
import math

import jax
import jax.numpy as jnp
from jax import lax
from jax.experimental import pallas as pl
from jax.experimental.pallas import tpu as pltpu
from jax.sharding import PartitionSpec as P

NOPE = 128
ROPE = 64
VDIM = 128
KV_RANK = 512
TOPK = 6
BLOCK = 256


EPSILON = 1e-06
HIGHEST = lax.Precision.HIGHEST


def angles(length, rope_width):
    half_width = rope_width // 2
    position = jnp.arange(length, dtype=jnp.float32)
    inverse = jnp.exp(jnp.arange(half_width, dtype=jnp.float32) * (-math.log(10000.0) / half_width))
    angle_table = position[:, None] * inverse[None, :]
    return (jnp.cos(angle_table), jnp.sin(angle_table))


def rotate(values, cosine, sine_table):
    half_width = values.shape[-1] // 2
    front_part = values[..., :half_width]
    second = values[..., half_width:]
    return jnp.concatenate(
        [front_part * cosine - second * sine_table, second * cosine + front_part * sine_table],
        axis=-1,
    )


def silu_parts(gate_val):
    sigmoid_val = jax.nn.sigmoid(gate_val)
    return (gate_val * sigmoid_val, sigmoid_val * (1.0 + gate_val * (1.0 - sigmoid_val)))


def norm_back(grad_norm, gain_vec, normed, inverse):
    scaled = grad_norm * gain_vec
    return inverse * (scaled - normed * jnp.mean(scaled * normed, axis=-1, keepdims=True))


def attention_scores(query_rot, key_nope, key_rope, score_scale, allowed):
    nope_scores = jnp.einsum(
        "qhd,khd->hqk", query_rot[..., :NOPE], key_nope, preferred_element_type=jnp.float32
    )
    rope_scores = jnp.einsum(
        "qhr,kr->hqk", query_rot[..., NOPE:], key_rope, preferred_element_type=jnp.float32
    )
    return jnp.where(allowed[None], (nope_scores + rope_scores) * score_scale, -1e30)


def expert_forward(received, w_expert_in, w_expert_out, sources):
    sectioned = received.reshape(sources, -1, received.shape[1], received.shape[2])
    gate_up = jnp.einsum(
        "secd,egdh->secgh", sectioned, w_expert_in, preferred_element_type=jnp.float32
    )
    gate_val, gate_slope = silu_parts(gate_up[..., 0, :])
    activated = (gate_val * gate_up[..., 1, :]).astype(jnp.bfloat16)
    produced = jnp.einsum(
        "sech,ehd->secd", activated, w_expert_out, preferred_element_type=jnp.float32
    )
    return (sectioned, gate_up, activated, produced.reshape(received.shape))


def body_slots(
    inputs,
    gain_attn,
    w_query,
    w_latent,
    gain_latent,
    w_latent_up,
    w_output,
    gain_ffn,
    w_router,
    w_shared_in,
    w_shared_out,
    w_expert_in,
    w_expert_out,
    expert_ids,
    slot_ids,
    cotangent,
):
    tokens, model_width = inputs.shape
    tp_count = lax.axis_size("tp")
    tp_index = lax.axis_index("tp")
    heads_here = w_output.shape[0] // VDIM
    experts = w_router.shape[1]
    local_experts = w_expert_in.shape[0]
    sources = experts // local_experts
    capacity = (9 * tokens * TOPK + 64 * experts - 1) // (64 * experts) * 8
    qk_width = NOPE + ROPE
    score_scale = qk_width ** (-0.5)
    rows_part = tokens // tp_count
    row_start = tp_index * rows_part
    resid = inputs.astype(jnp.float32)
    inv_first = lax.rsqrt(jnp.mean(resid * resid, axis=-1, keepdims=True) + EPSILON)
    normed_first = resid * inv_first
    hidden_attn = (normed_first * gain_attn).astype(jnp.bfloat16)
    cosine, sine_table = angles(tokens, ROPE)
    query_raw = jnp.dot(hidden_attn, w_query, preferred_element_type=jnp.float32).reshape(
        tokens, heads_here, qk_width
    )
    query_rot = jnp.concatenate(
        [
            query_raw[..., :NOPE],
            rotate(query_raw[..., NOPE:], cosine[:, None], sine_table[:, None]),
        ],
        axis=-1,
    ).astype(jnp.bfloat16)
    latent = jnp.dot(hidden_attn, w_latent, preferred_element_type=jnp.float32)
    compressed = latent[:, :KV_RANK]
    inv_latent = lax.rsqrt(jnp.mean(compressed * compressed, axis=-1, keepdims=True) + EPSILON)
    normed_latent = compressed * inv_latent
    latent_in = (normed_latent * gain_latent).astype(jnp.bfloat16)
    key_rope = rotate(latent[:, KV_RANK:], cosine, sine_table).astype(jnp.bfloat16)
    key_value = (
        jnp.dot(latent_in, w_latent_up, preferred_element_type=jnp.float32)
        .astype(jnp.bfloat16)
        .reshape(tokens, heads_here, NOPE + VDIM)
    )
    key_nope = key_value[..., :NOPE]
    values = key_value[..., NOPE:]
    block_ids = jnp.arange(tokens) // BLOCK
    allowed = block_ids[None, :] <= block_ids[:, None]
    scores = attention_scores(query_rot, key_nope, key_rope, score_scale, allowed)
    row_peak = jnp.max(scores, axis=-1, keepdims=True)
    exp_scores = jnp.exp(scores - row_peak)
    totals = jnp.sum(exp_scores, axis=-1, keepdims=True)
    attn_probs = exp_scores / totals
    log_total = row_peak + jnp.log(totals)
    attended = (
        jnp.einsum(
            "hqk,khd->qhd",
            attn_probs.astype(jnp.bfloat16),
            values,
            preferred_element_type=jnp.float32,
        )
        .astype(jnp.bfloat16)
        .reshape(tokens, heads_here * VDIM)
    )
    attn_full = lax.psum(
        jnp.dot(attended, w_output, preferred_element_type=jnp.float32).astype(jnp.bfloat16), "tp"
    ).astype(jnp.float32)
    middle = resid + attn_full
    inv_second = lax.rsqrt(jnp.mean(middle * middle, axis=-1, keepdims=True) + EPSILON)
    normed_second = middle * inv_second
    hidden_ffn = (normed_second * gain_ffn).astype(jnp.bfloat16)
    hidden_wide = hidden_ffn.astype(jnp.float32)
    logits = jnp.dot(hidden_wide, w_router, precision=HIGHEST, preferred_element_type=jnp.float32)
    logit_peak = jnp.max(logits, axis=-1, keepdims=True)
    exp_logits = jnp.exp(logits - logit_peak)
    router_probs = exp_logits / jnp.sum(exp_logits, axis=-1, keepdims=True)
    route_onehot = (
        expert_ids[:, :, None] == jnp.arange(experts, dtype=jnp.int32)[None, None, :]
    ).astype(jnp.float32)
    pair_gate = jnp.sum(route_onehot * router_probs[:, None, :], axis=-1)
    kept_pair = slot_ids < capacity
    flat_index = jnp.where(kept_pair, expert_ids * capacity + slot_ids, experts * capacity)
    row_numbers = jnp.broadcast_to(jnp.arange(tokens, dtype=jnp.int32)[:, None], (tokens, TOPK))
    owner_row = (
        jnp.full((experts * capacity,), tokens, jnp.int32)
        .at[flat_index.reshape(-1)]
        .set(row_numbers.reshape(-1), mode="drop")
    )
    outgoing = jnp.take(hidden_ffn, owner_row, axis=0, mode="fill", fill_value=0).reshape(
        experts, capacity, model_width
    )
    received = lax.all_to_all(outgoing, "ep", split_axis=0, concat_axis=0, tiled=True)
    sectioned, gate_up, activated, produced = expert_forward(
        received, w_expert_in, w_expert_out, sources
    )
    returned = lax.all_to_all(
        produced.astype(jnp.bfloat16), "ep", split_axis=0, concat_axis=0, tiled=True
    ).astype(produced.dtype)
    out_grad = cotangent.astype(jnp.float32)
    back_rows = returned.reshape(-1, model_width)
    combined = jnp.zeros((tokens, model_width), jnp.float32)
    gate_cols = []
    for pick_index in range(TOPK):
        taken_rows = jnp.take(
            back_rows, flat_index[:, pick_index], axis=0, mode="fill", fill_value=0.0
        )
        combined = combined + pair_gate[:, pick_index : pick_index + 1] * taken_rows
        gate_cols.append(jnp.sum(out_grad * taken_rows, axis=-1))
    gate_grad = jnp.stack(gate_cols, axis=1)
    shared_gate = jnp.dot(hidden_ffn, w_shared_in[0], preferred_element_type=jnp.float32)
    shared_up = jnp.dot(hidden_ffn, w_shared_in[1], preferred_element_type=jnp.float32)
    shared_val, shared_slope = silu_parts(shared_gate)
    shared_act = (shared_val * shared_up).astype(jnp.bfloat16)
    branch_part = jnp.dot(shared_act, w_shared_out, preferred_element_type=jnp.float32) + combined
    ffn_full = lax.psum(branch_part.astype(jnp.bfloat16), "tp").astype(jnp.float32)
    block_out = (middle + ffn_full).astype(jnp.bfloat16)
    slot_gate = (
        jnp.zeros((experts * capacity,), jnp.float32)
        .at[flat_index.reshape(-1)]
        .set(pair_gate.reshape(-1), mode="drop")
    )
    gathered_grad = jnp.take(cotangent, owner_row, axis=0, mode="fill", fill_value=0)
    slot_grad = (
        (slot_gate[:, None] * gathered_grad.astype(jnp.float32))
        .astype(jnp.bfloat16)
        .reshape(experts, capacity, model_width)
    )
    grad_arrived = lax.all_to_all(slot_grad, "ep", split_axis=0, concat_axis=0, tiled=True).reshape(
        sectioned.shape
    )
    act_grad = jnp.einsum(
        "secd,ehd->sech", grad_arrived, w_expert_out, preferred_element_type=jnp.float32
    )
    gate_val, gate_slope = silu_parts(gate_up[..., 0, :])
    up_val = gate_up[..., 1, :]
    gu_grad = jnp.stack([act_grad * up_val * gate_slope, act_grad * gate_val], axis=-2).astype(
        jnp.bfloat16
    )
    grad_expert_out = jnp.einsum(
        "sech,secd->ehd", activated, grad_arrived, preferred_element_type=jnp.float32
    )
    grad_expert_in = jnp.einsum(
        "secd,secgh->egdh", sectioned, gu_grad, preferred_element_type=jnp.float32
    )
    rows_grad = jnp.einsum(
        "secgh,egdh->secd", gu_grad, w_expert_in, preferred_element_type=jnp.float32
    ).reshape(received.shape)
    returned_grad = (
        lax.all_to_all(
            rows_grad.astype(jnp.bfloat16), "ep", split_axis=0, concat_axis=0, tiled=True
        )
        .astype(rows_grad.dtype)
        .reshape(-1, model_width)
    )
    routed_grad = jnp.zeros((tokens, model_width), jnp.float32)
    for pick_index in range(TOPK):
        routed_grad = routed_grad + jnp.take(
            returned_grad, flat_index[:, pick_index], axis=0, mode="fill", fill_value=0.0
        )
    shared_act_grad = jnp.einsum(
        "td,fd->tf", cotangent, w_shared_out, preferred_element_type=jnp.float32
    )
    shared_gate_grad = (shared_act_grad * shared_up * shared_slope).astype(jnp.bfloat16)
    shared_up_grad = (shared_act_grad * shared_val).astype(jnp.bfloat16)
    shared_out_grad = jnp.einsum(
        "tf,td->fd", shared_act, cotangent, preferred_element_type=jnp.float32
    )
    shared_in_grad = jnp.stack(
        [
            jnp.einsum(
                "td,tf->df", hidden_ffn, shared_gate_grad, preferred_element_type=jnp.float32
            ),
            jnp.einsum("td,tf->df", hidden_ffn, shared_up_grad, preferred_element_type=jnp.float32),
        ],
        axis=0,
    )
    shared_back = jnp.einsum(
        "tf,df->td", shared_gate_grad, w_shared_in[0], preferred_element_type=jnp.float32
    ) + jnp.einsum("tf,df->td", shared_up_grad, w_shared_in[1], preferred_element_type=jnp.float32)
    prob_grad = jnp.sum(route_onehot * gate_grad[:, :, None], axis=1)
    logit_grad = router_probs * (
        prob_grad - jnp.sum(router_probs * prob_grad, axis=-1, keepdims=True)
    )
    router_back = jnp.einsum(
        "te,de->td", logit_grad, w_router, precision=HIGHEST, preferred_element_type=jnp.float32
    )
    router_grad = jnp.einsum(
        "td,te->de", hidden_wide, logit_grad, precision=HIGHEST, preferred_element_type=jnp.float32
    )
    ffn_grad = lax.psum(
        (shared_back + routed_grad + router_back).astype(jnp.bfloat16), "tp"
    ).astype(jnp.float32)
    middle_grad = out_grad + norm_back(ffn_grad, gain_ffn, normed_second, inv_second)
    gain_ffn_grad = jnp.sum(
        lax.dynamic_slice_in_dim(ffn_grad * normed_second, row_start, rows_part, 0), axis=0
    )
    branch_grad = middle_grad.astype(jnp.bfloat16)
    output_w_grad = jnp.einsum(
        "tf,td->fd", attended, branch_grad, preferred_element_type=jnp.float32
    )
    attended_grad = (
        jnp.einsum("td,fd->tf", branch_grad, w_output, preferred_element_type=jnp.float32)
        .astype(jnp.bfloat16)
        .reshape(tokens, heads_here, VDIM)
    )
    scores_again = attention_scores(query_rot, key_nope, key_rope, score_scale, allowed)
    probs_again = jnp.exp(scores_again - log_total)
    values_grad = jnp.einsum(
        "hqk,qhd->khd",
        probs_again.astype(jnp.bfloat16),
        attended_grad,
        preferred_element_type=jnp.float32,
    )
    prob_part = jnp.einsum(
        "qhd,khd->hqk", attended_grad, values, preferred_element_type=jnp.float32
    )
    score_grad = (
        probs_again * (prob_part - jnp.sum(probs_again * prob_part, axis=-1, keepdims=True))
    ).astype(jnp.bfloat16)
    query_nope_grad = (
        jnp.einsum("hqk,khd->qhd", score_grad, key_nope, preferred_element_type=jnp.float32)
        * score_scale
    )
    query_rope_grad = (
        jnp.einsum("hqk,kr->qhr", score_grad, key_rope, preferred_element_type=jnp.float32)
        * score_scale
    )
    key_nope_grad = (
        jnp.einsum(
            "hqk,qhd->khd", score_grad, query_rot[..., :NOPE], preferred_element_type=jnp.float32
        )
        * score_scale
    )
    key_rope_grad = (
        jnp.einsum(
            "hqk,qhr->kr", score_grad, query_rot[..., NOPE:], preferred_element_type=jnp.float32
        )
        * score_scale
    )
    kv_grad = (
        jnp.concatenate([key_nope_grad, values_grad], axis=-1)
        .astype(jnp.bfloat16)
        .reshape(tokens, heads_here * (NOPE + VDIM))
    )
    latent_up_grad = jnp.einsum("tr,tf->rf", latent_in, kv_grad, preferred_element_type=jnp.float32)
    latent_in_grad = jnp.einsum(
        "tf,rf->tr", kv_grad, w_latent_up, preferred_element_type=jnp.float32
    )
    gain_latent_grad = jnp.sum(latent_in_grad * normed_latent, axis=0)
    latent_grad_part = jnp.concatenate(
        [
            norm_back(latent_in_grad, gain_latent, normed_latent, inv_latent),
            rotate(key_rope_grad, cosine, -sine_table),
        ],
        axis=-1,
    )
    query_grad = (
        jnp.concatenate(
            [query_nope_grad, rotate(query_rope_grad, cosine[:, None], -sine_table[:, None])],
            axis=-1,
        )
        .astype(jnp.bfloat16)
        .reshape(tokens, heads_here * qk_width)
    )
    query_w_grad = jnp.einsum(
        "td,tf->df", hidden_attn, query_grad, preferred_element_type=jnp.float32
    )
    hidden_part = jnp.einsum("tf,df->td", query_grad, w_query, preferred_element_type=jnp.float32)
    hidden_sum, latent_sum = (
        lax.psum(hidden_part.astype(jnp.bfloat16), "tp").astype(jnp.float32),
        lax.psum(latent_grad_part.astype(jnp.bfloat16), "tp").astype(jnp.float32),
    )
    latent_low = latent_sum.astype(jnp.bfloat16)
    attn_in_grad = hidden_sum + jnp.einsum(
        "tf,df->td", latent_low, w_latent, preferred_element_type=jnp.float32
    )
    latent_w_grad = jnp.einsum(
        "td,tf->df",
        lax.dynamic_slice_in_dim(hidden_attn, row_start, rows_part, 0),
        lax.dynamic_slice_in_dim(latent_low, row_start, rows_part, 0),
        preferred_element_type=jnp.float32,
    )
    gain_attn_grad = jnp.sum(
        lax.dynamic_slice_in_dim(attn_in_grad * normed_first, row_start, rows_part, 0), axis=0
    )
    grad_inputs = (
        middle_grad + norm_back(attn_in_grad, gain_attn, normed_first, inv_first)
    ).astype(jnp.bfloat16)
    grad_query, grad_latent_up, grad_output, grad_shared_in, grad_shared_out = (
        lax.psum_scatter(
            query_w_grad.astype(jnp.bfloat16), "ep", scatter_dimension=0, tiled=True
        ).astype(jnp.float32),
        lax.psum_scatter(
            latent_up_grad.astype(jnp.bfloat16), "ep", scatter_dimension=0, tiled=True
        ).astype(jnp.float32),
        lax.psum_scatter(
            output_w_grad.astype(jnp.bfloat16), "ep", scatter_dimension=1, tiled=True
        ).astype(jnp.float32),
        lax.psum_scatter(
            shared_in_grad.astype(jnp.bfloat16), "ep", scatter_dimension=1, tiled=True
        ).astype(jnp.float32),
        lax.psum_scatter(
            shared_out_grad.astype(jnp.bfloat16), "ep", scatter_dimension=1, tiled=True
        ).astype(jnp.float32),
    )
    grad_latent, grad_gain_latent, grad_gain_attn, grad_gain_ffn, grad_router = (
        lax.psum_scatter(latent_w_grad, ("ep", "tp"), scatter_dimension=0, tiled=True),
        lax.psum_scatter(gain_latent_grad, ("ep", "tp"), scatter_dimension=0, tiled=True),
        lax.psum_scatter(gain_attn_grad, ("ep", "tp"), scatter_dimension=0, tiled=True),
        lax.psum_scatter(gain_ffn_grad, ("ep", "tp"), scatter_dimension=0, tiled=True),
        lax.psum_scatter(router_grad, ("ep", "tp"), scatter_dimension=0, tiled=True),
    )
    return (
        block_out,
        grad_inputs,
        grad_gain_attn,
        grad_query,
        grad_latent,
        grad_gain_latent,
        grad_latent_up,
        grad_output,
        grad_gain_ffn,
        grad_router,
        grad_shared_in,
        grad_shared_out,
        grad_expert_in,
        grad_expert_out,
    )


MESH = pl.DeviceIdType.MESH


def plane_partners(ep):
    def flip(bit):
        return ep + bit - 2 * bit * lax.rem(lax.div(ep, bit), 2)

    return flip(1), flip(2), flip(4)


def line_order(tp):
    def pick(a, b, c, d):
        return jnp.where(tp == 0, a, jnp.where(tp == 1, b, jnp.where(tp == 2, c, d)))

    return (tp, pick(1, 0, 3, 2), pick(2, 2, 1, 1), pick(3, 3, 0, 0))


def greet(devices):
    barrier = pltpu.get_barrier_semaphore()
    for ep, tp in devices:
        pl.semaphore_signal(barrier, inc=1, device_id=(ep, tp), device_id_type=MESH)
    pl.semaphore_wait(barrier, len(devices))


def remote(src, dst, send, recv, device):
    return pltpu.make_async_remote_copy(
        src_ref=src, dst_ref=dst, send_sem=send, recv_sem=recv, device_id=device, device_id_type=MESH
    )


def experts_kernel(
    depth, blocks, routed, shared, experts,
    part_ref, resid_ref, gain_ref, cot_ref, kept_ref, w_in_ref, w_out_ref,
    middle_ref, h_out, cot_all, grads_out, gated_out, out_out, rows_out,
    h_all, got_z, resid_own, cot_tile, gu, act_grad, prob_lanes, diff_lanes, pair_lanes,
    grads_tile, gated_tile, out_tile, rows_tile,
    local_sem, z_send, z_recv, line_send, line_recv, h_send, h_recv, c_send, c_recv, tile_sem, store_sem,
):
    f32, bf16 = jnp.float32, jnp.bfloat16
    ep, tp = lax.axis_index("ep"), lax.axis_index("tp")
    pair, xn, yn = plane_partners(ep)
    parity = lax.rem(ep, 2)
    passed = jnp.where(parity == 0, xn, yn)
    onward = jnp.where(parity == 0, yn, xn)
    diag = xn + yn - ep
    rows = h_all.shape[2]
    width = h_all.shape[3]
    hidden = w_out_ref.shape[0]
    half = blocks // 2
    tile = half * rows
    up, down = jnp.minimum(tp + 1, depth - 1), jnp.maximum(tp - 1, 0)

    def twin(block):
        return block + pair - ep

    greet([(pair, tp), (xn, tp), (yn, tp)] + [(ep, lax.rem(tp + k, depth)) for k in range(1, depth)])

    def z_copy(k):
        to = lax.rem(tp + k, depth)
        start = pl.multiple_of(to * rows, rows)
        return remote(part_ref.at[pl.ds(start, rows)], got_z.at[k - 1], z_send.at[k - 1], z_recv.at[k - 1], (ep, to))

    for k in range(1, depth):
        z_copy(k).start()

    def h_copy(block, chunk, slot, to):
        ref = h_all.at[chunk, block]
        return remote(ref, ref, h_send.at[chunk, slot], h_recv.at[chunk, slot], (to, tp))

    def c_copy(block, chunk, slot, to):
        ref = cot_all.at[chunk, block]
        return remote(ref, ref, c_send.at[chunk, slot], c_recv.at[chunk, slot], (to, tp))

    def c_first(chunk, slot, to):
        src = cot_ref.at[pl.ds(pl.multiple_of(chunk * rows, rows), rows)]
        return remote(src, cot_all.at[chunk, ep], c_send.at[chunk, slot], c_recv.at[chunk, slot], (to, tp))

    def own_cot(chunk):
        src = cot_ref.at[pl.ds(pl.multiple_of(chunk * rows, rows), rows)]
        return pltpu.make_async_copy(src, cot_all.at[chunk, ep], local_sem.at[chunk])

    order = line_order(tp)

    def order_at(k):
        return jnp.where(k == 0, order[0], jnp.where(k == 1, order[1], jnp.where(k == 2, order[2], order[3])))

    resid_copy = pltpu.make_async_copy(
        resid_ref.at[pl.ds(pl.multiple_of(tp * rows, rows), rows)], resid_own, local_sem.at[depth]
    )
    resid_copy.start()
    for k in range(depth):
        c_first(order[k], 1, xn).start()
        c_first(order[k], 2, yn).start()
        c_first(order[k], 0, pair).start()
        own_cot(order[k]).start()
    resid_copy.wait()
    for k in range(1, depth):
        z_copy(k).wait_recv()

    def norm_rows(r, _):
        here = pl.ds(pl.multiple_of(r * 16, 16), 16)
        own = pl.ds(pl.multiple_of(tp * rows + r * 16, 16), 16)
        total = part_ref[own, :].astype(f32)
        for k in range(depth - 1):
            total = total + got_z[k, here, :].astype(f32)
        middle = resid_own[here, :].astype(f32) + total
        inverse = lax.rsqrt(jnp.mean(middle * middle, axis=-1, keepdims=True) + EPSILON)
        middle_ref[here, :] = middle
        h_all[tp, ep, here, :] = (middle * inverse * gain_ref[...]).astype(bf16)
        return 0

    lax.fori_loop(0, rows // 16, norm_rows, 0)

    def along(chunk, way, to):
        ref = h_all.at[chunk, ep]
        return remote(ref, ref, line_send.at[chunk, way], line_recv.at[chunk], (ep, to))

    def goes_up(chunk):
        return (chunk <= tp) & (tp < depth - 1)

    def goes_down(chunk):
        return (chunk >= tp) & (tp > 0)

    def send_chunk(k):
        chunk = order[k]
        if k > 0:
            along(chunk, 0, up).wait_recv()

        @pl.when(goes_up(chunk))
        def _():
            along(chunk, 0, up).start()

        @pl.when(goes_down(chunk))
        def _():
            along(chunk, 1, down).start()

        h_copy(ep, chunk, 1, xn).start()
        h_copy(ep, chunk, 2, yn).start()
        h_copy(ep, chunk, 0, pair).start()

    def forward_chunk(chunk):
        for copy in (h_copy, c_copy):
            copy(xn, chunk, 1, xn).wait_recv()
            copy(yn, chunk, 2, yn).wait_recv()
            copy(passed, chunk, 3, onward).start()
            copy(xn, chunk, 4, pair).start()
            copy(yn, chunk, 5, pair).start()

    def forward_diag(chunk):
        for copy in (h_copy, c_copy):
            copy(diag, chunk, 3, onward).wait_recv()
            copy(diag, chunk, 6, pair).start()

    def await_pair(chunk, slots):
        for copy in (h_copy, c_copy):
            for slot, block in slots:
                copy(block, chunk, slot, pair).wait_recv()

    send_chunk(0)
    send_chunk(1)

    lanes = lax.broadcasted_iota(jnp.int32, (1, 128), 1)
    base = routed + shared
    slab = base // 128 * 128
    lane0 = base - slab
    near_half = lax.div(ep, half)

    def tile_copies(i):
        k, side = lax.div(i, 2), lax.rem(i, 2)
        chunk = order_at(k)
        start = jnp.where(side == 0, near_half, 1 - near_half) * half
        group = pl.ds(start, half)
        slot = lax.rem(i, 2)
        stores = [
            pltpu.make_async_copy(h_all.at[chunk, group], h_out.at[chunk, group], store_sem.at[slot, 0]),
            pltpu.make_async_copy(grads_tile.at[slot], grads_out.at[chunk, group], store_sem.at[slot, 1]),
            pltpu.make_async_copy(gated_tile.at[slot], gated_out.at[chunk, group], store_sem.at[slot, 2]),
            pltpu.make_async_copy(out_tile.at[slot], out_out.at[group, chunk], store_sem.at[slot, 3]),
            pltpu.make_async_copy(rows_tile.at[slot], rows_out.at[chunk, group], store_sem.at[slot, 4]),
        ]
        load = pltpu.make_async_copy(cot_all.at[chunk, group], cot_tile, tile_sem)
        return chunk, start, slot, load, stores

    def step(i, _):
        k, side = lax.div(i, 2), lax.rem(i, 2)
        chunk, start, slot, load, stores = tile_copies(i)

        @pl.when(side == 0)
        def _():
            own_cot(chunk).wait()
            forward_chunk(chunk)

        @pl.when(i == 0)
        def _():
            send_chunk(2)

        @pl.when(side == 0)
        def _():
            await_pair(chunk, ((0, pair), (4, twin(xn))))

        @pl.when(side == 1)
        def _():
            forward_diag(chunk)

        @pl.when(i == 1)
        def _():
            send_chunk(3)

        @pl.when(side == 1)
        def _():
            await_pair(chunk, ((5, twin(yn)), (6, twin(diag))))

        load.start()

        @pl.when(i >= 2)
        def _():
            for copy in tile_copies(i - 2)[4]:
                copy.wait()

        group = pl.ds(start, half)
        stores[0].start()
        for n in range(0, 2 * hidden, 512):
            gu[:, n : n + 512] = jnp.dot(
                h_all[chunk, group].reshape(tile, width), w_in_ref[:, n : n + 512], preferred_element_type=f32
            )
        piece = gu[:, slab : slab + 128]
        logits = piece + pltpu.roll(piece, 128 - experts, 1) + pltpu.roll(piece, 128 - 2 * experts, 1)
        is_logit = (lanes >= lane0) & (lanes < lane0 + experts)
        logits = jnp.where(is_logit, logits, -1e30)
        exps = jnp.exp(logits - jnp.max(logits, axis=-1, keepdims=True))
        probs = exps / jnp.sum(exps, axis=-1, keepdims=True)
        here = (lanes == lane0 + ep).astype(f32)
        kept = kept_ref[chunk, group].reshape(tile, 128).astype(f32)
        prob_here = jnp.sum(probs * here * kept, axis=-1, keepdims=True)
        prob_lanes[...] = jnp.broadcast_to(prob_here, (tile, 128))
        diff_lanes[...] = here - probs
        load.wait()
        act_grad[...] = lax.dot_general(
            cot_tile[...].reshape(tile, width), w_out_ref[...], (((1,), (1,)), ((), ())), preferred_element_type=f32
        )
        strip = 64

        def strips(r, _):
            at = pl.ds(pl.multiple_of(r * strip, strip), strip)
            gate_here = prob_lanes[at, :]
            pair_sum = jnp.zeros((strip, 128), f32)
            per = rows // strip
            block, inner = lax.div(r, per), pl.ds(pl.multiple_of(lax.rem(r, per) * strip, strip), strip)
            for n in range(0, hidden, 128):
                gate = gu[at, n : n + 128]
                up_val = gu[at, hidden + n : hidden + n + 128]
                grad = act_grad[at, n : n + 128]
                if n + 128 <= routed:
                    scale = gate_here
                elif n >= routed:
                    scale = None
                else:
                    scale = jnp.where(lanes < routed - n, gate_here, 1.0)
                sig = jax.nn.sigmoid(gate)
                silu = gate * sig
                act = silu * up_val
                if n < routed:
                    both = act * grad
                    if n + 128 > routed:
                        both = jnp.where(lanes < routed - n, both, 0.0)
                    pair_sum = pair_sum + both
                    act = act * scale
                    grad = grad * scale
                gated_tile[slot, block, inner, n : n + 128] = act.astype(bf16)
                grads_tile[slot, block, inner, n : n + 128] = (
                    grad * up_val * (sig * (1.0 + gate * (1.0 - sig)))
                ).astype(bf16)
                grads_tile[slot, block, inner, hidden + n : hidden + n + 128] = (grad * silu).astype(bf16)
            pair_lanes[at, :] = pair_sum
            return 0

        lax.fori_loop(0, tile // strip, strips, 0)
        pair_grad = jnp.sum(pair_lanes[...], axis=-1, keepdims=True)
        logit_grad = pair_grad * prob_lanes[...] * diff_lanes[...]
        logit_grad = logit_grad + pltpu.roll(logit_grad, experts, 1) + pltpu.roll(logit_grad, 2 * experts, 1)
        old = grads_tile[slot, :, :, slab : slab + 128].reshape(tile, 128)
        grads_tile[slot, :, :, slab : slab + 128] = (
            jnp.where(lanes >= lane0, logit_grad.astype(bf16), old).reshape(half, rows, 128)
        )
        for n in range(0, width, 512):
            rows_tile[slot, :, :, n : n + 512] = (
                lax.dot_general(
                    grads_tile[slot].reshape(tile, 2 * hidden), w_in_ref[n : n + 512, :], (((1,), (1,)), ((), ())),
                    preferred_element_type=f32,
                ).astype(bf16).reshape(half, rows, 512)
            )
            out_tile[slot, :, :, n : n + 512] = (
                jnp.dot(gated_tile[slot].reshape(tile, hidden), w_out_ref[:, n : n + 512], preferred_element_type=f32)
                .astype(bf16).reshape(half, rows, 512)
            )
        for copy in stores[1:]:
            copy.start()
        return 0

    lax.fori_loop(0, 2 * depth, step, 0)
    for i in (2 * depth - 2, 2 * depth - 1):
        for copy in tile_copies(i)[4]:
            copy.wait()
    for k in range(1, depth):
        z_copy(k).wait_send()

    def drain(k, _):
        chunk = order_at(k)

        @pl.when(goes_up(chunk))
        def _():
            along(chunk, 0, up).wait_send()

        @pl.when(goes_down(chunk))
        def _():
            along(chunk, 1, down).wait_send()

        for slot in range(7):
            h_copy(ep, chunk, slot, pair).wait_send()
            c_copy(ep, chunk, slot, pair).wait_send()
        return 0

    lax.fori_loop(0, depth, drain, 0)


def experts_call(attn_part, inputs, gain, cotangent, kept, w_in, w_out, blocks, depth, routed, shared, experts, cid):
    f32, bf16 = jnp.float32, jnp.bfloat16
    tokens, width = inputs.shape
    rows = tokens // depth
    hidden = w_out.shape[0]
    half = blocks // 2
    tile = half * rows
    dma = pltpu.SemaphoreType.DMA
    vmem, anywhere = pl.BlockSpec(memory_space=pltpu.VMEM), pl.BlockSpec(memory_space=pl.ANY)

    def units(size):
        return jax.ShapeDtypeStruct((depth, blocks, rows, size), bf16)

    return pl.pallas_call(
        functools.partial(experts_kernel, depth, blocks, routed, shared, experts),
        out_shape=(
            jax.ShapeDtypeStruct((rows, width), f32),
            units(width), units(width), units(2 * hidden), units(hidden),
            jax.ShapeDtypeStruct((blocks, depth, rows, width), bf16), units(width),
        ),
        in_specs=[vmem, anywhere, vmem, anywhere, vmem, vmem, vmem],
        out_specs=(vmem,) + (anywhere,) * 6,
        scratch_shapes=[
            pltpu.VMEM((depth, blocks, rows, width), bf16),
            pltpu.VMEM((depth - 1, rows, width), bf16),
            pltpu.VMEM((rows, width), bf16),
            pltpu.VMEM((half, rows, width), bf16),
            pltpu.VMEM((tile, 2 * hidden), f32),
            pltpu.VMEM((tile, hidden), f32),
            pltpu.VMEM((tile, 128), f32),
            pltpu.VMEM((tile, 128), f32),
            pltpu.VMEM((tile, 128), f32),
            pltpu.VMEM((2, half, rows, 2 * hidden), bf16),
            pltpu.VMEM((2, half, rows, hidden), bf16),
            pltpu.VMEM((2, half, rows, width), bf16),
            pltpu.VMEM((2, half, rows, width), bf16),
            dma((depth + 1,)),
            dma((depth - 1,)), dma((depth - 1,)),
            dma((depth, 2)), dma((depth,)),
            dma((depth, 7)), dma((depth, 7)),
            dma((depth, 7)), dma((depth, 7)),
            dma, dma((2, 5)),
        ],
        compiler_params=pltpu.CompilerParams(collective_id=cid, has_side_effects=True, vmem_limit_bytes=60 << 20),
    )(attn_part, inputs, gain.reshape(1, width), cotangent, kept, w_in, w_out)


def sum_kernel(
    depth, part_ref, h_ref, grads_ref, gated_ref, cot_ref, out_ref, in_grad, out_grad,
    mine, got_pair, got_first, got_second, got_z, keep, h_tile, grads_tile, gated_tile, cot_tile,
    mine_sem, ps, pr, fs, fr, ss, sr, zs, zr, tile_sem,
):
    f32 = jnp.float32
    rows = part_ref.shape[2]
    ep, tp = lax.axis_index("ep"), lax.axis_index("tp")
    pair, xn, yn = plane_partners(ep)
    parity = lax.rem(ep, 2)
    first = jnp.where(parity == 0, xn, yn)
    second = jnp.where(parity == 0, yn, xn)
    diag = xn + yn - ep
    blocks = (first, diag, ep, second)
    pair_slot = (3, 1, 2, 0)
    greet([(pair, tp), (xn, tp), (yn, tp)] + [(ep, lax.rem(tp + k, depth)) for k in range(1, depth)])
    steps = [(k + 1) % depth for k in range(depth)]

    def chunk_of(i):
        return lax.rem(tp + steps[i], depth)

    def pair_copy(i, slot):
        src = part_ref.at[chunk_of(i), blocks[slot] + pair - ep]
        to = pair_slot[slot]
        return remote(src, got_pair.at[i, to], ps.at[i, slot], pr.at[i, to], (pair, tp))

    def pair_wait(i, slot):
        return remote(part_ref.at[0, 0], got_pair.at[i, slot], ps.at[i, slot], pr.at[i, slot], (pair, tp))

    def mine_copy(i, slot):
        return pltpu.make_async_copy(part_ref.at[chunk_of(i), blocks[slot]], mine.at[i, slot], mine_sem.at[i, slot])

    def first_copy(i, slot):
        return remote(mine.at[i, slot], got_first.at[i, slot], fs.at[i, slot], fr.at[i, slot], (first, tp))

    def second_copy(i):
        return remote(mine.at[i, 3], got_second.at[i], ss.at[i], sr.at[i], (second, tp))

    def z_copy(i):
        k = steps[i]
        return remote(mine.at[i, 2], got_z.at[k - 1], zs.at[k - 1], zr.at[k - 1], (ep, lax.rem(tp + k, depth)))

    def add(dst, a, b):
        def body(r, _):
            at = pl.ds(pl.multiple_of(r * 16, 16), 16)
            dst[at, :] = (a[at, :].astype(f32) + b[at, :].astype(f32)).astype(dst.dtype)
            return 0

        lax.fori_loop(0, rows // 16, body, 0)

    for i in range(depth):
        for slot in (3, 1, 2, 0):
            pair_copy(i, slot).start()
        for slot in range(4):
            mine_copy(i, slot).start()

    def tile_loads(c):
        return [
            pltpu.make_async_copy(src.at[c], dst, tile_sem.at[n])
            for n, (src, dst) in enumerate(
                ((h_ref, h_tile), (grads_ref, grads_tile), (gated_ref, gated_tile), (cot_ref, cot_tile))
            )
        ]

    def stage_a(i):
        for slot in range(4):
            mine_copy(i, slot).wait()
            pair_wait(i, slot).wait_recv()
            add(mine.at[i, slot], mine.at[i, slot], got_pair.at[i, slot])
            if slot < 2:
                first_copy(i, slot).start()

    def stage_b(i):
        first_copy(i, 1).wait_recv()
        add(mine.at[i, 3], mine.at[i, 3], got_first.at[i, 1])
        second_copy(i).start()
        first_copy(i, 0).wait_recv()
        add(mine.at[i, 2], mine.at[i, 2], got_first.at[i, 0])

    def stage_c(i):
        second_copy(i).wait_recv()
        if i < depth - 1:
            add(mine.at[i, 2], mine.at[i, 2], got_second.at[i])
            z_copy(i).start()
        else:
            add(keep, mine.at[i, 2], got_second.at[i])

    count = h_tile.shape[0] * rows
    width = h_tile.shape[2]
    hidden = gated_tile.shape[2]

    def weights(c):
        for load in tile_loads(c):
            load.wait()
        turned = (((0,), (0,)), ((), ()))

        def in_part(m, _):
            at = pl.ds(pl.multiple_of(m * 512, 512), 512)
            found = lax.dot_general(
                h_tile[:, :, at].reshape(count, 512), grads_tile[...].reshape(count, 2 * hidden), turned,
                preferred_element_type=f32,
            )
            in_grad[at, :] = found if c == 0 else in_grad[at, :] + found
            return 0

        lax.fori_loop(0, width // 512, in_part, 0)

        def out_part(m, _):
            at = pl.ds(pl.multiple_of(m * 512, 512), 512)
            found = lax.dot_general(
                gated_tile[...].reshape(count, hidden), cot_tile[:, :, at].reshape(count, 512), turned,
                preferred_element_type=f32,
            )
            out_grad[:, at] = found if c == 0 else out_grad[:, at] + found
            return 0

        lax.fori_loop(0, width // 512, out_part, 0)
        if c + 1 < depth:
            for load in tile_loads(c + 1):
                load.start()

    for load in tile_loads(0):
        load.start()
    for t in range(depth + 2):
        if t < depth:
            stage_a(t)
        if 0 <= t - 1 < depth:
            stage_b(t - 1)
        if 0 <= t - 2 < depth:
            stage_c(t - 2)
        if t < depth:
            weights(t)
    for i in range(depth - 1):
        z_copy(i).wait_recv()

    def total(r, _):
        at = pl.ds(pl.multiple_of(r * 16, 16), 16)
        value = keep[at, :]
        for k in range(depth - 1):
            value = value + got_z[k, at, :].astype(f32)
        out_ref[at, :] = value
        return 0

    lax.fori_loop(0, rows // 16, total, 0)
    for i in range(depth):
        for slot in range(4):
            pair_copy(i, slot).wait_send()
        for slot in range(2):
            first_copy(i, slot).wait_send()
        second_copy(i).wait_send()
        if i < depth - 1:
            z_copy(i).wait_send()


def sum_call(part, h_all, grads, gated, cot_all, cid):
    f32, bf16 = jnp.float32, jnp.bfloat16
    depth, blocks, rows, width = part.shape
    hidden = gated.shape[3]
    dma = pltpu.SemaphoreType.DMA
    vmem, anywhere = pl.BlockSpec(memory_space=pltpu.VMEM), pl.BlockSpec(memory_space=pl.ANY)
    return pl.pallas_call(
        functools.partial(sum_kernel, depth),
        out_shape=(
            jax.ShapeDtypeStruct((rows, width), f32),
            jax.ShapeDtypeStruct((width, 2 * hidden), f32),
            jax.ShapeDtypeStruct((hidden, width), f32),
        ),
        in_specs=[anywhere] * 5,
        out_specs=(vmem, vmem, vmem),
        scratch_shapes=[
            pltpu.VMEM((depth, 4, rows, width), bf16),
            pltpu.VMEM((depth, 4, rows, width), bf16),
            pltpu.VMEM((depth, 2, rows, width), bf16),
            pltpu.VMEM((depth, rows, width), bf16),
            pltpu.VMEM((depth - 1, rows, width), bf16),
            pltpu.VMEM((rows, width), f32),
            pltpu.VMEM((blocks, rows, width), bf16),
            pltpu.VMEM((blocks, rows, 2 * hidden), bf16),
            pltpu.VMEM((blocks, rows, hidden), bf16),
            pltpu.VMEM((blocks, rows, width), bf16),
            dma((depth, 4)), dma((depth, 4)), dma((depth, 4)), dma((depth, 2)), dma((depth, 2)),
            dma((depth,)), dma((depth,)), dma((depth - 1,)), dma((depth - 1,)), dma((4,)),
        ],
        compiler_params=pltpu.CompilerParams(collective_id=cid, has_side_effects=True, vmem_limit_bytes=62 << 20),
    )(part, h_all, grads, gated, cot_all)


def padded_hidden(routed, shared):
    return -(-(routed + shared + 24) // 128) * 128


def split_wide(values):
    high = values.astype(jnp.bfloat16)
    rest = values - high.astype(jnp.float32)
    mid = rest.astype(jnp.bfloat16)
    low = (rest - mid.astype(jnp.float32)).astype(jnp.bfloat16)
    return (high, mid, low)


def body_dense(
    inputs,
    gain_attn,
    w_query,
    w_latent,
    gain_latent,
    w_latent_up,
    w_output,
    gain_ffn,
    w_router,
    w_shared_in,
    w_shared_out,
    w_expert_in,
    w_expert_out,
    expert_ids,
    slot_ids,
    cotangent,
):
    f32, bf16 = jnp.float32, jnp.bfloat16
    tokens, model_width = inputs.shape
    ep_count, tp_count = lax.axis_size("ep"), lax.axis_size("tp")
    ep_index, tp_index = lax.axis_index("ep"), lax.axis_index("tp")
    heads_here = w_output.shape[0] // VDIM
    experts = w_router.shape[1]
    capacity = (9 * tokens * TOPK + 64 * experts - 1) // (64 * experts) * 8
    qk_width = NOPE + ROPE
    score_scale = qk_width ** (-0.5)
    rows_part = tokens // tp_count
    row_start = tp_index * rows_part

    expert_range = jnp.arange(experts, dtype=jnp.int32)
    kept = jnp.any(
        (expert_ids[:, :, None] == expert_range) & (slot_ids < capacity)[:, :, None], axis=1
    ).astype(f32)
    kept_here = lax.all_to_all(kept, "ep", split_axis=1, concat_axis=0, tiled=True)
    rows_part = tokens // tp_count
    kept_lanes = jnp.broadcast_to(
        kept_here.reshape(ep_count, tp_count, rows_part, 1).swapaxes(0, 1),
        (tp_count, ep_count, rows_part, 128),
    ).astype(bf16)

    routed = w_expert_in.shape[3]
    shared = w_shared_in.shape[2] // ep_count
    hidden = padded_hidden(routed, shared)
    shared_start = ep_index * shared
    shared_in = lax.dynamic_slice_in_dim(w_shared_in, shared_start, shared, 2)
    shared_out = lax.dynamic_slice_in_dim(w_shared_out, shared_start, shared, 0)
    router_parts = jnp.concatenate(split_wide(w_router), axis=1)
    fill = hidden - routed - shared
    w_in = jnp.concatenate(
        [
            w_expert_in[0, 0],
            shared_in[0],
            jnp.pad(router_parts, ((0, 0), (0, fill - router_parts.shape[1]))),
            w_expert_in[0, 1],
            shared_in[1],
            jnp.zeros((model_width, fill), bf16),
        ],
        axis=1,
    )
    w_out = jnp.concatenate(
        [w_expert_out[0], shared_out, jnp.zeros((fill, model_width), bf16)], axis=0
    )

    resid = inputs.astype(f32)
    inv_first = lax.rsqrt(jnp.mean(resid * resid, axis=-1, keepdims=True) + EPSILON)
    normed_first = resid * inv_first
    hidden_attn = (normed_first * gain_attn).astype(bf16)
    cosine, sine_table = angles(tokens, ROPE)
    query_raw = jnp.dot(hidden_attn, w_query, preferred_element_type=f32).reshape(
        tokens, heads_here, qk_width
    )
    query_rot = jnp.concatenate(
        [
            query_raw[..., :NOPE],
            rotate(query_raw[..., NOPE:], cosine[:, None], sine_table[:, None]),
        ],
        axis=-1,
    ).astype(bf16)
    latent = jnp.dot(hidden_attn, w_latent, preferred_element_type=f32)
    compressed = latent[:, :KV_RANK]
    inv_latent = lax.rsqrt(jnp.mean(compressed * compressed, axis=-1, keepdims=True) + EPSILON)
    normed_latent = compressed * inv_latent
    latent_in = (normed_latent * gain_latent).astype(bf16)
    key_rope = rotate(latent[:, KV_RANK:], cosine, sine_table).astype(bf16)
    key_value = (
        jnp.dot(latent_in, w_latent_up, preferred_element_type=f32)
        .astype(bf16)
        .reshape(tokens, heads_here, NOPE + VDIM)
    )
    key_nope = key_value[..., :NOPE]
    values = key_value[..., NOPE:]
    block_ids = jnp.arange(tokens) // BLOCK
    allowed = block_ids[None, :] <= block_ids[:, None]
    scores = attention_scores(query_rot, key_nope, key_rope, score_scale, allowed)
    row_peak = jnp.max(scores, axis=-1, keepdims=True)
    exp_scores = jnp.exp(scores - row_peak)
    totals = jnp.sum(exp_scores, axis=-1, keepdims=True)
    attn_probs = exp_scores / totals
    log_total = row_peak + jnp.log(totals)
    attended = (
        jnp.einsum("hqk,khd->qhd", attn_probs.astype(bf16), values, preferred_element_type=f32)
        .astype(bf16)
        .reshape(tokens, heads_here * VDIM)
    )
    attn_part = jnp.dot(attended, w_output, preferred_element_type=f32).astype(bf16)

    middle, hidden_all, cot_all, hidden_grads, gated, out_part, rows_grad = experts_call(
        attn_part, inputs, gain_ffn, cotangent, kept_lanes, w_in, w_out,
        ep_count, tp_count, routed, shared, experts, 0,
    )
    ffn_grad, in_grad_w, out_grad_w = sum_call(
        rows_grad, hidden_all, hidden_grads, gated, cot_all, 1
    )
    cot_rows = lax.dynamic_slice_in_dim(cotangent, row_start, rows_part, 0).astype(f32)
    inv_second = lax.rsqrt(jnp.mean(middle * middle, axis=-1, keepdims=True) + EPSILON)
    normed_second = middle * inv_second
    base = routed + shared
    in_grad_gate, in_grad_up = in_grad_w[:, :hidden], in_grad_w[:, hidden:]
    router_grad = in_grad_gate[:, base : base + experts]
    grad_expert_in = jnp.stack([in_grad_gate[:, :routed], in_grad_up[:, :routed]])[None]
    grad_expert_out = out_grad_w[None, :routed]
    shared_in_part = jnp.stack([in_grad_gate[:, routed:base], in_grad_up[:, routed:base]])
    grad_shared_in = lax.all_to_all(
        shared_in_part.astype(bf16), "ep", split_axis=1, concat_axis=2, tiled=True
    ).astype(f32)
    grad_shared_out = lax.all_to_all(
        out_grad_w[routed:base].astype(bf16), "ep", split_axis=1, concat_axis=0, tiled=True
    ).astype(f32)

    ffn_plane = lax.psum_scatter(
        out_part.reshape(ep_count * tokens, model_width),
        "ep",
        scatter_dimension=0,
        tiled=True,
    )
    ffn_rows = lax.psum_scatter(ffn_plane, "tp", scatter_dimension=0, tiled=True).astype(f32)
    block_out = lax.all_gather((middle + ffn_rows).astype(bf16), "tp", tiled=True)
    middle_grad = cot_rows + norm_back(ffn_grad, gain_ffn, normed_second, inv_second)
    gain_ffn_grad = jnp.sum(ffn_grad * normed_second, axis=0)
    branch_grad = lax.all_gather(middle_grad.astype(bf16), "tp", tiled=True)

    output_w_grad = jnp.einsum("tf,td->fd", attended, branch_grad, preferred_element_type=f32)
    attended_grad = (
        jnp.einsum("td,fd->tf", branch_grad, w_output, preferred_element_type=f32)
        .astype(bf16)
        .reshape(tokens, heads_here, VDIM)
    )
    scores_again = attention_scores(query_rot, key_nope, key_rope, score_scale, allowed)
    probs_again = jnp.exp(scores_again - log_total)
    values_grad = jnp.einsum(
        "hqk,qhd->khd", probs_again.astype(bf16), attended_grad, preferred_element_type=f32
    )
    prob_part = jnp.einsum("qhd,khd->hqk", attended_grad, values, preferred_element_type=f32)
    score_grad = (
        probs_again * (prob_part - jnp.sum(probs_again * prob_part, axis=-1, keepdims=True))
    ).astype(bf16)
    query_nope_grad = (
        jnp.einsum("hqk,khd->qhd", score_grad, key_nope, preferred_element_type=f32) * score_scale
    )
    query_rope_grad = (
        jnp.einsum("hqk,kr->qhr", score_grad, key_rope, preferred_element_type=f32) * score_scale
    )
    key_nope_grad = (
        jnp.einsum("hqk,qhd->khd", score_grad, query_rot[..., :NOPE], preferred_element_type=f32)
        * score_scale
    )
    key_rope_grad = (
        jnp.einsum("hqk,qhr->kr", score_grad, query_rot[..., NOPE:], preferred_element_type=f32)
        * score_scale
    )
    kv_grad = (
        jnp.concatenate([key_nope_grad, values_grad], axis=-1)
        .astype(bf16)
        .reshape(tokens, heads_here * (NOPE + VDIM))
    )
    latent_up_grad = jnp.einsum("tr,tf->rf", latent_in, kv_grad, preferred_element_type=f32)
    latent_in_grad = jnp.einsum("tf,rf->tr", kv_grad, w_latent_up, preferred_element_type=f32)
    gain_latent_grad = jnp.sum(latent_in_grad * normed_latent, axis=0)
    latent_grad_part = jnp.concatenate(
        [
            norm_back(latent_in_grad, gain_latent, normed_latent, inv_latent),
            rotate(key_rope_grad, cosine, -sine_table),
        ],
        axis=-1,
    ).astype(bf16)
    query_grad = (
        jnp.concatenate(
            [query_nope_grad, rotate(query_rope_grad, cosine[:, None], -sine_table[:, None])],
            axis=-1,
        )
        .astype(bf16)
        .reshape(tokens, heads_here * qk_width)
    )
    query_w_grad = jnp.einsum("td,tf->df", hidden_attn, query_grad, preferred_element_type=f32)
    hidden_part = (
        jnp.einsum("tf,df->td", query_grad, w_query, preferred_element_type=f32)
        + jnp.einsum("tf,df->td", latent_grad_part, w_latent, preferred_element_type=f32)
    ).astype(bf16)
    attn_in_grad = lax.psum_scatter(hidden_part, "tp", scatter_dimension=0, tiled=True).astype(f32)
    latent_w_grad = jnp.einsum(
        "td,tf->df", hidden_attn, latent_grad_part, preferred_element_type=f32
    )
    normed_rows = lax.dynamic_slice_in_dim(normed_first, row_start, rows_part, 0)
    inv_rows = lax.dynamic_slice_in_dim(inv_first, row_start, rows_part, 0)
    gain_attn_grad = jnp.sum(attn_in_grad * normed_rows, axis=0)
    grad_inputs = lax.all_gather(
        (middle_grad + norm_back(attn_in_grad, gain_attn, normed_rows, inv_rows)).astype(bf16),
        "tp",
        tiled=True,
    )
    grad_query, grad_latent_up, grad_output = (
        lax.psum_scatter(
            query_w_grad.astype(bf16), "ep", scatter_dimension=0, tiled=True
        ).astype(f32),
        lax.psum_scatter(
            latent_up_grad.astype(bf16), "ep", scatter_dimension=0, tiled=True
        ).astype(f32),
        lax.psum_scatter(
            output_w_grad.astype(bf16), "ep", scatter_dimension=1, tiled=True
        ).astype(f32),
    )

    def sum_all(part):
        plane = lax.psum_scatter(part, "ep", scatter_dimension=0, tiled=True)
        return lax.psum_scatter(plane, "tp", scatter_dimension=0, tiled=True)

    grad_latent, grad_gain_latent, grad_gain_attn, grad_gain_ffn, grad_router = (
        sum_all(latent_w_grad),
        sum_all(gain_latent_grad),
        sum_all(gain_attn_grad),
        sum_all(gain_ffn_grad),
        sum_all(router_grad),
    )
    return (
        block_out,
        grad_inputs,
        grad_gain_attn,
        grad_query,
        grad_latent,
        grad_gain_latent,
        grad_latent_up,
        grad_output,
        grad_gain_ffn,
        grad_router,
        grad_shared_in,
        grad_shared_out,
        grad_expert_in,
        grad_expert_out,
    )


def solution(mesh):
    near = mesh.shape["ep"] == 8 and mesh.shape["tp"] == 4
    body = body_dense if near else body_slots
    placed = (
        P("ep", None),
        P(),
        P(None, "tp"),
        P(),
        P(),
        P(None, "tp"),
        P("tp", None),
        P(),
        P(),
        P(None, None, "tp"),
        P("tp", None),
        P("ep", None, None, "tp"),
        P("ep", "tp", None),
        P("ep", None),
        P("ep", None),
        P("ep", None),
    )
    return jax.shard_map(
        body,
        mesh=mesh,
        in_specs=placed,
        out_specs=(
            P("ep", None),
            P("ep", None),
            P(("ep", "tp")),
            P("ep", "tp"),
            P(("ep", "tp"), None),
            P(("ep", "tp")),
            P("ep", "tp"),
            P("tp", "ep"),
            P(("ep", "tp")),
            P(("ep", "tp"), None),
            P(None, "ep", "tp"),
            P("tp", "ep"),
            P("ep", None, None, "tp"),
            P("ep", "tp", None),
        ),
        check_vma=False,
    )
```

```python
import functools
import math

import jax
import jax.numpy as jnp
from jax import lax
from jax.experimental import pallas as pl
from jax.experimental.pallas import tpu as pltpu
from jax.sharding import PartitionSpec as P

NOPE = 128
ROPE = 64
VDIM = 128
KV_RANK = 512
TOPK = 6
BLOCK = 256


EPSILON = 1e-06
HIGHEST = lax.Precision.HIGHEST


def angles(length, rope_width):
    half_width = rope_width // 2
    position = jnp.arange(length, dtype=jnp.float32)
    inverse = jnp.exp(jnp.arange(half_width, dtype=jnp.float32) * (-math.log(10000.0) / half_width))
    angle_table = position[:, None] * inverse[None, :]
    return (jnp.cos(angle_table), jnp.sin(angle_table))


def rotate(values, cosine, sine_table):
    half_width = values.shape[-1] // 2
    front_part = values[..., :half_width]
    second = values[..., half_width:]
    return jnp.concatenate(
        [front_part * cosine - second * sine_table, second * cosine + front_part * sine_table],
        axis=-1,
    )


def silu_parts(gate_val):
    sigmoid_val = jax.nn.sigmoid(gate_val)
    return (gate_val * sigmoid_val, sigmoid_val * (1.0 + gate_val * (1.0 - sigmoid_val)))


def norm_back(grad_norm, gain_vec, normed, inverse):
    scaled = grad_norm * gain_vec
    return inverse * (scaled - normed * jnp.mean(scaled * normed, axis=-1, keepdims=True))


def attention_scores(query_rot, key_nope, key_rope, score_scale, allowed):
    nope_scores = jnp.einsum(
        "qhd,khd->hqk", query_rot[..., :NOPE], key_nope, preferred_element_type=jnp.float32
    )
    rope_scores = jnp.einsum(
        "qhr,kr->hqk", query_rot[..., NOPE:], key_rope, preferred_element_type=jnp.float32
    )
    return jnp.where(allowed[None], (nope_scores + rope_scores) * score_scale, -1e30)


def expert_forward(received, w_expert_in, w_expert_out, sources):
    sectioned = received.reshape(sources, -1, received.shape[1], received.shape[2])
    gate_up = jnp.einsum(
        "secd,egdh->secgh", sectioned, w_expert_in, preferred_element_type=jnp.float32
    )
    gate_val, gate_slope = silu_parts(gate_up[..., 0, :])
    activated = (gate_val * gate_up[..., 1, :]).astype(jnp.bfloat16)
    produced = jnp.einsum(
        "sech,ehd->secd", activated, w_expert_out, preferred_element_type=jnp.float32
    )
    return (sectioned, gate_up, activated, produced.reshape(received.shape))


def body_slots(
    inputs,
    gain_attn,
    w_query,
    w_latent,
    gain_latent,
    w_latent_up,
    w_output,
    gain_ffn,
    w_router,
    w_shared_in,
    w_shared_out,
    w_expert_in,
    w_expert_out,
    expert_ids,
    slot_ids,
    cotangent,
):
    tokens, model_width = inputs.shape
    tp_count = lax.axis_size("tp")
    tp_index = lax.axis_index("tp")
    heads_here = w_output.shape[0] // VDIM
    experts = w_router.shape[1]
    local_experts = w_expert_in.shape[0]
    sources = experts // local_experts
    capacity = (9 * tokens * TOPK + 64 * experts - 1) // (64 * experts) * 8
    qk_width = NOPE + ROPE
    score_scale = qk_width ** (-0.5)
    rows_part = tokens // tp_count
    row_start = tp_index * rows_part
    resid = inputs.astype(jnp.float32)
    inv_first = lax.rsqrt(jnp.mean(resid * resid, axis=-1, keepdims=True) + EPSILON)
    normed_first = resid * inv_first
    hidden_attn = (normed_first * gain_attn).astype(jnp.bfloat16)
    cosine, sine_table = angles(tokens, ROPE)
    query_raw = jnp.dot(hidden_attn, w_query, preferred_element_type=jnp.float32).reshape(
        tokens, heads_here, qk_width
    )
    query_rot = jnp.concatenate(
        [
            query_raw[..., :NOPE],
            rotate(query_raw[..., NOPE:], cosine[:, None], sine_table[:, None]),
        ],
        axis=-1,
    ).astype(jnp.bfloat16)
    latent = jnp.dot(hidden_attn, w_latent, preferred_element_type=jnp.float32)
    compressed = latent[:, :KV_RANK]
    inv_latent = lax.rsqrt(jnp.mean(compressed * compressed, axis=-1, keepdims=True) + EPSILON)
    normed_latent = compressed * inv_latent
    latent_in = (normed_latent * gain_latent).astype(jnp.bfloat16)
    key_rope = rotate(latent[:, KV_RANK:], cosine, sine_table).astype(jnp.bfloat16)
    key_value = (
        jnp.dot(latent_in, w_latent_up, preferred_element_type=jnp.float32)
        .astype(jnp.bfloat16)
        .reshape(tokens, heads_here, NOPE + VDIM)
    )
    key_nope = key_value[..., :NOPE]
    values = key_value[..., NOPE:]
    block_ids = jnp.arange(tokens) // BLOCK
    allowed = block_ids[None, :] <= block_ids[:, None]
    scores = attention_scores(query_rot, key_nope, key_rope, score_scale, allowed)
    row_peak = jnp.max(scores, axis=-1, keepdims=True)
    exp_scores = jnp.exp(scores - row_peak)
    totals = jnp.sum(exp_scores, axis=-1, keepdims=True)
    attn_probs = exp_scores / totals
    log_total = row_peak + jnp.log(totals)
    attended = (
        jnp.einsum(
            "hqk,khd->qhd",
            attn_probs.astype(jnp.bfloat16),
            values,
            preferred_element_type=jnp.float32,
        )
        .astype(jnp.bfloat16)
        .reshape(tokens, heads_here * VDIM)
    )
    attn_full = lax.psum(
        jnp.dot(attended, w_output, preferred_element_type=jnp.float32).astype(jnp.bfloat16), "tp"
    ).astype(jnp.float32)
    middle = resid + attn_full
    inv_second = lax.rsqrt(jnp.mean(middle * middle, axis=-1, keepdims=True) + EPSILON)
    normed_second = middle * inv_second
    hidden_ffn = (normed_second * gain_ffn).astype(jnp.bfloat16)
    hidden_wide = hidden_ffn.astype(jnp.float32)
    logits = jnp.dot(hidden_wide, w_router, precision=HIGHEST, preferred_element_type=jnp.float32)
    logit_peak = jnp.max(logits, axis=-1, keepdims=True)
    exp_logits = jnp.exp(logits - logit_peak)
    router_probs = exp_logits / jnp.sum(exp_logits, axis=-1, keepdims=True)
    route_onehot = (
        expert_ids[:, :, None] == jnp.arange(experts, dtype=jnp.int32)[None, None, :]
    ).astype(jnp.float32)
    pair_gate = jnp.sum(route_onehot * router_probs[:, None, :], axis=-1)
    kept_pair = slot_ids < capacity
    flat_index = jnp.where(kept_pair, expert_ids * capacity + slot_ids, experts * capacity)
    row_numbers = jnp.broadcast_to(jnp.arange(tokens, dtype=jnp.int32)[:, None], (tokens, TOPK))
    owner_row = (
        jnp.full((experts * capacity,), tokens, jnp.int32)
        .at[flat_index.reshape(-1)]
        .set(row_numbers.reshape(-1), mode="drop")
    )
    outgoing = jnp.take(hidden_ffn, owner_row, axis=0, mode="fill", fill_value=0).reshape(
        experts, capacity, model_width
    )
    received = lax.all_to_all(outgoing, "ep", split_axis=0, concat_axis=0, tiled=True)
    sectioned, gate_up, activated, produced = expert_forward(
        received, w_expert_in, w_expert_out, sources
    )
    returned = lax.all_to_all(
        produced.astype(jnp.bfloat16), "ep", split_axis=0, concat_axis=0, tiled=True
    ).astype(produced.dtype)
    out_grad = cotangent.astype(jnp.float32)
    back_rows = returned.reshape(-1, model_width)
    combined = jnp.zeros((tokens, model_width), jnp.float32)
    gate_cols = []
    for pick_index in range(TOPK):
        taken_rows = jnp.take(
            back_rows, flat_index[:, pick_index], axis=0, mode="fill", fill_value=0.0
        )
        combined = combined + pair_gate[:, pick_index : pick_index + 1] * taken_rows
        gate_cols.append(jnp.sum(out_grad * taken_rows, axis=-1))
    gate_grad = jnp.stack(gate_cols, axis=1)
    shared_gate = jnp.dot(hidden_ffn, w_shared_in[0], preferred_element_type=jnp.float32)
    shared_up = jnp.dot(hidden_ffn, w_shared_in[1], preferred_element_type=jnp.float32)
    shared_val, shared_slope = silu_parts(shared_gate)
    shared_act = (shared_val * shared_up).astype(jnp.bfloat16)
    branch_part = jnp.dot(shared_act, w_shared_out, preferred_element_type=jnp.float32) + combined
    ffn_full = lax.psum(branch_part.astype(jnp.bfloat16), "tp").astype(jnp.float32)
    block_out = (middle + ffn_full).astype(jnp.bfloat16)
    slot_gate = (
        jnp.zeros((experts * capacity,), jnp.float32)
        .at[flat_index.reshape(-1)]
        .set(pair_gate.reshape(-1), mode="drop")
    )
    gathered_grad = jnp.take(cotangent, owner_row, axis=0, mode="fill", fill_value=0)
    slot_grad = (
        (slot_gate[:, None] * gathered_grad.astype(jnp.float32))
        .astype(jnp.bfloat16)
        .reshape(experts, capacity, model_width)
    )
    grad_arrived = lax.all_to_all(slot_grad, "ep", split_axis=0, concat_axis=0, tiled=True).reshape(
        sectioned.shape
    )
    act_grad = jnp.einsum(
        "secd,ehd->sech", grad_arrived, w_expert_out, preferred_element_type=jnp.float32
    )
    gate_val, gate_slope = silu_parts(gate_up[..., 0, :])
    up_val = gate_up[..., 1, :]
    gu_grad = jnp.stack([act_grad * up_val * gate_slope, act_grad * gate_val], axis=-2).astype(
        jnp.bfloat16
    )
    grad_expert_out = jnp.einsum(
        "sech,secd->ehd", activated, grad_arrived, preferred_element_type=jnp.float32
    )
    grad_expert_in = jnp.einsum(
        "secd,secgh->egdh", sectioned, gu_grad, preferred_element_type=jnp.float32
    )
    rows_grad = jnp.einsum(
        "secgh,egdh->secd", gu_grad, w_expert_in, preferred_element_type=jnp.float32
    ).reshape(received.shape)
    returned_grad = (
        lax.all_to_all(
            rows_grad.astype(jnp.bfloat16), "ep", split_axis=0, concat_axis=0, tiled=True
        )
        .astype(rows_grad.dtype)
        .reshape(-1, model_width)
    )
    routed_grad = jnp.zeros((tokens, model_width), jnp.float32)
    for pick_index in range(TOPK):
        routed_grad = routed_grad + jnp.take(
            returned_grad, flat_index[:, pick_index], axis=0, mode="fill", fill_value=0.0
        )
    shared_act_grad = jnp.einsum(
        "td,fd->tf", cotangent, w_shared_out, preferred_element_type=jnp.float32
    )
    shared_gate_grad = (shared_act_grad * shared_up * shared_slope).astype(jnp.bfloat16)
    shared_up_grad = (shared_act_grad * shared_val).astype(jnp.bfloat16)
    shared_out_grad = jnp.einsum(
        "tf,td->fd", shared_act, cotangent, preferred_element_type=jnp.float32
    )
    shared_in_grad = jnp.stack(
        [
            jnp.einsum(
                "td,tf->df", hidden_ffn, shared_gate_grad, preferred_element_type=jnp.float32
            ),
            jnp.einsum("td,tf->df", hidden_ffn, shared_up_grad, preferred_element_type=jnp.float32),
        ],
        axis=0,
    )
    shared_back = jnp.einsum(
        "tf,df->td", shared_gate_grad, w_shared_in[0], preferred_element_type=jnp.float32
    ) + jnp.einsum("tf,df->td", shared_up_grad, w_shared_in[1], preferred_element_type=jnp.float32)
    prob_grad = jnp.sum(route_onehot * gate_grad[:, :, None], axis=1)
    logit_grad = router_probs * (
        prob_grad - jnp.sum(router_probs * prob_grad, axis=-1, keepdims=True)
    )
    router_back = jnp.einsum(
        "te,de->td", logit_grad, w_router, precision=HIGHEST, preferred_element_type=jnp.float32
    )
    router_grad = jnp.einsum(
        "td,te->de", hidden_wide, logit_grad, precision=HIGHEST, preferred_element_type=jnp.float32
    )
    ffn_grad = lax.psum(
        (shared_back + routed_grad + router_back).astype(jnp.bfloat16), "tp"
    ).astype(jnp.float32)
    middle_grad = out_grad + norm_back(ffn_grad, gain_ffn, normed_second, inv_second)
    gain_ffn_grad = jnp.sum(
        lax.dynamic_slice_in_dim(ffn_grad * normed_second, row_start, rows_part, 0), axis=0
    )
    branch_grad = middle_grad.astype(jnp.bfloat16)
    output_w_grad = jnp.einsum(
        "tf,td->fd", attended, branch_grad, preferred_element_type=jnp.float32
    )
    attended_grad = (
        jnp.einsum("td,fd->tf", branch_grad, w_output, preferred_element_type=jnp.float32)
        .astype(jnp.bfloat16)
        .reshape(tokens, heads_here, VDIM)
    )
    scores_again = attention_scores(query_rot, key_nope, key_rope, score_scale, allowed)
    probs_again = jnp.exp(scores_again - log_total)
    values_grad = jnp.einsum(
        "hqk,qhd->khd",
        probs_again.astype(jnp.bfloat16),
        attended_grad,
        preferred_element_type=jnp.float32,
    )
    prob_part = jnp.einsum(
        "qhd,khd->hqk", attended_grad, values, preferred_element_type=jnp.float32
    )
    score_grad = (
        probs_again * (prob_part - jnp.sum(probs_again * prob_part, axis=-1, keepdims=True))
    ).astype(jnp.bfloat16)
    query_nope_grad = (
        jnp.einsum("hqk,khd->qhd", score_grad, key_nope, preferred_element_type=jnp.float32)
        * score_scale
    )
    query_rope_grad = (
        jnp.einsum("hqk,kr->qhr", score_grad, key_rope, preferred_element_type=jnp.float32)
        * score_scale
    )
    key_nope_grad = (
        jnp.einsum(
            "hqk,qhd->khd", score_grad, query_rot[..., :NOPE], preferred_element_type=jnp.float32
        )
        * score_scale
    )
    key_rope_grad = (
        jnp.einsum(
            "hqk,qhr->kr", score_grad, query_rot[..., NOPE:], preferred_element_type=jnp.float32
        )
        * score_scale
    )
    kv_grad = (
        jnp.concatenate([key_nope_grad, values_grad], axis=-1)
        .astype(jnp.bfloat16)
        .reshape(tokens, heads_here * (NOPE + VDIM))
    )
    latent_up_grad = jnp.einsum("tr,tf->rf", latent_in, kv_grad, preferred_element_type=jnp.float32)
    latent_in_grad = jnp.einsum(
        "tf,rf->tr", kv_grad, w_latent_up, preferred_element_type=jnp.float32
    )
    gain_latent_grad = jnp.sum(latent_in_grad * normed_latent, axis=0)
    latent_grad_part = jnp.concatenate(
        [
            norm_back(latent_in_grad, gain_latent, normed_latent, inv_latent),
            rotate(key_rope_grad, cosine, -sine_table),
        ],
        axis=-1,
    )
    query_grad = (
        jnp.concatenate(
            [query_nope_grad, rotate(query_rope_grad, cosine[:, None], -sine_table[:, None])],
            axis=-1,
        )
        .astype(jnp.bfloat16)
        .reshape(tokens, heads_here * qk_width)
    )
    query_w_grad = jnp.einsum(
        "td,tf->df", hidden_attn, query_grad, preferred_element_type=jnp.float32
    )
    hidden_part = jnp.einsum("tf,df->td", query_grad, w_query, preferred_element_type=jnp.float32)
    hidden_sum, latent_sum = (
        lax.psum(hidden_part.astype(jnp.bfloat16), "tp").astype(jnp.float32),
        lax.psum(latent_grad_part.astype(jnp.bfloat16), "tp").astype(jnp.float32),
    )
    latent_low = latent_sum.astype(jnp.bfloat16)
    attn_in_grad = hidden_sum + jnp.einsum(
        "tf,df->td", latent_low, w_latent, preferred_element_type=jnp.float32
    )
    latent_w_grad = jnp.einsum(
        "td,tf->df",
        lax.dynamic_slice_in_dim(hidden_attn, row_start, rows_part, 0),
        lax.dynamic_slice_in_dim(latent_low, row_start, rows_part, 0),
        preferred_element_type=jnp.float32,
    )
    gain_attn_grad = jnp.sum(
        lax.dynamic_slice_in_dim(attn_in_grad * normed_first, row_start, rows_part, 0), axis=0
    )
    grad_inputs = (
        middle_grad + norm_back(attn_in_grad, gain_attn, normed_first, inv_first)
    ).astype(jnp.bfloat16)
    grad_query, grad_latent_up, grad_output, grad_shared_in, grad_shared_out = (
        lax.psum_scatter(
            query_w_grad.astype(jnp.bfloat16), "ep", scatter_dimension=0, tiled=True
        ).astype(jnp.float32),
        lax.psum_scatter(
            latent_up_grad.astype(jnp.bfloat16), "ep", scatter_dimension=0, tiled=True
        ).astype(jnp.float32),
        lax.psum_scatter(
            output_w_grad.astype(jnp.bfloat16), "ep", scatter_dimension=1, tiled=True
        ).astype(jnp.float32),
        lax.psum_scatter(
            shared_in_grad.astype(jnp.bfloat16), "ep", scatter_dimension=1, tiled=True
        ).astype(jnp.float32),
        lax.psum_scatter(
            shared_out_grad.astype(jnp.bfloat16), "ep", scatter_dimension=1, tiled=True
        ).astype(jnp.float32),
    )
    grad_latent, grad_gain_latent, grad_gain_attn, grad_gain_ffn, grad_router = (
        lax.psum_scatter(latent_w_grad, ("ep", "tp"), scatter_dimension=0, tiled=True),
        lax.psum_scatter(gain_latent_grad, ("ep", "tp"), scatter_dimension=0, tiled=True),
        lax.psum_scatter(gain_attn_grad, ("ep", "tp"), scatter_dimension=0, tiled=True),
        lax.psum_scatter(gain_ffn_grad, ("ep", "tp"), scatter_dimension=0, tiled=True),
        lax.psum_scatter(router_grad, ("ep", "tp"), scatter_dimension=0, tiled=True),
    )
    return (
        block_out,
        grad_inputs,
        grad_gain_attn,
        grad_query,
        grad_latent,
        grad_gain_latent,
        grad_latent_up,
        grad_output,
        grad_gain_ffn,
        grad_router,
        grad_shared_in,
        grad_shared_out,
        grad_expert_in,
        grad_expert_out,
    )


MESH = pl.DeviceIdType.MESH


def plane_partners(ep):
    def flip(bit):
        return ep + bit - 2 * bit * lax.rem(lax.div(ep, bit), 2)

    return flip(1), flip(2), flip(4)


def line_order(tp):
    def pick(a, b, c, d):
        return jnp.where(tp == 0, a, jnp.where(tp == 1, b, jnp.where(tp == 2, c, d)))

    return (tp, pick(1, 0, 3, 2), pick(2, 2, 1, 1), pick(3, 3, 0, 0))


def greet(devices):
    barrier = pltpu.get_barrier_semaphore()
    for ep, tp in devices:
        pl.semaphore_signal(barrier, inc=1, device_id=(ep, tp), device_id_type=MESH)
    pl.semaphore_wait(barrier, len(devices))


def remote(src, dst, send, recv, device):
    return pltpu.make_async_remote_copy(
        src_ref=src, dst_ref=dst, send_sem=send, recv_sem=recv, device_id=device, device_id_type=MESH
    )


def experts_kernel(
    depth, blocks, routed, shared, experts,
    part_ref, resid_ref, gain_ref, cot_ref, kept_ref, w_in_ref, w_out_ref,
    middle_ref, h_out, cot_all, grads_out, gated_out, out_out, rows_out,
    h_all, got_z, resid_own, cot_tile, gu, act_grad, prob_lanes, diff_lanes, pair_lanes,
    grads_tile, gated_tile, out_tile, rows_tile,
    local_sem, z_send, z_recv, line_send, line_recv, h_send, h_recv, c_send, c_recv, tile_sem, store_sem,
):
    f32, bf16 = jnp.float32, jnp.bfloat16
    ep, tp = lax.axis_index("ep"), lax.axis_index("tp")
    pair, xn, yn = plane_partners(ep)
    parity = lax.rem(ep, 2)
    passed = jnp.where(parity == 0, xn, yn)
    onward = jnp.where(parity == 0, yn, xn)
    diag = xn + yn - ep
    rows = h_all.shape[2]
    width = h_all.shape[3]
    hidden = w_out_ref.shape[0]
    half = blocks // 2
    tile = half * rows
    up, down = jnp.minimum(tp + 1, depth - 1), jnp.maximum(tp - 1, 0)

    def twin(block):
        return block + pair - ep

    greet([(pair, tp), (xn, tp), (yn, tp)] + [(ep, lax.rem(tp + k, depth)) for k in range(1, depth)])

    def z_copy(k):
        to = lax.rem(tp + k, depth)
        start = pl.multiple_of(to * rows, rows)
        return remote(part_ref.at[pl.ds(start, rows)], got_z.at[k - 1], z_send.at[k - 1], z_recv.at[k - 1], (ep, to))

    for k in range(1, depth):
        z_copy(k).start()

    def h_copy(block, chunk, slot, to):
        ref = h_all.at[chunk, block]
        return remote(ref, ref, h_send.at[chunk, slot], h_recv.at[chunk, slot], (to, tp))

    def c_copy(block, chunk, slot, to):
        ref = cot_all.at[chunk, block]
        return remote(ref, ref, c_send.at[chunk, slot], c_recv.at[chunk, slot], (to, tp))

    def c_first(chunk, slot, to):
        src = cot_ref.at[pl.ds(pl.multiple_of(chunk * rows, rows), rows)]
        return remote(src, cot_all.at[chunk, ep], c_send.at[chunk, slot], c_recv.at[chunk, slot], (to, tp))

    def own_cot(chunk):
        src = cot_ref.at[pl.ds(pl.multiple_of(chunk * rows, rows), rows)]
        return pltpu.make_async_copy(src, cot_all.at[chunk, ep], local_sem.at[chunk])

    order = line_order(tp)

    def order_at(k):
        return jnp.where(k == 0, order[0], jnp.where(k == 1, order[1], jnp.where(k == 2, order[2], order[3])))

    resid_copy = pltpu.make_async_copy(
        resid_ref.at[pl.ds(pl.multiple_of(tp * rows, rows), rows)], resid_own, local_sem.at[depth]
    )
    resid_copy.start()
    for k in range(depth):
        c_first(order[k], 1, xn).start()
        c_first(order[k], 2, yn).start()
        c_first(order[k], 0, pair).start()
        own_cot(order[k]).start()
    resid_copy.wait()
    for k in range(1, depth):
        z_copy(k).wait_recv()

    def norm_rows(r, _):
        here = pl.ds(pl.multiple_of(r * 16, 16), 16)
        own = pl.ds(pl.multiple_of(tp * rows + r * 16, 16), 16)
        total = part_ref[own, :].astype(f32)
        for k in range(depth - 1):
            total = total + got_z[k, here, :].astype(f32)
        middle = resid_own[here, :].astype(f32) + total
        inverse = lax.rsqrt(jnp.mean(middle * middle, axis=-1, keepdims=True) + EPSILON)
        middle_ref[here, :] = middle
        h_all[tp, ep, here, :] = (middle * inverse * gain_ref[...]).astype(bf16)
        return 0

    lax.fori_loop(0, rows // 16, norm_rows, 0)

    def along(chunk, way, to):
        ref = h_all.at[chunk, ep]
        return remote(ref, ref, line_send.at[chunk, way], line_recv.at[chunk], (ep, to))

    def goes_up(chunk):
        return (chunk <= tp) & (tp < depth - 1)

    def goes_down(chunk):
        return (chunk >= tp) & (tp > 0)

    def send_chunk(k):
        chunk = order[k]
        if k > 0:
            along(chunk, 0, up).wait_recv()

        @pl.when(goes_up(chunk))
        def _():
            along(chunk, 0, up).start()

        @pl.when(goes_down(chunk))
        def _():
            along(chunk, 1, down).start()

        h_copy(ep, chunk, 1, xn).start()
        h_copy(ep, chunk, 2, yn).start()
        h_copy(ep, chunk, 0, pair).start()

    def forward_chunk(chunk):
        for copy in (h_copy, c_copy):
            copy(xn, chunk, 1, xn).wait_recv()
            copy(yn, chunk, 2, yn).wait_recv()
            copy(passed, chunk, 3, onward).start()
            copy(xn, chunk, 4, pair).start()
            copy(yn, chunk, 5, pair).start()

    def forward_diag(chunk):
        for copy in (h_copy, c_copy):
            copy(diag, chunk, 3, onward).wait_recv()
            copy(diag, chunk, 6, pair).start()

    def await_pair(chunk, slots):
        for copy in (h_copy, c_copy):
            for slot, block in slots:
                copy(block, chunk, slot, pair).wait_recv()

    send_chunk(0)
    send_chunk(1)

    lanes = lax.broadcasted_iota(jnp.int32, (1, 128), 1)
    base = routed + shared
    slab = base // 128 * 128
    lane0 = base - slab
    near_half = lax.div(ep, half)

    def tile_copies(i):
        k, side = lax.div(i, 2), lax.rem(i, 2)
        chunk = order_at(k)
        start = jnp.where(side == 0, near_half, 1 - near_half) * half
        group = pl.ds(start, half)
        slot = lax.rem(i, 2)
        stores = [
            pltpu.make_async_copy(h_all.at[chunk, group], h_out.at[chunk, group], store_sem.at[slot, 0]),
            pltpu.make_async_copy(grads_tile.at[slot], grads_out.at[chunk, group], store_sem.at[slot, 1]),
            pltpu.make_async_copy(gated_tile.at[slot], gated_out.at[chunk, group], store_sem.at[slot, 2]),
            pltpu.make_async_copy(out_tile.at[slot], out_out.at[group, chunk], store_sem.at[slot, 3]),
            pltpu.make_async_copy(rows_tile.at[slot], rows_out.at[chunk, group], store_sem.at[slot, 4]),
        ]
        load = pltpu.make_async_copy(cot_all.at[chunk, group], cot_tile, tile_sem)
        return chunk, start, slot, load, stores

    def step(i, _):
        k, side = lax.div(i, 2), lax.rem(i, 2)
        chunk, start, slot, load, stores = tile_copies(i)

        @pl.when(side == 0)
        def _():
            own_cot(chunk).wait()
            forward_chunk(chunk)

        @pl.when(i == 0)
        def _():
            send_chunk(2)

        @pl.when(side == 0)
        def _():
            await_pair(chunk, ((0, pair), (4, twin(xn))))

        @pl.when(side == 1)
        def _():
            forward_diag(chunk)

        @pl.when(i == 1)
        def _():
            send_chunk(3)

        @pl.when(side == 1)
        def _():
            await_pair(chunk, ((5, twin(yn)), (6, twin(diag))))

        load.start()

        @pl.when(i >= 2)
        def _():
            for copy in tile_copies(i - 2)[4]:
                copy.wait()

        group = pl.ds(start, half)
        stores[0].start()
        for n in range(0, 2 * hidden, 512):
            gu[:, n : n + 512] = jnp.dot(
                h_all[chunk, group].reshape(tile, width), w_in_ref[:, n : n + 512], preferred_element_type=f32
            )
        piece = gu[:, slab : slab + 128]
        logits = piece + pltpu.roll(piece, 128 - experts, 1) + pltpu.roll(piece, 128 - 2 * experts, 1)
        is_logit = (lanes >= lane0) & (lanes < lane0 + experts)
        logits = jnp.where(is_logit, logits, -1e30)
        exps = jnp.exp(logits - jnp.max(logits, axis=-1, keepdims=True))
        probs = exps / jnp.sum(exps, axis=-1, keepdims=True)
        here = (lanes == lane0 + ep).astype(f32)
        kept = kept_ref[chunk, group].reshape(tile, 128).astype(f32)
        prob_here = jnp.sum(probs * here * kept, axis=-1, keepdims=True)
        prob_lanes[...] = jnp.broadcast_to(prob_here, (tile, 128))
        diff_lanes[...] = here - probs
        load.wait()
        act_grad[...] = lax.dot_general(
            cot_tile[...].reshape(tile, width), w_out_ref[...], (((1,), (1,)), ((), ())), preferred_element_type=f32
        )
        strip = 64

        def strips(r, _):
            at = pl.ds(pl.multiple_of(r * strip, strip), strip)
            gate_here = prob_lanes[at, :]
            pair_sum = jnp.zeros((strip, 128), f32)
            per = rows // strip
            block, inner = lax.div(r, per), pl.ds(pl.multiple_of(lax.rem(r, per) * strip, strip), strip)
            for n in range(0, hidden, 128):
                gate = gu[at, n : n + 128]
                up_val = gu[at, hidden + n : hidden + n + 128]
                grad = act_grad[at, n : n + 128]
                if n + 128 <= routed:
                    scale = gate_here
                elif n >= routed:
                    scale = None
                else:
                    scale = jnp.where(lanes < routed - n, gate_here, 1.0)
                sig = jax.nn.sigmoid(gate)
                silu = gate * sig
                act = silu * up_val
                if n < routed:
                    both = act * grad
                    if n + 128 > routed:
                        both = jnp.where(lanes < routed - n, both, 0.0)
                    pair_sum = pair_sum + both
                    act = act * scale
                    grad = grad * scale
                gated_tile[slot, block, inner, n : n + 128] = act.astype(bf16)
                grads_tile[slot, block, inner, n : n + 128] = (
                    grad * up_val * (sig * (1.0 + gate * (1.0 - sig)))
                ).astype(bf16)
                grads_tile[slot, block, inner, hidden + n : hidden + n + 128] = (grad * silu).astype(bf16)
            pair_lanes[at, :] = pair_sum
            return 0

        lax.fori_loop(0, tile // strip, strips, 0)
        pair_grad = jnp.sum(pair_lanes[...], axis=-1, keepdims=True)
        logit_grad = pair_grad * prob_lanes[...] * diff_lanes[...]
        logit_grad = logit_grad + pltpu.roll(logit_grad, experts, 1) + pltpu.roll(logit_grad, 2 * experts, 1)
        old = grads_tile[slot, :, :, slab : slab + 128].reshape(tile, 128)
        grads_tile[slot, :, :, slab : slab + 128] = (
            jnp.where(lanes >= lane0, logit_grad.astype(bf16), old).reshape(half, rows, 128)
        )
        for n in range(0, width, 512):
            rows_tile[slot, :, :, n : n + 512] = (
                lax.dot_general(
                    grads_tile[slot].reshape(tile, 2 * hidden), w_in_ref[n : n + 512, :], (((1,), (1,)), ((), ())),
                    preferred_element_type=f32,
                ).astype(bf16).reshape(half, rows, 512)
            )
            out_tile[slot, :, :, n : n + 512] = (
                jnp.dot(gated_tile[slot].reshape(tile, hidden), w_out_ref[:, n : n + 512], preferred_element_type=f32)
                .astype(bf16).reshape(half, rows, 512)
            )
        for copy in stores[1:]:
            copy.start()
        return 0

    lax.fori_loop(0, 2 * depth, step, 0)
    for i in (2 * depth - 2, 2 * depth - 1):
        for copy in tile_copies(i)[4]:
            copy.wait()
    for k in range(1, depth):
        z_copy(k).wait_send()

    def drain(k, _):
        chunk = order_at(k)

        @pl.when(goes_up(chunk))
        def _():
            along(chunk, 0, up).wait_send()

        @pl.when(goes_down(chunk))
        def _():
            along(chunk, 1, down).wait_send()

        for slot in range(7):
            h_copy(ep, chunk, slot, pair).wait_send()
            c_copy(ep, chunk, slot, pair).wait_send()
        return 0

    lax.fori_loop(0, depth, drain, 0)


def experts_call(attn_part, inputs, gain, cotangent, kept, w_in, w_out, blocks, depth, routed, shared, experts, cid):
    f32, bf16 = jnp.float32, jnp.bfloat16
    tokens, width = inputs.shape
    rows = tokens // depth
    hidden = w_out.shape[0]
    half = blocks // 2
    tile = half * rows
    dma = pltpu.SemaphoreType.DMA
    vmem, anywhere = pl.BlockSpec(memory_space=pltpu.VMEM), pl.BlockSpec(memory_space=pl.ANY)

    def units(size):
        return jax.ShapeDtypeStruct((depth, blocks, rows, size), bf16)

    return pl.pallas_call(
        functools.partial(experts_kernel, depth, blocks, routed, shared, experts),
        out_shape=(
            jax.ShapeDtypeStruct((rows, width), f32),
            units(width), units(width), units(2 * hidden), units(hidden),
            jax.ShapeDtypeStruct((blocks, depth, rows, width), bf16), units(width),
        ),
        in_specs=[vmem, anywhere, vmem, anywhere, vmem, vmem, vmem],
        out_specs=(vmem,) + (anywhere,) * 6,
        scratch_shapes=[
            pltpu.VMEM((depth, blocks, rows, width), bf16),
            pltpu.VMEM((depth - 1, rows, width), bf16),
            pltpu.VMEM((rows, width), bf16),
            pltpu.VMEM((half, rows, width), bf16),
            pltpu.VMEM((tile, 2 * hidden), f32),
            pltpu.VMEM((tile, hidden), f32),
            pltpu.VMEM((tile, 128), f32),
            pltpu.VMEM((tile, 128), f32),
            pltpu.VMEM((tile, 128), f32),
            pltpu.VMEM((2, half, rows, 2 * hidden), bf16),
            pltpu.VMEM((2, half, rows, hidden), bf16),
            pltpu.VMEM((2, half, rows, width), bf16),
            pltpu.VMEM((2, half, rows, width), bf16),
            dma((depth + 1,)),
            dma((depth - 1,)), dma((depth - 1,)),
            dma((depth, 2)), dma((depth,)),
            dma((depth, 7)), dma((depth, 7)),
            dma((depth, 7)), dma((depth, 7)),
            dma, dma((2, 5)),
        ],
        compiler_params=pltpu.CompilerParams(collective_id=cid, has_side_effects=True, vmem_limit_bytes=60 << 20),
    )(attn_part, inputs, gain.reshape(1, width), cotangent, kept, w_in, w_out)


def sum_kernel(
    depth, part_ref, h_ref, grads_ref, gated_ref, cot_ref, middle_ref, gain_ref, middle_grad, branch, gain_part, in_grad, out_grad,
    mine, got_pair, got_first, got_second, got_z, keep, h_tile, grads_tile, gated_tile, cot_tile,
    own_cot, mine_sem, own_sem, ps, pr, fs, fr, ss, sr, zs, zr, tile_sem,
):
    f32 = jnp.float32
    rows = part_ref.shape[2]
    ep, tp = lax.axis_index("ep"), lax.axis_index("tp")
    pair, xn, yn = plane_partners(ep)
    parity = lax.rem(ep, 2)
    first = jnp.where(parity == 0, xn, yn)
    second = jnp.where(parity == 0, yn, xn)
    diag = xn + yn - ep
    blocks = (first, diag, ep, second)
    pair_slot = (3, 1, 2, 0)
    greet([(pair, tp), (xn, tp), (yn, tp)] + [(ep, lax.rem(tp + k, depth)) for k in range(1, depth)])
    steps = [(k + 1) % depth for k in range(depth)]

    def chunk_of(i):
        return lax.rem(tp + steps[i], depth)

    def pair_copy(i, slot):
        src = part_ref.at[chunk_of(i), blocks[slot] + pair - ep]
        to = pair_slot[slot]
        return remote(src, got_pair.at[i, to], ps.at[i, slot], pr.at[i, to], (pair, tp))

    def pair_wait(i, slot):
        return remote(part_ref.at[0, 0], got_pair.at[i, slot], ps.at[i, slot], pr.at[i, slot], (pair, tp))

    def mine_copy(i, slot):
        return pltpu.make_async_copy(part_ref.at[chunk_of(i), blocks[slot]], mine.at[i, slot], mine_sem.at[i, slot])

    def first_copy(i, slot):
        return remote(mine.at[i, slot], got_first.at[i, slot], fs.at[i, slot], fr.at[i, slot], (first, tp))

    def second_copy(i):
        return remote(mine.at[i, 3], got_second.at[i], ss.at[i], sr.at[i], (second, tp))

    def z_copy(i):
        k = steps[i]
        return remote(mine.at[i, 2], got_z.at[k - 1], zs.at[k - 1], zr.at[k - 1], (ep, lax.rem(tp + k, depth)))

    def add(dst, a, b):
        def body(r, _):
            at = pl.ds(pl.multiple_of(r * 16, 16), 16)
            dst[at, :] = (a[at, :].astype(f32) + b[at, :].astype(f32)).astype(dst.dtype)
            return 0

        lax.fori_loop(0, rows // 16, body, 0)

    for i in range(depth):
        for slot in (3, 1, 2, 0):
            pair_copy(i, slot).start()
        for slot in range(4):
            mine_copy(i, slot).start()

    def tile_loads(c):
        return [
            pltpu.make_async_copy(src.at[c], dst, tile_sem.at[n])
            for n, (src, dst) in enumerate(
                ((h_ref, h_tile), (grads_ref, grads_tile), (gated_ref, gated_tile), (cot_ref, cot_tile))
            )
        ]

    def stage_a(i):
        for slot in range(4):
            mine_copy(i, slot).wait()
            pair_wait(i, slot).wait_recv()
            add(mine.at[i, slot], mine.at[i, slot], got_pair.at[i, slot])
            if slot < 2:
                first_copy(i, slot).start()

    def stage_b(i):
        first_copy(i, 1).wait_recv()
        add(mine.at[i, 3], mine.at[i, 3], got_first.at[i, 1])
        second_copy(i).start()
        first_copy(i, 0).wait_recv()
        add(mine.at[i, 2], mine.at[i, 2], got_first.at[i, 0])

    def stage_c(i):
        second_copy(i).wait_recv()
        if i < depth - 1:
            add(mine.at[i, 2], mine.at[i, 2], got_second.at[i])
            z_copy(i).start()
        else:
            add(keep, mine.at[i, 2], got_second.at[i])

    count = h_tile.shape[0] * rows
    width = h_tile.shape[2]
    hidden = gated_tile.shape[2]

    def weights(c):
        for load in tile_loads(c):
            load.wait()
        turned = (((0,), (0,)), ((), ()))

        def in_part(m, _):
            at = pl.ds(pl.multiple_of(m * 512, 512), 512)
            found = lax.dot_general(
                h_tile[:, :, at].reshape(count, 512), grads_tile[...].reshape(count, 2 * hidden), turned,
                preferred_element_type=f32,
            )
            in_grad[at, :] = found if c == 0 else in_grad[at, :] + found
            return 0

        lax.fori_loop(0, width // 512, in_part, 0)

        def out_part(m, _):
            at = pl.ds(pl.multiple_of(m * 512, 512), 512)
            found = lax.dot_general(
                gated_tile[...].reshape(count, hidden), cot_tile[:, :, at].reshape(count, 512), turned,
                preferred_element_type=f32,
            )
            out_grad[:, at] = found if c == 0 else out_grad[:, at] + found
            return 0

        lax.fori_loop(0, width // 512, out_part, 0)
        if c + 1 < depth:
            for load in tile_loads(c + 1):
                load.start()

    own_copy = pltpu.make_async_copy(cot_ref.at[tp, ep], own_cot, own_sem)
    own_copy.start()
    for load in tile_loads(0):
        load.start()
    for t in range(depth + 2):
        if t < depth:
            stage_a(t)
        if 0 <= t - 1 < depth:
            stage_b(t - 1)
        if 0 <= t - 2 < depth:
            stage_c(t - 2)
        if t < depth:
            weights(t)
    for i in range(depth - 1):
        z_copy(i).wait_recv()

    own_copy.wait()

    def total(r, gain_sum):
        at = pl.ds(pl.multiple_of(r * 16, 16), 16)
        u = keep[at, :]
        for k in range(depth - 1):
            u = u + got_z[k, at, :].astype(f32)
        v = middle_ref[at, :]
        inverse = lax.rsqrt(jnp.mean(v * v, axis=-1, keepdims=True) + EPSILON)
        v_hat = v * inverse
        gain_sum = gain_sum + (u * v_hat)[:8] + (u * v_hat)[8:]
        s = u * gain_ref[...]
        back = inverse * (s - v_hat * jnp.mean(s * v_hat, axis=-1, keepdims=True))
        found = own_cot[at, :].astype(f32) + back
        middle_grad[at, :] = found
        branch[at, :] = found.astype(branch.dtype)
        return gain_sum

    gain_part[...] = lax.fori_loop(0, rows // 16, total, jnp.zeros((8, width), f32))
    for i in range(depth):
        for slot in range(4):
            pair_copy(i, slot).wait_send()
        for slot in range(2):
            first_copy(i, slot).wait_send()
        second_copy(i).wait_send()
        if i < depth - 1:
            z_copy(i).wait_send()


def sum_call(part, h_all, grads, gated, cot_all, middle, gain, cid):
    f32, bf16 = jnp.float32, jnp.bfloat16
    depth, blocks, rows, width = part.shape
    hidden = gated.shape[3]
    dma = pltpu.SemaphoreType.DMA
    vmem, anywhere = pl.BlockSpec(memory_space=pltpu.VMEM), pl.BlockSpec(memory_space=pl.ANY)
    return pl.pallas_call(
        functools.partial(sum_kernel, depth),
        out_shape=(
            jax.ShapeDtypeStruct((rows, width), f32),
            jax.ShapeDtypeStruct((rows, width), bf16),
            jax.ShapeDtypeStruct((8, width), f32),
            jax.ShapeDtypeStruct((width, 2 * hidden), f32),
            jax.ShapeDtypeStruct((hidden, width), f32),
        ),
        in_specs=[anywhere] * 5 + [vmem, vmem],
        out_specs=(vmem,) * 5,
        scratch_shapes=[
            pltpu.VMEM((depth, 4, rows, width), bf16),
            pltpu.VMEM((depth, 4, rows, width), bf16),
            pltpu.VMEM((depth, 2, rows, width), bf16),
            pltpu.VMEM((depth, rows, width), bf16),
            pltpu.VMEM((depth - 1, rows, width), bf16),
            pltpu.VMEM((rows, width), f32),
            pltpu.VMEM((blocks, rows, width), bf16),
            pltpu.VMEM((blocks, rows, 2 * hidden), bf16),
            pltpu.VMEM((blocks, rows, hidden), bf16),
            pltpu.VMEM((blocks, rows, width), bf16),
            pltpu.VMEM((rows, width), bf16),
            dma((depth, 4)), dma, dma((depth, 4)), dma((depth, 4)), dma((depth, 2)), dma((depth, 2)),
            dma((depth,)), dma((depth,)), dma((depth - 1,)), dma((depth - 1,)), dma((4,)),
        ],
        compiler_params=pltpu.CompilerParams(collective_id=cid, has_side_effects=True, vmem_limit_bytes=62 << 20),
    )(part, h_all, grads, gated, cot_all, middle, gain.reshape(1, width))


def line_gather(ref, own, send_sem, recv_sem, ep, tp, depth):
    up, down = jnp.minimum(tp + 1, depth - 1), jnp.maximum(tp - 1, 0)
    order = line_order(tp)

    def along(k, way, to):
        chunk = order[k]
        src = own if k == 0 else ref.at[chunk]
        return remote(src, ref.at[chunk], send_sem.at[chunk, way], recv_sem.at[chunk], (ep, to))

    def each_way(k, act):
        @pl.when((order[k] <= tp) & (tp < depth - 1))
        def _():
            act(along(k, 0, up))

        @pl.when((order[k] >= tp) & (tp > 0))
        def _():
            act(along(k, 1, down))

    def pass_on(k):
        each_way(k, lambda copy: copy.start())

    def await_chunk(k):
        along(k, 0, up).wait_recv()

    def drain():
        for k in range(depth):
            each_way(k, lambda copy: copy.wait_send())

    return pass_on, await_chunk, drain


def add_rows(dst, a, b):
    def body(r, _):
        at = pl.ds(pl.multiple_of(r * 16, 16), 16)
        dst[at, :] = (a[at, :].astype(jnp.float32) + b[at, :].astype(jnp.float32)).astype(dst.dtype)
        return 0

    lax.fori_loop(0, dst.shape[0] // 16, body, 0)


def turn(slab, table, sign):
    cosine, front, second = table
    return slab * cosine + sign * (pltpu.roll(slab, 96, 1) * front + pltpu.roll(slab, 32, 1) * second)


def tail_kernel(
    depth, heads,
    branch_ref, middle_grad_ref, middle_ref, part_ref, router_ref, gain_part_ref, inputs_ref,
    w_output, w_query, w_latent, w_up, hidden_ref, qn_ref, qr_ref, kv_ref, kr_ref, attended, latent_in, compressed,
    tables, gain_latent, gain_attn,
    block_ref, grad_in_ref, gains_ref, w_sum_ref, latent_sum_ref, landed, w_all,
    branch, load, held_rows, got_first, got_second, got_z, hidden_part, got_h, row_sum,
    d_out, d_kr, q_grad, kv_grad, l_grad, u_grad, w_stage, w_pair, w_first, w_second, w_z, resid, own_grad, own_block, gains,
    load_sem, ps, pr, fs, fr, ss, sr, zs, zr, bs, br, hs, hr, gs, gr, os, orr,
    wps, wpr, wfs, wfr, wss, wsr, wzs, wzr, as_, ar, misc_sem, stage_sem,
):
    f32, bf16 = jnp.float32, jnp.bfloat16
    ep, tp = lax.axis_index("ep"), lax.axis_index("tp")
    pair, xn, yn = plane_partners(ep)
    parity = lax.rem(ep, 2)
    first = jnp.where(parity == 0, xn, yn)
    second = jnp.where(parity == 0, yn, xn)
    diag = xn + yn - ep
    blocks = (first, diag, ep, second)
    pair_slot = (3, 1, 2, 0)
    rows, width = middle_ref.shape
    tokens = hidden_ref.shape[0]
    order = line_order(tp)
    score_scale = (NOPE + ROPE) ** (-0.5)
    greet([(pair, tp), (xn, tp), (yn, tp)] + [(ep, lax.rem(tp + k, depth)) for k in range(1, depth)])

    branch_on, branch_wait, branch_drain = line_gather(branch, branch_ref, bs, br, ep, tp, depth)
    grad_on, grad_wait, grad_drain = line_gather(grad_in_ref, own_grad, gs, gr, ep, tp, depth)
    block_on, block_wait, block_drain = line_gather(block_ref, own_block, os, orr, ep, tp, depth)

    steps = [(k + 1) % depth for k in range(depth)]

    def chunk_of(i):
        return lax.rem(tp + steps[i], depth)

    def pair_copy(i, slot):
        src = part_ref.at[blocks[slot] + pair - ep, chunk_of(i)]
        to = pair_slot[slot]
        return remote(src, landed.at[i, to], ps.at[i, slot], pr.at[i, to], (pair, tp))

    def pair_wait(i, slot):
        return remote(part_ref.at[0, 0], landed.at[i, slot], ps.at[i, slot], pr.at[i, slot], (pair, tp))

    def loads(i, slot):
        at = slot % 2
        return (
            pltpu.make_async_copy(part_ref.at[blocks[slot], chunk_of(i)], load.at[at, 0], load_sem.at[at, 0]),
            pltpu.make_async_copy(landed.at[i, slot], load.at[at, 1], load_sem.at[at, 1]),
        )

    def first_copy(i, slot):
        return remote(held_rows.at[i % 2, slot], got_first.at[i, slot], fs.at[i, slot], fr.at[i, slot], (first, tp))

    def second_copy(i):
        return remote(held_rows.at[i % 2, 3], got_second.at[i], ss.at[i], sr.at[i], (second, tp))

    def z_copy(i):
        k = steps[i]
        src = held_rows.at[i % 2, 2]
        return remote(src, got_z.at[k - 1], zs.at[k - 1], zr.at[k - 1], (ep, lax.rem(tp + k, depth)))

    def start_loads(i, slot):
        pair_wait(i, slot).wait_recv()
        for copy in loads(i, slot):
            copy.start()

    def stage_a(i):
        if i >= 2:
            for slot in range(2):
                first_copy(i - 2, slot).wait_send()
            second_copy(i - 2).wait_send()
            z_copy(i - 2).wait_send()
        start_loads(i, 0)
        for slot in range(4):
            if slot < 3:
                start_loads(i, slot + 1)
            for copy in loads(i, slot):
                copy.wait()
            add_rows(held_rows.at[i % 2, slot], load.at[slot % 2, 0], load.at[slot % 2, 1])
            if slot < 2:
                first_copy(i, slot).start()

    def stage_b(i):
        first_copy(i, 1).wait_recv()
        add_rows(held_rows.at[i % 2, 3], held_rows.at[i % 2, 3], got_first.at[i, 1])
        second_copy(i).start()
        first_copy(i, 0).wait_recv()
        add_rows(held_rows.at[i % 2, 2], held_rows.at[i % 2, 2], got_first.at[i, 0])

    def stage_c(i):
        second_copy(i).wait_recv()
        if i < depth - 1:
            add_rows(held_rows.at[i % 2, 2], held_rows.at[i % 2, 2], got_second.at[i])
            z_copy(i).start()
        else:
            add_rows(row_sum, held_rows.at[i % 2, 2], got_second.at[i])

    def w_pair_copy(slot):
        to = pair_slot[slot]
        return remote(w_all.at[blocks[slot] + pair - ep], w_pair.at[to], wps.at[slot], wpr.at[to], (pair, tp))

    def w_pair_wait(slot):
        return remote(w_all.at[0], w_pair.at[slot], wps.at[slot], wpr.at[slot], (pair, tp))

    def w_first_copy(slot):
        return remote(w_pair.at[slot], w_first.at[slot], wfs.at[slot], wfr.at[slot], (first, tp))

    def w_second_copy():
        return remote(w_pair.at[3], w_second, wss, wsr, (second, tp))

    def w_load(slot):
        return pltpu.make_async_copy(w_all.at[blocks[slot]], w_stage.at[slot % 2], stage_sem.at[slot % 2])

    def w_stage_a():
        for slot in range(4):
            if slot < 3:
                w_load(slot + 1).start()
            w_pair_wait(slot).wait_recv()
            w_load(slot).wait()
            add_rows(w_pair.at[slot], w_pair.at[slot], w_stage.at[slot % 2])
            if slot < 2:
                w_first_copy(slot).start()

    def w_stage_b():
        w_first_copy(1).wait_recv()
        add_rows(w_pair.at[3], w_pair.at[3], w_first.at[1])
        w_second_copy().start()
        w_first_copy(0).wait_recv()
        add_rows(w_pair.at[2], w_pair.at[2], w_first.at[0])

    def w_stage_c():
        w_second_copy().wait_recv()
        add_rows(w_sum_ref, w_pair.at[2], w_second)

    def h_copy(k):
        to = lax.rem(tp + k, depth)
        return remote(hidden_part.at[to], got_h.at[k - 1], hs.at[k - 1], hr.at[k - 1], (ep, to))

    branch_on(0)
    branch[tp] = branch_ref[...]
    for i in range(depth):
        for slot in (3, 1, 2, 0):
            pair_copy(i, slot).start()
    own_rows = pl.ds(pl.multiple_of(tp * rows, rows), rows)
    resid_copy = pltpu.make_async_copy(inputs_ref.at[own_rows], resid, misc_sem.at[0])
    resid_copy.start()

    stage_a(0)
    branch_wait(1)
    branch_on(1)
    stage_a(1)
    branch_wait(2)
    branch_on(2)
    stage_b(0)
    branch_wait(3)
    branch_on(3)

    turned, across = (((0,), (0,)), ((), ())), (((1,), (1,)), ((), ()))

    def dot(a, b, dims=(((1,), (0,)), ((), ()))):
        return lax.dot_general(a, b, dims, preferred_element_type=f32)

    for c in range(depth):
        d_out[c * rows : (c + 1) * rows, :] = dot(branch[c], w_output[...], across).astype(bf16)

    lanes = lax.broadcasted_iota(jnp.int32, (1, 128), 1)
    halves = tokens // BLOCK

    def head(h, even):
        mine = (lanes < 64) if even else (lanes >= 64)
        at_q = pl.ds(pl.multiple_of(h * NOPE, 128), 128)
        at_r = pl.ds(pl.multiple_of(lax.div(h, 2) * 128, 128), 128)
        at_k = pl.ds(pl.multiple_of(h * 256, 128), 128)
        at_v = pl.ds(pl.multiple_of(h * 256 + 128, 128), 128)
        kv_sum = [None, None]
        for b in reversed(range(halves)):
            own = slice(b * BLOCK, (b + 1) * BLOCK)
            keys = slice(0, (b + 1) * BLOCK)
            qn, qr = qn_ref[own, at_q], qr_ref[own, at_r]
            kn, kr = kv_ref[keys, at_k], kr_ref[0 if even else 1, keys, :]
            scores = (dot(qn, kn, across) + dot(qr, kr, across)) * score_scale
            exps = jnp.exp(scores - jnp.max(scores, axis=-1, keepdims=True))
            probs = exps / jnp.sum(exps, axis=-1, keepdims=True)
            grad = d_out[own, at_q]
            prob_part = dot(grad, kv_ref[keys, at_v], across)
            score_grad = (probs * (prob_part - jnp.sum(probs * prob_part, axis=-1, keepdims=True))).astype(bf16)
            found = (dot(score_grad, qn, turned) * score_scale, dot(probs.astype(bf16), grad, turned))
            r_grad = jnp.where(mine, dot(score_grad, qr, turned) * score_scale, 0.0)
            for n, at in enumerate((at_k, at_v)):
                if b < halves - 1:
                    kv_sum[n] = kv_sum[n] + found[n]
                else:
                    kv_sum[n] = found[n]
                kv_grad[own, at] = kv_sum[n][b * BLOCK :].astype(bf16)
                if b > 0:
                    kv_sum[n] = kv_sum[n][: b * BLOCK]
            d_kr[keys, :] = d_kr[keys, :] + r_grad
            q_grad[own, at_q] = (dot(score_grad, kn) * score_scale).astype(bf16)
            yield own, at_r, dot(score_grad, kr) * score_scale

    d_kr[...] = jnp.zeros_like(d_kr)

    def head_pair(p, _):
        evens = list(head(2 * p, True))
        odds = list(head(2 * p + 1, False))
        at = pl.ds(pl.multiple_of(heads * NOPE + p * 128, 128), 128)
        for (own, _, even_part), (_, _, odd_part) in zip(evens, odds):
            table = tuple(tables[n, own, :] for n in range(3))
            q_grad[own, at] = turn(even_part + odd_part, table, -1.0).astype(bf16)
        return 0

    lax.fori_loop(0, heads // 2, head_pair, 0)
    stage_c(0)
    stage_b(1)
    stage_a(2)

    latent_back = dot(kv_grad[...], w_up[...], across)
    held = compressed[...]
    inverse = lax.rsqrt(jnp.mean(held * held, axis=-1, keepdims=True) + EPSILON)
    normed = held * inverse
    gain_latent_part = jnp.sum(latent_back * normed, axis=0, keepdims=True)
    scaled = latent_back * gain_latent[...]
    rank = held.shape[1]
    l_grad[:, :rank] = (inverse * (scaled - normed * jnp.mean(scaled * normed, axis=-1, keepdims=True))).astype(bf16)
    rope = d_kr[...] + pltpu.roll(d_kr[...], 64, 1)
    rope = turn(rope, tuple(tables[n] for n in range(3)), -1.0)
    l_grad[:, rank:] = jnp.where(lanes < 64, rope, 0.0).astype(bf16)

    for n in range(0, width, 512):
        part = dot(q_grad[...], w_query[n : n + 512, :], across) + dot(l_grad[...], w_latent[n : n + 512, :], across)
        hidden_part[:, :, n : n + 512] = part.astype(bf16).reshape(depth, rows, 512)
    for k in range(1, depth):
        h_copy(k).start()

    stage_c(1)
    stage_b(2)
    stage_a(3)

    q_cols, l_cols = q_grad.shape[1], l_grad.shape[1]
    o_rows = attended.shape[1]
    count = w_all.shape[0]
    w_rows = w_all.shape[1]
    o_cols = width // count
    u_rows = rank // count
    u_cols = w_up.shape[1]
    o_start = q_cols + l_cols
    u_start = o_start + o_rows * o_cols // w_rows
    u_wide = u_rows * u_cols // w_rows

    u_grad[...] = dot(latent_in[...], kv_grad[...], turned).astype(bf16)

    def w_store(b):
        slot = lax.rem(b, 2)
        return pltpu.make_async_copy(w_stage.at[slot], w_all.at[b], stage_sem.at[slot])

    def w_block(b, _):
        slot = lax.rem(b, 2)

        @pl.when(b >= 2)
        def _():
            w_store(b - 2).wait()

        at = pl.ds(pl.multiple_of(b * w_rows, 256), w_rows)
        own = hidden_ref[:, at]
        w_stage[slot, :, 0:q_cols] = dot(own, q_grad[...], turned).astype(bf16)
        found = dot(own, l_grad[...], turned)
        w_stage[slot, :, q_cols : q_cols + rank] = found[:, :rank].astype(bf16)
        w_stage[slot, :, q_cols + rank : o_start] = found[:, rank:].astype(bf16) + router_ref[at, :]
        cols = pl.ds(pl.multiple_of(b * o_cols, 256), o_cols)
        found = dot(attended[...], branch[:, :, cols].reshape(tokens, o_cols), turned)
        for n in range(o_rows // w_rows):
            w_stage[slot, :, o_start + n * o_cols : o_start + (n + 1) * o_cols] = (
                found[n * w_rows : (n + 1) * w_rows].astype(bf16)
            )
        u_at = pl.ds(pl.multiple_of(b * u_rows, u_rows), u_rows)
        for n in range(u_cols // u_wide):
            w_stage[slot, n * u_rows : (n + 1) * u_rows, u_start : u_start + u_wide] = (
                u_grad[u_at, n * u_wide : (n + 1) * u_wide]
            )
        w_store(b).start()
        return 0

    lax.fori_loop(0, count, w_block, 0)
    w_store(count - 2).wait()
    w_store(count - 1).wait()
    for slot in (3, 1, 2, 0):
        w_pair_copy(slot).start()
    w_load(0).start()

    stage_b(3)
    stage_c(2)
    w_stage_a()
    stage_c(3)

    resid_copy.wait()
    for k in range(1, depth):
        h_copy(k).wait_recv()

    def input_rows(r, gain_sum):
        at = pl.ds(pl.multiple_of(r * 16, 16), 16)
        u = hidden_part[tp, at, :].astype(f32)
        for k in range(depth - 1):
            u = u + got_h[k, at, :].astype(f32)
        v = resid[at, :].astype(f32)
        inv = lax.rsqrt(jnp.mean(v * v, axis=-1, keepdims=True) + EPSILON)
        v_hat = v * inv
        gain_sum = gain_sum + (u * v_hat)[:8] + (u * v_hat)[8:]
        s = u * gain_attn[...]
        back = inv * (s - v_hat * jnp.mean(s * v_hat, axis=-1, keepdims=True))
        own_grad[at, :] = (middle_grad_ref[at, :] + back).astype(bf16)
        return gain_sum

    gain_sum = lax.fori_loop(0, rows // 16, input_rows, jnp.zeros((8, width), f32))
    grad_on(0)
    own_grad_copy = pltpu.make_async_copy(own_grad, grad_in_ref.at[tp], misc_sem.at[1])
    own_grad_copy.start()
    w_stage_b()
    for i in range(depth - 1):
        z_copy(i).wait_recv()

    def block_rows(r, _):
        at = pl.ds(pl.multiple_of(r * 16, 16), 16)
        value = middle_ref[at, :] + row_sum[at, :]
        for k in range(depth - 1):
            value = value + got_z[k, at, :].astype(f32)
        own_block[at, :] = value.astype(bf16)
        return 0

    lax.fori_loop(0, rows // 16, block_rows, 0)
    block_on(0)
    own_block_copy = pltpu.make_async_copy(own_block, block_ref.at[tp], misc_sem.at[2])
    own_block_copy.start()

    gains[0] = jnp.zeros_like(gains[0])
    gains[0, 0:1, :] = jnp.sum(gain_sum, axis=0, keepdims=True)
    gains[0, 1:2, :] = jnp.sum(gain_part_ref[...], axis=0, keepdims=True)
    gains[0, 2:3, 0:rank] = gain_latent_part
    flip_1 = tp + 1 - 2 * lax.rem(tp, 2)
    flip_2 = tp + 2 - 4 * lax.div(tp, 2)
    partners = ((pair, tp), (xn, tp), (yn, tp), (ep, flip_1), (ep, flip_2))

    def gain_copy(n):
        return remote(gains.at[2 * n], gains.at[2 * n + 1], as_.at[n], ar.at[n], partners[n])

    def gain_step(n):
        gain_copy(n).wait_recv()
        total = gains[2 * n] + gains[2 * n + 1]
        if n + 1 < len(partners):
            gains[2 * n + 2] = total
            gain_copy(n + 1).start()
        else:
            gains_ref[...] = total

    gain_copy(0).start()
    gain_step(0)
    gain_step(1)
    w_stage_c()
    w_part = w_rows // depth

    def w_z_copy(k):
        to = lax.rem(tp + k, depth)
        src = w_pair.at[1, pl.ds(pl.multiple_of(to * w_part, w_part), w_part), pl.ds(q_cols, l_cols)]
        return remote(src, w_z.at[k - 1], wzs.at[k - 1], wzr.at[k - 1], (ep, to))

    w_first_copy(1).wait_send()
    w_pair[1, :, q_cols:o_start] = w_sum_ref[:, q_cols:o_start].astype(bf16)
    for k in range(1, depth):
        w_z_copy(k).start()
    gain_step(2)
    grad_wait(1)
    grad_on(1)
    block_wait(1)
    block_on(1)
    gain_step(3)
    gain_step(4)
    for k in range(1, depth):
        w_z_copy(k).wait_recv()
    own = pl.ds(pl.multiple_of(tp * w_part, w_part), w_part)
    total = w_sum_ref[own, q_cols:o_start]
    for k in range(depth - 1):
        total = total + w_z[k].astype(f32)
    latent_sum_ref[...] = total
    for k in range(2, depth):
        grad_wait(k)
        grad_on(k)
        block_wait(k)
        block_on(k)

    own_grad_copy.wait()
    own_block_copy.wait()
    branch_drain()
    grad_drain()
    block_drain()
    for i in range(depth):
        for slot in range(4):
            pair_copy(i, slot).wait_send()
        if i >= depth - 2:
            for slot in range(2):
                first_copy(i, slot).wait_send()
            second_copy(i).wait_send()
            if i < depth - 1:
                z_copy(i).wait_send()
    for slot in range(4):
        w_pair_copy(slot).wait_send()
    w_first_copy(0).wait_send()
    w_second_copy().wait_send()
    for k in range(1, depth):
        h_copy(k).wait_send()
        w_z_copy(k).wait_send()
    for n in range(len(partners)):
        gain_copy(n).wait_send()


def tail_call(
    branch, middle_grad, middle, out_part, router, gain_part, inputs, w_output, w_query, w_latent, w_up,
    hidden, qn, qr, kv, kr, attended, latent_in, compressed, tables, gain_latent, gain_attn,
    heads, cid,
):
    f32, bf16 = jnp.float32, jnp.bfloat16
    blocks, depth, rows, width = out_part.shape
    tokens = hidden.shape[0]
    rank = compressed.shape[1]
    q_cols, l_cols = w_query.shape[1], w_latent.shape[1]
    w_rows = width // blocks
    w_cols = q_cols + l_cols + w_output.shape[0] + rank * w_up.shape[1] // width
    dma = pltpu.SemaphoreType.DMA
    vmem, anywhere = pl.BlockSpec(memory_space=pltpu.VMEM), pl.BlockSpec(memory_space=pl.ANY)
    return pl.pallas_call(
        functools.partial(tail_kernel, depth, heads),
        out_shape=(
            jax.ShapeDtypeStruct((depth, rows, width), bf16),
            jax.ShapeDtypeStruct((depth, rows, width), bf16),
            jax.ShapeDtypeStruct((8, width), f32),
            jax.ShapeDtypeStruct((w_rows, w_cols), f32),
            jax.ShapeDtypeStruct((w_rows // depth, l_cols), f32),
            jax.ShapeDtypeStruct((depth, 4, rows, width), bf16),
            jax.ShapeDtypeStruct((blocks, w_rows, w_cols), bf16),
        ),
        in_specs=[vmem, vmem, vmem, anywhere, vmem, vmem, anywhere] + [vmem] * 15,
        out_specs=(anywhere, anywhere, vmem, vmem, vmem, anywhere, anywhere),
        scratch_shapes=[
            pltpu.VMEM((depth, rows, width), bf16),
            pltpu.VMEM((2, 2, rows, width), bf16),
            pltpu.VMEM((2, 4, rows, width), bf16),
            pltpu.VMEM((depth, 2, rows, width), bf16),
            pltpu.VMEM((depth, rows, width), bf16),
            pltpu.VMEM((depth - 1, rows, width), bf16),
            pltpu.VMEM((depth, rows, width), bf16),
            pltpu.VMEM((depth - 1, rows, width), bf16),
            pltpu.VMEM((rows, width), f32),
            pltpu.VMEM((tokens, heads * VDIM), bf16),
            pltpu.VMEM((tokens, 128), f32),
            pltpu.VMEM((tokens, q_cols), bf16),
            pltpu.VMEM((tokens, heads * (NOPE + VDIM)), bf16),
            pltpu.VMEM((tokens, l_cols), bf16),
            pltpu.VMEM((rank, heads * (NOPE + VDIM)), bf16),
            pltpu.VMEM((2, w_rows, w_cols), bf16),
            pltpu.VMEM((4, w_rows, w_cols), bf16),
            pltpu.VMEM((2, w_rows, w_cols), bf16),
            pltpu.VMEM((w_rows, w_cols), bf16),
            pltpu.VMEM((depth - 1, w_rows // depth, l_cols), bf16),
            pltpu.VMEM((rows, width), bf16),
            pltpu.VMEM((rows, width), bf16),
            pltpu.VMEM((rows, width), bf16),
            pltpu.VMEM((10, 8, width), f32),
            dma((2, 2)),
            dma((depth, 4)), dma((depth, 4)), dma((depth, 2)), dma((depth, 2)), dma((depth,)), dma((depth,)),
            dma((depth - 1,)), dma((depth - 1,)),
            dma((depth, 2)), dma((depth,)),
            dma((depth - 1,)), dma((depth - 1,)),
            dma((depth, 2)), dma((depth,)),
            dma((depth, 2)), dma((depth,)),
            dma((4,)), dma((4,)), dma((2,)), dma((2,)), dma, dma, dma((depth - 1,)), dma((depth - 1,)),
            dma((5,)), dma((5,)), dma((3,)), dma((2,)),
        ],
        compiler_params=pltpu.CompilerParams(collective_id=cid, has_side_effects=True, vmem_limit_bytes=63 << 20),
    )(
        branch, middle_grad, middle, out_part, router, gain_part, inputs, w_output, w_query, w_latent, w_up,
        hidden, qn, qr, kv, kr, attended, latent_in, compressed, tables,
        gain_latent.reshape(1, rank), gain_attn.reshape(1, width),
    )


def padded_hidden(routed, shared):
    return -(-(routed + shared + 24) // 128) * 128


def split_wide(values):
    high = values.astype(jnp.bfloat16)
    rest = values - high.astype(jnp.float32)
    mid = rest.astype(jnp.bfloat16)
    low = (rest - mid.astype(jnp.float32)).astype(jnp.bfloat16)
    return (high, mid, low)


def body_dense(
    inputs,
    gain_attn,
    w_query,
    w_latent,
    gain_latent,
    w_latent_up,
    w_output,
    gain_ffn,
    w_router,
    w_shared_in,
    w_shared_out,
    w_expert_in,
    w_expert_out,
    expert_ids,
    slot_ids,
    cotangent,
):
    f32, bf16 = jnp.float32, jnp.bfloat16
    tokens, model_width = inputs.shape
    ep_count, tp_count = lax.axis_size("ep"), lax.axis_size("tp")
    ep_index, tp_index = lax.axis_index("ep"), lax.axis_index("tp")
    heads_here = w_output.shape[0] // VDIM
    experts = w_router.shape[1]
    capacity = (9 * tokens * TOPK + 64 * experts - 1) // (64 * experts) * 8
    qk_width = NOPE + ROPE
    score_scale = qk_width ** (-0.5)
    rows_part = tokens // tp_count

    expert_range = jnp.arange(experts, dtype=jnp.int32)
    kept = jnp.any(
        (expert_ids[:, :, None] == expert_range) & (slot_ids < capacity)[:, :, None], axis=1
    ).astype(f32)
    kept_here = lax.all_to_all(kept, "ep", split_axis=1, concat_axis=0, tiled=True)
    rows_part = tokens // tp_count
    kept_lanes = jnp.broadcast_to(
        kept_here.reshape(ep_count, tp_count, rows_part, 1).swapaxes(0, 1),
        (tp_count, ep_count, rows_part, 128),
    ).astype(bf16)

    routed = w_expert_in.shape[3]
    shared = w_shared_in.shape[2] // ep_count
    hidden = padded_hidden(routed, shared)
    shared_start = ep_index * shared
    shared_in = lax.dynamic_slice_in_dim(w_shared_in, shared_start, shared, 2)
    shared_out = lax.dynamic_slice_in_dim(w_shared_out, shared_start, shared, 0)
    router_parts = jnp.concatenate(split_wide(w_router), axis=1)
    fill = hidden - routed - shared
    w_in = jnp.concatenate(
        [
            w_expert_in[0, 0],
            shared_in[0],
            jnp.pad(router_parts, ((0, 0), (0, fill - router_parts.shape[1]))),
            w_expert_in[0, 1],
            shared_in[1],
            jnp.zeros((model_width, fill), bf16),
        ],
        axis=1,
    )
    w_out = jnp.concatenate(
        [w_expert_out[0], shared_out, jnp.zeros((fill, model_width), bf16)], axis=0
    )

    resid = inputs.astype(f32)
    inv_first = lax.rsqrt(jnp.mean(resid * resid, axis=-1, keepdims=True) + EPSILON)
    normed_first = resid * inv_first
    hidden_attn = (normed_first * gain_attn).astype(bf16)
    cosine, sine_table = angles(tokens, ROPE)
    zero = jnp.zeros_like(sine_table)
    tables = jnp.stack(
        [
            jnp.tile(cosine, (1, 4)),
            jnp.tile(jnp.concatenate([-sine_table, zero], axis=1), (1, 2)),
            jnp.tile(jnp.concatenate([zero, sine_table], axis=1), (1, 2)),
        ]
    )
    by_head = w_query.reshape(model_width, heads_here, qk_width)
    w_query_sorted = jnp.concatenate(
        [
            by_head[..., :NOPE].reshape(model_width, heads_here * NOPE),
            by_head[..., NOPE:].reshape(model_width, heads_here * ROPE),
        ],
        axis=1,
    )
    w_latent_wide = jnp.pad(w_latent, ((0, 0), (0, 128 - ROPE)))
    query_raw = jnp.dot(hidden_attn, w_query_sorted, preferred_element_type=f32)
    query_nope = query_raw[:, : heads_here * NOPE].astype(bf16)
    query_rope = rotate(
        query_raw[:, heads_here * NOPE :].reshape(tokens, heads_here, ROPE),
        cosine[:, None],
        sine_table[:, None],
    ).astype(bf16)
    latent = jnp.dot(hidden_attn, w_latent, preferred_element_type=f32)
    compressed = latent[:, :KV_RANK]
    inv_latent = lax.rsqrt(jnp.mean(compressed * compressed, axis=-1, keepdims=True) + EPSILON)
    latent_in = (compressed * inv_latent * gain_latent).astype(bf16)
    key_rope = rotate(latent[:, KV_RANK:], cosine, sine_table).astype(bf16)
    key_pair = jnp.stack(
        [jnp.pad(key_rope, ((0, 0), (0, ROPE))), jnp.pad(key_rope, ((0, 0), (ROPE, 0)))]
    )
    key_value = jnp.dot(latent_in, w_latent_up, preferred_element_type=f32).astype(bf16)
    per_head = key_value.reshape(tokens, heads_here, NOPE + VDIM)
    block_ids = jnp.arange(tokens) // BLOCK
    allowed = block_ids[None, :] <= block_ids[:, None]
    query_rot = jnp.concatenate(
        [query_nope.reshape(tokens, heads_here, NOPE), query_rope], axis=-1
    )
    scores = attention_scores(query_rot, per_head[..., :NOPE], key_rope, score_scale, allowed)
    exp_scores = jnp.exp(scores - jnp.max(scores, axis=-1, keepdims=True))
    attn_probs = exp_scores / jnp.sum(exp_scores, axis=-1, keepdims=True)
    attended = (
        jnp.einsum(
            "hqk,khd->qhd", attn_probs.astype(bf16), per_head[..., NOPE:], preferred_element_type=f32
        )
        .astype(bf16)
        .reshape(tokens, heads_here * VDIM)
    )
    attn_part = jnp.dot(attended, w_output, preferred_element_type=f32).astype(bf16)

    middle, hidden_all, cot_all, hidden_grads, gated, out_part, rows_grad = experts_call(
        attn_part, inputs, gain_ffn, cotangent, kept_lanes, w_in, w_out,
        ep_count, tp_count, routed, shared, experts, 0,
    )
    middle_grad, branch, gain_ffn_part, in_grad_w, out_grad_w = sum_call(
        rows_grad, hidden_all, hidden_grads, gated, cot_all, middle, gain_ffn, 1
    )
    base = routed + shared
    in_grad_gate, in_grad_up = in_grad_w[:, :hidden], in_grad_w[:, hidden:]
    router_wide = jnp.pad(
        in_grad_gate[:, base : base + experts], ((0, 0), (ROPE, 128 - ROPE - experts))
    ).astype(bf16)
    block_out, grad_inputs, gains, w_sum, latent_sum, _, _ = tail_call(
        branch, middle_grad, middle, out_part, router_wide, gain_ffn_part, inputs,
        w_output, w_query_sorted, w_latent_wide, w_latent_up, hidden_attn,
        query_nope, query_rope.reshape(tokens, heads_here * ROPE), key_value, key_pair,
        attended, latent_in, compressed, tables, gain_latent, gain_attn, heads_here, 2,
    )
    grad_expert_in = jnp.stack([in_grad_gate[:, :routed], in_grad_up[:, :routed]])[None]
    grad_expert_out = out_grad_w[None, :routed]
    shared_in_part = jnp.stack([in_grad_gate[:, routed:base], in_grad_up[:, routed:base]])
    grad_shared_in = lax.all_to_all(
        shared_in_part.astype(bf16), "ep", split_axis=1, concat_axis=2, tiled=True
    ).astype(f32)
    grad_shared_out = lax.all_to_all(
        out_grad_w[routed:base].astype(bf16), "ep", split_axis=1, concat_axis=0, tiled=True
    ).astype(f32)

    w_rows = model_width // ep_count
    nope_all, rope_all = heads_here * NOPE, heads_here * qk_width
    grad_query = jnp.concatenate(
        [
            w_sum[:, :nope_all].reshape(w_rows, heads_here, NOPE),
            w_sum[:, nope_all:rope_all].reshape(w_rows, heads_here, ROPE),
        ],
        axis=-1,
    ).reshape(w_rows, rope_all)
    o_start = rope_all + w_latent_wide.shape[1]
    o_cols = model_width // ep_count
    o_pieces = heads_here * VDIM // w_rows
    grad_output = jnp.concatenate(
        [w_sum[:, o_start + n * o_cols : o_start + (n + 1) * o_cols] for n in range(o_pieces)], axis=0
    )
    u_start = o_start + o_pieces * o_cols
    u_rows = KV_RANK // ep_count
    grad_latent_up = jnp.concatenate(
        [w_sum[n * u_rows : (n + 1) * u_rows, u_start:] for n in range(w_rows // u_rows)], axis=1
    )
    grad_latent = latent_sum[:, : KV_RANK + ROPE]
    grad_router = latent_sum[:, KV_RANK + ROPE : KV_RANK + ROPE + experts]
    flat = ep_index * tp_count + tp_index
    wide_part, rank_part = (n // (ep_count * tp_count) for n in (model_width, KV_RANK))
    grad_gain_attn = lax.dynamic_slice_in_dim(gains[0], flat * wide_part, wide_part, 0)
    grad_gain_ffn = lax.dynamic_slice_in_dim(gains[1], flat * wide_part, wide_part, 0)
    grad_gain_latent = lax.dynamic_slice_in_dim(gains[2], flat * rank_part, rank_part, 0)
    block_out = block_out.reshape(tokens, model_width)
    grad_inputs = grad_inputs.reshape(tokens, model_width)
    return (
        block_out,
        grad_inputs,
        grad_gain_attn,
        grad_query,
        grad_latent,
        grad_gain_latent,
        grad_latent_up,
        grad_output,
        grad_gain_ffn,
        grad_router,
        grad_shared_in,
        grad_shared_out,
        grad_expert_in,
        grad_expert_out,
    )


def solution(mesh):
    near = mesh.shape["ep"] == 8 and mesh.shape["tp"] == 4
    body = body_dense if near else body_slots
    placed = (
        P("ep", None),
        P(),
        P(None, "tp"),
        P(),
        P(),
        P(None, "tp"),
        P("tp", None),
        P(),
        P(),
        P(None, None, "tp"),
        P("tp", None),
        P("ep", None, None, "tp"),
        P("ep", "tp", None),
        P("ep", None),
        P("ep", None),
        P("ep", None),
    )
    return jax.shard_map(
        body,
        mesh=mesh,
        in_specs=placed,
        out_specs=(
            P("ep", None),
            P("ep", None),
            P(("ep", "tp")),
            P("ep", "tp"),
            P(("ep", "tp"), None),
            P(("ep", "tp")),
            P("ep", "tp"),
            P("tp", "ep"),
            P(("ep", "tp")),
            P(("ep", "tp"), None),
            P(None, "ep", "tp"),
            P("tp", "ep"),
            P("ep", None, None, "tp"),
            P("ep", "tp", None),
        ),
        check_vma=False,
    )
```

```python
import functools
import math

import jax
import jax.numpy as jnp
import numpy as np
from jax import lax
from jax.experimental import pallas as pl
from jax.experimental.pallas import tpu as pltpu
from jax.sharding import PartitionSpec as P

NOPE = 128
ROPE = 64
VDIM = 128
KV_RANK = 512
TOPK = 6
BLOCK = 256


EPSILON = 1e-06
HIGHEST = lax.Precision.HIGHEST


def angles(length, rope_width):
    half_width = rope_width // 2
    position = jnp.arange(length, dtype=jnp.float32)
    inverse = jnp.exp(jnp.arange(half_width, dtype=jnp.float32) * (-math.log(10000.0) / half_width))
    angle_table = position[:, None] * inverse[None, :]
    return (jnp.cos(angle_table), jnp.sin(angle_table))


def rotate(values, cosine, sine_table):
    half_width = values.shape[-1] // 2
    front_part = values[..., :half_width]
    second = values[..., half_width:]
    return jnp.concatenate(
        [front_part * cosine - second * sine_table, second * cosine + front_part * sine_table],
        axis=-1,
    )


def silu_parts(gate_val):
    sigmoid_val = jax.nn.sigmoid(gate_val)
    return (gate_val * sigmoid_val, sigmoid_val * (1.0 + gate_val * (1.0 - sigmoid_val)))


def norm_back(grad_norm, gain_vec, normed, inverse):
    scaled = grad_norm * gain_vec
    return inverse * (scaled - normed * jnp.mean(scaled * normed, axis=-1, keepdims=True))


def attention_scores(query_rot, key_nope, key_rope, score_scale, allowed):
    nope_scores = jnp.einsum(
        "qhd,khd->hqk", query_rot[..., :NOPE], key_nope, preferred_element_type=jnp.float32
    )
    rope_scores = jnp.einsum(
        "qhr,kr->hqk", query_rot[..., NOPE:], key_rope, preferred_element_type=jnp.float32
    )
    return jnp.where(allowed[None], (nope_scores + rope_scores) * score_scale, -1e30)


def expert_forward(received, w_expert_in, w_expert_out, sources):
    sectioned = received.reshape(sources, -1, received.shape[1], received.shape[2])
    gate_up = jnp.einsum(
        "secd,egdh->secgh", sectioned, w_expert_in, preferred_element_type=jnp.float32
    )
    gate_val, gate_slope = silu_parts(gate_up[..., 0, :])
    activated = (gate_val * gate_up[..., 1, :]).astype(jnp.bfloat16)
    produced = jnp.einsum(
        "sech,ehd->secd", activated, w_expert_out, preferred_element_type=jnp.float32
    )
    return (sectioned, gate_up, activated, produced.reshape(received.shape))


def body_slots(
    inputs,
    gain_attn,
    w_query,
    w_latent,
    gain_latent,
    w_latent_up,
    w_output,
    gain_ffn,
    w_router,
    w_shared_in,
    w_shared_out,
    w_expert_in,
    w_expert_out,
    expert_ids,
    slot_ids,
    cotangent,
):
    tokens, model_width = inputs.shape
    tp_count = lax.axis_size("tp")
    tp_index = lax.axis_index("tp")
    heads_here = w_output.shape[0] // VDIM
    experts = w_router.shape[1]
    local_experts = w_expert_in.shape[0]
    sources = experts // local_experts
    capacity = (9 * tokens * TOPK + 64 * experts - 1) // (64 * experts) * 8
    qk_width = NOPE + ROPE
    score_scale = qk_width ** (-0.5)
    rows_part = tokens // tp_count
    row_start = tp_index * rows_part
    resid = inputs.astype(jnp.float32)
    inv_first = lax.rsqrt(jnp.mean(resid * resid, axis=-1, keepdims=True) + EPSILON)
    normed_first = resid * inv_first
    hidden_attn = (normed_first * gain_attn).astype(jnp.bfloat16)
    cosine, sine_table = angles(tokens, ROPE)
    query_raw = jnp.dot(hidden_attn, w_query, preferred_element_type=jnp.float32).reshape(
        tokens, heads_here, qk_width
    )
    query_rot = jnp.concatenate(
        [
            query_raw[..., :NOPE],
            rotate(query_raw[..., NOPE:], cosine[:, None], sine_table[:, None]),
        ],
        axis=-1,
    ).astype(jnp.bfloat16)
    latent = jnp.dot(hidden_attn, w_latent, preferred_element_type=jnp.float32)
    compressed = latent[:, :KV_RANK]
    inv_latent = lax.rsqrt(jnp.mean(compressed * compressed, axis=-1, keepdims=True) + EPSILON)
    normed_latent = compressed * inv_latent
    latent_in = (normed_latent * gain_latent).astype(jnp.bfloat16)
    key_rope = rotate(latent[:, KV_RANK:], cosine, sine_table).astype(jnp.bfloat16)
    key_value = (
        jnp.dot(latent_in, w_latent_up, preferred_element_type=jnp.float32)
        .astype(jnp.bfloat16)
        .reshape(tokens, heads_here, NOPE + VDIM)
    )
    key_nope = key_value[..., :NOPE]
    values = key_value[..., NOPE:]
    block_ids = jnp.arange(tokens) // BLOCK
    allowed = block_ids[None, :] <= block_ids[:, None]
    scores = attention_scores(query_rot, key_nope, key_rope, score_scale, allowed)
    row_peak = jnp.max(scores, axis=-1, keepdims=True)
    exp_scores = jnp.exp(scores - row_peak)
    totals = jnp.sum(exp_scores, axis=-1, keepdims=True)
    attn_probs = exp_scores / totals
    log_total = row_peak + jnp.log(totals)
    attended = (
        jnp.einsum(
            "hqk,khd->qhd",
            attn_probs.astype(jnp.bfloat16),
            values,
            preferred_element_type=jnp.float32,
        )
        .astype(jnp.bfloat16)
        .reshape(tokens, heads_here * VDIM)
    )
    attn_full = lax.psum(
        jnp.dot(attended, w_output, preferred_element_type=jnp.float32).astype(jnp.bfloat16), "tp"
    ).astype(jnp.float32)
    middle = resid + attn_full
    inv_second = lax.rsqrt(jnp.mean(middle * middle, axis=-1, keepdims=True) + EPSILON)
    normed_second = middle * inv_second
    hidden_ffn = (normed_second * gain_ffn).astype(jnp.bfloat16)
    hidden_wide = hidden_ffn.astype(jnp.float32)
    logits = jnp.dot(hidden_wide, w_router, precision=HIGHEST, preferred_element_type=jnp.float32)
    logit_peak = jnp.max(logits, axis=-1, keepdims=True)
    exp_logits = jnp.exp(logits - logit_peak)
    router_probs = exp_logits / jnp.sum(exp_logits, axis=-1, keepdims=True)
    route_onehot = (
        expert_ids[:, :, None] == jnp.arange(experts, dtype=jnp.int32)[None, None, :]
    ).astype(jnp.float32)
    pair_gate = jnp.sum(route_onehot * router_probs[:, None, :], axis=-1)
    kept_pair = slot_ids < capacity
    flat_index = jnp.where(kept_pair, expert_ids * capacity + slot_ids, experts * capacity)
    row_numbers = jnp.broadcast_to(jnp.arange(tokens, dtype=jnp.int32)[:, None], (tokens, TOPK))
    owner_row = (
        jnp.full((experts * capacity,), tokens, jnp.int32)
        .at[flat_index.reshape(-1)]
        .set(row_numbers.reshape(-1), mode="drop")
    )
    outgoing = jnp.take(hidden_ffn, owner_row, axis=0, mode="fill", fill_value=0).reshape(
        experts, capacity, model_width
    )
    received = lax.all_to_all(outgoing, "ep", split_axis=0, concat_axis=0, tiled=True)
    sectioned, gate_up, activated, produced = expert_forward(
        received, w_expert_in, w_expert_out, sources
    )
    returned = lax.all_to_all(
        produced.astype(jnp.bfloat16), "ep", split_axis=0, concat_axis=0, tiled=True
    ).astype(produced.dtype)
    out_grad = cotangent.astype(jnp.float32)
    back_rows = returned.reshape(-1, model_width)
    combined = jnp.zeros((tokens, model_width), jnp.float32)
    gate_cols = []
    for pick_index in range(TOPK):
        taken_rows = jnp.take(
            back_rows, flat_index[:, pick_index], axis=0, mode="fill", fill_value=0.0
        )
        combined = combined + pair_gate[:, pick_index : pick_index + 1] * taken_rows
        gate_cols.append(jnp.sum(out_grad * taken_rows, axis=-1))
    gate_grad = jnp.stack(gate_cols, axis=1)
    shared_gate = jnp.dot(hidden_ffn, w_shared_in[0], preferred_element_type=jnp.float32)
    shared_up = jnp.dot(hidden_ffn, w_shared_in[1], preferred_element_type=jnp.float32)
    shared_val, shared_slope = silu_parts(shared_gate)
    shared_act = (shared_val * shared_up).astype(jnp.bfloat16)
    branch_part = jnp.dot(shared_act, w_shared_out, preferred_element_type=jnp.float32) + combined
    ffn_full = lax.psum(branch_part.astype(jnp.bfloat16), "tp").astype(jnp.float32)
    block_out = (middle + ffn_full).astype(jnp.bfloat16)
    slot_gate = (
        jnp.zeros((experts * capacity,), jnp.float32)
        .at[flat_index.reshape(-1)]
        .set(pair_gate.reshape(-1), mode="drop")
    )
    gathered_grad = jnp.take(cotangent, owner_row, axis=0, mode="fill", fill_value=0)
    slot_grad = (
        (slot_gate[:, None] * gathered_grad.astype(jnp.float32))
        .astype(jnp.bfloat16)
        .reshape(experts, capacity, model_width)
    )
    grad_arrived = lax.all_to_all(slot_grad, "ep", split_axis=0, concat_axis=0, tiled=True).reshape(
        sectioned.shape
    )
    act_grad = jnp.einsum(
        "secd,ehd->sech", grad_arrived, w_expert_out, preferred_element_type=jnp.float32
    )
    gate_val, gate_slope = silu_parts(gate_up[..., 0, :])
    up_val = gate_up[..., 1, :]
    gu_grad = jnp.stack([act_grad * up_val * gate_slope, act_grad * gate_val], axis=-2).astype(
        jnp.bfloat16
    )
    grad_expert_out = jnp.einsum(
        "sech,secd->ehd", activated, grad_arrived, preferred_element_type=jnp.float32
    )
    grad_expert_in = jnp.einsum(
        "secd,secgh->egdh", sectioned, gu_grad, preferred_element_type=jnp.float32
    )
    rows_grad = jnp.einsum(
        "secgh,egdh->secd", gu_grad, w_expert_in, preferred_element_type=jnp.float32
    ).reshape(received.shape)
    returned_grad = (
        lax.all_to_all(
            rows_grad.astype(jnp.bfloat16), "ep", split_axis=0, concat_axis=0, tiled=True
        )
        .astype(rows_grad.dtype)
        .reshape(-1, model_width)
    )
    routed_grad = jnp.zeros((tokens, model_width), jnp.float32)
    for pick_index in range(TOPK):
        routed_grad = routed_grad + jnp.take(
            returned_grad, flat_index[:, pick_index], axis=0, mode="fill", fill_value=0.0
        )
    shared_act_grad = jnp.einsum(
        "td,fd->tf", cotangent, w_shared_out, preferred_element_type=jnp.float32
    )
    shared_gate_grad = (shared_act_grad * shared_up * shared_slope).astype(jnp.bfloat16)
    shared_up_grad = (shared_act_grad * shared_val).astype(jnp.bfloat16)
    shared_out_grad = jnp.einsum(
        "tf,td->fd", shared_act, cotangent, preferred_element_type=jnp.float32
    )
    shared_in_grad = jnp.stack(
        [
            jnp.einsum(
                "td,tf->df", hidden_ffn, shared_gate_grad, preferred_element_type=jnp.float32
            ),
            jnp.einsum("td,tf->df", hidden_ffn, shared_up_grad, preferred_element_type=jnp.float32),
        ],
        axis=0,
    )
    shared_back = jnp.einsum(
        "tf,df->td", shared_gate_grad, w_shared_in[0], preferred_element_type=jnp.float32
    ) + jnp.einsum("tf,df->td", shared_up_grad, w_shared_in[1], preferred_element_type=jnp.float32)
    prob_grad = jnp.sum(route_onehot * gate_grad[:, :, None], axis=1)
    logit_grad = router_probs * (
        prob_grad - jnp.sum(router_probs * prob_grad, axis=-1, keepdims=True)
    )
    router_back = jnp.einsum(
        "te,de->td", logit_grad, w_router, precision=HIGHEST, preferred_element_type=jnp.float32
    )
    router_grad = jnp.einsum(
        "td,te->de", hidden_wide, logit_grad, precision=HIGHEST, preferred_element_type=jnp.float32
    )
    ffn_grad = lax.psum(
        (shared_back + routed_grad + router_back).astype(jnp.bfloat16), "tp"
    ).astype(jnp.float32)
    middle_grad = out_grad + norm_back(ffn_grad, gain_ffn, normed_second, inv_second)
    gain_ffn_grad = jnp.sum(
        lax.dynamic_slice_in_dim(ffn_grad * normed_second, row_start, rows_part, 0), axis=0
    )
    branch_grad = middle_grad.astype(jnp.bfloat16)
    output_w_grad = jnp.einsum(
        "tf,td->fd", attended, branch_grad, preferred_element_type=jnp.float32
    )
    attended_grad = (
        jnp.einsum("td,fd->tf", branch_grad, w_output, preferred_element_type=jnp.float32)
        .astype(jnp.bfloat16)
        .reshape(tokens, heads_here, VDIM)
    )
    scores_again = attention_scores(query_rot, key_nope, key_rope, score_scale, allowed)
    probs_again = jnp.exp(scores_again - log_total)
    values_grad = jnp.einsum(
        "hqk,qhd->khd",
        probs_again.astype(jnp.bfloat16),
        attended_grad,
        preferred_element_type=jnp.float32,
    )
    prob_part = jnp.einsum(
        "qhd,khd->hqk", attended_grad, values, preferred_element_type=jnp.float32
    )
    score_grad = (
        probs_again * (prob_part - jnp.sum(probs_again * prob_part, axis=-1, keepdims=True))
    ).astype(jnp.bfloat16)
    query_nope_grad = (
        jnp.einsum("hqk,khd->qhd", score_grad, key_nope, preferred_element_type=jnp.float32)
        * score_scale
    )
    query_rope_grad = (
        jnp.einsum("hqk,kr->qhr", score_grad, key_rope, preferred_element_type=jnp.float32)
        * score_scale
    )
    key_nope_grad = (
        jnp.einsum(
            "hqk,qhd->khd", score_grad, query_rot[..., :NOPE], preferred_element_type=jnp.float32
        )
        * score_scale
    )
    key_rope_grad = (
        jnp.einsum(
            "hqk,qhr->kr", score_grad, query_rot[..., NOPE:], preferred_element_type=jnp.float32
        )
        * score_scale
    )
    kv_grad = (
        jnp.concatenate([key_nope_grad, values_grad], axis=-1)
        .astype(jnp.bfloat16)
        .reshape(tokens, heads_here * (NOPE + VDIM))
    )
    latent_up_grad = jnp.einsum("tr,tf->rf", latent_in, kv_grad, preferred_element_type=jnp.float32)
    latent_in_grad = jnp.einsum(
        "tf,rf->tr", kv_grad, w_latent_up, preferred_element_type=jnp.float32
    )
    gain_latent_grad = jnp.sum(latent_in_grad * normed_latent, axis=0)
    latent_grad_part = jnp.concatenate(
        [
            norm_back(latent_in_grad, gain_latent, normed_latent, inv_latent),
            rotate(key_rope_grad, cosine, -sine_table),
        ],
        axis=-1,
    )
    query_grad = (
        jnp.concatenate(
            [query_nope_grad, rotate(query_rope_grad, cosine[:, None], -sine_table[:, None])],
            axis=-1,
        )
        .astype(jnp.bfloat16)
        .reshape(tokens, heads_here * qk_width)
    )
    query_w_grad = jnp.einsum(
        "td,tf->df", hidden_attn, query_grad, preferred_element_type=jnp.float32
    )
    hidden_part = jnp.einsum("tf,df->td", query_grad, w_query, preferred_element_type=jnp.float32)
    hidden_sum, latent_sum = (
        lax.psum(hidden_part.astype(jnp.bfloat16), "tp").astype(jnp.float32),
        lax.psum(latent_grad_part.astype(jnp.bfloat16), "tp").astype(jnp.float32),
    )
    latent_low = latent_sum.astype(jnp.bfloat16)
    attn_in_grad = hidden_sum + jnp.einsum(
        "tf,df->td", latent_low, w_latent, preferred_element_type=jnp.float32
    )
    latent_w_grad = jnp.einsum(
        "td,tf->df",
        lax.dynamic_slice_in_dim(hidden_attn, row_start, rows_part, 0),
        lax.dynamic_slice_in_dim(latent_low, row_start, rows_part, 0),
        preferred_element_type=jnp.float32,
    )
    gain_attn_grad = jnp.sum(
        lax.dynamic_slice_in_dim(attn_in_grad * normed_first, row_start, rows_part, 0), axis=0
    )
    grad_inputs = (
        middle_grad + norm_back(attn_in_grad, gain_attn, normed_first, inv_first)
    ).astype(jnp.bfloat16)
    grad_query, grad_latent_up, grad_output, grad_shared_in, grad_shared_out = (
        lax.psum_scatter(
            query_w_grad.astype(jnp.bfloat16), "ep", scatter_dimension=0, tiled=True
        ).astype(jnp.float32),
        lax.psum_scatter(
            latent_up_grad.astype(jnp.bfloat16), "ep", scatter_dimension=0, tiled=True
        ).astype(jnp.float32),
        lax.psum_scatter(
            output_w_grad.astype(jnp.bfloat16), "ep", scatter_dimension=1, tiled=True
        ).astype(jnp.float32),
        lax.psum_scatter(
            shared_in_grad.astype(jnp.bfloat16), "ep", scatter_dimension=1, tiled=True
        ).astype(jnp.float32),
        lax.psum_scatter(
            shared_out_grad.astype(jnp.bfloat16), "ep", scatter_dimension=1, tiled=True
        ).astype(jnp.float32),
    )
    grad_latent, grad_gain_latent, grad_gain_attn, grad_gain_ffn, grad_router = (
        lax.psum_scatter(latent_w_grad, ("ep", "tp"), scatter_dimension=0, tiled=True),
        lax.psum_scatter(gain_latent_grad, ("ep", "tp"), scatter_dimension=0, tiled=True),
        lax.psum_scatter(gain_attn_grad, ("ep", "tp"), scatter_dimension=0, tiled=True),
        lax.psum_scatter(gain_ffn_grad, ("ep", "tp"), scatter_dimension=0, tiled=True),
        lax.psum_scatter(router_grad, ("ep", "tp"), scatter_dimension=0, tiled=True),
    )
    return (
        block_out,
        grad_inputs,
        grad_gain_attn,
        grad_query,
        grad_latent,
        grad_gain_latent,
        grad_latent_up,
        grad_output,
        grad_gain_ffn,
        grad_router,
        grad_shared_in,
        grad_shared_out,
        grad_expert_in,
        grad_expert_out,
    )


MESH = pl.DeviceIdType.MESH


def plane_partners(ep):
    def flip(bit):
        return ep + bit - 2 * bit * lax.rem(lax.div(ep, bit), 2)

    return flip(1), flip(2), flip(4)


def line_order(tp):
    def pick(a, b, c, d):
        return jnp.where(tp == 0, a, jnp.where(tp == 1, b, jnp.where(tp == 2, c, d)))

    return (tp, pick(1, 0, 3, 2), pick(2, 2, 1, 1), pick(3, 3, 0, 0))


def greet(devices):
    barrier = pltpu.get_barrier_semaphore()
    for ep, tp in devices:
        pl.semaphore_signal(barrier, inc=1, device_id=(ep, tp), device_id_type=MESH)
    pl.semaphore_wait(barrier, len(devices))


def remote(src, dst, send, recv, device):
    return pltpu.make_async_remote_copy(
        src_ref=src, dst_ref=dst, send_sem=send, recv_sem=recv, device_id=device, device_id_type=MESH
    )


def add_rows(dst, a, b):
    def body(r, _):
        at = pl.ds(pl.multiple_of(r * 16, 16), 16)
        dst[at, :] = (a[at, :].astype(jnp.float32) + b[at, :].astype(jnp.float32)).astype(dst.dtype)
        return 0

    lax.fori_loop(0, dst.shape[0] // 16, body, 0)


def turn(slab, table, sign):
    cosine, front, second = table
    return slab * cosine + sign * (pltpu.roll(slab, 96, 1) * front + pltpu.roll(slab, 32, 1) * second)


def attention_kernel(
    heads,
    inputs, gain_attn, w_query, w_latent, gain_latent, w_up, w_output, tables,
    part, hidden, qn_ref, qr_ref, kv, kr_ref, attended, latent_in, compressed,
    rope_slab,
):
    f32, bf16 = jnp.float32, jnp.bfloat16
    tokens, width = inputs.shape
    rank = compressed.shape[1]
    across = (((1,), (1,)), ((), ()))
    score_scale = (NOPE + ROPE) ** (-0.5)

    def dot(a, b, dims=(((1,), (0,)), ((), ()))):
        return lax.dot_general(a, b, dims, preferred_element_type=f32)

    def norm_rows(r, _):
        at = pl.ds(pl.multiple_of(r * 16, 16), 16)
        v = inputs[at, :].astype(f32)
        inverse = lax.rsqrt(jnp.mean(v * v, axis=-1, keepdims=True) + EPSILON)
        hidden[at, :] = (v * inverse * gain_attn[...]).astype(bf16)
        return 0

    lax.fori_loop(0, tokens // 16, norm_rows, 0)
    lanes = lax.broadcasted_iota(jnp.int32, (1, 128), 1)
    table = tuple(tables[n] for n in range(3))
    latent = dot(hidden[...], w_latent[...])
    held = latent[:, :rank]
    compressed[...] = held
    inverse = lax.rsqrt(jnp.mean(held * held, axis=-1, keepdims=True) + EPSILON)
    latent_in[...] = (held * inverse * gain_latent[...]).astype(bf16)
    rope_slab[...] = jnp.zeros_like(rope_slab)
    rope_slab[:, 0:ROPE] = latent[:, rank:]
    key = turn(rope_slab[...], table, 1.0)
    kr_ref[0] = key.astype(bf16)
    kr_ref[1] = pltpu.roll(key, 64, 1).astype(bf16)
    kv[...] = dot(latent_in[...], w_up[...]).astype(bf16)
    pair = 2 * (NOPE + ROPE)
    for p in range(heads // 2):
        found = dot(hidden[...], w_query[:, p * pair : (p + 1) * pair])
        slabs = [found[:, n : n + 128] for n in (0, 128, 256)]
        qn_ref[:, 2 * p * NOPE : (2 * p + 1) * NOPE] = slabs[0].astype(bf16)
        odd = pltpu.roll(jnp.where(lanes < 64, slabs[2], slabs[1]), 64, 1)
        qn_ref[:, (2 * p + 1) * NOPE : (2 * p + 2) * NOPE] = odd.astype(bf16)
        qr_ref[:, p * 128 : (p + 1) * 128] = turn(jnp.where(lanes < 64, slabs[1], slabs[2]), table, 1.0).astype(bf16)
    for h in range(heads):
        for b in range(tokens // BLOCK):
            own = slice(b * BLOCK, (b + 1) * BLOCK)
            keys = slice(0, (b + 1) * BLOCK)
            slab = slice(h // 2 * 128, h // 2 * 128 + 128)
            at = slice(h * 128, h * 128 + 128)
            scores = dot(qn_ref[own, at], kv[keys, h * 256 : h * 256 + 128], across)
            scores = (scores + dot(qr_ref[own, slab], kr_ref[h % 2, keys, :], across)) * score_scale
            exps = jnp.exp(scores - jnp.max(scores, axis=-1, keepdims=True))
            probs = exps / jnp.sum(exps, axis=-1, keepdims=True)
            attended[own, at] = dot(probs.astype(bf16), kv[keys, h * 256 + 128 : h * 256 + 256]).astype(bf16)
    for n in range(0, width, 512):
        part[:, n : n + 512] = dot(attended[...], w_output[:, n : n + 512]).astype(bf16)


def attention_call(inputs, gain_attn, w_query, w_latent, gain_latent, w_up, w_output, tables, heads):
    f32, bf16 = jnp.float32, jnp.bfloat16
    tokens, width = inputs.shape
    rank = w_up.shape[0]
    vmem = pl.BlockSpec(memory_space=pltpu.VMEM)

    def shape(*size, kind=bf16):
        return jax.ShapeDtypeStruct(size, kind)

    return pl.pallas_call(
        functools.partial(attention_kernel, heads),
        out_shape=(
            shape(tokens, width), shape(tokens, width), shape(tokens, heads * NOPE), shape(tokens, heads * ROPE),
            shape(tokens, heads * (NOPE + VDIM)), shape(2, tokens, 128), shape(tokens, heads * VDIM),
            shape(tokens, rank), shape(tokens, rank, kind=f32),
        ),
        in_specs=[vmem] * 8,
        out_specs=(vmem,) * 9,
        scratch_shapes=[pltpu.VMEM((tokens, 128), f32)],
        compiler_params=pltpu.CompilerParams(vmem_limit_bytes=48 << 20),
    )(inputs, gain_attn.reshape(1, width), w_query, w_latent, gain_latent.reshape(1, rank), w_up, w_output, tables)


def experts_kernel(
    depth, blocks, routed, shared, experts,
    part_ref, resid_ref, gain_ref, cot_ref, kept_ref, w_in_ref, w_out_ref,
    middle_ref, h_out, cot_all, grads_out, gated_out, out_out, rows_out,
    h_all, got_z, resid_own, cot_tile, gu, act_grad, prob_lanes, diff_lanes, pair_lanes,
    grads_tile, gated_tile, out_tile, rows_tile,
    local_sem, z_send, z_recv, line_send, line_recv, h_send, h_recv, c_send, c_recv, tile_sem, store_sem,
):
    f32, bf16 = jnp.float32, jnp.bfloat16
    ep, tp = lax.axis_index("ep"), lax.axis_index("tp")
    pair, xn, yn = plane_partners(ep)
    parity = lax.rem(ep, 2)
    passed = jnp.where(parity == 0, xn, yn)
    onward = jnp.where(parity == 0, yn, xn)
    diag = xn + yn - ep
    rows = h_all.shape[2]
    width = h_all.shape[3]
    hidden = w_out_ref.shape[0]
    half = blocks // 2
    tile = half * rows
    up, down = jnp.minimum(tp + 1, depth - 1), jnp.maximum(tp - 1, 0)

    def twin(block):
        return block + pair - ep

    greet([(pair, tp), (xn, tp), (yn, tp)] + [(ep, lax.rem(tp + k, depth)) for k in range(1, depth)])

    def z_copy(k):
        to = lax.rem(tp + k, depth)
        start = pl.multiple_of(to * rows, rows)
        return remote(part_ref.at[pl.ds(start, rows)], got_z.at[k - 1], z_send.at[k - 1], z_recv.at[k - 1], (ep, to))

    for k in range(1, depth):
        z_copy(k).start()

    def h_copy(block, chunk, slot, to):
        ref = h_all.at[chunk, block]
        return remote(ref, ref, h_send.at[chunk, slot], h_recv.at[chunk, slot], (to, tp))

    def c_copy(block, chunk, slot, to):
        ref = cot_all.at[chunk, block]
        return remote(ref, ref, c_send.at[chunk, slot], c_recv.at[chunk, slot], (to, tp))

    def c_first(chunk, slot, to):
        src = cot_ref.at[pl.ds(pl.multiple_of(chunk * rows, rows), rows)]
        return remote(src, cot_all.at[chunk, ep], c_send.at[chunk, slot], c_recv.at[chunk, slot], (to, tp))

    def own_cot_in(chunk):
        src = cot_ref.at[pl.ds(pl.multiple_of(chunk * rows, rows), rows)]
        return pltpu.make_async_copy(src, out_tile.at[0, chunk], local_sem.at[chunk])

    def own_cot_out(chunk):
        return pltpu.make_async_copy(out_tile.at[0, chunk], cot_all.at[chunk, ep], local_sem.at[chunk])

    order = line_order(tp)

    def order_at(k):
        return jnp.where(k == 0, order[0], jnp.where(k == 1, order[1], jnp.where(k == 2, order[2], order[3])))

    resid_copy = pltpu.make_async_copy(
        resid_ref.at[pl.ds(pl.multiple_of(tp * rows, rows), rows)], resid_own, local_sem.at[depth]
    )
    resid_copy.start()
    for k in range(depth):
        c_first(order[k], 1, xn).start()
        c_first(order[k], 2, yn).start()
        c_first(order[k], 0, pair).start()
        own_cot_in(k).start()
    resid_copy.wait()
    for k in range(depth):
        own_cot_in(k).wait()
        own_cot_out(k).start()
    for k in range(1, depth):
        z_copy(k).wait_recv()

    def norm_rows(r, _):
        here = pl.ds(pl.multiple_of(r * 16, 16), 16)
        own = pl.ds(pl.multiple_of(tp * rows + r * 16, 16), 16)
        total = part_ref[own, :].astype(f32)
        for k in range(depth - 1):
            total = total + got_z[k, here, :].astype(f32)
        middle = resid_own[here, :].astype(f32) + total
        inverse = lax.rsqrt(jnp.mean(middle * middle, axis=-1, keepdims=True) + EPSILON)
        middle_ref[here, :] = middle
        h_all[tp, ep, here, :] = (middle * inverse * gain_ref[...]).astype(bf16)
        return 0

    lax.fori_loop(0, rows // 16, norm_rows, 0)
    for k in range(depth):
        own_cot_out(k).wait()

    def along(chunk, way, to):
        ref = h_all.at[chunk, ep]
        return remote(ref, ref, line_send.at[chunk, way], line_recv.at[chunk], (ep, to))

    def goes_up(chunk):
        return (chunk <= tp) & (tp < depth - 1)

    def goes_down(chunk):
        return (chunk >= tp) & (tp > 0)

    def send_chunk(k):
        chunk = order[k]
        if k > 0:
            along(chunk, 0, up).wait_recv()

        @pl.when(goes_up(chunk))
        def _():
            along(chunk, 0, up).start()

        @pl.when(goes_down(chunk))
        def _():
            along(chunk, 1, down).start()

        h_copy(ep, chunk, 1, xn).start()
        h_copy(ep, chunk, 2, yn).start()
        h_copy(ep, chunk, 0, pair).start()

    def forward_chunk(copy, chunk):
        copy(xn, chunk, 1, xn).wait_recv()
        copy(yn, chunk, 2, yn).wait_recv()
        copy(passed, chunk, 3, onward).start()
        copy(xn, chunk, 4, pair).start()
        copy(yn, chunk, 5, pair).start()

    def forward_diag(chunk):
        for copy in (h_copy, c_copy):
            copy(diag, chunk, 3, onward).wait_recv()
            copy(diag, chunk, 6, pair).start()

    def await_pair(chunk, slots):
        for copy in (h_copy, c_copy):
            for slot, block in slots:
                copy(block, chunk, slot, pair).wait_recv()

    send_chunk(0)
    forward_chunk(c_copy, order[0])
    forward_chunk(c_copy, order[1])
    send_chunk(1)
    forward_chunk(h_copy, order[0])

    lanes = lax.broadcasted_iota(jnp.int32, (1, 128), 1)
    base = routed + shared
    slab = base // 128 * 128
    lane0 = base - slab
    near_half = lax.div(ep, half)

    def tile_copies(i):
        k, side = lax.div(i, 2), lax.rem(i, 2)
        chunk = order_at(k)
        start = jnp.where(side == 0, near_half, 1 - near_half) * half
        group = pl.ds(start, half)
        slot = lax.rem(i, 2)
        stores = [
            pltpu.make_async_copy(h_all.at[chunk, group], h_out.at[chunk, group], store_sem.at[slot, 0]),
            pltpu.make_async_copy(grads_tile.at[slot], grads_out.at[chunk, group], store_sem.at[slot, 1]),
            pltpu.make_async_copy(gated_tile.at[slot], gated_out.at[chunk, group], store_sem.at[slot, 2]),
            pltpu.make_async_copy(out_tile.at[slot], out_out.at[group, chunk], store_sem.at[slot, 3]),
            pltpu.make_async_copy(rows_tile.at[slot], rows_out.at[chunk, group], store_sem.at[slot, 4]),
        ]
        load = pltpu.make_async_copy(cot_all.at[chunk, group], cot_tile, tile_sem)
        return chunk, start, slot, load, stores

    def step(i, _):
        k, side = lax.div(i, 2), lax.rem(i, 2)
        chunk, start, slot, load, stores = tile_copies(i)

        @pl.when(i == 0)
        def _():
            send_chunk(2)

        @pl.when(side == 0)
        def _():
            await_pair(chunk, ((0, pair), (4, twin(xn))))

        @pl.when(i == 1)
        def _():
            forward_chunk(h_copy, order[1])
            send_chunk(3)

        @pl.when(i == 2)
        def _():
            forward_chunk(c_copy, order[2])
            forward_chunk(h_copy, order[2])

        @pl.when(i == 3)
        def _():
            forward_chunk(c_copy, order[3])
            forward_chunk(h_copy, order[3])

        @pl.when(side == 1)
        def _():
            forward_diag(chunk)
            await_pair(chunk, ((5, twin(yn)), (6, twin(diag))))

        load.start()

        @pl.when(i >= 2)
        def _():
            for copy in tile_copies(i - 2)[4]:
                copy.wait()

        group = pl.ds(start, half)
        stores[0].start()
        for n in range(0, 2 * hidden, 512):
            gu[:, n : n + 512] = jnp.dot(
                h_all[chunk, group].reshape(tile, width), w_in_ref[:, n : n + 512], preferred_element_type=f32
            )
        piece = gu[:, slab : slab + 128]
        logits = piece + pltpu.roll(piece, 128 - experts, 1) + pltpu.roll(piece, 128 - 2 * experts, 1)
        is_logit = (lanes >= lane0) & (lanes < lane0 + experts)
        logits = jnp.where(is_logit, logits, -1e30)
        exps = jnp.exp(logits - jnp.max(logits, axis=-1, keepdims=True))
        probs = exps / jnp.sum(exps, axis=-1, keepdims=True)
        here = (lanes == lane0 + ep).astype(f32)
        kept = kept_ref[chunk, group].reshape(tile, 128).astype(f32)
        prob_here = jnp.sum(probs * here * kept, axis=-1, keepdims=True)
        prob_lanes[...] = jnp.broadcast_to(prob_here, (tile, 128))
        diff_lanes[...] = here - probs
        load.wait()
        act_grad[...] = lax.dot_general(
            cot_tile[...].reshape(tile, width), w_out_ref[...], (((1,), (1,)), ((), ())), preferred_element_type=f32
        )
        strip = 64

        def strips(r, _):
            at = pl.ds(pl.multiple_of(r * strip, strip), strip)
            gate_here = prob_lanes[at, :]
            pair_sum = jnp.zeros((strip, 128), f32)
            per = rows // strip
            block, inner = lax.div(r, per), pl.ds(pl.multiple_of(lax.rem(r, per) * strip, strip), strip)
            for n in range(0, hidden, 128):
                gate = gu[at, n : n + 128]
                up_val = gu[at, hidden + n : hidden + n + 128]
                grad = act_grad[at, n : n + 128]
                if n + 128 <= routed:
                    scale = gate_here
                elif n >= routed:
                    scale = None
                else:
                    scale = jnp.where(lanes < routed - n, gate_here, 1.0)
                sig = jax.nn.sigmoid(gate)
                silu = gate * sig
                act = silu * up_val
                if n < routed:
                    both = act * grad
                    if n + 128 > routed:
                        both = jnp.where(lanes < routed - n, both, 0.0)
                    pair_sum = pair_sum + both
                    act = act * scale
                    grad = grad * scale
                gated_tile[slot, block, inner, n : n + 128] = act.astype(bf16)
                grads_tile[slot, block, inner, n : n + 128] = (
                    grad * up_val * (sig * (1.0 + gate * (1.0 - sig)))
                ).astype(bf16)
                grads_tile[slot, block, inner, hidden + n : hidden + n + 128] = (grad * silu).astype(bf16)
            pair_lanes[at, :] = pair_sum
            return 0

        lax.fori_loop(0, tile // strip, strips, 0)
        pair_grad = jnp.sum(pair_lanes[...], axis=-1, keepdims=True)
        logit_grad = pair_grad * prob_lanes[...] * diff_lanes[...]
        logit_grad = logit_grad + pltpu.roll(logit_grad, experts, 1) + pltpu.roll(logit_grad, 2 * experts, 1)
        old = grads_tile[slot, :, :, slab : slab + 128].reshape(tile, 128)
        grads_tile[slot, :, :, slab : slab + 128] = (
            jnp.where(lanes >= lane0, logit_grad.astype(bf16), old).reshape(half, rows, 128)
        )
        for n in range(0, width, 512):
            rows_tile[slot, :, :, n : n + 512] = (
                lax.dot_general(
                    grads_tile[slot].reshape(tile, 2 * hidden), w_in_ref[n : n + 512, :], (((1,), (1,)), ((), ())),
                    preferred_element_type=f32,
                ).astype(bf16).reshape(half, rows, 512)
            )
            out_tile[slot, :, :, n : n + 512] = (
                jnp.dot(gated_tile[slot].reshape(tile, hidden), w_out_ref[:, n : n + 512], preferred_element_type=f32)
                .astype(bf16).reshape(half, rows, 512)
            )
        for copy in stores[1:]:
            copy.start()
        return 0

    lax.fori_loop(0, 2 * depth, step, 0)
    for i in (2 * depth - 2, 2 * depth - 1):
        for copy in tile_copies(i)[4]:
            copy.wait()
    for k in range(1, depth):
        z_copy(k).wait_send()

    def drain(k, _):
        chunk = order_at(k)

        @pl.when(goes_up(chunk))
        def _():
            along(chunk, 0, up).wait_send()

        @pl.when(goes_down(chunk))
        def _():
            along(chunk, 1, down).wait_send()

        for slot in range(7):
            h_copy(ep, chunk, slot, pair).wait_send()
            c_copy(ep, chunk, slot, pair).wait_send()
        return 0

    lax.fori_loop(0, depth, drain, 0)


def experts_call(attn_part, inputs, gain, cotangent, kept, w_in, w_out, blocks, depth, routed, shared, experts, cid):
    f32, bf16 = jnp.float32, jnp.bfloat16
    tokens, width = inputs.shape
    rows = tokens // depth
    hidden = w_out.shape[0]
    half = blocks // 2
    tile = half * rows
    dma = pltpu.SemaphoreType.DMA
    vmem, anywhere = pl.BlockSpec(memory_space=pltpu.VMEM), pl.BlockSpec(memory_space=pl.ANY)

    def units(size):
        return jax.ShapeDtypeStruct((depth, blocks, rows, size), bf16)

    return pl.pallas_call(
        functools.partial(experts_kernel, depth, blocks, routed, shared, experts),
        out_shape=(
            jax.ShapeDtypeStruct((rows, width), f32),
            units(width), units(width), units(2 * hidden), units(hidden),
            jax.ShapeDtypeStruct((blocks, depth, rows, width), bf16), units(width),
        ),
        in_specs=[vmem, anywhere, vmem, anywhere, vmem, vmem, vmem],
        out_specs=(vmem,) + (anywhere,) * 6,
        scratch_shapes=[
            pltpu.VMEM((depth, blocks, rows, width), bf16),
            pltpu.VMEM((depth - 1, rows, width), bf16),
            pltpu.VMEM((rows, width), bf16),
            pltpu.VMEM((half, rows, width), bf16),
            pltpu.VMEM((tile, 2 * hidden), f32),
            pltpu.VMEM((tile, hidden), f32),
            pltpu.VMEM((tile, 128), f32),
            pltpu.VMEM((tile, 128), f32),
            pltpu.VMEM((tile, 128), f32),
            pltpu.VMEM((2, half, rows, 2 * hidden), bf16),
            pltpu.VMEM((2, half, rows, hidden), bf16),
            pltpu.VMEM((2, half, rows, width), bf16),
            pltpu.VMEM((2, half, rows, width), bf16),
            dma((depth + 1,)),
            dma((depth - 1,)), dma((depth - 1,)),
            dma((depth, 2)), dma((depth,)),
            dma((depth, 7)), dma((depth, 7)),
            dma((depth, 7)), dma((depth, 7)),
            dma, dma((2, 5)),
        ],
        compiler_params=pltpu.CompilerParams(collective_id=cid, has_side_effects=True, vmem_limit_bytes=60 << 20),
    )(attn_part, inputs, gain.reshape(1, width), cotangent, kept, w_in, w_out)


def sum_kernel(
    depth, routed, shared, experts, part_ref, layer_ref, h_ref, grads_ref, gated_ref, cot_ref, middle_ref, gain_ref,
    middle_grad, branch, gain_part, expert_in, expert_out, s_in, s_out, router, layer_sum, landed,
    in_grad, out_grad, e_stage, s_stage,
    load, store, got_pair, got_first, got_second, got_z, keep, h_tile, grads_tile, gated_tile, cot_tile,
    own_cot, load_sem, store_sem, own_sem, lps, lpr, ps, pr, fs, fr, ss, sr, zs, zr, tile_sem, e_sem, s_sem, o_sem,
):
    f32 = jnp.float32
    rows = part_ref.shape[2]
    ep, tp = lax.axis_index("ep"), lax.axis_index("tp")
    pair, xn, yn = plane_partners(ep)
    parity = lax.rem(ep, 2)
    first = jnp.where(parity == 0, xn, yn)
    second = jnp.where(parity == 0, yn, xn)
    diag = xn + yn - ep
    blocks = (first, diag, ep, second)
    pair_slot = (3, 1, 2, 0)
    greet([(pair, tp), (xn, tp), (yn, tp)] + [(ep, lax.rem(tp + k, depth)) for k in range(1, depth)])
    steps = [(k + 1) % depth for k in range(depth)]

    def chunk_of(i):
        return lax.rem(tp + steps[i], depth)

    def pair_copy(i, slot):
        src = part_ref.at[chunk_of(i), blocks[slot] + pair - ep]
        to = pair_slot[slot]
        return remote(src, got_pair.at[i, to], ps.at[i, slot], pr.at[i, to], (pair, tp))

    def pair_wait(i, slot):
        return remote(part_ref.at[0, 0], got_pair.at[i, slot], ps.at[i, slot], pr.at[i, slot], (pair, tp))

    def own_load(i, slot):
        return pltpu.make_async_copy(part_ref.at[chunk_of(i), blocks[slot]], load.at[slot], load_sem.at[slot])

    def first_copy(i, slot):
        return remote(got_pair.at[i, slot], got_first.at[i, slot], fs.at[i, slot], fr.at[i, slot], (first, tp))

    def second_copy(i):
        return remote(got_pair.at[i, 3], got_second.at[i], ss.at[i], sr.at[i], (second, tp))

    def z_copy(i):
        k = steps[i]
        return remote(got_pair.at[i, 2], got_z.at[k - 1], zs.at[k - 1], zr.at[k - 1], (ep, lax.rem(tp + k, depth)))

    def layer_pair(i, slot):
        src = layer_ref.at[blocks[slot] + pair - ep, chunk_of(i)]
        to = pair_slot[slot]
        return remote(src, landed.at[i, to], lps.at[i, slot], lpr.at[i, to], (pair, tp))

    def layer_wait(i, slot):
        return remote(layer_ref.at[0, 0], landed.at[i, slot], lps.at[i, slot], lpr.at[i, slot], (pair, tp))

    def layer_loads(i, slot):
        at = 2 * (slot % 2)
        return (
            pltpu.make_async_copy(layer_ref.at[blocks[slot], chunk_of(i)], load.at[at], load_sem.at[at]),
            pltpu.make_async_copy(landed.at[i, slot], load.at[at + 1], load_sem.at[at + 1]),
        )

    def layer_store(i, slot):
        return pltpu.make_async_copy(store.at[slot % 2], layer_sum.at[i, slot], store_sem.at[slot % 2])

    def layer_stage(i):
        def start(slot):
            layer_wait(i, slot).wait_recv()
            for copy in layer_loads(i, slot):
                copy.start()

        start(0)
        for slot in range(4):
            if slot < 3:
                start(slot + 1)
            for copy in layer_loads(i, slot):
                copy.wait()
            if slot >= 2:
                layer_store(i, slot - 2).wait()
            at = 2 * (slot % 2)
            add_rows(store.at[slot % 2], load.at[at], load.at[at + 1])
            layer_store(i, slot).start()
        layer_store(i, 2).wait()
        layer_store(i, 3).wait()

    for i in range(depth):
        for slot in (3, 1, 2, 0):
            pair_copy(i, slot).start()
    for i in range(depth):
        for slot in (3, 1, 2, 0):
            layer_pair(i, slot).start()

    def tile_loads(c):
        return [
            pltpu.make_async_copy(src.at[c], dst, tile_sem.at[n])
            for n, (src, dst) in enumerate(
                ((h_ref, h_tile), (grads_ref, grads_tile), (gated_ref, gated_tile), (cot_ref, cot_tile))
            )
        ]

    def stage_a(i):
        for slot in range(4):
            own_load(i, slot).start()
        for slot in range(4):
            pair_wait(i, slot).wait_recv()
            own_load(i, slot).wait()
            add_rows(got_pair.at[i, slot], got_pair.at[i, slot], load.at[slot])
            if slot < 2:
                first_copy(i, slot).start()

    def stage_b(i):
        first_copy(i, 1).wait_recv()
        add_rows(got_pair.at[i, 3], got_pair.at[i, 3], got_first.at[i, 1])
        second_copy(i).start()
        first_copy(i, 0).wait_recv()
        add_rows(got_pair.at[i, 2], got_pair.at[i, 2], got_first.at[i, 0])

    def stage_c(i):
        second_copy(i).wait_recv()
        if i < depth - 1:
            add_rows(got_pair.at[i, 2], got_pair.at[i, 2], got_second.at[i])
            z_copy(i).start()
        else:
            add_rows(keep, got_pair.at[i, 2], got_second.at[i])

    count = h_tile.shape[0] * rows
    width = h_tile.shape[2]
    hidden = gated_tile.shape[2]

    blocks_all = h_tile.shape[0]
    lanes = lax.broadcasted_iota(jnp.int32, (1, 128), 1)
    slab = routed // 128 * 128
    shift = 128 - (routed - slab)
    router_shift = (ROPE - (routed + shared) % 128) % 128

    def expert_out_copy():
        return pltpu.make_async_copy(out_grad.at[pl.ds(0, routed)], expert_out.at[0], o_sem)

    def place_copies(m):
        side = lax.rem(m, 2)
        at = pl.ds(pl.multiple_of(m * 512, 512), 512)
        per = 512 // (width // blocks_all)
        return (
            pltpu.make_async_copy(e_stage.at[side], expert_in.at[0, :, at], e_sem.at[side]),
            pltpu.make_async_copy(s_stage.at[side], s_in.at[pl.ds(m * per, per)], s_sem.at[side]),
        )

    def place(m, found):
        side = lax.rem(m, 2)

        @pl.when(m >= 2)
        def _():
            for copy in place_copies(m - 2):
                copy.wait()

        wide = width // blocks_all
        for g in range(2):
            e_stage[side, g] = found[:, g * hidden : g * hidden + routed]
            first_slab = found[:, g * hidden + slab : g * hidden + slab + 128]
            second_slab = found[:, g * hidden + slab + 128 : g * hidden + slab + 256]
            units = jnp.where(lanes < shift, pltpu.roll(first_slab, shift, 1), pltpu.roll(second_slab, shift, 1))
            s_stage[side, :, g] = units.astype(s_stage.dtype).reshape(512 // wide, wide, 128)
        last_slab = pltpu.roll(found[:, (routed + shared) // 128 * 128 : (routed + shared) // 128 * 128 + 128], router_shift, 1)
        inside = (lanes >= ROPE) & (lanes < ROPE + experts)
        router[pl.ds(pl.multiple_of(m * 512, 512), 512), :] = jnp.where(inside, last_slab, 0.0).astype(router.dtype)
        for copy in place_copies(m):
            copy.start()

    def weights(c):
        for copy in tile_loads(c):
            copy.wait()
        turned = (((0,), (0,)), ((), ()))

        last = c == depth - 1

        def in_part(m, _):
            at = pl.ds(pl.multiple_of(m * 512, 512), 512)
            found = lax.dot_general(
                h_tile[:, :, at].reshape(count, 512), grads_tile[...].reshape(count, 2 * hidden), turned,
                preferred_element_type=f32,
            )
            if c > 0:
                found = in_grad[at, :] + found
            if last:
                place(m, found)
            else:
                in_grad[at, :] = found
            return 0

        lax.fori_loop(0, width // 512, in_part, 0)

        def out_part(m, _):
            at = pl.ds(pl.multiple_of(m * 512, 512), 512)
            found = lax.dot_general(
                gated_tile[...].reshape(count, hidden), cot_tile[:, :, at].reshape(count, 512), turned,
                preferred_element_type=f32,
            )
            out_grad[:, at] = found if c == 0 else out_grad[:, at] + found
            return 0

        lax.fori_loop(0, width // 512, out_part, 0)
        if last:
            expert_out_copy().start()
            wide = width // blocks_all
            for b in range(blocks_all):
                s_out[b] = out_grad[routed : routed + s_out.shape[1], b * wide : (b + 1) * wide].astype(s_out.dtype)
        if c + 1 < depth:
            for copy in tile_loads(c + 1):
                copy.start()

    own_copy = pltpu.make_async_copy(cot_ref.at[tp, ep], own_cot, own_sem)
    own_copy.start()
    for copy in tile_loads(0):
        copy.start()
    for t in range(depth + 2):
        if t < depth:
            stage_a(t)
        if 0 <= t - 1 < depth:
            stage_b(t - 1)
        if 0 <= t - 2 < depth:
            stage_c(t - 2)
        if t < depth:
            weights(t)
            layer_stage(t)
    for i in range(depth - 1):
        z_copy(i).wait_recv()
    own_copy.wait()

    def total(r, gain_sum):
        at = pl.ds(pl.multiple_of(r * 16, 16), 16)
        u = keep[at, :]
        for k in range(depth - 1):
            u = u + got_z[k, at, :].astype(f32)
        v = middle_ref[at, :]
        inverse = lax.rsqrt(jnp.mean(v * v, axis=-1, keepdims=True) + EPSILON)
        v_hat = v * inverse
        gain_sum = gain_sum + (u * v_hat)[:8] + (u * v_hat)[8:]
        s = u * gain_ref[...]
        back = inverse * (s - v_hat * jnp.mean(s * v_hat, axis=-1, keepdims=True))
        found = own_cot[at, :].astype(f32) + back
        middle_grad[at, :] = found
        branch[at, :] = found.astype(branch.dtype)
        return gain_sum

    gain_part[...] = lax.fori_loop(0, rows // 16, total, jnp.zeros((8, width), f32))
    expert_out_copy().wait()
    for m in (width // 512 - 2, width // 512 - 1):
        for copy in place_copies(m):
            copy.wait()
    for i in range(depth):
        for slot in range(4):
            pair_copy(i, slot).wait_send()
            layer_pair(i, slot).wait_send()
        for slot in range(2):
            first_copy(i, slot).wait_send()
        second_copy(i).wait_send()
        if i < depth - 1:
            z_copy(i).wait_send()


def sum_call(part, layer, h_all, grads, gated, cot_all, middle, gain, routed, shared, experts, cid):
    f32, bf16 = jnp.float32, jnp.bfloat16
    depth, blocks, rows, width = part.shape
    hidden = gated.shape[3]
    dma = pltpu.SemaphoreType.DMA
    vmem, anywhere = pl.BlockSpec(memory_space=pltpu.VMEM), pl.BlockSpec(memory_space=pl.ANY)
    return pl.pallas_call(
        functools.partial(sum_kernel, depth, routed, shared, experts),
        out_shape=(
            jax.ShapeDtypeStruct((rows, width), f32),
            jax.ShapeDtypeStruct((rows, width), bf16),
            jax.ShapeDtypeStruct((8, width), f32),
            jax.ShapeDtypeStruct((1, 2, width, routed), f32),
            jax.ShapeDtypeStruct((1, routed, width), f32),
            jax.ShapeDtypeStruct((blocks, 2, width // blocks, 128), bf16),
            jax.ShapeDtypeStruct((blocks, -(-shared // 16) * 16, width // blocks), bf16),
            jax.ShapeDtypeStruct((width, 128), bf16),
            jax.ShapeDtypeStruct((depth, 4, rows, width), bf16),
            jax.ShapeDtypeStruct((depth, 4, rows, width), bf16),
        ),
        in_specs=[anywhere] * 6 + [vmem, vmem],
        out_specs=(vmem,) * 3 + (anywhere,) * 3 + (vmem,) * 2 + (anywhere,) * 2,
        scratch_shapes=[
            pltpu.VMEM((width, 2 * hidden), f32),
            pltpu.VMEM((hidden, width), f32),
            pltpu.VMEM((2, 2, 512, routed), f32),
            pltpu.VMEM((2, 512 // (width // blocks), 2, width // blocks, 128), bf16),
            pltpu.VMEM((4, rows, width), bf16),
            pltpu.VMEM((2, rows, width), bf16),
            pltpu.VMEM((depth, 4, rows, width), bf16),
            pltpu.VMEM((depth, 2, rows, width), bf16),
            pltpu.VMEM((depth, rows, width), bf16),
            pltpu.VMEM((depth - 1, rows, width), bf16),
            pltpu.VMEM((rows, width), f32),
            pltpu.VMEM((blocks, rows, width), bf16),
            pltpu.VMEM((blocks, rows, 2 * hidden), bf16),
            pltpu.VMEM((blocks, rows, hidden), bf16),
            pltpu.VMEM((blocks, rows, width), bf16),
            pltpu.VMEM((rows, width), bf16),
            dma((4,)), dma((2,)), dma, dma((depth, 4)), dma((depth, 4)), dma((depth, 4)), dma((depth, 4)), dma((depth, 2)), dma((depth, 2)),
            dma((depth,)), dma((depth,)), dma((depth - 1,)), dma((depth - 1,)), dma((4,)), dma((2,)), dma((2,)), dma,
        ],
        compiler_params=pltpu.CompilerParams(collective_id=cid, has_side_effects=True, vmem_limit_bytes=62 << 20),
    )(part, layer, h_all, grads, gated, cot_all, middle, gain.reshape(1, width))


def line_gather(ref, own, send_sem, recv_sem, ep, tp, depth):
    up, down = jnp.minimum(tp + 1, depth - 1), jnp.maximum(tp - 1, 0)
    order = line_order(tp)

    def along(k, way, to):
        chunk = order[k]
        src = own if k == 0 else ref.at[chunk]
        return remote(src, ref.at[chunk], send_sem.at[chunk, way], recv_sem.at[chunk], (ep, to))

    def each_way(k, act):
        @pl.when((order[k] <= tp) & (tp < depth - 1))
        def _():
            act(along(k, 0, up))

        @pl.when((order[k] >= tp) & (tp > 0))
        def _():
            act(along(k, 1, down))

    def pass_on(k):
        each_way(k, lambda copy: copy.start())

    def await_chunk(k):
        along(k, 0, up).wait_recv()

    def drain():
        for k in range(depth):
            each_way(k, lambda copy: copy.wait_send())

    return pass_on, await_chunk, drain


def tail_kernel(
    depth, heads, shared,
    branch_ref, middle_grad_ref, middle_ref, part_ref, router_ref, gain_part_ref, inputs_ref, s_in, s_out,
    w_output, w_query, w_latent, w_up, hidden_ref, qn_ref, qr_ref, kv_ref, kr_ref, attended, latent_in, compressed,
    tables, gain_latent, gain_attn,
    block_ref, grad_in_ref, gains_ref, query_ref, output_ref, up_ref, latent_ref, shared_in, shared_out, w_all,
    branch, held_rows, got_first, got_second, got_z, hidden_part, got_h, row_sum,
    d_out, d_kr, q_grad, kv_grad, l_grad, u_grad, w_stage, w_pair, w_first, w_second, w_z, latent_part, s_in_land, s_out_land, resid, own_grad, own_block, gains,
    load_sem, fs, fr, ss, sr, zs, zr, bs, br, hs, hr, gs, gr, os, orr,
    wps, wpr, wfs, wfr, wss, wsr, wzs, wzr, as_, ar, misc_sem, stage_sem, sis, sir, sos, sor,
):
    f32, bf16 = jnp.float32, jnp.bfloat16
    ep, tp = lax.axis_index("ep"), lax.axis_index("tp")
    pair, xn, yn = plane_partners(ep)
    parity = lax.rem(ep, 2)
    first = jnp.where(parity == 0, xn, yn)
    second = jnp.where(parity == 0, yn, xn)
    diag = xn + yn - ep
    blocks = (first, diag, ep, second)
    pair_slot = (3, 1, 2, 0)
    rows, width = middle_ref.shape
    tokens = hidden_ref.shape[0]
    rank = compressed.shape[1]
    q_cols, l_cols = q_grad.shape[1], l_grad.shape[1]
    o_rows = attended.shape[1]
    count = w_all.shape[0]
    w_rows = w_all.shape[1]
    o_cols = width // count
    u_rows = rank // count
    u_cols = w_up.shape[1]
    o_start = q_cols + l_cols
    u_start = o_start + o_rows * o_cols // w_rows
    u_wide = u_rows * u_cols // w_rows
    order = line_order(tp)
    score_scale = (NOPE + ROPE) ** (-0.5)
    plane = [ep + sum(((pair, xn, yn)[n] - ep) * (m >> n & 1) for n in range(3)) for m in range(8)]
    greet([(to, tp) for to in plane[1:]] + [(ep, lax.rem(tp + k, depth)) for k in range(1, depth)])

    branch_on, branch_wait, branch_drain = line_gather(branch, branch_ref, bs, br, ep, tp, depth)
    grad_on, grad_wait, grad_drain = line_gather(grad_in_ref, own_grad, gs, gr, ep, tp, depth)
    block_on, block_wait, block_drain = line_gather(block_ref, own_block, os, orr, ep, tp, depth)

    steps = [(k + 1) % depth for k in range(depth)]

    def chunk_of(i):
        return lax.rem(tp + steps[i], depth)

    def held_load(i, slot):
        return pltpu.make_async_copy(part_ref.at[i, slot], held_rows.at[i, slot - 2], load_sem.at[i, slot - 2])

    def first_copy(i, slot):
        return remote(part_ref.at[i, slot], got_first.at[i, slot], fs.at[i, slot], fr.at[i, slot], (first, tp))

    def second_copy(i):
        return remote(held_rows.at[i, 1], got_second.at[i], ss.at[i], sr.at[i], (second, tp))

    def z_copy(i):
        k = steps[i]
        src = held_rows.at[i, 0]
        return remote(src, got_z.at[k - 1], zs.at[k - 1], zr.at[k - 1], (ep, lax.rem(tp + k, depth)))

    def stage_b(i):
        held_load(i, 3).wait()
        first_copy(i, 1).wait_recv()
        add_rows(held_rows.at[i, 1], held_rows.at[i, 1], got_first.at[i, 1])
        second_copy(i).start()
        held_load(i, 2).wait()
        first_copy(i, 0).wait_recv()
        add_rows(held_rows.at[i, 0], held_rows.at[i, 0], got_first.at[i, 0])

    def stage_c(i):
        second_copy(i).wait_recv()
        if i < depth - 1:
            add_rows(held_rows.at[i, 0], held_rows.at[i, 0], got_second.at[i])
            z_copy(i).start()
        else:
            add_rows(row_sum, held_rows.at[i, 0], got_second.at[i])

    def w_pair_copy(slot):
        to = pair_slot[slot]
        return remote(w_all.at[blocks[slot] + pair - ep], w_pair.at[to], wps.at[slot], wpr.at[to], (pair, tp))

    def w_pair_wait(slot):
        return remote(w_all.at[0], w_pair.at[slot], wps.at[slot], wpr.at[slot], (pair, tp))

    def w_first_copy(slot):
        return remote(w_pair.at[slot], w_first.at[slot], wfs.at[slot], wfr.at[slot], (first, tp))

    def w_second_copy():
        return remote(w_pair.at[3], w_second, wss, wsr, (second, tp))

    def w_load(slot):
        return pltpu.make_async_copy(w_all.at[blocks[slot]], w_stage.at[slot % 2], stage_sem.at[slot % 2])

    def w_stage_a():
        for slot in range(4):
            if slot < 3:
                w_load(slot + 1).start()
            w_pair_wait(slot).wait_recv()
            w_load(slot).wait()
            add_rows(w_pair.at[slot], w_pair.at[slot], w_stage.at[slot % 2])
            if slot < 2:
                w_first_copy(slot).start()

    def w_stage_b():
        w_first_copy(1).wait_recv()
        add_rows(w_pair.at[3], w_pair.at[3], w_first.at[1])
        w_second_copy().start()
        w_first_copy(0).wait_recv()
        add_rows(w_pair.at[2], w_pair.at[2], w_first.at[0])

    def w_stage_c():
        w_second_copy().wait_recv()

        def total(cols, at=slice(None)):
            return w_pair[2, at, cols].astype(f32) + w_second[at, cols].astype(f32)

        query_ref[...] = total(slice(0, q_cols))
        latent_part[...] = total(slice(q_cols, o_start))
        for n in range(o_rows // w_rows):
            output_ref[n * w_rows : (n + 1) * w_rows, :] = total(slice(o_start + n * o_cols, o_start + (n + 1) * o_cols))
        for n in range(u_cols // u_wide):
            up_ref[:, n * u_wide : (n + 1) * u_wide] = total(
                slice(u_start, u_start + u_wide), slice(n * u_rows, (n + 1) * u_rows)
            )

    def shared_copies(m):
        to = plane[m]
        return (
            remote(s_in.at[to], s_in_land.at[ep], sis.at[m], sir.at[m], (to, tp)),
            remote(s_out.at[to], s_out_land.at[ep], sos.at[m], sor.at[m], (to, tp)),
        )

    def shared_own():
        return (
            pltpu.make_async_copy(s_in.at[ep], s_in_land.at[ep], sis.at[0]),
            pltpu.make_async_copy(s_out.at[ep], s_out_land.at[ep], sos.at[0]),
        )

    def shared_place():
        for m in range(1, 8):
            for copy in shared_copies(m):
                copy.wait_recv()
        for copy in shared_own():
            copy.wait()
        for n in range(s_in_land.shape[0]):
            at = slice(n * shared, (n + 1) * shared)
            for g in range(2):
                shared_in[g, :, at] = s_in_land[n, g].astype(f32)[:, :shared]
            shared_out[at, :] = s_out_land[n].astype(f32)[:shared]

    def h_copy(k):
        to = lax.rem(tp + k, depth)
        return remote(hidden_part.at[to], got_h.at[k - 1], hs.at[k - 1], hr.at[k - 1], (ep, to))

    branch_on(0)
    branch[tp] = branch_ref[...]
    for i in range(depth):
        first_copy(i, 1).start()
        first_copy(i, 0).start()
        held_load(i, 3).start()
        held_load(i, 2).start()
    own_rows = pl.ds(pl.multiple_of(tp * rows, rows), rows)
    resid_copy = pltpu.make_async_copy(inputs_ref.at[own_rows], resid, misc_sem.at[0])
    resid_copy.start()

    branch_wait(1)
    branch_on(1)
    stage_b(0)
    branch_wait(2)
    branch_on(2)
    stage_c(0)
    branch_wait(3)
    branch_on(3)

    turned, across = (((0,), (0,)), ((), ())), (((1,), (1,)), ((), ()))

    def dot(a, b, dims=(((1,), (0,)), ((), ()))):
        return lax.dot_general(a, b, dims, preferred_element_type=f32)

    for c in range(depth):
        d_out[c * rows : (c + 1) * rows, :] = dot(branch[c], w_output[...], across).astype(bf16)

    lanes = lax.broadcasted_iota(jnp.int32, (1, 128), 1)
    halves = tokens // BLOCK

    def head(h, even):
        mine = (lanes < 64) if even else (lanes >= 64)
        at_q = pl.ds(pl.multiple_of(h * NOPE, 128), 128)
        at_r = pl.ds(pl.multiple_of(lax.div(h, 2) * 128, 128), 128)
        at_k = pl.ds(pl.multiple_of(h * 256, 128), 128)
        at_v = pl.ds(pl.multiple_of(h * 256 + 128, 128), 128)
        kv_sum = [None, None]
        for b in reversed(range(halves)):
            own = slice(b * BLOCK, (b + 1) * BLOCK)
            keys = slice(0, (b + 1) * BLOCK)
            qn, qr = qn_ref[own, at_q], qr_ref[own, at_r]
            kn, kr = kv_ref[keys, at_k], kr_ref[0 if even else 1, keys, :]
            scores = (dot(qn, kn, across) + dot(qr, kr, across)) * score_scale
            exps = jnp.exp(scores - jnp.max(scores, axis=-1, keepdims=True))
            probs = exps / jnp.sum(exps, axis=-1, keepdims=True)
            grad = d_out[own, at_q]
            prob_part = dot(grad, kv_ref[keys, at_v], across)
            score_grad = (probs * (prob_part - jnp.sum(probs * prob_part, axis=-1, keepdims=True))).astype(bf16)
            found = (dot(score_grad, qn, turned) * score_scale, dot(probs.astype(bf16), grad, turned))
            r_grad = jnp.where(mine, dot(score_grad, qr, turned) * score_scale, 0.0)
            for n, at in enumerate((at_k, at_v)):
                if b < halves - 1:
                    kv_sum[n] = kv_sum[n] + found[n]
                else:
                    kv_sum[n] = found[n]
                kv_grad[own, at] = kv_sum[n][b * BLOCK :].astype(bf16)
                if b > 0:
                    kv_sum[n] = kv_sum[n][: b * BLOCK]
            d_kr[keys, :] = d_kr[keys, :] + r_grad
            yield own, dot(score_grad, kn) * score_scale, dot(score_grad, kr) * score_scale

    d_kr[...] = jnp.zeros_like(d_kr)

    def head_pair(p, _):
        evens = list(head(2 * p, True))
        odds = list(head(2 * p + 1, False))
        at = [pl.ds(pl.multiple_of(p * (2 * (NOPE + ROPE)) + n, 128), 128) for n in (0, 128, 256)]
        for (own, even, even_rope), (_, odd, odd_rope) in zip(evens, odds):
            table = tuple(tables[n, own, :] for n in range(3))
            rope = turn(even_rope + odd_rope, table, -1.0)
            odd = pltpu.roll(odd, 64, 1)
            q_grad[own, at[0]] = even.astype(bf16)
            q_grad[own, at[1]] = jnp.where(lanes < 64, rope, odd).astype(bf16)
            q_grad[own, at[2]] = jnp.where(lanes < 64, odd, rope).astype(bf16)
        return 0

    lax.fori_loop(0, heads // 2, head_pair, 0)
    stage_b(1)

    latent_back = dot(kv_grad[...], w_up[...], across)
    held = compressed[...]
    inverse = lax.rsqrt(jnp.mean(held * held, axis=-1, keepdims=True) + EPSILON)
    normed = held * inverse
    gain_latent_part = jnp.sum(latent_back * normed, axis=0, keepdims=True)
    scaled = latent_back * gain_latent[...]
    l_grad[:, :rank] = (inverse * (scaled - normed * jnp.mean(scaled * normed, axis=-1, keepdims=True))).astype(bf16)
    rope = d_kr[...] + pltpu.roll(d_kr[...], 64, 1)
    rope = turn(rope, tuple(tables[n] for n in range(3)), -1.0)
    l_grad[:, rank:] = jnp.where(lanes < 64, rope, 0.0).astype(bf16)

    for n in range(0, width, 512):
        part = dot(q_grad[...], w_query[n : n + 512, :], across) + dot(l_grad[:, : rank + ROPE], w_latent[n : n + 512, :], across)
        hidden_part[:, :, n : n + 512] = part.astype(bf16).reshape(depth, rows, 512)
    for k in range(1, depth):
        h_copy(k).start()

    stage_c(1)
    stage_b(2)

    u_grad[...] = dot(latent_in[...], kv_grad[...], turned).astype(bf16)

    def w_store(b):
        slot = lax.rem(b, 2)
        return pltpu.make_async_copy(w_stage.at[slot], w_all.at[b], stage_sem.at[slot])

    def w_block(b, _):
        slot = lax.rem(b, 2)

        @pl.when(b >= 2)
        def _():
            w_store(b - 2).wait()

        at = pl.ds(pl.multiple_of(b * w_rows, 256), w_rows)
        own = hidden_ref[:, at]
        w_stage[slot, :, 0:q_cols] = dot(own, q_grad[...], turned).astype(bf16)
        found = dot(own, l_grad[...], turned)
        w_stage[slot, :, q_cols : q_cols + rank] = found[:, :rank].astype(bf16)
        w_stage[slot, :, q_cols + rank : o_start] = found[:, rank:].astype(bf16) + router_ref[at, :]
        cols = pl.ds(pl.multiple_of(b * o_cols, 256), o_cols)
        found = dot(attended[...], branch[:, :, cols].reshape(tokens, o_cols), turned)
        for n in range(o_rows // w_rows):
            w_stage[slot, :, o_start + n * o_cols : o_start + (n + 1) * o_cols] = (
                found[n * w_rows : (n + 1) * w_rows].astype(bf16)
            )
        u_at = pl.ds(pl.multiple_of(b * u_rows, u_rows), u_rows)
        for n in range(u_cols // u_wide):
            w_stage[slot, n * u_rows : (n + 1) * u_rows, u_start : u_start + u_wide] = (
                u_grad[u_at, n * u_wide : (n + 1) * u_wide]
            )
        w_store(b).start()
        return 0

    lax.fori_loop(0, count, w_block, 0)
    w_store(count - 2).wait()
    w_store(count - 1).wait()
    for slot in (3, 1, 2, 0):
        w_pair_copy(slot).start()
    for copy in shared_own():
        copy.start()
    for m in range(1, 8):
        for copy in shared_copies(m):
            copy.start()
    w_load(0).start()

    stage_c(2)
    stage_b(3)
    w_stage_a()

    resid_copy.wait()
    for k in range(1, depth):
        h_copy(k).wait_recv()

    def input_rows(r, gain_sum):
        at = pl.ds(pl.multiple_of(r * 16, 16), 16)
        u = hidden_part[tp, at, :].astype(f32)
        for k in range(depth - 1):
            u = u + got_h[k, at, :].astype(f32)
        v = resid[at, :].astype(f32)
        inv = lax.rsqrt(jnp.mean(v * v, axis=-1, keepdims=True) + EPSILON)
        v_hat = v * inv
        gain_sum = gain_sum + (u * v_hat)[:8] + (u * v_hat)[8:]
        s = u * gain_attn[...]
        back = inv * (s - v_hat * jnp.mean(s * v_hat, axis=-1, keepdims=True))
        own_grad[at, :] = (middle_grad_ref[at, :] + back).astype(bf16)
        return gain_sum

    gain_sum = lax.fori_loop(0, rows // 16, input_rows, jnp.zeros((8, width), f32))
    grad_on(0)
    own_grad_copy = pltpu.make_async_copy(own_grad, grad_in_ref.at[tp], misc_sem.at[1])
    own_grad_copy.start()
    stage_c(3)
    for i in range(depth - 1):
        z_copy(i).wait_recv()

    def block_rows(r, _):
        at = pl.ds(pl.multiple_of(r * 16, 16), 16)
        value = middle_ref[at, :] + row_sum[at, :]
        for k in range(depth - 1):
            value = value + got_z[k, at, :].astype(f32)
        own_block[at, :] = value.astype(bf16)
        return 0

    lax.fori_loop(0, rows // 16, block_rows, 0)
    block_on(0)
    own_block_copy = pltpu.make_async_copy(own_block, block_ref.at[tp], misc_sem.at[2])
    own_block_copy.start()
    w_stage_b()

    gains[0] = jnp.zeros_like(gains[0])
    gains[0, 0:1, :] = jnp.sum(gain_sum, axis=0, keepdims=True)
    gains[0, 1:2, :] = jnp.sum(gain_part_ref[...], axis=0, keepdims=True)
    gains[0, 2:3, 0:rank] = gain_latent_part
    flip_1 = tp + 1 - 2 * lax.rem(tp, 2)
    flip_2 = tp + 2 - 4 * lax.div(tp, 2)
    partners = ((pair, tp), (xn, tp), (yn, tp), (ep, flip_1), (ep, flip_2))

    def gain_copy(n):
        return remote(gains.at[2 * n], gains.at[2 * n + 1], as_.at[n], ar.at[n], partners[n])

    def gain_step(n):
        gain_copy(n).wait_recv()
        total = gains[2 * n] + gains[2 * n + 1]
        if n + 1 < len(partners):
            gains[2 * n + 2] = total
            gain_copy(n + 1).start()
        else:
            gains_ref[...] = total

    gain_copy(0).start()
    gain_step(0)
    gain_step(1)
    w_stage_c()
    w_part = w_rows // depth

    def w_z_copy(k):
        to = lax.rem(tp + k, depth)
        src = w_pair.at[1, pl.ds(pl.multiple_of(to * w_part, w_part), w_part), pl.ds(q_cols, l_cols)]
        return remote(src, w_z.at[k - 1], wzs.at[k - 1], wzr.at[k - 1], (ep, to))

    w_first_copy(1).wait_send()
    w_pair[1, :, q_cols:o_start] = latent_part[...].astype(bf16)
    for k in range(1, depth):
        w_z_copy(k).start()
    gain_step(2)
    grad_wait(1)
    grad_on(1)
    block_wait(1)
    block_on(1)
    gain_step(3)
    gain_step(4)
    for k in range(1, depth):
        w_z_copy(k).wait_recv()
    own = pl.ds(pl.multiple_of(tp * w_part, w_part), w_part)
    total = latent_part[own, :]
    for k in range(depth - 1):
        total = total + w_z[k].astype(f32)
    latent_ref[...] = total
    shared_place()
    for k in range(2, depth):
        grad_wait(k)
        grad_on(k)
        block_wait(k)
        block_on(k)

    own_grad_copy.wait()
    own_block_copy.wait()
    branch_drain()
    grad_drain()
    block_drain()
    for i in range(depth):
        for slot in range(2):
            first_copy(i, slot).wait_send()
        second_copy(i).wait_send()
        if i < depth - 1:
            z_copy(i).wait_send()
    for slot in range(4):
        w_pair_copy(slot).wait_send()
    w_first_copy(0).wait_send()
    w_second_copy().wait_send()
    for k in range(1, depth):
        h_copy(k).wait_send()
        w_z_copy(k).wait_send()
    for n in range(len(partners)):
        gain_copy(n).wait_send()
    for m in range(1, 8):
        for copy in shared_copies(m):
            copy.wait_send()


def tail_call(
    branch, middle_grad, middle, out_part, router, gain_part, inputs, s_in, s_out, w_output, w_query, w_latent, w_up,
    hidden, qn, qr, kv, kr, attended, latent_in, compressed, tables, gain_latent, gain_attn,
    heads, shared, cid,
):
    f32, bf16 = jnp.float32, jnp.bfloat16
    depth, _, rows, width = out_part.shape
    tokens = hidden.shape[0]
    blocks = s_in.shape[0]
    rank = compressed.shape[1]
    q_cols, l_cols = w_query.shape[1], rank + 128
    w_rows = width // blocks
    w_cols = q_cols + l_cols + w_output.shape[0] + rank * w_up.shape[1] // width
    dma = pltpu.SemaphoreType.DMA
    vmem, anywhere = pl.BlockSpec(memory_space=pltpu.VMEM), pl.BlockSpec(memory_space=pl.ANY)
    return pl.pallas_call(
        functools.partial(tail_kernel, depth, heads, shared),
        out_shape=(
            jax.ShapeDtypeStruct((depth, rows, width), bf16),
            jax.ShapeDtypeStruct((depth, rows, width), bf16),
            jax.ShapeDtypeStruct((8, width), f32),
            jax.ShapeDtypeStruct((w_rows, q_cols), f32),
            jax.ShapeDtypeStruct((w_output.shape[0], w_rows), f32),
            jax.ShapeDtypeStruct((rank // blocks, w_up.shape[1]), f32),
            jax.ShapeDtypeStruct((w_rows // depth, l_cols), f32),
            jax.ShapeDtypeStruct((2, w_rows, blocks * shared), f32),
            jax.ShapeDtypeStruct((blocks * shared, w_rows), f32),
            jax.ShapeDtypeStruct((blocks, w_rows, w_cols), bf16),
        ),
        in_specs=[vmem, vmem, vmem, anywhere, vmem, vmem, anywhere, anywhere, anywhere] + [vmem] * 15,
        out_specs=(anywhere, anywhere) + (vmem,) * 7 + (anywhere,),
        scratch_shapes=[
            pltpu.VMEM((depth, rows, width), bf16),
            pltpu.VMEM((depth, 2, rows, width), bf16),
            pltpu.VMEM((depth, 2, rows, width), bf16),
            pltpu.VMEM((depth, rows, width), bf16),
            pltpu.VMEM((depth - 1, rows, width), bf16),
            pltpu.VMEM((depth, rows, width), bf16),
            pltpu.VMEM((depth - 1, rows, width), bf16),
            pltpu.VMEM((rows, width), f32),
            pltpu.VMEM((tokens, heads * VDIM), bf16),
            pltpu.VMEM((tokens, 128), f32),
            pltpu.VMEM((tokens, q_cols), bf16),
            pltpu.VMEM((tokens, heads * (NOPE + VDIM)), bf16),
            pltpu.VMEM((tokens, l_cols), bf16),
            pltpu.VMEM((rank, heads * (NOPE + VDIM)), bf16),
            pltpu.VMEM((2, w_rows, w_cols), bf16),
            pltpu.VMEM((4, w_rows, w_cols), bf16),
            pltpu.VMEM((2, w_rows, w_cols), bf16),
            pltpu.VMEM((w_rows, w_cols), bf16),
            pltpu.VMEM((depth - 1, w_rows // depth, l_cols), bf16),
            pltpu.VMEM((w_rows, l_cols), f32),
            pltpu.VMEM(s_in.shape, bf16),
            pltpu.VMEM(s_out.shape, bf16),
            pltpu.VMEM((rows, width), bf16),
            pltpu.VMEM((rows, width), bf16),
            pltpu.VMEM((rows, width), bf16),
            pltpu.VMEM((10, 8, width), f32),
            dma((depth, 2)),
            dma((depth, 2)), dma((depth, 2)), dma((depth,)), dma((depth,)),
            dma((depth - 1,)), dma((depth - 1,)),
            dma((depth, 2)), dma((depth,)),
            dma((depth - 1,)), dma((depth - 1,)),
            dma((depth, 2)), dma((depth,)),
            dma((depth, 2)), dma((depth,)),
            dma((4,)), dma((4,)), dma((2,)), dma((2,)), dma, dma, dma((depth - 1,)), dma((depth - 1,)),
            dma((5,)), dma((5,)), dma((3,)), dma((2,)), dma((8,)), dma((8,)), dma((8,)), dma((8,)),
        ],
        compiler_params=pltpu.CompilerParams(collective_id=cid, has_side_effects=True, vmem_limit_bytes=63 << 20),
    )(
        branch, middle_grad, middle, out_part, router, gain_part, inputs, s_in, s_out, w_output, w_query, w_latent, w_up,
        hidden, qn, qr, kv, kr, attended, latent_in, compressed, tables,
        gain_latent.reshape(1, rank), gain_attn.reshape(1, width),
    )


def rope_tables(length):
    half = ROPE // 2
    inverse = np.exp(np.arange(half) * (-math.log(10000.0) / half))
    angle = np.arange(length)[:, None] * inverse[None, :]
    cosine, sine = np.cos(angle), np.sin(angle)
    zero = np.zeros_like(sine)
    parts = ([cosine] * 4, [-sine, zero] * 2, [zero, sine] * 2)
    return jnp.asarray(np.stack([np.concatenate(p, axis=1) for p in parts]), jnp.float32)


def padded_hidden(routed, shared):
    return -(-(routed + shared + 24) // 128) * 128


def split_wide(values):
    high = values.astype(jnp.bfloat16)
    rest = values - high.astype(jnp.float32)
    mid = rest.astype(jnp.bfloat16)
    low = (rest - mid.astype(jnp.float32)).astype(jnp.bfloat16)
    return (high, mid, low)


def body_dense(
    inputs,
    gain_attn,
    w_query,
    w_latent,
    gain_latent,
    w_latent_up,
    w_output,
    gain_ffn,
    w_router,
    w_shared_in,
    w_shared_out,
    w_expert_in,
    w_expert_out,
    expert_ids,
    slot_ids,
    cotangent,
):
    f32, bf16 = jnp.float32, jnp.bfloat16
    tokens, model_width = inputs.shape
    ep_count, tp_count = lax.axis_size("ep"), lax.axis_size("tp")
    ep_index, tp_index = lax.axis_index("ep"), lax.axis_index("tp")
    heads_here = w_output.shape[0] // VDIM
    experts = w_router.shape[1]
    capacity = (9 * tokens * TOPK + 64 * experts - 1) // (64 * experts) * 8
    qk_width = NOPE + ROPE
    score_scale = qk_width ** (-0.5)
    rows_part = tokens // tp_count

    expert_range = jnp.arange(experts, dtype=jnp.int32)
    kept = jnp.any(
        (expert_ids[:, :, None] == expert_range) & (slot_ids < capacity)[:, :, None], axis=1
    ).astype(f32)
    kept_here = lax.all_to_all(kept, "ep", split_axis=1, concat_axis=0, tiled=True)
    rows_part = tokens // tp_count
    kept_lanes = jnp.broadcast_to(
        kept_here.reshape(ep_count, tp_count, rows_part, 1).swapaxes(0, 1),
        (tp_count, ep_count, rows_part, 128),
    ).astype(bf16)

    routed = w_expert_in.shape[3]
    shared = w_shared_in.shape[2] // ep_count
    hidden = padded_hidden(routed, shared)
    shared_start = ep_index * shared
    shared_in = lax.dynamic_slice_in_dim(w_shared_in, shared_start, shared, 2)
    shared_out = lax.dynamic_slice_in_dim(w_shared_out, shared_start, shared, 0)
    router_parts = jnp.concatenate(split_wide(w_router), axis=1)
    fill = hidden - routed - shared
    w_in = jnp.concatenate(
        [
            w_expert_in[0, 0],
            shared_in[0],
            jnp.pad(router_parts, ((0, 0), (0, fill - router_parts.shape[1]))),
            w_expert_in[0, 1],
            shared_in[1],
            jnp.zeros((model_width, fill), bf16),
        ],
        axis=1,
    )
    w_out = jnp.concatenate(
        [w_expert_out[0], shared_out, jnp.zeros((fill, model_width), bf16)], axis=0
    )

    attn_part, hidden_attn, query_nope, query_rope, key_value, key_pair, attended, latent_in, compressed = (
        attention_call(
            inputs, gain_attn, w_query, w_latent, gain_latent, w_latent_up, w_output, rope_tables(tokens), heads_here
        )
    )
    middle, hidden_all, cot_all, hidden_grads, gated, out_part, rows_grad = experts_call(
        attn_part, inputs, gain_ffn, cotangent, kept_lanes, w_in, w_out,
        ep_count, tp_count, routed, shared, experts, 0,
    )
    middle_grad, branch, gain_ffn_part, grad_expert_in, grad_expert_out, shared_in_part, shared_out_part, router_part, layer_sum, _ = (
        sum_call(
            rows_grad, out_part, hidden_all, hidden_grads, gated, cot_all, middle, gain_ffn, routed, shared, experts, 1
        )
    )
    block_out, grad_inputs, gains, grad_query, grad_output, grad_latent_up, latent_sum, grad_shared_in, grad_shared_out, _ = (
        tail_call(
            branch, middle_grad, middle, layer_sum, router_part, gain_ffn_part, inputs, shared_in_part, shared_out_part,
            w_output, w_query, w_latent, w_latent_up, hidden_attn,
            query_nope, query_rope, key_value, key_pair,
            attended, latent_in, compressed, rope_tables(tokens), gain_latent, gain_attn, heads_here, shared, 2,
        )
    )
    grad_latent = latent_sum[:, : KV_RANK + ROPE]
    grad_router = latent_sum[:, KV_RANK + ROPE : KV_RANK + ROPE + experts]
    flat = ep_index * tp_count + tp_index
    wide_part, rank_part = (n // (ep_count * tp_count) for n in (model_width, KV_RANK))
    grad_gain_attn = lax.dynamic_slice_in_dim(gains[0], flat * wide_part, wide_part, 0)
    grad_gain_ffn = lax.dynamic_slice_in_dim(gains[1], flat * wide_part, wide_part, 0)
    grad_gain_latent = lax.dynamic_slice_in_dim(gains[2], flat * rank_part, rank_part, 0)
    block_out = block_out.reshape(tokens, model_width)
    grad_inputs = grad_inputs.reshape(tokens, model_width)
    return (
        block_out,
        grad_inputs,
        grad_gain_attn,
        grad_query,
        grad_latent,
        grad_gain_latent,
        grad_latent_up,
        grad_output,
        grad_gain_ffn,
        grad_router,
        grad_shared_in,
        grad_shared_out,
        grad_expert_in,
        grad_expert_out,
    )


def solution(mesh):
    near = mesh.shape["ep"] == 8 and mesh.shape["tp"] == 4
    body = body_dense if near else body_slots
    placed = (
        P("ep", None),
        P(),
        P(None, "tp"),
        P(),
        P(),
        P(None, "tp"),
        P("tp", None),
        P(),
        P(),
        P(None, None, "tp"),
        P("tp", None),
        P("ep", None, None, "tp"),
        P("ep", "tp", None),
        P("ep", None),
        P("ep", None),
        P("ep", None),
    )
    return jax.shard_map(
        body,
        mesh=mesh,
        in_specs=placed,
        out_specs=(
            P("ep", None),
            P("ep", None),
            P(("ep", "tp")),
            P("ep", "tp"),
            P(("ep", "tp"), None),
            P(("ep", "tp")),
            P("ep", "tp"),
            P("tp", "ep"),
            P(("ep", "tp")),
            P(("ep", "tp"), None),
            P(None, "ep", "tp"),
            P("tp", "ep"),
            P("ep", None, None, "tp"),
            P("ep", "tp", None),
        ),
        check_vma=False,
    )
```

```python
import functools
import math

import jax
import jax.numpy as jnp
import numpy as np
from jax import lax
from jax.experimental import pallas as pl
from jax.experimental.pallas import tpu as pltpu
from jax.sharding import PartitionSpec as P

NOPE = 128
ROPE = 64
VDIM = 128
KV_RANK = 512
TOPK = 6
BLOCK = 256


EPSILON = 1e-06
HIGHEST = lax.Precision.HIGHEST


def angles(length, rope_width):
    half_width = rope_width // 2
    position = jnp.arange(length, dtype=jnp.float32)
    inverse = jnp.exp(jnp.arange(half_width, dtype=jnp.float32) * (-math.log(10000.0) / half_width))
    angle_table = position[:, None] * inverse[None, :]
    return (jnp.cos(angle_table), jnp.sin(angle_table))


def rotate(values, cosine, sine_table):
    half_width = values.shape[-1] // 2
    front_part = values[..., :half_width]
    second = values[..., half_width:]
    return jnp.concatenate(
        [front_part * cosine - second * sine_table, second * cosine + front_part * sine_table],
        axis=-1,
    )


def silu_parts(gate_val):
    sigmoid_val = jax.nn.sigmoid(gate_val)
    return (gate_val * sigmoid_val, sigmoid_val * (1.0 + gate_val * (1.0 - sigmoid_val)))


def norm_back(grad_norm, gain_vec, normed, inverse):
    scaled = grad_norm * gain_vec
    return inverse * (scaled - normed * jnp.mean(scaled * normed, axis=-1, keepdims=True))


def attention_scores(query_rot, key_nope, key_rope, score_scale, allowed):
    nope_scores = jnp.einsum(
        "qhd,khd->hqk", query_rot[..., :NOPE], key_nope, preferred_element_type=jnp.float32
    )
    rope_scores = jnp.einsum(
        "qhr,kr->hqk", query_rot[..., NOPE:], key_rope, preferred_element_type=jnp.float32
    )
    return jnp.where(allowed[None], (nope_scores + rope_scores) * score_scale, -1e30)


def expert_forward(received, w_expert_in, w_expert_out, sources):
    sectioned = received.reshape(sources, -1, received.shape[1], received.shape[2])
    gate_up = jnp.einsum(
        "secd,egdh->secgh", sectioned, w_expert_in, preferred_element_type=jnp.float32
    )
    gate_val, gate_slope = silu_parts(gate_up[..., 0, :])
    activated = (gate_val * gate_up[..., 1, :]).astype(jnp.bfloat16)
    produced = jnp.einsum(
        "sech,ehd->secd", activated, w_expert_out, preferred_element_type=jnp.float32
    )
    return (sectioned, gate_up, activated, produced.reshape(received.shape))


def body_slots(
    inputs,
    gain_attn,
    w_query,
    w_latent,
    gain_latent,
    w_latent_up,
    w_output,
    gain_ffn,
    w_router,
    w_shared_in,
    w_shared_out,
    w_expert_in,
    w_expert_out,
    expert_ids,
    slot_ids,
    cotangent,
):
    tokens, model_width = inputs.shape
    tp_count = lax.axis_size("tp")
    tp_index = lax.axis_index("tp")
    heads_here = w_output.shape[0] // VDIM
    experts = w_router.shape[1]
    local_experts = w_expert_in.shape[0]
    sources = experts // local_experts
    capacity = (9 * tokens * TOPK + 64 * experts - 1) // (64 * experts) * 8
    qk_width = NOPE + ROPE
    score_scale = qk_width ** (-0.5)
    rows_part = tokens // tp_count
    row_start = tp_index * rows_part
    resid = inputs.astype(jnp.float32)
    inv_first = lax.rsqrt(jnp.mean(resid * resid, axis=-1, keepdims=True) + EPSILON)
    normed_first = resid * inv_first
    hidden_attn = (normed_first * gain_attn).astype(jnp.bfloat16)
    cosine, sine_table = angles(tokens, ROPE)
    query_raw = jnp.dot(hidden_attn, w_query, preferred_element_type=jnp.float32).reshape(
        tokens, heads_here, qk_width
    )
    query_rot = jnp.concatenate(
        [
            query_raw[..., :NOPE],
            rotate(query_raw[..., NOPE:], cosine[:, None], sine_table[:, None]),
        ],
        axis=-1,
    ).astype(jnp.bfloat16)
    latent = jnp.dot(hidden_attn, w_latent, preferred_element_type=jnp.float32)
    compressed = latent[:, :KV_RANK]
    inv_latent = lax.rsqrt(jnp.mean(compressed * compressed, axis=-1, keepdims=True) + EPSILON)
    normed_latent = compressed * inv_latent
    latent_in = (normed_latent * gain_latent).astype(jnp.bfloat16)
    key_rope = rotate(latent[:, KV_RANK:], cosine, sine_table).astype(jnp.bfloat16)
    key_value = (
        jnp.dot(latent_in, w_latent_up, preferred_element_type=jnp.float32)
        .astype(jnp.bfloat16)
        .reshape(tokens, heads_here, NOPE + VDIM)
    )
    key_nope = key_value[..., :NOPE]
    values = key_value[..., NOPE:]
    block_ids = jnp.arange(tokens) // BLOCK
    allowed = block_ids[None, :] <= block_ids[:, None]
    scores = attention_scores(query_rot, key_nope, key_rope, score_scale, allowed)
    row_peak = jnp.max(scores, axis=-1, keepdims=True)
    exp_scores = jnp.exp(scores - row_peak)
    totals = jnp.sum(exp_scores, axis=-1, keepdims=True)
    attn_probs = exp_scores / totals
    log_total = row_peak + jnp.log(totals)
    attended = (
        jnp.einsum(
            "hqk,khd->qhd",
            attn_probs.astype(jnp.bfloat16),
            values,
            preferred_element_type=jnp.float32,
        )
        .astype(jnp.bfloat16)
        .reshape(tokens, heads_here * VDIM)
    )
    attn_full = lax.psum(
        jnp.dot(attended, w_output, preferred_element_type=jnp.float32).astype(jnp.bfloat16), "tp"
    ).astype(jnp.float32)
    middle = resid + attn_full
    inv_second = lax.rsqrt(jnp.mean(middle * middle, axis=-1, keepdims=True) + EPSILON)
    normed_second = middle * inv_second
    hidden_ffn = (normed_second * gain_ffn).astype(jnp.bfloat16)
    hidden_wide = hidden_ffn.astype(jnp.float32)
    logits = jnp.dot(hidden_wide, w_router, precision=HIGHEST, preferred_element_type=jnp.float32)
    logit_peak = jnp.max(logits, axis=-1, keepdims=True)
    exp_logits = jnp.exp(logits - logit_peak)
    router_probs = exp_logits / jnp.sum(exp_logits, axis=-1, keepdims=True)
    route_onehot = (
        expert_ids[:, :, None] == jnp.arange(experts, dtype=jnp.int32)[None, None, :]
    ).astype(jnp.float32)
    pair_gate = jnp.sum(route_onehot * router_probs[:, None, :], axis=-1)
    kept_pair = slot_ids < capacity
    flat_index = jnp.where(kept_pair, expert_ids * capacity + slot_ids, experts * capacity)
    row_numbers = jnp.broadcast_to(jnp.arange(tokens, dtype=jnp.int32)[:, None], (tokens, TOPK))
    owner_row = (
        jnp.full((experts * capacity,), tokens, jnp.int32)
        .at[flat_index.reshape(-1)]
        .set(row_numbers.reshape(-1), mode="drop")
    )
    outgoing = jnp.take(hidden_ffn, owner_row, axis=0, mode="fill", fill_value=0).reshape(
        experts, capacity, model_width
    )
    received = lax.all_to_all(outgoing, "ep", split_axis=0, concat_axis=0, tiled=True)
    sectioned, gate_up, activated, produced = expert_forward(
        received, w_expert_in, w_expert_out, sources
    )
    returned = lax.all_to_all(
        produced.astype(jnp.bfloat16), "ep", split_axis=0, concat_axis=0, tiled=True
    ).astype(produced.dtype)
    out_grad = cotangent.astype(jnp.float32)
    back_rows = returned.reshape(-1, model_width)
    combined = jnp.zeros((tokens, model_width), jnp.float32)
    gate_cols = []
    for pick_index in range(TOPK):
        taken_rows = jnp.take(
            back_rows, flat_index[:, pick_index], axis=0, mode="fill", fill_value=0.0
        )
        combined = combined + pair_gate[:, pick_index : pick_index + 1] * taken_rows
        gate_cols.append(jnp.sum(out_grad * taken_rows, axis=-1))
    gate_grad = jnp.stack(gate_cols, axis=1)
    shared_gate = jnp.dot(hidden_ffn, w_shared_in[0], preferred_element_type=jnp.float32)
    shared_up = jnp.dot(hidden_ffn, w_shared_in[1], preferred_element_type=jnp.float32)
    shared_val, shared_slope = silu_parts(shared_gate)
    shared_act = (shared_val * shared_up).astype(jnp.bfloat16)
    branch_part = jnp.dot(shared_act, w_shared_out, preferred_element_type=jnp.float32) + combined
    ffn_full = lax.psum(branch_part.astype(jnp.bfloat16), "tp").astype(jnp.float32)
    block_out = (middle + ffn_full).astype(jnp.bfloat16)
    slot_gate = (
        jnp.zeros((experts * capacity,), jnp.float32)
        .at[flat_index.reshape(-1)]
        .set(pair_gate.reshape(-1), mode="drop")
    )
    gathered_grad = jnp.take(cotangent, owner_row, axis=0, mode="fill", fill_value=0)
    slot_grad = (
        (slot_gate[:, None] * gathered_grad.astype(jnp.float32))
        .astype(jnp.bfloat16)
        .reshape(experts, capacity, model_width)
    )
    grad_arrived = lax.all_to_all(slot_grad, "ep", split_axis=0, concat_axis=0, tiled=True).reshape(
        sectioned.shape
    )
    act_grad = jnp.einsum(
        "secd,ehd->sech", grad_arrived, w_expert_out, preferred_element_type=jnp.float32
    )
    gate_val, gate_slope = silu_parts(gate_up[..., 0, :])
    up_val = gate_up[..., 1, :]
    gu_grad = jnp.stack([act_grad * up_val * gate_slope, act_grad * gate_val], axis=-2).astype(
        jnp.bfloat16
    )
    grad_expert_out = jnp.einsum(
        "sech,secd->ehd", activated, grad_arrived, preferred_element_type=jnp.float32
    )
    grad_expert_in = jnp.einsum(
        "secd,secgh->egdh", sectioned, gu_grad, preferred_element_type=jnp.float32
    )
    rows_grad = jnp.einsum(
        "secgh,egdh->secd", gu_grad, w_expert_in, preferred_element_type=jnp.float32
    ).reshape(received.shape)
    returned_grad = (
        lax.all_to_all(
            rows_grad.astype(jnp.bfloat16), "ep", split_axis=0, concat_axis=0, tiled=True
        )
        .astype(rows_grad.dtype)
        .reshape(-1, model_width)
    )
    routed_grad = jnp.zeros((tokens, model_width), jnp.float32)
    for pick_index in range(TOPK):
        routed_grad = routed_grad + jnp.take(
            returned_grad, flat_index[:, pick_index], axis=0, mode="fill", fill_value=0.0
        )
    shared_act_grad = jnp.einsum(
        "td,fd->tf", cotangent, w_shared_out, preferred_element_type=jnp.float32
    )
    shared_gate_grad = (shared_act_grad * shared_up * shared_slope).astype(jnp.bfloat16)
    shared_up_grad = (shared_act_grad * shared_val).astype(jnp.bfloat16)
    shared_out_grad = jnp.einsum(
        "tf,td->fd", shared_act, cotangent, preferred_element_type=jnp.float32
    )
    shared_in_grad = jnp.stack(
        [
            jnp.einsum(
                "td,tf->df", hidden_ffn, shared_gate_grad, preferred_element_type=jnp.float32
            ),
            jnp.einsum("td,tf->df", hidden_ffn, shared_up_grad, preferred_element_type=jnp.float32),
        ],
        axis=0,
    )
    shared_back = jnp.einsum(
        "tf,df->td", shared_gate_grad, w_shared_in[0], preferred_element_type=jnp.float32
    ) + jnp.einsum("tf,df->td", shared_up_grad, w_shared_in[1], preferred_element_type=jnp.float32)
    prob_grad = jnp.sum(route_onehot * gate_grad[:, :, None], axis=1)
    logit_grad = router_probs * (
        prob_grad - jnp.sum(router_probs * prob_grad, axis=-1, keepdims=True)
    )
    router_back = jnp.einsum(
        "te,de->td", logit_grad, w_router, precision=HIGHEST, preferred_element_type=jnp.float32
    )
    router_grad = jnp.einsum(
        "td,te->de", hidden_wide, logit_grad, precision=HIGHEST, preferred_element_type=jnp.float32
    )
    ffn_grad = lax.psum(
        (shared_back + routed_grad + router_back).astype(jnp.bfloat16), "tp"
    ).astype(jnp.float32)
    middle_grad = out_grad + norm_back(ffn_grad, gain_ffn, normed_second, inv_second)
    gain_ffn_grad = jnp.sum(
        lax.dynamic_slice_in_dim(ffn_grad * normed_second, row_start, rows_part, 0), axis=0
    )
    branch_grad = middle_grad.astype(jnp.bfloat16)
    output_w_grad = jnp.einsum(
        "tf,td->fd", attended, branch_grad, preferred_element_type=jnp.float32
    )
    attended_grad = (
        jnp.einsum("td,fd->tf", branch_grad, w_output, preferred_element_type=jnp.float32)
        .astype(jnp.bfloat16)
        .reshape(tokens, heads_here, VDIM)
    )
    scores_again = attention_scores(query_rot, key_nope, key_rope, score_scale, allowed)
    probs_again = jnp.exp(scores_again - log_total)
    values_grad = jnp.einsum(
        "hqk,qhd->khd",
        probs_again.astype(jnp.bfloat16),
        attended_grad,
        preferred_element_type=jnp.float32,
    )
    prob_part = jnp.einsum(
        "qhd,khd->hqk", attended_grad, values, preferred_element_type=jnp.float32
    )
    score_grad = (
        probs_again * (prob_part - jnp.sum(probs_again * prob_part, axis=-1, keepdims=True))
    ).astype(jnp.bfloat16)
    query_nope_grad = (
        jnp.einsum("hqk,khd->qhd", score_grad, key_nope, preferred_element_type=jnp.float32)
        * score_scale
    )
    query_rope_grad = (
        jnp.einsum("hqk,kr->qhr", score_grad, key_rope, preferred_element_type=jnp.float32)
        * score_scale
    )
    key_nope_grad = (
        jnp.einsum(
            "hqk,qhd->khd", score_grad, query_rot[..., :NOPE], preferred_element_type=jnp.float32
        )
        * score_scale
    )
    key_rope_grad = (
        jnp.einsum(
            "hqk,qhr->kr", score_grad, query_rot[..., NOPE:], preferred_element_type=jnp.float32
        )
        * score_scale
    )
    kv_grad = (
        jnp.concatenate([key_nope_grad, values_grad], axis=-1)
        .astype(jnp.bfloat16)
        .reshape(tokens, heads_here * (NOPE + VDIM))
    )
    latent_up_grad = jnp.einsum("tr,tf->rf", latent_in, kv_grad, preferred_element_type=jnp.float32)
    latent_in_grad = jnp.einsum(
        "tf,rf->tr", kv_grad, w_latent_up, preferred_element_type=jnp.float32
    )
    gain_latent_grad = jnp.sum(latent_in_grad * normed_latent, axis=0)
    latent_grad_part = jnp.concatenate(
        [
            norm_back(latent_in_grad, gain_latent, normed_latent, inv_latent),
            rotate(key_rope_grad, cosine, -sine_table),
        ],
        axis=-1,
    )
    query_grad = (
        jnp.concatenate(
            [query_nope_grad, rotate(query_rope_grad, cosine[:, None], -sine_table[:, None])],
            axis=-1,
        )
        .astype(jnp.bfloat16)
        .reshape(tokens, heads_here * qk_width)
    )
    query_w_grad = jnp.einsum(
        "td,tf->df", hidden_attn, query_grad, preferred_element_type=jnp.float32
    )
    hidden_part = jnp.einsum("tf,df->td", query_grad, w_query, preferred_element_type=jnp.float32)
    hidden_sum, latent_sum = (
        lax.psum(hidden_part.astype(jnp.bfloat16), "tp").astype(jnp.float32),
        lax.psum(latent_grad_part.astype(jnp.bfloat16), "tp").astype(jnp.float32),
    )
    latent_low = latent_sum.astype(jnp.bfloat16)
    attn_in_grad = hidden_sum + jnp.einsum(
        "tf,df->td", latent_low, w_latent, preferred_element_type=jnp.float32
    )
    latent_w_grad = jnp.einsum(
        "td,tf->df",
        lax.dynamic_slice_in_dim(hidden_attn, row_start, rows_part, 0),
        lax.dynamic_slice_in_dim(latent_low, row_start, rows_part, 0),
        preferred_element_type=jnp.float32,
    )
    gain_attn_grad = jnp.sum(
        lax.dynamic_slice_in_dim(attn_in_grad * normed_first, row_start, rows_part, 0), axis=0
    )
    grad_inputs = (
        middle_grad + norm_back(attn_in_grad, gain_attn, normed_first, inv_first)
    ).astype(jnp.bfloat16)
    grad_query, grad_latent_up, grad_output, grad_shared_in, grad_shared_out = (
        lax.psum_scatter(
            query_w_grad.astype(jnp.bfloat16), "ep", scatter_dimension=0, tiled=True
        ).astype(jnp.float32),
        lax.psum_scatter(
            latent_up_grad.astype(jnp.bfloat16), "ep", scatter_dimension=0, tiled=True
        ).astype(jnp.float32),
        lax.psum_scatter(
            output_w_grad.astype(jnp.bfloat16), "ep", scatter_dimension=1, tiled=True
        ).astype(jnp.float32),
        lax.psum_scatter(
            shared_in_grad.astype(jnp.bfloat16), "ep", scatter_dimension=1, tiled=True
        ).astype(jnp.float32),
        lax.psum_scatter(
            shared_out_grad.astype(jnp.bfloat16), "ep", scatter_dimension=1, tiled=True
        ).astype(jnp.float32),
    )
    grad_latent, grad_gain_latent, grad_gain_attn, grad_gain_ffn, grad_router = (
        lax.psum_scatter(latent_w_grad, ("ep", "tp"), scatter_dimension=0, tiled=True),
        lax.psum_scatter(gain_latent_grad, ("ep", "tp"), scatter_dimension=0, tiled=True),
        lax.psum_scatter(gain_attn_grad, ("ep", "tp"), scatter_dimension=0, tiled=True),
        lax.psum_scatter(gain_ffn_grad, ("ep", "tp"), scatter_dimension=0, tiled=True),
        lax.psum_scatter(router_grad, ("ep", "tp"), scatter_dimension=0, tiled=True),
    )
    return (
        block_out,
        grad_inputs,
        grad_gain_attn,
        grad_query,
        grad_latent,
        grad_gain_latent,
        grad_latent_up,
        grad_output,
        grad_gain_ffn,
        grad_router,
        grad_shared_in,
        grad_shared_out,
        grad_expert_in,
        grad_expert_out,
    )


MESH = pl.DeviceIdType.MESH


def plane_partners(ep):
    def flip(bit):
        return ep + bit - 2 * bit * lax.rem(lax.div(ep, bit), 2)

    return flip(1), flip(2), flip(4)


def line_order(tp):
    def pick(a, b, c, d):
        return jnp.where(tp == 0, a, jnp.where(tp == 1, b, jnp.where(tp == 2, c, d)))

    return (tp, pick(1, 0, 3, 2), pick(2, 2, 1, 1), pick(3, 3, 0, 0))


def greet(devices):
    barrier = pltpu.get_barrier_semaphore()
    for ep, tp in devices:
        pl.semaphore_signal(barrier, inc=1, device_id=(ep, tp), device_id_type=MESH)
    pl.semaphore_wait(barrier, len(devices))


def remote(src, dst, send, recv, device):
    return pltpu.make_async_remote_copy(
        src_ref=src, dst_ref=dst, send_sem=send, recv_sem=recv, device_id=device, device_id_type=MESH
    )


def add_rows(dst, a, b):
    def body(r, _):
        at = pl.ds(pl.multiple_of(r * 16, 16), 16)
        dst[at, :] = (a[at, :].astype(jnp.float32) + b[at, :].astype(jnp.float32)).astype(dst.dtype)
        return 0

    lax.fori_loop(0, dst.shape[0] // 16, body, 0)


def line_sum(own_of, got, send_sem, recv_sem, ep, tp, depth):
    far = line_order(tp)[::-1]
    between = (tp > 0) & (tp < depth - 1)
    near = jnp.where(tp > 0, tp - 1, tp + 1)

    def copy(n, src):
        chunk = far[n]
        to = jnp.where(chunk > tp, tp + 1, tp - 1)
        slot = jnp.where(chunk == tp - 1, depth, chunk)
        return remote(src, got.at[slot], send_sem.at[n], recv_sem.at[slot], (ep, to))

    def arrive(slot):
        remote(got.at[0], got.at[slot], send_sem.at[0], recv_sem.at[slot], (ep, near)).wait_recv()

    def start(n):
        @pl.when(jnp.logical_not(between))
        def _():
            copy(n, own_of(n)).start()

    def pass_on(n):
        @pl.when(between)
        def _():
            held = got.at[far[n]]
            arrive(far[n])
            add_rows(held, own_of(n), held)
            copy(n, held).start()

    def clear():
        @pl.when(tp == 0)
        def _():
            got[0] = jnp.zeros_like(got[0])

        @pl.when(tp == depth - 1)
        def _():
            got[depth] = jnp.zeros_like(got[depth])

    def finish():
        @pl.when(tp > 0)
        def _():
            arrive(tp)

        @pl.when(tp < depth - 1)
        def _():
            arrive(depth)

    def drain():
        for n in range(depth - 1):
            copy(n, got.at[0]).wait_send()

    return clear, start, pass_on, finish, drain


def turn(slab, table, sign):
    cosine, front, second = table
    return slab * cosine + sign * (pltpu.roll(slab, 96, 1) * front + pltpu.roll(slab, 32, 1) * second)


def experts_kernel(
    depth, blocks, heads, routed, shared, experts,
    inputs_ref, gain_attn, w_query, w_latent, gain_latent, w_up, w_output, tables,
    gain_ref, cot_ref, kept_hbm, e_in, e_out, s_in, s_out,
    middle_ref, h_out, cot_all, grads_out, gated_out, rows_out,
    hidden_out, qn_out, qr_out, kv_out, kr_out, attended_out, latent_in_out, compressed_out, w_out_out,
    part_ref, hidden, qn_ref, qr_ref, kv, kr_ref, attended, latent_in, compressed, rope_slab,
    kept_ref, w_in_ref, w_out_ref, e_stage,
    h_all, got_z, cot_tile, gu, act_grad, prob_lanes, diff_lanes, pair_lanes,
    grads_tile, gated_tile, rows_tile,
    weight_sem, stage_sem, save_sem, local_sem, z_send, z_recv, line_send, line_recv, h_send, h_recv, c_send, c_recv, b_send, b_recv, tile_sem, store_sem,
):
    f32, bf16 = jnp.float32, jnp.bfloat16
    ep, tp = lax.axis_index("ep"), lax.axis_index("tp")
    pair, xn, yn = plane_partners(ep)
    parity = lax.rem(ep, 2)
    passed = jnp.where(parity == 0, xn, yn)
    onward = jnp.where(parity == 0, yn, xn)
    diag = xn + yn - ep
    rows = h_all.shape[2]
    width = h_all.shape[3]
    hidden_units = w_out_ref.shape[0]
    tokens = inputs_ref.shape[0]
    rank = compressed.shape[1]
    lanes = lax.broadcasted_iota(jnp.int32, (1, 128), 1)
    across = (((1,), (1,)), ((), ()))
    score_scale = (NOPE + ROPE) ** (-0.5)

    def dot(a, b, dims=(((1,), (0,)), ((), ()))):
        return lax.dot_general(a, b, dims, preferred_element_type=f32)

    half = blocks // 2
    tile = half * rows
    up, down = jnp.minimum(tp + 1, depth - 1), jnp.maximum(tp - 1, 0)

    def twin(block):
        return block + pair - ep

    greet([(pair, tp), (xn, tp), (yn, tp)] + [(ep, lax.rem(tp + k, depth)) for k in range(1, depth)])

    def part_rows(n):
        return part_ref.at[pl.ds(pl.multiple_of(line_order(tp)[depth - 1 - n] * rows, rows), rows)]

    z_clear, z_start, z_pass, z_finish, z_drain = line_sum(part_rows, got_z, z_send, z_recv, ep, tp, depth)
    z_clear()
    weight_loads = [
        pltpu.make_async_copy(kept_hbm, kept_ref, weight_sem.at[0]),
        pltpu.make_async_copy(e_out.at[0], w_out_ref.at[pl.ds(0, routed)], weight_sem.at[1]),
        pltpu.make_async_copy(s_out, w_out_ref.at[pl.ds(routed, hidden_units - routed)], weight_sem.at[2]),
    ]
    for g in range(2):
        at = pl.ds(g * hidden_units + routed // 128 * 128, s_in.shape[2])
        weight_loads.append(pltpu.make_async_copy(s_in.at[g], w_in_ref.at[:, at], weight_sem.at[3 + g]))
    piece = e_stage.shape[1]
    pieces = width // piece

    def e_load(n):
        at = pl.ds(pl.multiple_of(lax.rem(n, pieces) * piece, piece), piece)
        return pltpu.make_async_copy(e_in.at[0, lax.div(n, pieces), at], e_stage.at[lax.rem(n, 2)], stage_sem.at[lax.rem(n, 2)])

    def h_copy(block, chunk, slot, to):
        ref = h_all.at[chunk, block]
        return remote(ref, ref, h_send.at[chunk, slot], h_recv.at[chunk, slot], (to, tp))

    def c_copy(block, chunk, slot, to):
        ref = cot_all.at[chunk, block]
        return remote(ref, ref, c_send.at[chunk, slot], c_recv.at[chunk, slot], (to, tp))

    def c_first(chunk, slot, to):
        src = cot_ref.at[pl.ds(pl.multiple_of(chunk * rows, rows), rows)]
        return remote(src, cot_all.at[chunk, ep], c_send.at[chunk, slot], c_recv.at[chunk, slot], (to, tp))

    buddy = tp + 1 - 2 * lax.rem(tp, 2)
    skipped, theirs = depth - 1 - tp, depth - 1 - buddy

    def buddy_copy(n, chunk):
        ref = cot_all.at[chunk, (xn, yn, diag)[n]]
        return remote(ref, ref, b_send.at[n], b_recv.at[n], (ep, buddy))

    def own_cot_in(chunk):
        src = cot_ref.at[pl.ds(pl.multiple_of(chunk * rows, rows), rows)]
        return pltpu.make_async_copy(src, rows_tile.at[0, chunk], local_sem.at[chunk])

    def own_cot_out(chunk):
        return pltpu.make_async_copy(rows_tile.at[0, chunk], cot_all.at[chunk, ep], local_sem.at[chunk])

    order = line_order(tp)

    def order_at(k):
        return jnp.where(k == 0, order[0], jnp.where(k == 1, order[1], jnp.where(k == 2, order[2], order[3])))

    for k in range(depth):

        @pl.when(order[k] != skipped)
        def _():
            c_first(order[k], 1, xn).start()
            c_first(order[k], 2, yn).start()

        c_first(order[k], 0, pair).start()
        own_cot_in(k).start()
    for copy in weight_loads:
        copy.start()
    e_load(0).start()

    def first_norm(r, _):
        at = pl.ds(pl.multiple_of(r * 16, 16), 16)
        v = inputs_ref[at, :].astype(f32)
        inverse = lax.rsqrt(jnp.mean(v * v, axis=-1, keepdims=True) + EPSILON)
        hidden[at, :] = (v * inverse * gain_attn[...]).astype(bf16)
        return 0

    lax.fori_loop(0, tokens // 16, first_norm, 0)
    table = tuple(tables[n] for n in range(3))
    latent = dot(hidden[...], w_latent[...])
    held = latent[:, :rank]
    compressed[...] = held
    inverse = lax.rsqrt(jnp.mean(held * held, axis=-1, keepdims=True) + EPSILON)
    latent_in[...] = (held * inverse * gain_latent[...]).astype(bf16)
    rope_slab[...] = jnp.zeros_like(rope_slab)
    rope_slab[:, 0:ROPE] = latent[:, rank:]
    key = turn(rope_slab[...], table, 1.0)
    kr_ref[0] = key.astype(bf16)
    kr_ref[1] = pltpu.roll(key, 64, 1).astype(bf16)
    kv[...] = dot(latent_in[...], w_up[...]).astype(bf16)
    wide = 2 * (NOPE + ROPE)
    for p in range(heads // 2):
        found = dot(hidden[...], w_query[:, p * wide : (p + 1) * wide])
        slabs = [found[:, n : n + 128] for n in (0, 128, 256)]
        qn_ref[:, 2 * p * NOPE : (2 * p + 1) * NOPE] = slabs[0].astype(bf16)
        odd = pltpu.roll(jnp.where(lanes < 64, slabs[2], slabs[1]), 64, 1)
        qn_ref[:, (2 * p + 1) * NOPE : (2 * p + 2) * NOPE] = odd.astype(bf16)
        qr_ref[:, p * 128 : (p + 1) * 128] = turn(jnp.where(lanes < 64, slabs[1], slabs[2]), table, 1.0).astype(bf16)
    for h in range(heads):
        for b in range(tokens // BLOCK):
            own = slice(b * BLOCK, (b + 1) * BLOCK)
            keys = slice(0, (b + 1) * BLOCK)
            slab = slice(h // 2 * 128, h // 2 * 128 + 128)
            at = slice(h * 128, h * 128 + 128)
            scores = dot(qn_ref[own, at], kv[keys, h * 256 : h * 256 + 128], across)
            scores = (scores + dot(qr_ref[own, slab], kr_ref[h % 2, keys, :], across)) * score_scale
            exps = jnp.exp(scores - jnp.max(scores, axis=-1, keepdims=True))
            probs = exps / jnp.sum(exps, axis=-1, keepdims=True)
            attended[own, at] = dot(probs.astype(bf16), kv[keys, h * 256 + 128 : h * 256 + 256]).astype(bf16)
    for n in range(0, width, 512):
        part_ref[:, n : n + 512] = dot(attended[...], w_output[:, n : n + 512]).astype(bf16)
    for n in range(depth - 1):
        z_start(n)
    saves = [
        pltpu.make_async_copy(src, dst, save_sem.at[n])
        for n, (src, dst) in enumerate(
            (
                (hidden, hidden_out), (qn_ref, qn_out), (qr_ref, qr_out), (kv, kv_out), (kr_ref, kr_out),
                (attended, attended_out), (latent_in, latent_in_out), (compressed, compressed_out),
            )
        )
    ]
    for copy in saves:
        copy.start()
    for k in range(depth):
        own_cot_in(k).wait()
        own_cot_out(k).start()

    def e_place(n, _):
        e_load(n).wait()

        @pl.when(n + 1 < 2 * pieces)
        def _():
            e_load(n + 1).start()

        at = pl.ds(pl.multiple_of(lax.rem(n, pieces) * piece, piece), piece)

        @pl.when(n < pieces)
        def _():
            w_in_ref[at, 0:routed] = e_stage[lax.rem(n, 2)]

        @pl.when(n >= pieces)
        def _():
            w_in_ref[at, hidden_units : hidden_units + routed] = e_stage[lax.rem(n, 2)]

        return 0

    for copy in weight_loads:
        copy.wait()
    w_out_save = pltpu.make_async_copy(w_out_ref, w_out_out, save_sem.at[8])
    w_out_save.start()
    lax.fori_loop(0, pieces, e_place, 0)
    z_pass(0)
    lax.fori_loop(pieces, 2 * pieces, e_place, 0)
    z_pass(1)
    z_pass(2)
    z_finish()

    def norm_rows(r, _):
        here = pl.ds(pl.multiple_of(r * 16, 16), 16)
        own = pl.ds(pl.multiple_of(tp * rows + r * 16, 16), 16)
        total = part_ref[own, :].astype(f32)
        total = total + got_z[tp, here, :].astype(f32) + got_z[depth, here, :].astype(f32)
        middle = inputs_ref[own, :].astype(f32) + total
        inverse = lax.rsqrt(jnp.mean(middle * middle, axis=-1, keepdims=True) + EPSILON)
        middle_ref[here, :] = middle
        h_all[tp, ep, here, :] = (middle * inverse * gain_ref[...]).astype(bf16)
        return 0

    lax.fori_loop(0, rows // 16, norm_rows, 0)
    for k in range(depth):
        own_cot_out(k).wait()

    def along(chunk, way, to):
        ref = h_all.at[chunk, ep]
        return remote(ref, ref, line_send.at[chunk, way], line_recv.at[chunk], (ep, to))

    def goes_up(chunk):
        return (chunk <= tp) & (tp < depth - 1)

    def goes_down(chunk):
        return (chunk >= tp) & (tp > 0)

    def send_chunk(k):
        chunk = order[k]
        if k > 0:
            along(chunk, 0, up).wait_recv()

        @pl.when(goes_up(chunk))
        def _():
            along(chunk, 0, up).start()

        @pl.when(goes_down(chunk))
        def _():
            along(chunk, 1, down).start()

        h_copy(ep, chunk, 1, xn).start()
        h_copy(ep, chunk, 2, yn).start()
        h_copy(ep, chunk, 0, pair).start()

    def forward_chunk(copy, chunk):
        copy(xn, chunk, 1, xn).wait_recv()
        copy(yn, chunk, 2, yn).wait_recv()
        copy(passed, chunk, 3, onward).start()
        copy(xn, chunk, 4, pair).start()
        copy(yn, chunk, 5, pair).start()

    def forward_diag(copy, chunk):
        copy(diag, chunk, 3, onward).wait_recv()
        copy(diag, chunk, 6, pair).start()

    def forward_skipped():
        for n, (block, slot) in enumerate(((xn, 4), (yn, 5), (diag, 6))):
            buddy_copy(n, skipped).wait_recv()
            c_copy(block, skipped, slot, pair).start()

    def await_pair(chunk, slots):
        for copy in (h_copy, c_copy):
            for slot, block in slots:
                copy(block, chunk, slot, pair).wait_recv()

    send_chunk(0)
    forward_chunk(c_copy, order[0])
    forward_chunk(c_copy, theirs)
    buddy_copy(0, theirs).start()
    buddy_copy(1, theirs).start()
    send_chunk(1)
    forward_chunk(h_copy, order[0])

    base = routed + shared
    slab = base // 128 * 128
    lane0 = base - slab
    near_half = lax.div(ep, half)

    def tile_copies(i):
        k, side = lax.div(i, 2), lax.rem(i, 2)
        chunk = order_at(k)
        start = jnp.where(side == 0, near_half, 1 - near_half) * half
        group = pl.ds(start, half)
        slot = lax.rem(i, 2)
        stores = [
            pltpu.make_async_copy(h_all.at[chunk, group], h_out.at[chunk, group], store_sem.at[slot, 0]),
            pltpu.make_async_copy(grads_tile.at[slot], grads_out.at[chunk, group], store_sem.at[slot, 1]),
            pltpu.make_async_copy(gated_tile.at[slot], gated_out.at[chunk, group], store_sem.at[slot, 2]),
            pltpu.make_async_copy(rows_tile.at[slot], rows_out.at[chunk, group], store_sem.at[slot, 3]),
        ]
        load = pltpu.make_async_copy(cot_all.at[chunk, group], cot_tile, tile_sem)
        return chunk, start, slot, load, stores

    def step(i, _):
        k, side = lax.div(i, 2), lax.rem(i, 2)
        chunk, start, slot, load, stores = tile_copies(i)

        @pl.when(side == 0)
        def _():
            await_pair(chunk, ((0, pair), (4, twin(xn))))

        @pl.when(i == 1)
        def _():
            send_chunk(2)
            forward_chunk(c_copy, order[1])
            forward_chunk(h_copy, order[1])
            forward_diag(c_copy, order[0])
            forward_diag(c_copy, theirs)
            buddy_copy(2, theirs).start()

        @pl.when(i == 2)
        def _():
            send_chunk(3)
            forward_chunk(h_copy, order[2])

        @pl.when(i == 3)
        def _():
            forward_skipped()
            forward_chunk(h_copy, order[3])
            forward_diag(c_copy, order[1])

        @pl.when(side == 1)
        def _():
            forward_diag(h_copy, chunk)
            await_pair(chunk, ((5, twin(yn)), (6, twin(diag))))

        load.start()

        @pl.when(i >= 2)
        def _():
            for copy in tile_copies(i - 2)[4]:
                copy.wait()

        group = pl.ds(start, half)
        stores[0].start()
        for n in range(0, 2 * hidden_units, 512):
            gu[:, n : n + 512] = jnp.dot(
                h_all[chunk, group].reshape(tile, width), w_in_ref[:, n : n + 512], preferred_element_type=f32
            )
        piece = gu[:, slab : slab + 128]
        logits = piece + pltpu.roll(piece, 128 - experts, 1) + pltpu.roll(piece, 128 - 2 * experts, 1)
        is_logit = (lanes >= lane0) & (lanes < lane0 + experts)
        logits = jnp.where(is_logit, logits, -1e30)
        exps = jnp.exp(logits - jnp.max(logits, axis=-1, keepdims=True))
        probs = exps / jnp.sum(exps, axis=-1, keepdims=True)
        here = (lanes == lane0 + ep).astype(f32)
        kept = kept_ref[chunk, group].reshape(tile, 128).astype(f32)
        prob_here = jnp.sum(probs * here * kept, axis=-1, keepdims=True)
        prob_lanes[...] = jnp.broadcast_to(prob_here, (tile, 128))
        diff_lanes[...] = here - probs
        load.wait()
        act_grad[...] = lax.dot_general(
            cot_tile[...].reshape(tile, width), w_out_ref[...], (((1,), (1,)), ((), ())), preferred_element_type=f32
        )
        strip = 64

        def strips(r, _):
            at = pl.ds(pl.multiple_of(r * strip, strip), strip)
            gate_here = prob_lanes[at, :]
            pair_sum = jnp.zeros((strip, 128), f32)
            per = rows // strip
            block, inner = lax.div(r, per), pl.ds(pl.multiple_of(lax.rem(r, per) * strip, strip), strip)
            for n in range(0, hidden_units, 128):
                gate = gu[at, n : n + 128]
                up_val = gu[at, hidden_units + n : hidden_units + n + 128]
                grad = act_grad[at, n : n + 128]
                if n + 128 <= routed:
                    scale = gate_here
                elif n >= routed:
                    scale = None
                else:
                    scale = jnp.where(lanes < routed - n, gate_here, 1.0)
                sig = jax.nn.sigmoid(gate)
                silu = gate * sig
                act = silu * up_val
                if n < routed:
                    both = act * grad
                    if n + 128 > routed:
                        both = jnp.where(lanes < routed - n, both, 0.0)
                    pair_sum = pair_sum + both
                    act = act * scale
                    grad = grad * scale
                gated_tile[slot, block, inner, n : n + 128] = act.astype(bf16)
                grads_tile[slot, block, inner, n : n + 128] = (
                    grad * up_val * (sig * (1.0 + gate * (1.0 - sig)))
                ).astype(bf16)
                grads_tile[slot, block, inner, hidden_units + n : hidden_units + n + 128] = (grad * silu).astype(bf16)
            pair_lanes[at, :] = pair_sum
            return 0

        lax.fori_loop(0, tile // strip, strips, 0)
        pair_grad = jnp.sum(pair_lanes[...], axis=-1, keepdims=True)
        logit_grad = pair_grad * prob_lanes[...] * diff_lanes[...]
        logit_grad = logit_grad + pltpu.roll(logit_grad, experts, 1) + pltpu.roll(logit_grad, 2 * experts, 1)
        old = grads_tile[slot, :, :, slab : slab + 128].reshape(tile, 128)
        grads_tile[slot, :, :, slab : slab + 128] = (
            jnp.where(lanes >= lane0, logit_grad.astype(bf16), old).reshape(half, rows, 128)
        )
        for n in range(0, width, 512):
            rows_tile[slot, :, :, n : n + 512] = (
                lax.dot_general(
                    grads_tile[slot].reshape(tile, 2 * hidden_units), w_in_ref[n : n + 512, :], (((1,), (1,)), ((), ())),
                    preferred_element_type=f32,
                ).astype(bf16).reshape(half, rows, 512)
            )
        for copy in stores[1:]:
            copy.start()
        return 0

    lax.fori_loop(0, 2 * depth, step, 0)
    for i in (2 * depth - 2, 2 * depth - 1):
        for copy in tile_copies(i)[4]:
            copy.wait()
    z_drain()
    for copy in saves:
        copy.wait()
    w_out_save.wait()

    def drain(k, _):
        chunk = order_at(k)

        @pl.when(goes_up(chunk))
        def _():
            along(chunk, 0, up).wait_send()

        @pl.when(goes_down(chunk))
        def _():
            along(chunk, 1, down).wait_send()

        for slot in range(7):
            h_copy(ep, chunk, slot, pair).wait_send()
        for slot in (0, 4, 5, 6):
            c_copy(ep, chunk, slot, pair).wait_send()

        @pl.when(chunk != skipped)
        def _():
            for slot in (1, 2, 3):
                c_copy(ep, chunk, slot, pair).wait_send()

        return 0

    lax.fori_loop(0, depth, drain, 0)
    for n in range(3):
        buddy_copy(n, theirs).wait_send()


def experts_call(
    inputs, gain_attn, w_query, w_latent, gain_latent, w_up, w_output, tables, gain, cotangent, kept, e_in, e_out, s_in, s_out,
    blocks, depth, heads, shared, experts, cid,
):
    f32, bf16 = jnp.float32, jnp.bfloat16
    tokens, width = inputs.shape
    rows = tokens // depth
    routed = e_out.shape[1]
    hidden = routed + s_out.shape[0]
    rank = w_up.shape[0]
    half = blocks // 2
    tile = half * rows
    dma = pltpu.SemaphoreType.DMA
    vmem, anywhere = pl.BlockSpec(memory_space=pltpu.VMEM), pl.BlockSpec(memory_space=pl.ANY)

    def units(size):
        return jax.ShapeDtypeStruct((depth, blocks, rows, size), bf16)

    kept_sizes = (
        ((tokens, width), bf16), ((tokens, heads * NOPE), bf16), ((tokens, heads * ROPE), bf16),
        ((tokens, heads * (NOPE + VDIM)), bf16), ((2, tokens, 128), bf16), ((tokens, heads * VDIM), bf16),
        ((tokens, rank), bf16), ((tokens, rank), f32),
    )

    return pl.pallas_call(
        functools.partial(experts_kernel, depth, blocks, heads, routed, shared, experts),
        out_shape=(
            jax.ShapeDtypeStruct((rows, width), f32),
            units(width), units(width), units(2 * hidden), units(hidden), units(width),
        )
        + tuple(jax.ShapeDtypeStruct(*size) for size in kept_sizes)
        + (jax.ShapeDtypeStruct((hidden, width), bf16),),
        in_specs=[vmem] * 9 + [anywhere] * 6,
        out_specs=(vmem,) + (anywhere,) * 14,
        scratch_shapes=[
            pltpu.VMEM((tokens, width), bf16),
            *(pltpu.VMEM(*size) for size in kept_sizes),
            pltpu.VMEM((tokens, 128), f32),
            pltpu.VMEM((depth, blocks, rows, 128), bf16),
            pltpu.VMEM((width, 2 * hidden), bf16),
            pltpu.VMEM((hidden, width), bf16),
            pltpu.VMEM((2, 256, routed), bf16),
            pltpu.VMEM((depth, blocks, rows, width), bf16),
            pltpu.VMEM((depth + 1, rows, width), bf16),
            pltpu.VMEM((half, rows, width), bf16),
            pltpu.VMEM((tile, 2 * hidden), f32),
            pltpu.VMEM((tile, hidden), f32),
            pltpu.VMEM((tile, 128), f32),
            pltpu.VMEM((tile, 128), f32),
            pltpu.VMEM((tile, 128), f32),
            pltpu.VMEM((2, half, rows, 2 * hidden), bf16),
            pltpu.VMEM((2, half, rows, hidden), bf16),
            pltpu.VMEM((2, half, rows, width), bf16),
            dma((5,)), dma((2,)), dma((9,)), dma((depth,)),
            dma((depth - 1,)), dma((depth + 1,)),
            dma((depth, 2)), dma((depth,)),
            dma((depth, 7)), dma((depth, 7)),
            dma((depth, 7)), dma((depth, 7)),
            dma((3,)), dma((3,)), dma, dma((2, 4)),
        ],
        compiler_params=pltpu.CompilerParams(collective_id=cid, has_side_effects=True, vmem_limit_bytes=63 << 20),
    )(
        inputs, gain_attn.reshape(1, width), w_query, w_latent, gain_latent.reshape(1, rank), w_up, w_output, tables,
        gain.reshape(1, width), cotangent, kept, e_in, e_out, s_in, s_out,
    )


def sum_kernel(
    depth, routed, shared, experts, part_ref, h_ref, grads_ref, gated_ref, cot_ref, middle_ref, gain_ref, w_out_ref,
    middle_grad, branch, gain_part, expert_in, expert_out, s_in, s_out, router, layer_sum, landed,
    in_grad, out_grad, e_stage, s_stage,
    load, store, layer, got_pair, got_first, got_second, got_z, keep, h_tile, grads_tile, gated_tile, cot_tile,
    own_cot, load_sem, store_sem, own_sem, lps, lpr, ps, pr, fs, fr, ss, sr, zs, zr, tile_sem, e_sem, s_sem, o_sem,
):
    f32 = jnp.float32
    rows = part_ref.shape[2]
    count = h_tile.shape[0] * rows
    width = h_tile.shape[2]
    hidden = gated_tile.shape[2]
    ep, tp = lax.axis_index("ep"), lax.axis_index("tp")
    pair, xn, yn = plane_partners(ep)
    parity = lax.rem(ep, 2)
    first = jnp.where(parity == 0, xn, yn)
    second = jnp.where(parity == 0, yn, xn)
    diag = xn + yn - ep
    blocks = (first, diag, ep, second)
    pair_slot = (3, 1, 2, 0)
    greet([(pair, tp), (xn, tp), (yn, tp)] + [(ep, lax.rem(tp + k, depth)) for k in range(1, depth)])
    steps = [(k + 1) % depth for k in range(depth)]

    def chunk_of(i):
        return lax.rem(tp + steps[i], depth)

    def pair_copy(i, slot):
        src = part_ref.at[chunk_of(i), blocks[slot] + pair - ep]
        to = pair_slot[slot]
        return remote(src, got_pair.at[i, to], ps.at[i, slot], pr.at[i, to], (pair, tp))

    def pair_wait(i, slot):
        return remote(part_ref.at[0, 0], got_pair.at[i, slot], ps.at[i, slot], pr.at[i, slot], (pair, tp))

    def own_load(i, slot):
        return pltpu.make_async_copy(part_ref.at[chunk_of(i), blocks[slot]], load.at[slot], load_sem.at[slot])

    def first_copy(i, slot):
        return remote(got_pair.at[i, slot], got_first.at[i, slot], fs.at[i, slot], fr.at[i, slot], (first, tp))

    def second_copy(i):
        return remote(got_pair.at[i, 3], got_second.at[i], ss.at[i], sr.at[i], (second, tp))

    def z_copy(i):
        k = steps[i]
        return remote(got_pair.at[i, 2], got_z.at[k - 1], zs.at[k - 1], zr.at[k - 1], (ep, lax.rem(tp + k, depth)))

    far = line_order(tp)[::-1]

    def layer_pair(i, slot):
        src = layer.at[blocks[slot] + pair - ep]
        to = pair_slot[slot]
        return remote(src, landed.at[i, to], lps.at[i, slot], lpr.at[i, to], (pair, tp))

    def layer_load(i, slot):
        return pltpu.make_async_copy(landed.at[i, slot], load.at[slot], load_sem.at[slot])

    def layer_store(i, slot):
        return pltpu.make_async_copy(store.at[slot % 2], layer_sum.at[i, slot], store_sem.at[slot % 2])

    def layer_send(i):
        def columns(m, _):
            at = pl.ds(pl.multiple_of(m * 512, 512), 512)
            found = jnp.dot(gated_tile[...].reshape(count, hidden), w_out_ref[:, at], preferred_element_type=f32)
            layer[:, :, at] = found.astype(layer.dtype).reshape(layer.shape[0], rows, 512)
            return 0

        lax.fori_loop(0, width // 512, columns, 0)
        for slot in (3, 1, 2, 0):
            layer_pair(i, slot).start()

    def layer_add(i):
        for slot in range(4):
            layer_pair(i, pair_slot[slot]).wait_recv()
            layer_load(i, slot).start()
        for slot in range(4):
            layer_load(i, slot).wait()
            if slot >= 2:
                layer_store(i, slot - 2).wait()
            add_rows(store.at[slot % 2], load.at[slot], layer.at[blocks[slot]])
            layer_store(i, slot).start()
        layer_store(i, 2).wait()
        layer_store(i, 3).wait()
        for slot in range(4):
            layer_pair(i, slot).wait_send()

    for i in range(depth):
        for slot in (3, 1, 2, 0):
            pair_copy(i, slot).start()

    def tile_loads(c):
        return [
            pltpu.make_async_copy(src.at[far[c]], dst, tile_sem.at[n])
            for n, (src, dst) in enumerate(
                ((h_ref, h_tile), (grads_ref, grads_tile), (gated_ref, gated_tile), (cot_ref, cot_tile))
            )
        ]

    def stage_a(i):
        for slot in range(4):
            own_load(i, slot).start()
        for slot in range(4):
            pair_wait(i, slot).wait_recv()
            own_load(i, slot).wait()
            add_rows(got_pair.at[i, slot], got_pair.at[i, slot], load.at[slot])
            if slot < 2:
                first_copy(i, slot).start()

    def stage_b(i):
        first_copy(i, 1).wait_recv()
        add_rows(got_pair.at[i, 3], got_pair.at[i, 3], got_first.at[i, 1])
        second_copy(i).start()
        first_copy(i, 0).wait_recv()
        add_rows(got_pair.at[i, 2], got_pair.at[i, 2], got_first.at[i, 0])

    def stage_c(i):
        second_copy(i).wait_recv()
        if i < depth - 1:
            add_rows(got_pair.at[i, 2], got_pair.at[i, 2], got_second.at[i])
            z_copy(i).start()
        else:
            add_rows(keep, got_pair.at[i, 2], got_second.at[i])


    blocks_all = h_tile.shape[0]
    lanes = lax.broadcasted_iota(jnp.int32, (1, 128), 1)
    slab = routed // 128 * 128
    shift = 128 - (routed - slab)
    router_shift = (ROPE - (routed + shared) % 128) % 128

    def expert_out_copy():
        return pltpu.make_async_copy(out_grad.at[pl.ds(0, routed)], expert_out.at[0], o_sem)

    def place_copies(m):
        side = lax.rem(m, 2)
        at = pl.ds(pl.multiple_of(m * 512, 512), 512)
        per = 512 // (width // blocks_all)
        return (
            pltpu.make_async_copy(e_stage.at[side], expert_in.at[0, :, at], e_sem.at[side]),
            pltpu.make_async_copy(s_stage.at[side], s_in.at[pl.ds(m * per, per)], s_sem.at[side]),
        )

    def place(m, found):
        side = lax.rem(m, 2)

        @pl.when(m >= 2)
        def _():
            for copy in place_copies(m - 2):
                copy.wait()

        wide = width // blocks_all
        for g in range(2):
            e_stage[side, g] = found[:, g * hidden : g * hidden + routed]
            first_slab = found[:, g * hidden + slab : g * hidden + slab + 128]
            second_slab = found[:, g * hidden + slab + 128 : g * hidden + slab + 256]
            units = jnp.where(lanes < shift, pltpu.roll(first_slab, shift, 1), pltpu.roll(second_slab, shift, 1))
            s_stage[side, :, g] = units.astype(s_stage.dtype).reshape(512 // wide, wide, 128)
        last_slab = pltpu.roll(found[:, (routed + shared) // 128 * 128 : (routed + shared) // 128 * 128 + 128], router_shift, 1)
        inside = (lanes >= ROPE) & (lanes < ROPE + experts)
        router[pl.ds(pl.multiple_of(m * 512, 512), 512), :] = jnp.where(inside, last_slab, 0.0).astype(router.dtype)
        for copy in place_copies(m):
            copy.start()

    def weights(c):
        for copy in tile_loads(c):
            copy.wait()
        turned = (((0,), (0,)), ((), ()))

        last = c == depth - 1

        def in_part(m, _):
            at = pl.ds(pl.multiple_of(m * 512, 512), 512)
            found = lax.dot_general(
                h_tile[:, :, at].reshape(count, 512), grads_tile[...].reshape(count, 2 * hidden), turned,
                preferred_element_type=f32,
            )
            if c > 0:
                found = in_grad[at, :] + found
            if last:
                place(m, found)
            else:
                in_grad[at, :] = found
            return 0

        lax.fori_loop(0, width // 512, in_part, 0)

        def out_part(m, _):
            at = pl.ds(pl.multiple_of(m * 512, 512), 512)
            found = lax.dot_general(
                gated_tile[...].reshape(count, hidden), cot_tile[:, :, at].reshape(count, 512), turned,
                preferred_element_type=f32,
            )
            out_grad[:, at] = found if c == 0 else out_grad[:, at] + found
            return 0

        lax.fori_loop(0, width // 512, out_part, 0)
        if last:
            expert_out_copy().start()
            wide = width // blocks_all
            for b in range(blocks_all):
                s_out[b] = out_grad[routed : routed + s_out.shape[1], b * wide : (b + 1) * wide].astype(s_out.dtype)
        if c > 0:
            layer_add(c - 1)
        layer_send(c)
        if c + 1 < depth:
            for copy in tile_loads(c + 1):
                copy.start()

    own_copy = pltpu.make_async_copy(cot_ref.at[tp, ep], own_cot, own_sem)
    own_copy.start()
    for copy in tile_loads(0):
        copy.start()
    stage_a(0)
    stage_a(1)
    weights(0)
    stage_b(0)
    stage_a(2)
    weights(1)
    stage_b(1)
    stage_a(3)
    stage_c(0)
    weights(2)
    stage_b(2)
    stage_c(1)
    stage_b(3)
    weights(3)
    stage_c(2)
    stage_c(3)
    layer_add(depth - 1)
    for i in range(depth - 1):
        z_copy(i).wait_recv()
    own_copy.wait()

    def total(r, gain_sum):
        at = pl.ds(pl.multiple_of(r * 16, 16), 16)
        u = keep[at, :]
        for k in range(depth - 1):
            u = u + got_z[k, at, :].astype(f32)
        v = middle_ref[at, :]
        inverse = lax.rsqrt(jnp.mean(v * v, axis=-1, keepdims=True) + EPSILON)
        v_hat = v * inverse
        gain_sum = gain_sum + (u * v_hat)[:8] + (u * v_hat)[8:]
        s = u * gain_ref[...]
        back = inverse * (s - v_hat * jnp.mean(s * v_hat, axis=-1, keepdims=True))
        found = own_cot[at, :].astype(f32) + back
        middle_grad[at, :] = found
        branch[at, :] = found.astype(branch.dtype)
        return gain_sum

    gain_part[...] = lax.fori_loop(0, rows // 16, total, jnp.zeros((8, width), f32))
    expert_out_copy().wait()
    for m in (width // 512 - 2, width // 512 - 1):
        for copy in place_copies(m):
            copy.wait()
    for i in range(depth):
        for slot in range(4):
            pair_copy(i, slot).wait_send()
        for slot in range(2):
            first_copy(i, slot).wait_send()
        second_copy(i).wait_send()
        if i < depth - 1:
            z_copy(i).wait_send()


def sum_call(part, h_all, grads, gated, cot_all, middle, gain, w_out, routed, shared, experts, cid):
    f32, bf16 = jnp.float32, jnp.bfloat16
    depth, blocks, rows, width = part.shape
    hidden = gated.shape[3]
    dma = pltpu.SemaphoreType.DMA
    vmem, anywhere = pl.BlockSpec(memory_space=pltpu.VMEM), pl.BlockSpec(memory_space=pl.ANY)
    return pl.pallas_call(
        functools.partial(sum_kernel, depth, routed, shared, experts),
        out_shape=(
            jax.ShapeDtypeStruct((rows, width), f32),
            jax.ShapeDtypeStruct((rows, width), bf16),
            jax.ShapeDtypeStruct((8, width), f32),
            jax.ShapeDtypeStruct((1, 2, width, routed), f32),
            jax.ShapeDtypeStruct((1, routed, width), f32),
            jax.ShapeDtypeStruct((blocks, 2, width // blocks, 128), bf16),
            jax.ShapeDtypeStruct((blocks, -(-shared // 16) * 16, width // blocks), bf16),
            jax.ShapeDtypeStruct((width, 128), bf16),
            jax.ShapeDtypeStruct((depth, 4, rows, width), bf16),
            jax.ShapeDtypeStruct((depth, 4, rows, width), bf16),
        ),
        in_specs=[anywhere] * 5 + [vmem] * 3,
        out_specs=(vmem,) * 3 + (anywhere,) * 3 + (vmem,) * 2 + (anywhere,) * 2,
        scratch_shapes=[
            pltpu.VMEM((width, 2 * hidden), f32),
            pltpu.VMEM((hidden, width), f32),
            pltpu.VMEM((2, 2, 512, routed), f32),
            pltpu.VMEM((2, 512 // (width // blocks), 2, width // blocks, 128), bf16),
            pltpu.VMEM((4, rows, width), bf16),
            pltpu.VMEM((2, rows, width), bf16),
            pltpu.VMEM((blocks, rows, width), bf16),
            pltpu.VMEM((depth, 4, rows, width), bf16),
            pltpu.VMEM((depth, 2, rows, width), bf16),
            pltpu.VMEM((depth, rows, width), bf16),
            pltpu.VMEM((depth - 1, rows, width), bf16),
            pltpu.VMEM((rows, width), f32),
            pltpu.VMEM((blocks, rows, width), bf16),
            pltpu.VMEM((blocks, rows, 2 * hidden), bf16),
            pltpu.VMEM((blocks, rows, hidden), bf16),
            pltpu.VMEM((blocks, rows, width), bf16),
            pltpu.VMEM((rows, width), bf16),
            dma((4,)), dma((2,)), dma, dma((depth, 4)), dma((depth, 4)), dma((depth, 4)), dma((depth, 4)), dma((depth, 2)), dma((depth, 2)),
            dma((depth,)), dma((depth,)), dma((depth - 1,)), dma((depth - 1,)), dma((4,)), dma((2,)), dma((2,)), dma,
        ],
        compiler_params=pltpu.CompilerParams(collective_id=cid, has_side_effects=True, vmem_limit_bytes=62 << 20),
    )(part, h_all, grads, gated, cot_all, middle, gain.reshape(1, width), w_out)


def line_gather(ref, own, send_sem, recv_sem, ep, tp, depth):
    up, down = jnp.minimum(tp + 1, depth - 1), jnp.maximum(tp - 1, 0)
    order = line_order(tp)

    def along(k, way, to):
        chunk = order[k]
        src = own if k == 0 else ref.at[chunk]
        return remote(src, ref.at[chunk], send_sem.at[chunk, way], recv_sem.at[chunk], (ep, to))

    def each_way(k, act):
        @pl.when((order[k] <= tp) & (tp < depth - 1))
        def _():
            act(along(k, 0, up))

        @pl.when((order[k] >= tp) & (tp > 0))
        def _():
            act(along(k, 1, down))

    def pass_on(k):
        each_way(k, lambda copy: copy.start())

    def await_chunk(k):
        along(k, 0, up).wait_recv()

    def drain():
        for k in range(depth):
            each_way(k, lambda copy: copy.wait_send())

    return pass_on, await_chunk, drain


def tail_kernel(
    depth, heads, shared,
    branch_ref, middle_grad_ref, middle_ref, part_ref, router_ref, gain_part_ref, inputs_ref, s_in, s_out,
    w_output, w_query, w_latent, w_up, hidden_ref, qn_ref, qr_ref, kv_ref, kr_ref, attended, latent_in, compressed,
    tables, gain_latent, gain_attn,
    block_ref, grad_in_ref, gains_ref, query_ref, output_ref, up_ref, latent_ref, shared_in, shared_out, w_all,
    branch, held_rows, got_first, got_second, got_z, hidden_part, got_h, row_sum,
    d_out, d_kr, q_grad, kv_grad, l_grad, u_grad, w_stage, w_pair, w_first, w_second, w_z, latent_part, s_in_land, s_out_land, resid, own_grad, own_block, gains,
    load_sem, fs, fr, ss, sr, zs, zr, bs, br, hs, hr, gs, gr, os, orr,
    wps, wpr, wfs, wfr, wss, wsr, wzs, wzr, as_, ar, misc_sem, stage_sem, sis, sir, sos, sor,
):
    f32, bf16 = jnp.float32, jnp.bfloat16
    ep, tp = lax.axis_index("ep"), lax.axis_index("tp")
    pair, xn, yn = plane_partners(ep)
    parity = lax.rem(ep, 2)
    first = jnp.where(parity == 0, xn, yn)
    second = jnp.where(parity == 0, yn, xn)
    diag = xn + yn - ep
    blocks = (first, diag, ep, second)
    pair_slot = (3, 1, 2, 0)
    rows, width = middle_ref.shape
    tokens = hidden_ref.shape[0]
    rank = compressed.shape[1]
    q_cols, l_cols = q_grad.shape[1], l_grad.shape[1]
    o_rows = attended.shape[1]
    count = w_all.shape[0]
    w_rows = w_all.shape[1]
    o_cols = width // count
    u_rows = rank // count
    u_cols = w_up.shape[1]
    o_start = q_cols + l_cols
    u_start = o_start + o_rows * o_cols // w_rows
    u_wide = u_rows * u_cols // w_rows
    order = line_order(tp)
    score_scale = (NOPE + ROPE) ** (-0.5)
    plane = [ep + sum(((pair, xn, yn)[n] - ep) * (m >> n & 1) for n in range(3)) for m in range(8)]
    greet([(to, tp) for to in plane[1:]] + [(ep, lax.rem(tp + k, depth)) for k in range(1, depth)])

    branch_on, branch_wait, branch_drain = line_gather(branch, branch_ref, bs, br, ep, tp, depth)
    grad_on, grad_wait, grad_drain = line_gather(grad_in_ref, own_grad, gs, gr, ep, tp, depth)
    block_on, block_wait, block_drain = line_gather(block_ref, own_block, os, orr, ep, tp, depth)

    middle_copy = pltpu.make_async_copy(middle_ref, row_sum, misc_sem.at[3])

    def held_load(i, slot):
        return pltpu.make_async_copy(part_ref.at[i, slot], held_rows.at[i, slot - 2], load_sem.at[i, slot - 2])

    def first_copy(i, slot):
        return remote(part_ref.at[i, slot], got_first.at[i, slot], fs.at[i, slot], fr.at[i, slot], (first, tp))

    def second_copy(i):
        return remote(held_rows.at[i, 1], got_second.at[i], ss.at[i], sr.at[i], (second, tp))

    z_clear, z_start, z_pass, z_finish, z_drain = line_sum(
        lambda n: held_rows.at[n, 0], got_z, zs, zr, ep, tp, depth
    )
    far = order[::-1]
    h_clear, h_start, h_pass, h_finish, h_drain = line_sum(
        lambda n: hidden_part.at[far[n]], got_h, hs, hr, ep, tp, depth
    )

    def stage_b(i):
        held_load(i, 3).wait()
        first_copy(i, 1).wait_recv()
        add_rows(held_rows.at[i, 1], held_rows.at[i, 1], got_first.at[i, 1])
        second_copy(i).start()
        held_load(i, 2).wait()
        first_copy(i, 0).wait_recv()
        add_rows(held_rows.at[i, 0], held_rows.at[i, 0], got_first.at[i, 0])

    def stage_c(i):
        second_copy(i).wait_recv()
        if i < depth - 1:
            add_rows(held_rows.at[i, 0], held_rows.at[i, 0], got_second.at[i])
            z_start(i)
        else:
            middle_copy.wait()
            add_rows(held_rows.at[i, 0], held_rows.at[i, 0], got_second.at[i])

    def w_pair_copy(slot):
        to = pair_slot[slot]
        return remote(w_all.at[blocks[slot] + pair - ep], w_pair.at[to], wps.at[slot], wpr.at[to], (pair, tp))

    def w_pair_wait(slot):
        return remote(w_all.at[0], w_pair.at[slot], wps.at[slot], wpr.at[slot], (pair, tp))

    def w_first_copy(slot):
        return remote(w_pair.at[slot], w_first.at[slot], wfs.at[slot], wfr.at[slot], (first, tp))

    def w_second_copy():
        return remote(w_pair.at[3], w_second, wss, wsr, (second, tp))

    def w_load(slot):
        return pltpu.make_async_copy(w_all.at[blocks[slot]], w_stage.at[slot % 2], stage_sem.at[slot % 2])

    def w_stage_a():
        for slot in range(4):
            if slot < 3:
                w_load(slot + 1).start()
            w_pair_wait(slot).wait_recv()
            w_load(slot).wait()
            add_rows(w_pair.at[slot], w_pair.at[slot], w_stage.at[slot % 2])
            if slot < 2:
                w_first_copy(slot).start()

    def w_stage_b():
        w_first_copy(1).wait_recv()
        add_rows(w_pair.at[3], w_pair.at[3], w_first.at[1])
        w_second_copy().start()
        w_first_copy(0).wait_recv()
        add_rows(w_pair.at[2], w_pair.at[2], w_first.at[0])

    def w_stage_c():
        w_second_copy().wait_recv()

        def total(cols, at=slice(None)):
            return w_pair[2, at, cols].astype(f32) + w_second[at, cols].astype(f32)

        query_ref[...] = total(slice(0, q_cols))
        latent_part[...] = total(slice(q_cols, o_start))
        for n in range(o_rows // w_rows):
            output_ref[n * w_rows : (n + 1) * w_rows, :] = total(slice(o_start + n * o_cols, o_start + (n + 1) * o_cols))
        for n in range(u_cols // u_wide):
            up_ref[:, n * u_wide : (n + 1) * u_wide] = total(
                slice(u_start, u_start + u_wide), slice(n * u_rows, (n + 1) * u_rows)
            )

    def shared_copies(m):
        to = plane[m]
        return (
            remote(s_in.at[to], s_in_land.at[ep], sis.at[m], sir.at[m], (to, tp)),
            remote(s_out.at[to], s_out_land.at[ep], sos.at[m], sor.at[m], (to, tp)),
        )

    def shared_own():
        return (
            pltpu.make_async_copy(s_in.at[ep], s_in_land.at[ep], sis.at[0]),
            pltpu.make_async_copy(s_out.at[ep], s_out_land.at[ep], sos.at[0]),
        )

    def shared_place():
        for m in range(1, 8):
            for copy in shared_copies(m):
                copy.wait_recv()
        for copy in shared_own():
            copy.wait()
        for n in range(s_in_land.shape[0]):
            at = slice(n * shared, (n + 1) * shared)
            for g in range(2):
                shared_in[g, :, at] = s_in_land[n, g].astype(f32)[:, :shared]
            shared_out[at, :] = s_out_land[n].astype(f32)[:shared]

    z_clear()
    h_clear()
    branch_on(0)
    branch[tp] = branch_ref[...]
    for i in range(depth):
        first_copy(i, 1).start()
        first_copy(i, 0).start()
        held_load(i, 3).start()
        held_load(i, 2).start()
    own_rows = pl.ds(pl.multiple_of(tp * rows, rows), rows)
    resid_copy = pltpu.make_async_copy(inputs_ref.at[own_rows], resid, misc_sem.at[0])
    resid_copy.start()
    middle_copy.start()

    branch_wait(1)
    branch_on(1)
    stage_b(0)
    branch_wait(2)
    branch_on(2)
    stage_c(0)
    stage_b(1)
    branch_wait(3)
    branch_on(3)
    stage_c(1)
    z_pass(0)

    turned, across = (((0,), (0,)), ((), ())), (((1,), (1,)), ((), ()))

    def dot(a, b, dims=(((1,), (0,)), ((), ()))):
        return lax.dot_general(a, b, dims, preferred_element_type=f32)

    for c in range(depth):
        d_out[c * rows : (c + 1) * rows, :] = dot(branch[c], w_output[...], across).astype(bf16)

    lanes = lax.broadcasted_iota(jnp.int32, (1, 128), 1)
    halves = tokens // BLOCK

    def head(h, even):
        mine = (lanes < 64) if even else (lanes >= 64)
        at_q = pl.ds(pl.multiple_of(h * NOPE, 128), 128)
        at_r = pl.ds(pl.multiple_of(lax.div(h, 2) * 128, 128), 128)
        at_k = pl.ds(pl.multiple_of(h * 256, 128), 128)
        at_v = pl.ds(pl.multiple_of(h * 256 + 128, 128), 128)
        kv_sum = [None, None]
        for b in reversed(range(halves)):
            own = slice(b * BLOCK, (b + 1) * BLOCK)
            keys = slice(0, (b + 1) * BLOCK)
            qn, qr = qn_ref[own, at_q], qr_ref[own, at_r]
            kn, kr = kv_ref[keys, at_k], kr_ref[0 if even else 1, keys, :]
            scores = (dot(qn, kn, across) + dot(qr, kr, across)) * score_scale
            exps = jnp.exp(scores - jnp.max(scores, axis=-1, keepdims=True))
            probs = exps / jnp.sum(exps, axis=-1, keepdims=True)
            grad = d_out[own, at_q]
            prob_part = dot(grad, kv_ref[keys, at_v], across)
            score_grad = (probs * (prob_part - jnp.sum(probs * prob_part, axis=-1, keepdims=True))).astype(bf16)
            found = (dot(score_grad, qn, turned) * score_scale, dot(probs.astype(bf16), grad, turned))
            r_grad = jnp.where(mine, dot(score_grad, qr, turned) * score_scale, 0.0)
            for n, at in enumerate((at_k, at_v)):
                if b < halves - 1:
                    kv_sum[n] = kv_sum[n] + found[n]
                else:
                    kv_sum[n] = found[n]
                kv_grad[own, at] = kv_sum[n][b * BLOCK :].astype(bf16)
                if b > 0:
                    kv_sum[n] = kv_sum[n][: b * BLOCK]
            d_kr[keys, :] = d_kr[keys, :] + r_grad
            yield own, dot(score_grad, kn) * score_scale, dot(score_grad, kr) * score_scale

    d_kr[...] = jnp.zeros_like(d_kr)

    def head_pair(p, _):
        evens = list(head(2 * p, True))
        odds = list(head(2 * p + 1, False))
        at = [pl.ds(pl.multiple_of(p * (2 * (NOPE + ROPE)) + n, 128), 128) for n in (0, 128, 256)]
        for (own, even, even_rope), (_, odd, odd_rope) in zip(evens, odds):
            table = tuple(tables[n, own, :] for n in range(3))
            rope = turn(even_rope + odd_rope, table, -1.0)
            odd = pltpu.roll(odd, 64, 1)
            q_grad[own, at[0]] = even.astype(bf16)
            q_grad[own, at[1]] = jnp.where(lanes < 64, rope, odd).astype(bf16)
            q_grad[own, at[2]] = jnp.where(lanes < 64, odd, rope).astype(bf16)
        return 0

    def head_pairs(p, _):
        head_pair(p, 0)

        @pl.when(p == 0)
        def _():
            stage_b(2)

        return 0

    lax.fori_loop(0, heads // 2, head_pairs, 0)
    stage_c(2)
    z_pass(1)
    stage_b(3)

    latent_back = dot(kv_grad[...], w_up[...], across)
    held = compressed[...]
    inverse = lax.rsqrt(jnp.mean(held * held, axis=-1, keepdims=True) + EPSILON)
    normed = held * inverse
    gain_latent_part = jnp.sum(latent_back * normed, axis=0, keepdims=True)
    scaled = latent_back * gain_latent[...]
    l_grad[:, :rank] = (inverse * (scaled - normed * jnp.mean(scaled * normed, axis=-1, keepdims=True))).astype(bf16)
    rope = d_kr[...] + pltpu.roll(d_kr[...], 64, 1)
    rope = turn(rope, tuple(tables[n] for n in range(3)), -1.0)
    l_grad[:, rank:] = jnp.where(lanes < 64, rope, 0.0).astype(bf16)

    for n in range(0, width, 512):
        part = dot(q_grad[...], w_query[n : n + 512, :], across) + dot(l_grad[:, : rank + ROPE], w_latent[n : n + 512, :], across)
        hidden_part[:, :, n : n + 512] = part.astype(bf16).reshape(depth, rows, 512)
    for n in range(depth - 1):
        h_start(n)
    z_pass(2)
    stage_c(3)

    u_grad[...] = dot(latent_in[...], kv_grad[...], turned).astype(bf16)

    def w_store(b):
        slot = lax.rem(b, 2)
        return pltpu.make_async_copy(w_stage.at[slot], w_all.at[b], stage_sem.at[slot])

    def w_block(b, _):
        slot = lax.rem(b, 2)

        @pl.when(b >= 2)
        def _():
            w_store(b - 2).wait()

        at = pl.ds(pl.multiple_of(b * w_rows, 256), w_rows)
        own = hidden_ref[:, at]
        w_stage[slot, :, 0:q_cols] = dot(own, q_grad[...], turned).astype(bf16)
        found = dot(own, l_grad[...], turned)
        w_stage[slot, :, q_cols : q_cols + rank] = found[:, :rank].astype(bf16)
        w_stage[slot, :, q_cols + rank : o_start] = found[:, rank:].astype(bf16) + router_ref[at, :]
        cols = pl.ds(pl.multiple_of(b * o_cols, 256), o_cols)
        found = dot(attended[...], branch[:, :, cols].reshape(tokens, o_cols), turned)
        for n in range(o_rows // w_rows):
            w_stage[slot, :, o_start + n * o_cols : o_start + (n + 1) * o_cols] = (
                found[n * w_rows : (n + 1) * w_rows].astype(bf16)
            )
        u_at = pl.ds(pl.multiple_of(b * u_rows, u_rows), u_rows)
        for n in range(u_cols // u_wide):
            w_stage[slot, n * u_rows : (n + 1) * u_rows, u_start : u_start + u_wide] = (
                u_grad[u_at, n * u_wide : (n + 1) * u_wide]
            )
        w_store(b).start()
        return 0

    lax.fori_loop(0, count, w_block, 0)
    w_store(count - 2).wait()
    w_store(count - 1).wait()
    for slot in (3, 1, 2, 0):
        w_pair_copy(slot).start()
    for copy in shared_own():
        copy.start()
    for m in range(1, 8):
        for copy in shared_copies(m):
            copy.start()
    w_load(0).start()

    z_finish()

    def block_rows(r, _):
        at = pl.ds(pl.multiple_of(r * 16, 16), 16)
        value = row_sum[at, :] + held_rows[depth - 1, 0, at, :].astype(f32)
        value = value + got_z[tp, at, :].astype(f32) + got_z[depth, at, :].astype(f32)
        own_block[at, :] = value.astype(bf16)
        return 0

    lax.fori_loop(0, rows // 16, block_rows, 0)
    block_on(0)
    own_block_copy = pltpu.make_async_copy(own_block, block_ref.at[tp], misc_sem.at[2])
    own_block_copy.start()
    h_pass(0)
    w_stage_a()
    h_pass(1)
    block_wait(1)
    block_on(1)
    h_pass(2)

    resid_copy.wait()
    h_finish()

    def input_rows(r, gain_sum):
        at = pl.ds(pl.multiple_of(r * 16, 16), 16)
        u = hidden_part[tp, at, :].astype(f32)
        u = u + got_h[tp, at, :].astype(f32) + got_h[depth, at, :].astype(f32)
        v = resid[at, :].astype(f32)
        inv = lax.rsqrt(jnp.mean(v * v, axis=-1, keepdims=True) + EPSILON)
        v_hat = v * inv
        gain_sum = gain_sum + (u * v_hat)[:8] + (u * v_hat)[8:]
        s = u * gain_attn[...]
        back = inv * (s - v_hat * jnp.mean(s * v_hat, axis=-1, keepdims=True))
        own_grad[at, :] = (middle_grad_ref[at, :] + back).astype(bf16)
        return gain_sum

    gain_sum = lax.fori_loop(0, rows // 16, input_rows, jnp.zeros((8, width), f32))
    grad_on(0)
    own_grad_copy = pltpu.make_async_copy(own_grad, grad_in_ref.at[tp], misc_sem.at[1])
    own_grad_copy.start()

    gains[0] = jnp.zeros_like(gains[0])
    gains[0, 0:1, :] = jnp.sum(gain_sum, axis=0, keepdims=True)
    gains[0, 1:2, :] = jnp.sum(gain_part_ref[...], axis=0, keepdims=True)
    gains[0, 2:3, 0:rank] = gain_latent_part
    flip_1 = tp + 1 - 2 * lax.rem(tp, 2)
    flip_2 = tp + 2 - 4 * lax.div(tp, 2)
    partners = ((pair, tp), (xn, tp), (yn, tp), (ep, flip_1), (ep, flip_2))

    def gain_copy(n):
        return remote(gains.at[2 * n], gains.at[2 * n + 1], as_.at[n], ar.at[n], partners[n])

    def gain_step(n):
        gain_copy(n).wait_recv()
        total = gains[2 * n] + gains[2 * n + 1]
        if n + 1 < len(partners):
            gains[2 * n + 2] = total
            gain_copy(n + 1).start()
        else:
            gains_ref[...] = total

    gain_copy(0).start()
    block_wait(2)
    block_on(2)
    w_stage_b()
    gain_step(0)
    grad_wait(1)
    grad_on(1)
    gain_step(1)
    w_stage_c()
    w_part = w_rows // depth

    def w_z_copy(k):
        to = lax.rem(tp + k, depth)
        src = w_pair.at[1, pl.ds(pl.multiple_of(to * w_part, w_part), w_part), pl.ds(q_cols, l_cols)]
        return remote(src, w_z.at[k - 1], wzs.at[k - 1], wzr.at[k - 1], (ep, to))

    w_first_copy(1).wait_send()
    w_pair[1, :, q_cols:o_start] = latent_part[...].astype(bf16)
    for k in range(1, depth):
        w_z_copy(k).start()
    grad_wait(2)
    grad_on(2)
    gain_step(2)
    block_wait(3)
    block_on(3)
    gain_step(3)
    shared_place()
    gain_step(4)
    for k in range(1, depth):
        w_z_copy(k).wait_recv()
    own = pl.ds(pl.multiple_of(tp * w_part, w_part), w_part)
    total = latent_part[own, :]
    for k in range(depth - 1):
        total = total + w_z[k].astype(f32)
    latent_ref[...] = total
    grad_wait(3)
    grad_on(3)

    own_grad_copy.wait()
    own_block_copy.wait()
    branch_drain()
    grad_drain()
    block_drain()
    for i in range(depth):
        for slot in range(2):
            first_copy(i, slot).wait_send()
        second_copy(i).wait_send()
    z_drain()
    h_drain()
    for slot in range(4):
        w_pair_copy(slot).wait_send()
    w_first_copy(0).wait_send()
    w_second_copy().wait_send()
    for k in range(1, depth):
        w_z_copy(k).wait_send()
    for n in range(len(partners)):
        gain_copy(n).wait_send()
    for m in range(1, 8):
        for copy in shared_copies(m):
            copy.wait_send()


def tail_call(
    branch, middle_grad, middle, out_part, router, gain_part, inputs, s_in, s_out, w_output, w_query, w_latent, w_up,
    hidden, qn, qr, kv, kr, attended, latent_in, compressed, tables, gain_latent, gain_attn,
    heads, shared, cid,
):
    f32, bf16 = jnp.float32, jnp.bfloat16
    depth, _, rows, width = out_part.shape
    tokens = hidden.shape[0]
    blocks = s_in.shape[0]
    rank = compressed.shape[1]
    q_cols, l_cols = w_query.shape[1], rank + 128
    w_rows = width // blocks
    w_cols = q_cols + l_cols + w_output.shape[0] + rank * w_up.shape[1] // width
    dma = pltpu.SemaphoreType.DMA
    vmem, anywhere = pl.BlockSpec(memory_space=pltpu.VMEM), pl.BlockSpec(memory_space=pl.ANY)
    return pl.pallas_call(
        functools.partial(tail_kernel, depth, heads, shared),
        out_shape=(
            jax.ShapeDtypeStruct((depth, rows, width), bf16),
            jax.ShapeDtypeStruct((depth, rows, width), bf16),
            jax.ShapeDtypeStruct((8, width), f32),
            jax.ShapeDtypeStruct((w_rows, q_cols), f32),
            jax.ShapeDtypeStruct((w_output.shape[0], w_rows), f32),
            jax.ShapeDtypeStruct((rank // blocks, w_up.shape[1]), f32),
            jax.ShapeDtypeStruct((w_rows // depth, l_cols), f32),
            jax.ShapeDtypeStruct((2, w_rows, blocks * shared), f32),
            jax.ShapeDtypeStruct((blocks * shared, w_rows), f32),
            jax.ShapeDtypeStruct((blocks, w_rows, w_cols), bf16),
        ),
        in_specs=[vmem, vmem, anywhere, anywhere, vmem, vmem, anywhere, anywhere, anywhere] + [vmem] * 15,
        out_specs=(anywhere, anywhere) + (vmem,) * 7 + (anywhere,),
        scratch_shapes=[
            pltpu.VMEM((depth, rows, width), bf16),
            pltpu.VMEM((depth, 2, rows, width), bf16),
            pltpu.VMEM((depth, 2, rows, width), bf16),
            pltpu.VMEM((depth, rows, width), bf16),
            pltpu.VMEM((depth + 1, rows, width), bf16),
            pltpu.VMEM((depth, rows, width), bf16),
            pltpu.VMEM((depth + 1, rows, width), bf16),
            pltpu.VMEM((rows, width), f32),
            pltpu.VMEM((tokens, heads * VDIM), bf16),
            pltpu.VMEM((tokens, 128), f32),
            pltpu.VMEM((tokens, q_cols), bf16),
            pltpu.VMEM((tokens, heads * (NOPE + VDIM)), bf16),
            pltpu.VMEM((tokens, l_cols), bf16),
            pltpu.VMEM((rank, heads * (NOPE + VDIM)), bf16),
            pltpu.VMEM((2, w_rows, w_cols), bf16),
            pltpu.VMEM((4, w_rows, w_cols), bf16),
            pltpu.VMEM((2, w_rows, w_cols), bf16),
            pltpu.VMEM((w_rows, w_cols), bf16),
            pltpu.VMEM((depth - 1, w_rows // depth, l_cols), bf16),
            pltpu.VMEM((w_rows, l_cols), f32),
            pltpu.VMEM(s_in.shape, bf16),
            pltpu.VMEM(s_out.shape, bf16),
            pltpu.VMEM((rows, width), bf16),
            pltpu.VMEM((rows, width), bf16),
            pltpu.VMEM((rows, width), bf16),
            pltpu.VMEM((10, 8, width), f32),
            dma((depth, 2)),
            dma((depth, 2)), dma((depth, 2)), dma((depth,)), dma((depth,)),
            dma((depth - 1,)), dma((depth + 1,)),
            dma((depth, 2)), dma((depth,)),
            dma((depth - 1,)), dma((depth + 1,)),
            dma((depth, 2)), dma((depth,)),
            dma((depth, 2)), dma((depth,)),
            dma((4,)), dma((4,)), dma((2,)), dma((2,)), dma, dma, dma((depth - 1,)), dma((depth - 1,)),
            dma((5,)), dma((5,)), dma((4,)), dma((2,)), dma((8,)), dma((8,)), dma((8,)), dma((8,)),
        ],
        compiler_params=pltpu.CompilerParams(collective_id=cid, has_side_effects=True, vmem_limit_bytes=63 << 20),
    )(
        branch, middle_grad, middle, out_part, router, gain_part, inputs, s_in, s_out, w_output, w_query, w_latent, w_up,
        hidden, qn, qr, kv, kr, attended, latent_in, compressed, tables,
        gain_latent.reshape(1, rank), gain_attn.reshape(1, width),
    )


def rope_tables(length):
    half = ROPE // 2
    inverse = np.exp(np.arange(half) * (-math.log(10000.0) / half))
    angle = np.arange(length)[:, None] * inverse[None, :]
    cosine, sine = np.cos(angle), np.sin(angle)
    zero = np.zeros_like(sine)
    parts = ([cosine] * 4, [-sine, zero] * 2, [zero, sine] * 2)
    return jnp.asarray(np.stack([np.concatenate(p, axis=1) for p in parts]), jnp.float32)


def padded_hidden(routed, shared):
    return -(-(routed + shared + 24) // 128) * 128


def split_wide(values):
    high = values.astype(jnp.bfloat16)
    rest = values - high.astype(jnp.float32)
    mid = rest.astype(jnp.bfloat16)
    low = (rest - mid.astype(jnp.float32)).astype(jnp.bfloat16)
    return (high, mid, low)


def body_dense(
    inputs,
    gain_attn,
    w_query,
    w_latent,
    gain_latent,
    w_latent_up,
    w_output,
    gain_ffn,
    w_router,
    w_shared_in,
    w_shared_out,
    w_expert_in,
    w_expert_out,
    expert_ids,
    slot_ids,
    cotangent,
):
    f32, bf16 = jnp.float32, jnp.bfloat16
    tokens, model_width = inputs.shape
    ep_count, tp_count = lax.axis_size("ep"), lax.axis_size("tp")
    ep_index, tp_index = lax.axis_index("ep"), lax.axis_index("tp")
    heads_here = w_output.shape[0] // VDIM
    experts = w_router.shape[1]
    capacity = (9 * tokens * TOPK + 64 * experts - 1) // (64 * experts) * 8
    qk_width = NOPE + ROPE
    score_scale = qk_width ** (-0.5)
    rows_part = tokens // tp_count

    expert_range = jnp.arange(experts, dtype=jnp.int32)
    kept = jnp.any(
        (expert_ids[:, :, None] == expert_range) & (slot_ids < capacity)[:, :, None], axis=1
    ).astype(f32)
    kept_here = lax.all_to_all(kept, "ep", split_axis=1, concat_axis=0, tiled=True)
    rows_part = tokens // tp_count
    kept_lanes = jnp.broadcast_to(
        kept_here.reshape(ep_count, tp_count, rows_part, 1).swapaxes(0, 1),
        (tp_count, ep_count, rows_part, 128),
    ).astype(bf16)

    routed = w_expert_in.shape[3]
    shared = w_shared_in.shape[2] // ep_count
    hidden = padded_hidden(routed, shared)
    shared_start = ep_index * shared
    slab = routed // 128 * 128
    before, after = routed - slab, hidden - routed - shared
    router_parts = jnp.concatenate(split_wide(w_router), axis=1)
    beside = jnp.stack(
        [
            jnp.pad(router_parts, ((0, 0), (0, after - router_parts.shape[1]))),
            jnp.zeros((model_width, after), bf16),
        ]
    )
    shared_in = lax.dynamic_slice_in_dim(w_shared_in, shared_start, shared, 2)
    shared_in = jnp.concatenate([jnp.zeros((2, model_width, before), bf16), shared_in, beside], axis=2)
    shared_out = lax.dynamic_slice_in_dim(w_shared_out, shared_start, shared, 0)
    shared_out = jnp.pad(shared_out, ((0, after), (0, 0)))
    tables = rope_tables(tokens)
    (
        middle, hidden_all, cot_all, hidden_grads, gated, rows_grad,
        hidden_attn, query_nope, query_rope, key_value, key_pair, attended, latent_in, compressed, w_out,
    ) = experts_call(
        inputs, gain_attn, w_query, w_latent, gain_latent, w_latent_up, w_output, tables, gain_ffn, cotangent, kept_lanes,
        w_expert_in, w_expert_out, shared_in, shared_out, ep_count, tp_count, heads_here, shared, experts, 0,
    )
    middle_grad, branch, gain_ffn_part, grad_expert_in, grad_expert_out, shared_in_part, shared_out_part, router_part, layer_sum, _ = (
        sum_call(
            rows_grad, hidden_all, hidden_grads, gated, cot_all, middle, gain_ffn, w_out, routed, shared, experts, 1
        )
    )
    block_out, grad_inputs, gains, grad_query, grad_output, grad_latent_up, latent_sum, grad_shared_in, grad_shared_out, _ = (
        tail_call(
            branch, middle_grad, middle, layer_sum, router_part, gain_ffn_part, inputs, shared_in_part, shared_out_part,
            w_output, w_query, w_latent, w_latent_up, hidden_attn,
            query_nope, query_rope, key_value, key_pair,
            attended, latent_in, compressed, tables, gain_latent, gain_attn, heads_here, shared, 2,
        )
    )
    grad_latent = latent_sum[:, : KV_RANK + ROPE]
    grad_router = latent_sum[:, KV_RANK + ROPE : KV_RANK + ROPE + experts]
    flat = ep_index * tp_count + tp_index
    wide_part, rank_part = (n // (ep_count * tp_count) for n in (model_width, KV_RANK))
    grad_gain_attn = lax.dynamic_slice_in_dim(gains[0], flat * wide_part, wide_part, 0)
    grad_gain_ffn = lax.dynamic_slice_in_dim(gains[1], flat * wide_part, wide_part, 0)
    grad_gain_latent = lax.dynamic_slice_in_dim(gains[2], flat * rank_part, rank_part, 0)
    block_out = block_out.reshape(tokens, model_width)
    grad_inputs = grad_inputs.reshape(tokens, model_width)
    return (
        block_out,
        grad_inputs,
        grad_gain_attn,
        grad_query,
        grad_latent,
        grad_gain_latent,
        grad_latent_up,
        grad_output,
        grad_gain_ffn,
        grad_router,
        grad_shared_in,
        grad_shared_out,
        grad_expert_in,
        grad_expert_out,
    )


def solution(mesh):
    near = mesh.shape["ep"] == 8 and mesh.shape["tp"] == 4
    body = body_dense if near else body_slots
    placed = (
        P("ep", None),
        P(),
        P(None, "tp"),
        P(),
        P(),
        P(None, "tp"),
        P("tp", None),
        P(),
        P(),
        P(None, None, "tp"),
        P("tp", None),
        P("ep", None, None, "tp"),
        P("ep", "tp", None),
        P("ep", None),
        P("ep", None),
        P("ep", None),
    )
    return jax.shard_map(
        body,
        mesh=mesh,
        in_specs=placed,
        out_specs=(
            P("ep", None),
            P("ep", None),
            P(("ep", "tp")),
            P("ep", "tp"),
            P(("ep", "tp"), None),
            P(("ep", "tp")),
            P("ep", "tp"),
            P("tp", "ep"),
            P(("ep", "tp")),
            P(("ep", "tp"), None),
            P(None, "ep", "tp"),
            P("tp", "ep"),
            P("ep", None, None, "tp"),
            P("ep", "tp", None),
        ),
        check_vma=False,
    )
```

```python
import functools
import math

import jax
import jax.numpy as jnp
import numpy as np
from jax import lax
from jax.experimental import pallas as pl
from jax.experimental.pallas import tpu as pltpu
from jax.sharding import PartitionSpec as P

NOPE = 128
ROPE = 64
VDIM = 128
KV_RANK = 512
TOPK = 6
BLOCK = 256


EPSILON = 1e-06
HIGHEST = lax.Precision.HIGHEST


def angles(length, rope_width):
    half_width = rope_width // 2
    position = jnp.arange(length, dtype=jnp.float32)
    inverse = jnp.exp(jnp.arange(half_width, dtype=jnp.float32) * (-math.log(10000.0) / half_width))
    angle_table = position[:, None] * inverse[None, :]
    return (jnp.cos(angle_table), jnp.sin(angle_table))


def rotate(values, cosine, sine_table):
    half_width = values.shape[-1] // 2
    front_part = values[..., :half_width]
    second = values[..., half_width:]
    return jnp.concatenate(
        [front_part * cosine - second * sine_table, second * cosine + front_part * sine_table],
        axis=-1,
    )


def silu_parts(gate_val):
    sigmoid_val = jax.nn.sigmoid(gate_val)
    return (gate_val * sigmoid_val, sigmoid_val * (1.0 + gate_val * (1.0 - sigmoid_val)))


def norm_back(grad_norm, gain_vec, normed, inverse):
    scaled = grad_norm * gain_vec
    return inverse * (scaled - normed * jnp.mean(scaled * normed, axis=-1, keepdims=True))


def attention_scores(query_rot, key_nope, key_rope, score_scale, allowed):
    nope_scores = jnp.einsum(
        "qhd,khd->hqk", query_rot[..., :NOPE], key_nope, preferred_element_type=jnp.float32
    )
    rope_scores = jnp.einsum(
        "qhr,kr->hqk", query_rot[..., NOPE:], key_rope, preferred_element_type=jnp.float32
    )
    return jnp.where(allowed[None], (nope_scores + rope_scores) * score_scale, -1e30)


def expert_forward(received, w_expert_in, w_expert_out, sources):
    sectioned = received.reshape(sources, -1, received.shape[1], received.shape[2])
    gate_up = jnp.einsum(
        "secd,egdh->secgh", sectioned, w_expert_in, preferred_element_type=jnp.float32
    )
    gate_val, gate_slope = silu_parts(gate_up[..., 0, :])
    activated = (gate_val * gate_up[..., 1, :]).astype(jnp.bfloat16)
    produced = jnp.einsum(
        "sech,ehd->secd", activated, w_expert_out, preferred_element_type=jnp.float32
    )
    return (sectioned, gate_up, activated, produced.reshape(received.shape))


def body_slots(
    inputs,
    gain_attn,
    w_query,
    w_latent,
    gain_latent,
    w_latent_up,
    w_output,
    gain_ffn,
    w_router,
    w_shared_in,
    w_shared_out,
    w_expert_in,
    w_expert_out,
    expert_ids,
    slot_ids,
    cotangent,
):
    tokens, model_width = inputs.shape
    tp_count = lax.axis_size("tp")
    tp_index = lax.axis_index("tp")
    heads_here = w_output.shape[0] // VDIM
    experts = w_router.shape[1]
    local_experts = w_expert_in.shape[0]
    sources = experts // local_experts
    capacity = (9 * tokens * TOPK + 64 * experts - 1) // (64 * experts) * 8
    qk_width = NOPE + ROPE
    score_scale = qk_width ** (-0.5)
    rows_part = tokens // tp_count
    row_start = tp_index * rows_part
    resid = inputs.astype(jnp.float32)
    inv_first = lax.rsqrt(jnp.mean(resid * resid, axis=-1, keepdims=True) + EPSILON)
    normed_first = resid * inv_first
    hidden_attn = (normed_first * gain_attn).astype(jnp.bfloat16)
    cosine, sine_table = angles(tokens, ROPE)
    query_raw = jnp.dot(hidden_attn, w_query, preferred_element_type=jnp.float32).reshape(
        tokens, heads_here, qk_width
    )
    query_rot = jnp.concatenate(
        [
            query_raw[..., :NOPE],
            rotate(query_raw[..., NOPE:], cosine[:, None], sine_table[:, None]),
        ],
        axis=-1,
    ).astype(jnp.bfloat16)
    latent = jnp.dot(hidden_attn, w_latent, preferred_element_type=jnp.float32)
    compressed = latent[:, :KV_RANK]
    inv_latent = lax.rsqrt(jnp.mean(compressed * compressed, axis=-1, keepdims=True) + EPSILON)
    normed_latent = compressed * inv_latent
    latent_in = (normed_latent * gain_latent).astype(jnp.bfloat16)
    key_rope = rotate(latent[:, KV_RANK:], cosine, sine_table).astype(jnp.bfloat16)
    key_value = (
        jnp.dot(latent_in, w_latent_up, preferred_element_type=jnp.float32)
        .astype(jnp.bfloat16)
        .reshape(tokens, heads_here, NOPE + VDIM)
    )
    key_nope = key_value[..., :NOPE]
    values = key_value[..., NOPE:]
    block_ids = jnp.arange(tokens) // BLOCK
    allowed = block_ids[None, :] <= block_ids[:, None]
    scores = attention_scores(query_rot, key_nope, key_rope, score_scale, allowed)
    row_peak = jnp.max(scores, axis=-1, keepdims=True)
    exp_scores = jnp.exp(scores - row_peak)
    totals = jnp.sum(exp_scores, axis=-1, keepdims=True)
    attn_probs = exp_scores / totals
    log_total = row_peak + jnp.log(totals)
    attended = (
        jnp.einsum(
            "hqk,khd->qhd",
            attn_probs.astype(jnp.bfloat16),
            values,
            preferred_element_type=jnp.float32,
        )
        .astype(jnp.bfloat16)
        .reshape(tokens, heads_here * VDIM)
    )
    attn_full = lax.psum(
        jnp.dot(attended, w_output, preferred_element_type=jnp.float32).astype(jnp.bfloat16), "tp"
    ).astype(jnp.float32)
    middle = resid + attn_full
    inv_second = lax.rsqrt(jnp.mean(middle * middle, axis=-1, keepdims=True) + EPSILON)
    normed_second = middle * inv_second
    hidden_ffn = (normed_second * gain_ffn).astype(jnp.bfloat16)
    hidden_wide = hidden_ffn.astype(jnp.float32)
    logits = jnp.dot(hidden_wide, w_router, precision=HIGHEST, preferred_element_type=jnp.float32)
    logit_peak = jnp.max(logits, axis=-1, keepdims=True)
    exp_logits = jnp.exp(logits - logit_peak)
    router_probs = exp_logits / jnp.sum(exp_logits, axis=-1, keepdims=True)
    route_onehot = (
        expert_ids[:, :, None] == jnp.arange(experts, dtype=jnp.int32)[None, None, :]
    ).astype(jnp.float32)
    pair_gate = jnp.sum(route_onehot * router_probs[:, None, :], axis=-1)
    kept_pair = slot_ids < capacity
    flat_index = jnp.where(kept_pair, expert_ids * capacity + slot_ids, experts * capacity)
    row_numbers = jnp.broadcast_to(jnp.arange(tokens, dtype=jnp.int32)[:, None], (tokens, TOPK))
    owner_row = (
        jnp.full((experts * capacity,), tokens, jnp.int32)
        .at[flat_index.reshape(-1)]
        .set(row_numbers.reshape(-1), mode="drop")
    )
    outgoing = jnp.take(hidden_ffn, owner_row, axis=0, mode="fill", fill_value=0).reshape(
        experts, capacity, model_width
    )
    received = lax.all_to_all(outgoing, "ep", split_axis=0, concat_axis=0, tiled=True)
    sectioned, gate_up, activated, produced = expert_forward(
        received, w_expert_in, w_expert_out, sources
    )
    returned = lax.all_to_all(
        produced.astype(jnp.bfloat16), "ep", split_axis=0, concat_axis=0, tiled=True
    ).astype(produced.dtype)
    out_grad = cotangent.astype(jnp.float32)
    back_rows = returned.reshape(-1, model_width)
    combined = jnp.zeros((tokens, model_width), jnp.float32)
    gate_cols = []
    for pick_index in range(TOPK):
        taken_rows = jnp.take(
            back_rows, flat_index[:, pick_index], axis=0, mode="fill", fill_value=0.0
        )
        combined = combined + pair_gate[:, pick_index : pick_index + 1] * taken_rows
        gate_cols.append(jnp.sum(out_grad * taken_rows, axis=-1))
    gate_grad = jnp.stack(gate_cols, axis=1)
    shared_gate = jnp.dot(hidden_ffn, w_shared_in[0], preferred_element_type=jnp.float32)
    shared_up = jnp.dot(hidden_ffn, w_shared_in[1], preferred_element_type=jnp.float32)
    shared_val, shared_slope = silu_parts(shared_gate)
    shared_act = (shared_val * shared_up).astype(jnp.bfloat16)
    branch_part = jnp.dot(shared_act, w_shared_out, preferred_element_type=jnp.float32) + combined
    ffn_full = lax.psum(branch_part.astype(jnp.bfloat16), "tp").astype(jnp.float32)
    block_out = (middle + ffn_full).astype(jnp.bfloat16)
    slot_gate = (
        jnp.zeros((experts * capacity,), jnp.float32)
        .at[flat_index.reshape(-1)]
        .set(pair_gate.reshape(-1), mode="drop")
    )
    gathered_grad = jnp.take(cotangent, owner_row, axis=0, mode="fill", fill_value=0)
    slot_grad = (
        (slot_gate[:, None] * gathered_grad.astype(jnp.float32))
        .astype(jnp.bfloat16)
        .reshape(experts, capacity, model_width)
    )
    grad_arrived = lax.all_to_all(slot_grad, "ep", split_axis=0, concat_axis=0, tiled=True).reshape(
        sectioned.shape
    )
    act_grad = jnp.einsum(
        "secd,ehd->sech", grad_arrived, w_expert_out, preferred_element_type=jnp.float32
    )
    gate_val, gate_slope = silu_parts(gate_up[..., 0, :])
    up_val = gate_up[..., 1, :]
    gu_grad = jnp.stack([act_grad * up_val * gate_slope, act_grad * gate_val], axis=-2).astype(
        jnp.bfloat16
    )
    grad_expert_out = jnp.einsum(
        "sech,secd->ehd", activated, grad_arrived, preferred_element_type=jnp.float32
    )
    grad_expert_in = jnp.einsum(
        "secd,secgh->egdh", sectioned, gu_grad, preferred_element_type=jnp.float32
    )
    rows_grad = jnp.einsum(
        "secgh,egdh->secd", gu_grad, w_expert_in, preferred_element_type=jnp.float32
    ).reshape(received.shape)
    returned_grad = (
        lax.all_to_all(
            rows_grad.astype(jnp.bfloat16), "ep", split_axis=0, concat_axis=0, tiled=True
        )
        .astype(rows_grad.dtype)
        .reshape(-1, model_width)
    )
    routed_grad = jnp.zeros((tokens, model_width), jnp.float32)
    for pick_index in range(TOPK):
        routed_grad = routed_grad + jnp.take(
            returned_grad, flat_index[:, pick_index], axis=0, mode="fill", fill_value=0.0
        )
    shared_act_grad = jnp.einsum(
        "td,fd->tf", cotangent, w_shared_out, preferred_element_type=jnp.float32
    )
    shared_gate_grad = (shared_act_grad * shared_up * shared_slope).astype(jnp.bfloat16)
    shared_up_grad = (shared_act_grad * shared_val).astype(jnp.bfloat16)
    shared_out_grad = jnp.einsum(
        "tf,td->fd", shared_act, cotangent, preferred_element_type=jnp.float32
    )
    shared_in_grad = jnp.stack(
        [
            jnp.einsum(
                "td,tf->df", hidden_ffn, shared_gate_grad, preferred_element_type=jnp.float32
            ),
            jnp.einsum("td,tf->df", hidden_ffn, shared_up_grad, preferred_element_type=jnp.float32),
        ],
        axis=0,
    )
    shared_back = jnp.einsum(
        "tf,df->td", shared_gate_grad, w_shared_in[0], preferred_element_type=jnp.float32
    ) + jnp.einsum("tf,df->td", shared_up_grad, w_shared_in[1], preferred_element_type=jnp.float32)
    prob_grad = jnp.sum(route_onehot * gate_grad[:, :, None], axis=1)
    logit_grad = router_probs * (
        prob_grad - jnp.sum(router_probs * prob_grad, axis=-1, keepdims=True)
    )
    router_back = jnp.einsum(
        "te,de->td", logit_grad, w_router, precision=HIGHEST, preferred_element_type=jnp.float32
    )
    router_grad = jnp.einsum(
        "td,te->de", hidden_wide, logit_grad, precision=HIGHEST, preferred_element_type=jnp.float32
    )
    ffn_grad = lax.psum(
        (shared_back + routed_grad + router_back).astype(jnp.bfloat16), "tp"
    ).astype(jnp.float32)
    middle_grad = out_grad + norm_back(ffn_grad, gain_ffn, normed_second, inv_second)
    gain_ffn_grad = jnp.sum(
        lax.dynamic_slice_in_dim(ffn_grad * normed_second, row_start, rows_part, 0), axis=0
    )
    branch_grad = middle_grad.astype(jnp.bfloat16)
    output_w_grad = jnp.einsum(
        "tf,td->fd", attended, branch_grad, preferred_element_type=jnp.float32
    )
    attended_grad = (
        jnp.einsum("td,fd->tf", branch_grad, w_output, preferred_element_type=jnp.float32)
        .astype(jnp.bfloat16)
        .reshape(tokens, heads_here, VDIM)
    )
    scores_again = attention_scores(query_rot, key_nope, key_rope, score_scale, allowed)
    probs_again = jnp.exp(scores_again - log_total)
    values_grad = jnp.einsum(
        "hqk,qhd->khd",
        probs_again.astype(jnp.bfloat16),
        attended_grad,
        preferred_element_type=jnp.float32,
    )
    prob_part = jnp.einsum(
        "qhd,khd->hqk", attended_grad, values, preferred_element_type=jnp.float32
    )
    score_grad = (
        probs_again * (prob_part - jnp.sum(probs_again * prob_part, axis=-1, keepdims=True))
    ).astype(jnp.bfloat16)
    query_nope_grad = (
        jnp.einsum("hqk,khd->qhd", score_grad, key_nope, preferred_element_type=jnp.float32)
        * score_scale
    )
    query_rope_grad = (
        jnp.einsum("hqk,kr->qhr", score_grad, key_rope, preferred_element_type=jnp.float32)
        * score_scale
    )
    key_nope_grad = (
        jnp.einsum(
            "hqk,qhd->khd", score_grad, query_rot[..., :NOPE], preferred_element_type=jnp.float32
        )
        * score_scale
    )
    key_rope_grad = (
        jnp.einsum(
            "hqk,qhr->kr", score_grad, query_rot[..., NOPE:], preferred_element_type=jnp.float32
        )
        * score_scale
    )
    kv_grad = (
        jnp.concatenate([key_nope_grad, values_grad], axis=-1)
        .astype(jnp.bfloat16)
        .reshape(tokens, heads_here * (NOPE + VDIM))
    )
    latent_up_grad = jnp.einsum("tr,tf->rf", latent_in, kv_grad, preferred_element_type=jnp.float32)
    latent_in_grad = jnp.einsum(
        "tf,rf->tr", kv_grad, w_latent_up, preferred_element_type=jnp.float32
    )
    gain_latent_grad = jnp.sum(latent_in_grad * normed_latent, axis=0)
    latent_grad_part = jnp.concatenate(
        [
            norm_back(latent_in_grad, gain_latent, normed_latent, inv_latent),
            rotate(key_rope_grad, cosine, -sine_table),
        ],
        axis=-1,
    )
    query_grad = (
        jnp.concatenate(
            [query_nope_grad, rotate(query_rope_grad, cosine[:, None], -sine_table[:, None])],
            axis=-1,
        )
        .astype(jnp.bfloat16)
        .reshape(tokens, heads_here * qk_width)
    )
    query_w_grad = jnp.einsum(
        "td,tf->df", hidden_attn, query_grad, preferred_element_type=jnp.float32
    )
    hidden_part = jnp.einsum("tf,df->td", query_grad, w_query, preferred_element_type=jnp.float32)
    hidden_sum, latent_sum = (
        lax.psum(hidden_part.astype(jnp.bfloat16), "tp").astype(jnp.float32),
        lax.psum(latent_grad_part.astype(jnp.bfloat16), "tp").astype(jnp.float32),
    )
    latent_low = latent_sum.astype(jnp.bfloat16)
    attn_in_grad = hidden_sum + jnp.einsum(
        "tf,df->td", latent_low, w_latent, preferred_element_type=jnp.float32
    )
    latent_w_grad = jnp.einsum(
        "td,tf->df",
        lax.dynamic_slice_in_dim(hidden_attn, row_start, rows_part, 0),
        lax.dynamic_slice_in_dim(latent_low, row_start, rows_part, 0),
        preferred_element_type=jnp.float32,
    )
    gain_attn_grad = jnp.sum(
        lax.dynamic_slice_in_dim(attn_in_grad * normed_first, row_start, rows_part, 0), axis=0
    )
    grad_inputs = (
        middle_grad + norm_back(attn_in_grad, gain_attn, normed_first, inv_first)
    ).astype(jnp.bfloat16)
    grad_query, grad_latent_up, grad_output, grad_shared_in, grad_shared_out = (
        lax.psum_scatter(
            query_w_grad.astype(jnp.bfloat16), "ep", scatter_dimension=0, tiled=True
        ).astype(jnp.float32),
        lax.psum_scatter(
            latent_up_grad.astype(jnp.bfloat16), "ep", scatter_dimension=0, tiled=True
        ).astype(jnp.float32),
        lax.psum_scatter(
            output_w_grad.astype(jnp.bfloat16), "ep", scatter_dimension=1, tiled=True
        ).astype(jnp.float32),
        lax.psum_scatter(
            shared_in_grad.astype(jnp.bfloat16), "ep", scatter_dimension=1, tiled=True
        ).astype(jnp.float32),
        lax.psum_scatter(
            shared_out_grad.astype(jnp.bfloat16), "ep", scatter_dimension=1, tiled=True
        ).astype(jnp.float32),
    )
    grad_latent, grad_gain_latent, grad_gain_attn, grad_gain_ffn, grad_router = (
        lax.psum_scatter(latent_w_grad, ("ep", "tp"), scatter_dimension=0, tiled=True),
        lax.psum_scatter(gain_latent_grad, ("ep", "tp"), scatter_dimension=0, tiled=True),
        lax.psum_scatter(gain_attn_grad, ("ep", "tp"), scatter_dimension=0, tiled=True),
        lax.psum_scatter(gain_ffn_grad, ("ep", "tp"), scatter_dimension=0, tiled=True),
        lax.psum_scatter(router_grad, ("ep", "tp"), scatter_dimension=0, tiled=True),
    )
    return (
        block_out,
        grad_inputs,
        grad_gain_attn,
        grad_query,
        grad_latent,
        grad_gain_latent,
        grad_latent_up,
        grad_output,
        grad_gain_ffn,
        grad_router,
        grad_shared_in,
        grad_shared_out,
        grad_expert_in,
        grad_expert_out,
    )


MESH = pl.DeviceIdType.MESH


def plane_partners(ep):
    def flip(bit):
        return ep + bit - 2 * bit * lax.rem(lax.div(ep, bit), 2)

    return flip(1), flip(2), flip(4)


def line_order(tp):
    def pick(a, b, c, d):
        return jnp.where(tp == 0, a, jnp.where(tp == 1, b, jnp.where(tp == 2, c, d)))

    return (tp, pick(1, 0, 3, 2), pick(2, 2, 1, 1), pick(3, 3, 0, 0))


def greet(devices):
    barrier = pltpu.get_barrier_semaphore()
    for ep, tp in devices:
        pl.semaphore_signal(barrier, inc=1, device_id=(ep, tp), device_id_type=MESH)
    pl.semaphore_wait(barrier, len(devices))


def remote(src, dst, send, recv, device):
    return pltpu.make_async_remote_copy(
        src_ref=src, dst_ref=dst, send_sem=send, recv_sem=recv, device_id=device, device_id_type=MESH
    )


def add_rows(dst, a, b):
    def body(r, _):
        at = pl.ds(pl.multiple_of(r * 16, 16), 16)
        dst[at, :] = (a[at, :].astype(jnp.float32) + b[at, :].astype(jnp.float32)).astype(dst.dtype)
        return 0

    lax.fori_loop(0, dst.shape[0] // 16, body, 0)


def line_sum(own_of, got, send_sem, recv_sem, ep, tp, depth):
    far = line_order(tp)[::-1]
    between = (tp > 0) & (tp < depth - 1)
    near = jnp.where(tp > 0, tp - 1, tp + 1)

    def copy(n, src):
        chunk = far[n]
        to = jnp.where(chunk > tp, tp + 1, tp - 1)
        slot = jnp.where(chunk == tp - 1, depth, chunk)
        return remote(src, got.at[slot], send_sem.at[n], recv_sem.at[slot], (ep, to))

    def arrive(slot):
        remote(got.at[0], got.at[slot], send_sem.at[0], recv_sem.at[slot], (ep, near)).wait_recv()

    def start(n):
        @pl.when(jnp.logical_not(between))
        def _():
            copy(n, own_of(n)).start()

    def pass_on(n):
        @pl.when(between)
        def _():
            held = got.at[far[n]]
            arrive(far[n])
            add_rows(held, own_of(n), held)
            copy(n, held).start()

    def clear():
        @pl.when(tp == 0)
        def _():
            got[0] = jnp.zeros_like(got[0])

        @pl.when(tp == depth - 1)
        def _():
            got[depth] = jnp.zeros_like(got[depth])

    def finish():
        @pl.when(tp > 0)
        def _():
            arrive(tp)

        @pl.when(tp < depth - 1)
        def _():
            arrive(depth)

    def drain():
        for n in range(depth - 1):
            copy(n, got.at[0]).wait_send()

    return clear, start, pass_on, finish, drain


def line_total(own_of, pieces, up, down, up_send, up_recv, down_send, down_recv, ep, tp, depth):
    between = (tp > 0) & (tp < depth - 1)
    lowest, highest = tp == 0, tp == depth - 1
    above, below = jnp.minimum(tp + 1, depth - 1), jnp.maximum(tp - 1, 0)

    def up_copy(n, src):
        return remote(src, up.at[n], up_send.at[n], up_recv.at[n], (ep, above))

    def down_copy(n, src):
        return remote(src, down.at[n], down_send.at[n], down_recv.at[n], (ep, below))

    def start(n):
        @pl.when(lowest)
        def _():
            up_copy(n, own_of(n)).start()

        @pl.when(highest)
        def _():
            down_copy(n, own_of(n)).start()

    def hop(k, n):
        @pl.when(between & (tp == k))
        def _():
            up_copy(n, up.at[n]).wait_recv()
            add_rows(up.at[n], up.at[n], own_of(n))
            up_copy(n, up.at[n]).start()

        @pl.when(between & (tp == depth - 1 - k))
        def _():
            down_copy(n, down.at[n]).wait_recv()
            add_rows(down.at[n], down.at[n], own_of(n))
            down_copy(n, down.at[n]).start()

    def finish(n):
        @pl.when(lowest)
        def _():
            up[n] = own_of(n)[...]
            down_copy(n, down.at[n]).wait_recv()
            add_rows(down.at[n], down.at[n], own_of(n))

        @pl.when(highest)
        def _():
            down[n] = own_of(n)[...]
            up_copy(n, up.at[n]).wait_recv()
            add_rows(up.at[n], up.at[n], own_of(n))

    def drain():
        for n in range(pieces):

            @pl.when(jnp.logical_not(highest))
            def _():
                up_copy(n, up.at[n]).wait_send()

            @pl.when(jnp.logical_not(lowest))
            def _():
                down_copy(n, down.at[n]).wait_send()

    return start, hop, finish, drain


def turn(slab, table, sign):
    cosine, front, second = table
    return slab * cosine + sign * (pltpu.roll(slab, 96, 1) * front + pltpu.roll(slab, 32, 1) * second)


def experts_kernel(
    depth, blocks, heads, routed, shared, experts,
    inputs_ref, gain_attn, w_query, w_latent, gain_latent, w_up, w_output, tables,
    gain_ref, cot_ref, kept_hbm, e_in, e_out, s_in, s_out,
    middle_ref, h_out, cot_all, grads_out, gated_out, rows_out,
    hidden_out, qn_out, qr_out, kv_out, kr_out, attended_out, latent_in_out, compressed_out, w_out_out,
    part_ref, hidden, qn_ref, qr_ref, kv, kr_ref, attended, latent_in, compressed, rope_slab,
    kept_ref, w_in_ref, w_out_ref, e_stage,
    h_all, got_z, cot_tile, gu, act_grad, prob_lanes, diff_lanes, pair_lanes,
    grads_tile, gated_tile, rows_tile,
    weight_sem, stage_sem, save_sem, local_sem, z_send, z_recv, line_send, line_recv, h_send, h_recv, c_send, c_recv, b_send, b_recv, tile_sem, store_sem,
):
    f32, bf16 = jnp.float32, jnp.bfloat16
    ep, tp = lax.axis_index("ep"), lax.axis_index("tp")
    pair, xn, yn = plane_partners(ep)
    parity = lax.rem(ep, 2)
    passed = jnp.where(parity == 0, xn, yn)
    onward = jnp.where(parity == 0, yn, xn)
    diag = xn + yn - ep
    rows = h_all.shape[2]
    width = h_all.shape[3]
    hidden_units = w_out_ref.shape[0]
    tokens = inputs_ref.shape[0]
    rank = compressed.shape[1]
    lanes = lax.broadcasted_iota(jnp.int32, (1, 128), 1)
    across = (((1,), (1,)), ((), ()))
    score_scale = (NOPE + ROPE) ** (-0.5)

    def dot(a, b, dims=(((1,), (0,)), ((), ()))):
        return lax.dot_general(a, b, dims, preferred_element_type=f32)

    half = blocks // 2
    tile = half * rows
    up, down = jnp.minimum(tp + 1, depth - 1), jnp.maximum(tp - 1, 0)

    def twin(block):
        return block + pair - ep

    greet([(pair, tp), (xn, tp), (yn, tp)] + [(ep, lax.rem(tp + k, depth)) for k in range(1, depth)])

    def part_rows(n):
        return part_ref.at[pl.ds(pl.multiple_of(line_order(tp)[depth - 1 - n] * rows, rows), rows)]

    z_clear, z_start, z_pass, z_finish, z_drain = line_sum(part_rows, got_z, z_send, z_recv, ep, tp, depth)
    z_clear()
    weight_loads = [
        pltpu.make_async_copy(kept_hbm, kept_ref, weight_sem.at[0]),
        pltpu.make_async_copy(e_out.at[0], w_out_ref.at[pl.ds(0, routed)], weight_sem.at[1]),
        pltpu.make_async_copy(s_out, w_out_ref.at[pl.ds(routed, hidden_units - routed)], weight_sem.at[2]),
    ]
    for g in range(2):
        at = pl.ds(g * hidden_units + routed // 128 * 128, s_in.shape[2])
        weight_loads.append(pltpu.make_async_copy(s_in.at[g], w_in_ref.at[:, at], weight_sem.at[3 + g]))
    piece = e_stage.shape[1]
    pieces = width // piece

    def e_load(n):
        at = pl.ds(pl.multiple_of(lax.rem(n, pieces) * piece, piece), piece)
        return pltpu.make_async_copy(e_in.at[0, lax.div(n, pieces), at], e_stage.at[lax.rem(n, 2)], stage_sem.at[lax.rem(n, 2)])

    def h_copy(block, chunk, slot, to):
        ref = h_all.at[chunk, block]
        return remote(ref, ref, h_send.at[chunk, slot], h_recv.at[chunk, slot], (to, tp))

    def c_copy(block, chunk, slot, to):
        ref = cot_all.at[chunk, block]
        return remote(ref, ref, c_send.at[chunk, slot], c_recv.at[chunk, slot], (to, tp))

    def c_first(chunk, slot, to):
        src = cot_ref.at[pl.ds(pl.multiple_of(chunk * rows, rows), rows)]
        return remote(src, cot_all.at[chunk, ep], c_send.at[chunk, slot], c_recv.at[chunk, slot], (to, tp))

    buddy = tp + 1 - 2 * lax.rem(tp, 2)
    skipped, theirs = depth - 1 - tp, depth - 1 - buddy

    def buddy_copy(n, chunk):
        ref = cot_all.at[chunk, (xn, yn, diag)[n]]
        return remote(ref, ref, b_send.at[n], b_recv.at[n], (ep, buddy))

    def own_cot_in(chunk):
        src = cot_ref.at[pl.ds(pl.multiple_of(chunk * rows, rows), rows)]
        return pltpu.make_async_copy(src, rows_tile.at[0, chunk], local_sem.at[chunk])

    def own_cot_out(chunk):
        return pltpu.make_async_copy(rows_tile.at[0, chunk], cot_all.at[chunk, ep], local_sem.at[chunk])

    order = line_order(tp)

    def order_at(k):
        return jnp.where(k == 0, order[0], jnp.where(k == 1, order[1], jnp.where(k == 2, order[2], order[3])))

    for k in range(depth):

        @pl.when(order[k] != skipped)
        def _():
            c_first(order[k], 1, xn).start()
            c_first(order[k], 2, yn).start()

        c_first(order[k], 0, pair).start()
        own_cot_in(k).start()
    for copy in weight_loads:
        copy.start()
    e_load(0).start()

    def first_norm(r, _):
        at = pl.ds(pl.multiple_of(r * 16, 16), 16)
        v = inputs_ref[at, :].astype(f32)
        inverse = lax.rsqrt(jnp.mean(v * v, axis=-1, keepdims=True) + EPSILON)
        hidden[at, :] = (v * inverse * gain_attn[...]).astype(bf16)
        return 0

    lax.fori_loop(0, tokens // 16, first_norm, 0)
    table = tuple(tables[n] for n in range(3))
    latent = dot(hidden[...], w_latent[...])
    held = latent[:, :rank]
    compressed[...] = held
    inverse = lax.rsqrt(jnp.mean(held * held, axis=-1, keepdims=True) + EPSILON)
    latent_in[...] = (held * inverse * gain_latent[...]).astype(bf16)
    rope_slab[...] = jnp.zeros_like(rope_slab)
    rope_slab[:, 0:ROPE] = latent[:, rank:]
    key = turn(rope_slab[...], table, 1.0)
    kr_ref[0] = key.astype(bf16)
    kr_ref[1] = pltpu.roll(key, 64, 1).astype(bf16)
    kv[...] = dot(latent_in[...], w_up[...]).astype(bf16)
    wide = 2 * (NOPE + ROPE)
    for p in range(heads // 2):
        found = dot(hidden[...], w_query[:, p * wide : (p + 1) * wide])
        slabs = [found[:, n : n + 128] for n in (0, 128, 256)]
        qn_ref[:, 2 * p * NOPE : (2 * p + 1) * NOPE] = slabs[0].astype(bf16)
        odd = pltpu.roll(jnp.where(lanes < 64, slabs[2], slabs[1]), 64, 1)
        qn_ref[:, (2 * p + 1) * NOPE : (2 * p + 2) * NOPE] = odd.astype(bf16)
        qr_ref[:, p * 128 : (p + 1) * 128] = turn(jnp.where(lanes < 64, slabs[1], slabs[2]), table, 1.0).astype(bf16)
    for h in range(heads):
        for b in range(tokens // BLOCK):
            own = slice(b * BLOCK, (b + 1) * BLOCK)
            keys = slice(0, (b + 1) * BLOCK)
            slab = slice(h // 2 * 128, h // 2 * 128 + 128)
            at = slice(h * 128, h * 128 + 128)
            scores = dot(qn_ref[own, at], kv[keys, h * 256 : h * 256 + 128], across)
            scores = (scores + dot(qr_ref[own, slab], kr_ref[h % 2, keys, :], across)) * score_scale
            exps = jnp.exp(scores - jnp.max(scores, axis=-1, keepdims=True))
            probs = exps / jnp.sum(exps, axis=-1, keepdims=True)
            attended[own, at] = dot(probs.astype(bf16), kv[keys, h * 256 + 128 : h * 256 + 256]).astype(bf16)
    for n in range(0, width, 512):
        part_ref[:, n : n + 512] = dot(attended[...], w_output[:, n : n + 512]).astype(bf16)
    for n in range(depth - 1):
        z_start(n)
    saves = [
        pltpu.make_async_copy(src, dst, save_sem.at[n])
        for n, (src, dst) in enumerate(
            (
                (hidden, hidden_out), (qn_ref, qn_out), (qr_ref, qr_out), (kv, kv_out), (kr_ref, kr_out),
                (attended, attended_out), (latent_in, latent_in_out), (compressed, compressed_out),
            )
        )
    ]
    for copy in saves:
        copy.start()
    for k in range(depth):
        own_cot_in(k).wait()
        own_cot_out(k).start()

    def e_place(n, _):
        e_load(n).wait()

        @pl.when(n + 1 < 2 * pieces)
        def _():
            e_load(n + 1).start()

        at = pl.ds(pl.multiple_of(lax.rem(n, pieces) * piece, piece), piece)

        @pl.when(n < pieces)
        def _():
            w_in_ref[at, 0:routed] = e_stage[lax.rem(n, 2)]

        @pl.when(n >= pieces)
        def _():
            w_in_ref[at, hidden_units : hidden_units + routed] = e_stage[lax.rem(n, 2)]

        return 0

    for copy in weight_loads:
        copy.wait()
    w_out_save = pltpu.make_async_copy(w_out_ref, w_out_out, save_sem.at[8])
    w_out_save.start()
    lax.fori_loop(0, pieces, e_place, 0)
    z_pass(0)
    lax.fori_loop(pieces, 2 * pieces, e_place, 0)
    z_pass(1)
    z_pass(2)
    z_finish()

    def norm_rows(r, _):
        here = pl.ds(pl.multiple_of(r * 16, 16), 16)
        own = pl.ds(pl.multiple_of(tp * rows + r * 16, 16), 16)
        total = part_ref[own, :].astype(f32)
        total = total + got_z[tp, here, :].astype(f32) + got_z[depth, here, :].astype(f32)
        middle = inputs_ref[own, :].astype(f32) + total
        inverse = lax.rsqrt(jnp.mean(middle * middle, axis=-1, keepdims=True) + EPSILON)
        middle_ref[here, :] = middle
        h_all[tp, ep, here, :] = (middle * inverse * gain_ref[...]).astype(bf16)
        return 0

    lax.fori_loop(0, rows // 16, norm_rows, 0)
    for k in range(depth):
        own_cot_out(k).wait()

    def along(chunk, way, to):
        ref = h_all.at[chunk, ep]
        return remote(ref, ref, line_send.at[chunk, way], line_recv.at[chunk], (ep, to))

    def goes_up(chunk):
        return (chunk <= tp) & (tp < depth - 1)

    def goes_down(chunk):
        return (chunk >= tp) & (tp > 0)

    def send_chunk(k):
        chunk = order[k]
        if k > 0:
            along(chunk, 0, up).wait_recv()

        @pl.when(goes_up(chunk))
        def _():
            along(chunk, 0, up).start()

        @pl.when(goes_down(chunk))
        def _():
            along(chunk, 1, down).start()

        h_copy(ep, chunk, 1, xn).start()
        h_copy(ep, chunk, 2, yn).start()
        h_copy(ep, chunk, 0, pair).start()

    def forward_chunk(copy, chunk):
        copy(xn, chunk, 1, xn).wait_recv()
        copy(yn, chunk, 2, yn).wait_recv()
        copy(passed, chunk, 3, onward).start()
        copy(xn, chunk, 4, pair).start()
        copy(yn, chunk, 5, pair).start()

    def forward_diag(copy, chunk):
        copy(diag, chunk, 3, onward).wait_recv()
        copy(diag, chunk, 6, pair).start()

    def forward_skipped():
        for n, (block, slot) in enumerate(((xn, 4), (yn, 5), (diag, 6))):
            buddy_copy(n, skipped).wait_recv()
            c_copy(block, skipped, slot, pair).start()

    def await_pair(chunk, slots):
        for copy in (h_copy, c_copy):
            for slot, block in slots:
                copy(block, chunk, slot, pair).wait_recv()

    send_chunk(0)
    forward_chunk(c_copy, order[0])
    forward_chunk(c_copy, theirs)
    buddy_copy(0, theirs).start()
    buddy_copy(1, theirs).start()
    send_chunk(1)
    forward_chunk(h_copy, order[0])

    base = routed + shared
    slab = base // 128 * 128
    lane0 = base - slab
    near_half = lax.div(ep, half)

    def tile_copies(i):
        k, side = lax.div(i, 2), lax.rem(i, 2)
        chunk = order_at(k)
        start = jnp.where(side == 0, near_half, 1 - near_half) * half
        group = pl.ds(start, half)
        slot = lax.rem(i, 2)
        stores = [
            pltpu.make_async_copy(h_all.at[chunk, group], h_out.at[chunk, group], store_sem.at[slot, 0]),
            pltpu.make_async_copy(grads_tile.at[slot], grads_out.at[chunk, group], store_sem.at[slot, 1]),
            pltpu.make_async_copy(gated_tile.at[slot], gated_out.at[chunk, group], store_sem.at[slot, 2]),
            pltpu.make_async_copy(rows_tile.at[slot], rows_out.at[chunk, group], store_sem.at[slot, 3]),
        ]
        load = pltpu.make_async_copy(cot_all.at[chunk, group], cot_tile, tile_sem)
        return chunk, start, slot, load, stores

    def step(i, _):
        k, side = lax.div(i, 2), lax.rem(i, 2)
        chunk, start, slot, load, stores = tile_copies(i)

        @pl.when(side == 0)
        def _():
            await_pair(chunk, ((0, pair), (4, twin(xn))))

        @pl.when(i == 1)
        def _():
            send_chunk(2)
            forward_chunk(c_copy, order[1])
            forward_chunk(h_copy, order[1])
            forward_diag(c_copy, order[0])
            forward_diag(c_copy, theirs)
            buddy_copy(2, theirs).start()

        @pl.when(i == 2)
        def _():
            send_chunk(3)
            forward_chunk(h_copy, order[2])

        @pl.when(i == 3)
        def _():
            forward_skipped()
            forward_chunk(h_copy, order[3])
            forward_diag(c_copy, order[1])

        @pl.when(side == 1)
        def _():
            forward_diag(h_copy, chunk)
            await_pair(chunk, ((5, twin(yn)), (6, twin(diag))))

        load.start()

        @pl.when(i >= 2)
        def _():
            for copy in tile_copies(i - 2)[4]:
                copy.wait()

        group = pl.ds(start, half)
        stores[0].start()
        for n in range(0, 2 * hidden_units, 512):
            gu[:, n : n + 512] = jnp.dot(
                h_all[chunk, group].reshape(tile, width), w_in_ref[:, n : n + 512], preferred_element_type=f32
            )
        piece = gu[:, slab : slab + 128]
        logits = piece + pltpu.roll(piece, 128 - experts, 1) + pltpu.roll(piece, 128 - 2 * experts, 1)
        is_logit = (lanes >= lane0) & (lanes < lane0 + experts)
        logits = jnp.where(is_logit, logits, -1e30)
        exps = jnp.exp(logits - jnp.max(logits, axis=-1, keepdims=True))
        probs = exps / jnp.sum(exps, axis=-1, keepdims=True)
        here = (lanes == lane0 + ep).astype(f32)
        kept = kept_ref[chunk, group].reshape(tile, 128).astype(f32)
        prob_here = jnp.sum(probs * here * kept, axis=-1, keepdims=True)
        prob_lanes[...] = jnp.broadcast_to(prob_here, (tile, 128))
        diff_lanes[...] = here - probs
        load.wait()
        act_grad[...] = lax.dot_general(
            cot_tile[...].reshape(tile, width), w_out_ref[...], (((1,), (1,)), ((), ())), preferred_element_type=f32
        )
        strip = 64

        def strips(r, _):
            at = pl.ds(pl.multiple_of(r * strip, strip), strip)
            gate_here = prob_lanes[at, :]
            pair_sum = jnp.zeros((strip, 128), f32)
            per = rows // strip
            block, inner = lax.div(r, per), pl.ds(pl.multiple_of(lax.rem(r, per) * strip, strip), strip)
            for n in range(0, hidden_units, 128):
                gate = gu[at, n : n + 128]
                up_val = gu[at, hidden_units + n : hidden_units + n + 128]
                grad = act_grad[at, n : n + 128]
                if n + 128 <= routed:
                    scale = gate_here
                elif n >= routed:
                    scale = None
                else:
                    scale = jnp.where(lanes < routed - n, gate_here, 1.0)
                sig = jax.nn.sigmoid(gate)
                silu = gate * sig
                act = silu * up_val
                if n < routed:
                    both = act * grad
                    if n + 128 > routed:
                        both = jnp.where(lanes < routed - n, both, 0.0)
                    pair_sum = pair_sum + both
                    act = act * scale
                    grad = grad * scale
                gated_tile[slot, block, inner, n : n + 128] = act.astype(bf16)
                grads_tile[slot, block, inner, n : n + 128] = (
                    grad * up_val * (sig * (1.0 + gate * (1.0 - sig)))
                ).astype(bf16)
                grads_tile[slot, block, inner, hidden_units + n : hidden_units + n + 128] = (grad * silu).astype(bf16)
            pair_lanes[at, :] = pair_sum
            return 0

        lax.fori_loop(0, tile // strip, strips, 0)
        pair_grad = jnp.sum(pair_lanes[...], axis=-1, keepdims=True)
        logit_grad = pair_grad * prob_lanes[...] * diff_lanes[...]
        logit_grad = logit_grad + pltpu.roll(logit_grad, experts, 1) + pltpu.roll(logit_grad, 2 * experts, 1)
        old = grads_tile[slot, :, :, slab : slab + 128].reshape(tile, 128)
        grads_tile[slot, :, :, slab : slab + 128] = (
            jnp.where(lanes >= lane0, logit_grad.astype(bf16), old).reshape(half, rows, 128)
        )
        for n in range(0, width, 512):
            rows_tile[slot, :, :, n : n + 512] = (
                lax.dot_general(
                    grads_tile[slot].reshape(tile, 2 * hidden_units), w_in_ref[n : n + 512, :], (((1,), (1,)), ((), ())),
                    preferred_element_type=f32,
                ).astype(bf16).reshape(half, rows, 512)
            )
        for copy in stores[1:]:
            copy.start()
        return 0

    lax.fori_loop(0, 2 * depth, step, 0)
    for i in (2 * depth - 2, 2 * depth - 1):
        for copy in tile_copies(i)[4]:
            copy.wait()
    z_drain()
    for copy in saves:
        copy.wait()
    w_out_save.wait()

    def drain(k, _):
        chunk = order_at(k)

        @pl.when(goes_up(chunk))
        def _():
            along(chunk, 0, up).wait_send()

        @pl.when(goes_down(chunk))
        def _():
            along(chunk, 1, down).wait_send()

        for slot in range(7):
            h_copy(ep, chunk, slot, pair).wait_send()
        for slot in (0, 4, 5, 6):
            c_copy(ep, chunk, slot, pair).wait_send()

        @pl.when(chunk != skipped)
        def _():
            for slot in (1, 2, 3):
                c_copy(ep, chunk, slot, pair).wait_send()

        return 0

    lax.fori_loop(0, depth, drain, 0)
    for n in range(3):
        buddy_copy(n, theirs).wait_send()


def experts_call(
    inputs, gain_attn, w_query, w_latent, gain_latent, w_up, w_output, tables, gain, cotangent, kept, e_in, e_out, s_in, s_out,
    blocks, depth, heads, shared, experts, cid,
):
    f32, bf16 = jnp.float32, jnp.bfloat16
    tokens, width = inputs.shape
    rows = tokens // depth
    routed = e_out.shape[1]
    hidden = routed + s_out.shape[0]
    rank = w_up.shape[0]
    half = blocks // 2
    tile = half * rows
    dma = pltpu.SemaphoreType.DMA
    vmem, anywhere = pl.BlockSpec(memory_space=pltpu.VMEM), pl.BlockSpec(memory_space=pl.ANY)

    def units(size):
        return jax.ShapeDtypeStruct((depth, blocks, rows, size), bf16)

    kept_sizes = (
        ((tokens, width), bf16), ((tokens, heads * NOPE), bf16), ((tokens, heads * ROPE), bf16),
        ((tokens, heads * (NOPE + VDIM)), bf16), ((2, tokens, 128), bf16), ((tokens, heads * VDIM), bf16),
        ((tokens, rank), bf16), ((tokens, rank), f32),
    )

    return pl.pallas_call(
        functools.partial(experts_kernel, depth, blocks, heads, routed, shared, experts),
        out_shape=(
            jax.ShapeDtypeStruct((rows, width), f32),
            units(width), units(width), units(2 * hidden), units(hidden), units(width),
        )
        + tuple(jax.ShapeDtypeStruct(*size) for size in kept_sizes)
        + (jax.ShapeDtypeStruct((hidden, width), bf16),),
        in_specs=[vmem] * 9 + [anywhere] * 6,
        out_specs=(vmem,) + (anywhere,) * 14,
        scratch_shapes=[
            pltpu.VMEM((tokens, width), bf16),
            *(pltpu.VMEM(*size) for size in kept_sizes),
            pltpu.VMEM((tokens, 128), f32),
            pltpu.VMEM((depth, blocks, rows, 128), bf16),
            pltpu.VMEM((width, 2 * hidden), bf16),
            pltpu.VMEM((hidden, width), bf16),
            pltpu.VMEM((2, 256, routed), bf16),
            pltpu.VMEM((depth, blocks, rows, width), bf16),
            pltpu.VMEM((depth + 1, rows, width), bf16),
            pltpu.VMEM((half, rows, width), bf16),
            pltpu.VMEM((tile, 2 * hidden), f32),
            pltpu.VMEM((tile, hidden), f32),
            pltpu.VMEM((tile, 128), f32),
            pltpu.VMEM((tile, 128), f32),
            pltpu.VMEM((tile, 128), f32),
            pltpu.VMEM((2, half, rows, 2 * hidden), bf16),
            pltpu.VMEM((2, half, rows, hidden), bf16),
            pltpu.VMEM((2, half, rows, width), bf16),
            dma((5,)), dma((2,)), dma((9,)), dma((depth,)),
            dma((depth - 1,)), dma((depth + 1,)),
            dma((depth, 2)), dma((depth,)),
            dma((depth, 7)), dma((depth, 7)),
            dma((depth, 7)), dma((depth, 7)),
            dma((3,)), dma((3,)), dma, dma((2, 4)),
        ],
        compiler_params=pltpu.CompilerParams(collective_id=cid, has_side_effects=True, vmem_limit_bytes=63 << 20),
    )(
        inputs, gain_attn.reshape(1, width), w_query, w_latent, gain_latent.reshape(1, rank), w_up, w_output, tables,
        gain.reshape(1, width), cotangent, kept, e_in, e_out, s_in, s_out,
    )


def sum_kernel(
    depth, routed, shared, experts, part_ref, h_ref, grads_ref, gated_ref, cot_ref, middle_ref, gain_ref, w_out_ref,
    branch, gain_part, expert_in, expert_out, s_in, s_out, router, layer_sum, landed,
    in_grad, out_grad, e_stage, s_stage,
    load, store, layer, got_pair, got_first, got_second, got_z, keep, h_tile, grads_tile, gated_tile, cot_tile,
    own_cot, load_sem, store_sem, own_sem, lps, lpr, ps, pr, fs, fr, ss, sr, zs, zr, tile_sem, e_sem, s_sem, o_sem,
):
    f32 = jnp.float32
    rows = part_ref.shape[2]
    count = h_tile.shape[0] * rows
    width = h_tile.shape[2]
    hidden = gated_tile.shape[2]
    ep, tp = lax.axis_index("ep"), lax.axis_index("tp")
    pair, xn, yn = plane_partners(ep)
    parity = lax.rem(ep, 2)
    first = jnp.where(parity == 0, xn, yn)
    second = jnp.where(parity == 0, yn, xn)
    diag = xn + yn - ep
    blocks = (first, diag, ep, second)
    pair_slot = (3, 1, 2, 0)
    greet([(pair, tp), (xn, tp), (yn, tp)] + [(ep, lax.rem(tp + k, depth)) for k in range(1, depth)])
    steps = [(k + 1) % depth for k in range(depth)]

    def chunk_of(i):
        return lax.rem(tp + steps[i], depth)

    def pair_copy(i, slot):
        src = part_ref.at[chunk_of(i), blocks[slot] + pair - ep]
        to = pair_slot[slot]
        return remote(src, got_pair.at[i, to], ps.at[i, slot], pr.at[i, to], (pair, tp))

    def pair_wait(i, slot):
        return remote(part_ref.at[0, 0], got_pair.at[i, slot], ps.at[i, slot], pr.at[i, slot], (pair, tp))

    def own_load(i, slot):
        return pltpu.make_async_copy(part_ref.at[chunk_of(i), blocks[slot]], load.at[slot], load_sem.at[slot])

    def first_copy(i, slot):
        return remote(got_pair.at[i, slot], got_first.at[i, slot], fs.at[i, slot], fr.at[i, slot], (first, tp))

    def second_copy(i):
        return remote(got_pair.at[i, 3], got_second.at[i], ss.at[i], sr.at[i], (second, tp))

    def z_copy(i):
        k = steps[i]
        return remote(got_pair.at[i, 2], got_z.at[k - 1], zs.at[k - 1], zr.at[k - 1], (ep, lax.rem(tp + k, depth)))

    def layer_pair(i, slot):
        src = layer.at[blocks[slot] + pair - ep]
        to = pair_slot[slot]
        return remote(src, landed.at[i, to], lps.at[i, slot], lpr.at[i, to], (pair, tp))

    def layer_load(i, slot):
        return pltpu.make_async_copy(landed.at[i, slot], load.at[slot], load_sem.at[slot])

    def layer_store(i, slot):
        return pltpu.make_async_copy(store.at[slot % 2], layer_sum.at[i, slot], store_sem.at[slot % 2])

    def layer_send(i):
        def columns(m, _):
            at = pl.ds(pl.multiple_of(m * 512, 512), 512)
            found = jnp.dot(gated_tile[...].reshape(count, hidden), w_out_ref[:, at], preferred_element_type=f32)
            layer[:, :, at] = found.astype(layer.dtype).reshape(layer.shape[0], rows, 512)
            return 0

        lax.fori_loop(0, width // 512, columns, 0)
        for slot in (3, 1, 2, 0):
            layer_pair(i, slot).start()

    def layer_add(i):
        for slot in range(4):
            layer_pair(i, pair_slot[slot]).wait_recv()
            layer_load(i, slot).start()
        for slot in range(4):
            layer_load(i, slot).wait()
            if slot >= 2:
                layer_store(i, slot - 2).wait()
            add_rows(store.at[slot % 2], load.at[slot], layer.at[blocks[slot]])
            layer_store(i, slot).start()
        layer_store(i, 2).wait()
        layer_store(i, 3).wait()
        for slot in range(4):
            layer_pair(i, slot).wait_send()

    for i in range(depth):
        for slot in (3, 1, 2, 0):
            pair_copy(i, slot).start()

    def tile_loads(c):
        return [
            pltpu.make_async_copy(src.at[c], dst, tile_sem.at[n])
            for n, (src, dst) in enumerate(
                ((h_ref, h_tile), (grads_ref, grads_tile), (gated_ref, gated_tile), (cot_ref, cot_tile))
            )
        ]

    def stage_a(i):
        for slot in range(4):
            own_load(i, slot).start()
        for slot in range(4):
            pair_wait(i, slot).wait_recv()
            own_load(i, slot).wait()
            add_rows(got_pair.at[i, slot], got_pair.at[i, slot], load.at[slot])
            if slot < 2:
                first_copy(i, slot).start()

    def stage_b(i):
        first_copy(i, 1).wait_recv()
        add_rows(got_pair.at[i, 3], got_pair.at[i, 3], got_first.at[i, 1])
        second_copy(i).start()
        first_copy(i, 0).wait_recv()
        add_rows(got_pair.at[i, 2], got_pair.at[i, 2], got_first.at[i, 0])

    def stage_c(i):
        second_copy(i).wait_recv()
        if i < depth - 1:
            add_rows(got_pair.at[i, 2], got_pair.at[i, 2], got_second.at[i])
            z_copy(i).start()
        else:
            add_rows(keep, got_pair.at[i, 2], got_second.at[i])


    blocks_all = h_tile.shape[0]
    lanes = lax.broadcasted_iota(jnp.int32, (1, 128), 1)
    slab = routed // 128 * 128
    shift = 128 - (routed - slab)
    router_shift = (ROPE - (routed + shared) % 128) % 128

    def expert_out_copy():
        return pltpu.make_async_copy(out_grad.at[pl.ds(0, routed)], expert_out.at[0], o_sem)

    def place_copies(m):
        side = lax.rem(m, 2)
        at = pl.ds(pl.multiple_of(m * 512, 512), 512)
        per = 512 // (width // blocks_all)
        return (
            pltpu.make_async_copy(e_stage.at[side], expert_in.at[0, :, at], e_sem.at[side]),
            pltpu.make_async_copy(s_stage.at[side], s_in.at[pl.ds(m * per, per)], s_sem.at[side]),
        )

    def place(m, found):
        side = lax.rem(m, 2)

        @pl.when(m >= 2)
        def _():
            for copy in place_copies(m - 2):
                copy.wait()

        wide = width // blocks_all
        for g in range(2):
            e_stage[side, g] = found[:, g * hidden : g * hidden + routed]
            first_slab = found[:, g * hidden + slab : g * hidden + slab + 128]
            second_slab = found[:, g * hidden + slab + 128 : g * hidden + slab + 256]
            units = jnp.where(lanes < shift, pltpu.roll(first_slab, shift, 1), pltpu.roll(second_slab, shift, 1))
            s_stage[side, :, g] = units.astype(s_stage.dtype).reshape(512 // wide, wide, 128)
        last_slab = pltpu.roll(found[:, (routed + shared) // 128 * 128 : (routed + shared) // 128 * 128 + 128], router_shift, 1)
        inside = (lanes >= ROPE) & (lanes < ROPE + experts)
        router[pl.ds(pl.multiple_of(m * 512, 512), 512), :] = jnp.where(inside, last_slab, 0.0).astype(router.dtype)
        for copy in place_copies(m):
            copy.start()

    def weights(c):
        for copy in tile_loads(c):
            copy.wait()
        turned = (((0,), (0,)), ((), ()))

        last = c == depth - 1

        def in_part(m, _):
            at = pl.ds(pl.multiple_of(m * 512, 512), 512)
            found = lax.dot_general(
                h_tile[:, :, at].reshape(count, 512), grads_tile[...].reshape(count, 2 * hidden), turned,
                preferred_element_type=f32,
            )
            if c > 0:
                found = in_grad[at, :] + found
            if last:
                place(m, found)
            else:
                in_grad[at, :] = found
            return 0

        lax.fori_loop(0, width // 512, in_part, 0)

        def out_part(m, _):
            at = pl.ds(pl.multiple_of(m * 512, 512), 512)
            found = lax.dot_general(
                gated_tile[...].reshape(count, hidden), cot_tile[:, :, at].reshape(count, 512), turned,
                preferred_element_type=f32,
            )
            out_grad[:, at] = found if c == 0 else out_grad[:, at] + found
            return 0

        lax.fori_loop(0, width // 512, out_part, 0)
        if last:
            expert_out_copy().start()
            wide = width // blocks_all
            for b in range(blocks_all):
                s_out[b] = out_grad[routed : routed + s_out.shape[1], b * wide : (b + 1) * wide].astype(s_out.dtype)
        if c > 0:
            layer_add(c - 1)
        layer_send(c)
        if c + 1 < depth:
            for copy in tile_loads(c + 1):
                copy.start()

    own_copy = pltpu.make_async_copy(cot_ref.at[tp, ep], own_cot, own_sem)
    own_copy.start()
    for copy in tile_loads(0):
        copy.start()
    stage_a(0)
    stage_a(1)
    weights(0)
    stage_b(0)
    stage_a(2)
    weights(1)
    stage_b(1)
    stage_a(3)
    stage_c(0)
    weights(2)
    stage_b(2)
    stage_c(1)
    stage_b(3)
    weights(3)
    stage_c(2)
    stage_c(3)
    layer_add(depth - 1)
    for i in range(depth - 1):
        z_copy(i).wait_recv()
    own_copy.wait()

    def total(r, gain_sum):
        at = pl.ds(pl.multiple_of(r * 16, 16), 16)
        u = keep[at, :]
        for k in range(depth - 1):
            u = u + got_z[k, at, :].astype(f32)
        v = middle_ref[at, :]
        inverse = lax.rsqrt(jnp.mean(v * v, axis=-1, keepdims=True) + EPSILON)
        v_hat = v * inverse
        gain_sum = gain_sum + (u * v_hat)[:8] + (u * v_hat)[8:]
        s = u * gain_ref[...]
        back = inverse * (s - v_hat * jnp.mean(s * v_hat, axis=-1, keepdims=True))
        found = own_cot[at, :].astype(f32) + back
        branch[at, :] = found.astype(branch.dtype)
        return gain_sum

    gain_part[...] = lax.fori_loop(0, rows // 16, total, jnp.zeros((8, width), f32))
    expert_out_copy().wait()
    for m in (width // 512 - 2, width // 512 - 1):
        for copy in place_copies(m):
            copy.wait()
    for i in range(depth):
        for slot in range(4):
            pair_copy(i, slot).wait_send()
        for slot in range(2):
            first_copy(i, slot).wait_send()
        second_copy(i).wait_send()
        if i < depth - 1:
            z_copy(i).wait_send()


def sum_call(part, h_all, grads, gated, cot_all, middle, gain, w_out, routed, shared, experts, cid):
    f32, bf16 = jnp.float32, jnp.bfloat16
    depth, blocks, rows, width = part.shape
    hidden = gated.shape[3]
    dma = pltpu.SemaphoreType.DMA
    vmem, anywhere = pl.BlockSpec(memory_space=pltpu.VMEM), pl.BlockSpec(memory_space=pl.ANY)
    return pl.pallas_call(
        functools.partial(sum_kernel, depth, routed, shared, experts),
        out_shape=(
            jax.ShapeDtypeStruct((rows, width), bf16),
            jax.ShapeDtypeStruct((8, width), f32),
            jax.ShapeDtypeStruct((1, 2, width, routed), f32),
            jax.ShapeDtypeStruct((1, routed, width), f32),
            jax.ShapeDtypeStruct((blocks, 2, width // blocks, 128), bf16),
            jax.ShapeDtypeStruct((blocks, -(-shared // 16) * 16, width // blocks), bf16),
            jax.ShapeDtypeStruct((width, 128), bf16),
            jax.ShapeDtypeStruct((depth, 4, rows, width), bf16),
            jax.ShapeDtypeStruct((depth, 4, rows, width), bf16),
        ),
        in_specs=[anywhere] * 5 + [vmem] * 3,
        out_specs=(vmem,) * 2 + (anywhere,) * 3 + (vmem,) * 2 + (anywhere,) * 2,
        scratch_shapes=[
            pltpu.VMEM((width, 2 * hidden), f32),
            pltpu.VMEM((hidden, width), f32),
            pltpu.VMEM((2, 2, 512, routed), f32),
            pltpu.VMEM((2, 512 // (width // blocks), 2, width // blocks, 128), bf16),
            pltpu.VMEM((4, rows, width), bf16),
            pltpu.VMEM((2, rows, width), bf16),
            pltpu.VMEM((blocks, rows, width), bf16),
            pltpu.VMEM((depth, 4, rows, width), bf16),
            pltpu.VMEM((depth, 2, rows, width), bf16),
            pltpu.VMEM((depth, rows, width), bf16),
            pltpu.VMEM((depth - 1, rows, width), bf16),
            pltpu.VMEM((rows, width), f32),
            pltpu.VMEM((blocks, rows, width), bf16),
            pltpu.VMEM((blocks, rows, 2 * hidden), bf16),
            pltpu.VMEM((blocks, rows, hidden), bf16),
            pltpu.VMEM((blocks, rows, width), bf16),
            pltpu.VMEM((rows, width), bf16),
            dma((4,)), dma((2,)), dma, dma((depth, 4)), dma((depth, 4)), dma((depth, 4)), dma((depth, 4)), dma((depth, 2)), dma((depth, 2)),
            dma((depth,)), dma((depth,)), dma((depth - 1,)), dma((depth - 1,)), dma((4,)), dma((2,)), dma((2,)), dma,
        ],
        compiler_params=pltpu.CompilerParams(collective_id=cid, has_side_effects=True, vmem_limit_bytes=62 << 20),
    )(part, h_all, grads, gated, cot_all, middle, gain.reshape(1, width), w_out)


def line_gather(ref, own, send_sem, recv_sem, ep, tp, depth):
    up, down = jnp.minimum(tp + 1, depth - 1), jnp.maximum(tp - 1, 0)
    order = line_order(tp)

    def along(k, way, to):
        chunk = order[k]
        src = own if k == 0 else ref.at[chunk]
        return remote(src, ref.at[chunk], send_sem.at[chunk, way], recv_sem.at[chunk], (ep, to))

    def each_way(k, act):
        @pl.when((order[k] <= tp) & (tp < depth - 1))
        def _():
            act(along(k, 0, up))

        @pl.when((order[k] >= tp) & (tp > 0))
        def _():
            act(along(k, 1, down))

    def pass_on(k):
        each_way(k, lambda copy: copy.start())

    def await_chunk(k):
        along(k, 0, up).wait_recv()

    def drain():
        for k in range(depth):
            each_way(k, lambda copy: copy.wait_send())

    return pass_on, await_chunk, drain


def tail_kernel(
    depth, heads, shared,
    branch_ref, middle_ref, part_ref, router_in, gain_part_ref, inputs_ref, s_in, s_out,
    w_output_in, w_query_in, w_latent_in, w_up_in, hidden_in, qn_in, qr_in, kv_in, kr_in, attended_in, latent_in_in, compressed_in,
    tables_in, gain_latent, gain_attn,
    block_ref, grad_in_ref, gains_ref, query_ref, output_ref, up_ref, latent_ref, shared_in, shared_out, w_all, w_first,
    w_output, w_query, w_latent, w_up, hidden_ref, qn_ref, qr_ref, kv_ref, kr_ref, attended, latent_in, compressed,
    tables, router_ref, load_in_sem,
    branch, held_rows, got_first, got_second, z_up, z_down, hidden_part, h_up, h_down, middle,
    d_out, d_kr, q_grad, kv_grad, l_grad, u_grad, w_stage, w_pair, w_second, w_z, latent_part, s_in_land, s_out_land, resid, grad_tile, block_tile, gains, attn_gains,
    load_sem, fs, fr, ss, sr, zus, zur, zds, zdr, bs, br, hus, hur, hds, hdr,
    wps, wpr, wfs, wfr, wss, wsr, wzs, wzr, as_, ar, ns, nr, misc_sem, resid_sem, grad_sem, block_sem, stage_sem, sis, sir, sos, sor,
):
    f32, bf16 = jnp.float32, jnp.bfloat16
    ep, tp = lax.axis_index("ep"), lax.axis_index("tp")
    pair, xn, yn = plane_partners(ep)
    parity = lax.rem(ep, 2)
    first = jnp.where(parity == 0, xn, yn)
    second = jnp.where(parity == 0, yn, xn)
    diag = xn + yn - ep
    blocks = (first, diag, ep, second)
    pair_slot = (3, 1, 2, 0)
    rows, width = middle.shape
    tokens = hidden_ref.shape[0]
    rank = compressed.shape[1]
    q_cols, l_cols = q_grad.shape[1], l_grad.shape[1]
    o_rows = attended.shape[1]
    count = w_all.shape[0]
    w_rows = w_all.shape[1]
    o_cols = width // count
    u_rows = rank // count
    u_cols = w_up.shape[1]
    o_start = q_cols + l_cols
    u_start = o_start + o_rows * o_cols // w_rows
    u_wide = u_rows * u_cols // w_rows
    order = line_order(tp)
    score_scale = (NOPE + ROPE) ** (-0.5)
    plane = [ep + sum(((pair, xn, yn)[n] - ep) * (m >> n & 1) for n in range(3)) for m in range(8)]
    greet([(to, tp) for to in plane[1:]] + [(ep, lax.rem(tp + k, depth)) for k in range(1, depth)])

    loads = [
        pltpu.make_async_copy(src, dst, load_in_sem.at[n])
        for n, (src, dst) in enumerate(
            (
                (w_output_in, w_output),
                (qn_in, qn_ref), (qr_in, qr_ref), (kv_in, kv_ref), (kr_in, kr_ref), (tables_in, tables),
                (w_up_in, w_up), (compressed_in, compressed), (w_query_in, w_query), (w_latent_in, w_latent),
                (hidden_in, hidden_ref), (attended_in, attended), (latent_in_in, latent_in), (router_in, router_ref),
            )
        )
    ]

    def loaded(first_load, last_load):
        for copy in loads[first_load:last_load]:
            copy.wait()

    branch_on, branch_wait, branch_drain = line_gather(branch, branch_ref, bs, br, ep, tp, depth)

    middle_copy = pltpu.make_async_copy(middle_ref, middle, misc_sem.at[1])

    def held_load(i, slot):
        return pltpu.make_async_copy(part_ref.at[i, slot], held_rows.at[i, slot - 2], load_sem.at[i, slot - 2])

    def first_copy(i, slot):
        return remote(part_ref.at[i, slot], got_first.at[i, slot], fs.at[i, slot], fr.at[i, slot], (first, tp))

    def second_copy(i):
        return remote(held_rows.at[i, 1], got_second.at[i], ss.at[i], sr.at[i], (second, tp))

    pieces, piece = h_up.shape[0], h_up.shape[1]
    per = rows // piece
    z_start, z_hop, z_finish, z_drain = line_total(
        lambda n: held_rows.at[n // per, 0, pl.ds(n % per * piece, piece)],
        pieces, z_up, z_down, zus, zur, zds, zdr, ep, tp, depth,
    )
    h_start, h_hop, h_finish, h_drain = line_total(
        lambda n: hidden_part.at[n], pieces, h_up, h_down, hus, hur, hds, hdr, ep, tp, depth
    )

    def stage_b(i):
        held_load(i, 3).wait()
        first_copy(i, 1).wait_recv()
        add_rows(held_rows.at[i, 1], held_rows.at[i, 1], got_first.at[i, 1])
        second_copy(i).start()
        held_load(i, 2).wait()
        first_copy(i, 0).wait_recv()
        add_rows(held_rows.at[i, 0], held_rows.at[i, 0], got_first.at[i, 0])

    def stage_c(i):
        second_copy(i).wait_recv()
        add_rows(held_rows.at[i, 0], held_rows.at[i, 0], got_second.at[i])

        @pl.when(tp == i)
        def _():
            middle_copy.wait()
            add_rows(held_rows.at[i, 0], held_rows.at[i, 0], middle)

        for n in range(per * i, per * i + per):
            z_start(n)

    def w_pair_copy(slot):
        to = pair_slot[slot]
        return remote(w_all.at[blocks[slot] + pair - ep], w_pair.at[to], wps.at[slot], wpr.at[to], (pair, tp))

    def w_pair_wait(slot):
        return remote(w_all.at[0], w_pair.at[slot], wps.at[slot], wpr.at[slot], (pair, tp))

    def w_first_copy(slot):
        return remote(w_pair.at[slot], w_first.at[slot], wfs.at[slot], wfr.at[slot], (first, tp))

    def w_second_copy():
        return remote(w_pair.at[3], w_second, wss, wsr, (second, tp))

    def w_load(slot):
        return pltpu.make_async_copy(w_all.at[blocks[slot]], w_stage.at[slot % 2], stage_sem.at[slot % 2])

    def w_stage_a():
        for slot in range(4):
            if slot < 3:
                w_load(slot + 1).start()
            w_pair_wait(slot).wait_recv()
            w_load(slot).wait()
            add_rows(w_pair.at[slot], w_pair.at[slot], w_stage.at[slot % 2])
            if slot < 2:
                w_first_copy(slot).start()

    def w_stage_b():
        def load(slot):
            return pltpu.make_async_copy(w_first.at[slot], w_stage.at[slot], stage_sem.at[slot])

        w_first_copy(1).wait_recv()
        load(1).start()
        w_first_copy(0).wait_recv()
        load(0).start()
        load(1).wait()
        add_rows(w_pair.at[3], w_pair.at[3], w_stage.at[1])
        w_second_copy().start()
        load(0).wait()
        add_rows(w_pair.at[2], w_pair.at[2], w_stage.at[0])

    def w_stage_c():
        w_second_copy().wait_recv()

        def total(cols, at=slice(None)):
            return w_pair[2, at, cols].astype(f32) + w_second[at, cols].astype(f32)

        query_ref[...] = total(slice(0, q_cols))
        latent_part[...] = total(slice(q_cols, o_start))
        for n in range(o_rows // w_rows):
            output_ref[n * w_rows : (n + 1) * w_rows, :] = total(slice(o_start + n * o_cols, o_start + (n + 1) * o_cols))
        for n in range(u_cols // u_wide):
            up_ref[:, n * u_wide : (n + 1) * u_wide] = total(
                slice(u_start, u_start + u_wide), slice(n * u_rows, (n + 1) * u_rows)
            )

    def shared_copies(m):
        to = plane[m]
        return (
            remote(s_in.at[to], s_in_land.at[ep], sis.at[m], sir.at[m], (to, tp)),
            remote(s_out.at[to], s_out_land.at[ep], sos.at[m], sor.at[m], (to, tp)),
        )

    def shared_own():
        return (
            pltpu.make_async_copy(s_in.at[ep], s_in_land.at[ep], sis.at[0]),
            pltpu.make_async_copy(s_out.at[ep], s_out_land.at[ep], sos.at[0]),
        )

    def shared_place():
        for m in range(1, 8):
            for copy in shared_copies(m):
                copy.wait_recv()
        for copy in shared_own():
            copy.wait()
        for n in range(s_in_land.shape[0]):
            at = slice(n * shared, (n + 1) * shared)
            for g in range(2):
                shared_in[g, :, at] = s_in_land[n, g].astype(f32)[:, :shared]
            shared_out[at, :] = s_out_land[n].astype(f32)[:shared]

    branch_on(0)
    branch[tp] = branch_ref[...]
    for i in range(depth):
        first_copy(i, 1).start()
        first_copy(i, 0).start()
        held_load(i, 3).start()
        held_load(i, 2).start()

    def resid_copy(n):
        return pltpu.make_async_copy(inputs_ref.at[pl.ds(n * piece, piece)], resid.at[n % 2], resid_sem.at[n % 2])

    for copy in loads:
        copy.start()
    resid_copy(0).start()
    resid_copy(1).start()
    middle_copy.start()

    turned, across = (((0,), (0,)), ((), ())), (((1,), (1,)), ((), ()))

    def dot(a, b, dims=(((1,), (0,)), ((), ()))):
        return lax.dot_general(a, b, dims, preferred_element_type=f32)

    def attended_grad(k):
        at = pl.ds(pl.multiple_of(order[k] * rows, rows), rows)
        d_out[at, :] = dot(branch[order[k]], w_output[...], across).astype(bf16)

    loaded(0, 1)
    attended_grad(0)
    branch_wait(1)
    branch_on(1)
    attended_grad(1)
    stage_b(0)
    branch_wait(2)
    branch_on(2)
    attended_grad(2)
    stage_c(0)
    stage_b(1)
    loaded(1, 6)
    branch_wait(3)
    branch_on(3)
    attended_grad(3)

    lanes = lax.broadcasted_iota(jnp.int32, (1, 128), 1)
    halves = tokens // BLOCK

    def head(h, even):
        mine = (lanes < 64) if even else (lanes >= 64)
        at_q = pl.ds(pl.multiple_of(h * NOPE, 128), 128)
        at_r = pl.ds(pl.multiple_of(lax.div(h, 2) * 128, 128), 128)
        at_k = pl.ds(pl.multiple_of(h * 256, 128), 128)
        at_v = pl.ds(pl.multiple_of(h * 256 + 128, 128), 128)
        kv_sum = [None, None]
        for b in reversed(range(halves)):
            own = slice(b * BLOCK, (b + 1) * BLOCK)
            keys = slice(0, (b + 1) * BLOCK)
            qn, qr = qn_ref[own, at_q], qr_ref[own, at_r]
            kn, kr = kv_ref[keys, at_k], kr_ref[0 if even else 1, keys, :]
            scores = (dot(qn, kn, across) + dot(qr, kr, across)) * score_scale
            exps = jnp.exp(scores - jnp.max(scores, axis=-1, keepdims=True))
            probs = exps / jnp.sum(exps, axis=-1, keepdims=True)
            grad = d_out[own, at_q]
            prob_part = dot(grad, kv_ref[keys, at_v], across)
            score_grad = (probs * (prob_part - jnp.sum(probs * prob_part, axis=-1, keepdims=True))).astype(bf16)
            found = (dot(score_grad, qn, turned) * score_scale, dot(probs.astype(bf16), grad, turned))
            r_grad = jnp.where(mine, dot(score_grad, qr, turned) * score_scale, 0.0)
            for n, at in enumerate((at_k, at_v)):
                if b < halves - 1:
                    kv_sum[n] = kv_sum[n] + found[n]
                else:
                    kv_sum[n] = found[n]
                kv_grad[own, at] = kv_sum[n][b * BLOCK :].astype(bf16)
                if b > 0:
                    kv_sum[n] = kv_sum[n][: b * BLOCK]
            d_kr[keys, :] = d_kr[keys, :] + r_grad
            yield own, dot(score_grad, kn) * score_scale, dot(score_grad, kr) * score_scale

    d_kr[...] = jnp.zeros_like(d_kr)

    def head_pair(p, _):
        evens = list(head(2 * p, True))
        odds = list(head(2 * p + 1, False))
        at = [pl.ds(pl.multiple_of(p * (2 * (NOPE + ROPE)) + n, 128), 128) for n in (0, 128, 256)]
        for (own, even, even_rope), (_, odd, odd_rope) in zip(evens, odds):
            table = tuple(tables[n, own, :] for n in range(3))
            rope = turn(even_rope + odd_rope, table, -1.0)
            odd = pltpu.roll(odd, 64, 1)
            q_grad[own, at[0]] = even.astype(bf16)
            q_grad[own, at[1]] = jnp.where(lanes < 64, rope, odd).astype(bf16)
            q_grad[own, at[2]] = jnp.where(lanes < 64, odd, rope).astype(bf16)
        return 0

    def head_pairs(p, _):
        head_pair(p, 0)

        @pl.when(p == 0)
        def _():
            stage_c(1)
            for n in range(per):
                z_hop(1, n)

        return 0

    lax.fori_loop(0, heads // 2, head_pairs, 0)
    for n in range(per):
        z_hop(2, n)
        z_hop(1, per + n)
    stage_b(2)

    loaded(6, 10)
    latent_back = dot(kv_grad[...], w_up[...], across)
    held = compressed[...]
    inverse = lax.rsqrt(jnp.mean(held * held, axis=-1, keepdims=True) + EPSILON)
    normed = held * inverse
    gain_latent_part = jnp.sum(latent_back * normed, axis=0, keepdims=True)
    scaled = latent_back * gain_latent[...]
    l_grad[:, :rank] = (inverse * (scaled - normed * jnp.mean(scaled * normed, axis=-1, keepdims=True))).astype(bf16)
    rope = d_kr[...] + pltpu.roll(d_kr[...], 64, 1)
    rope = turn(rope, tuple(tables[n] for n in range(3)), -1.0)
    l_grad[:, rank:] = jnp.where(lanes < 64, rope, 0.0).astype(bf16)

    for n in range(0, width, 512):
        part = dot(q_grad[...], w_query[n : n + 512, :], across) + dot(l_grad[:, : rank + ROPE], w_latent[n : n + 512, :], across)
        hidden_part[:, :, n : n + 512] = part.astype(bf16).reshape(pieces, piece, 512)
    for n in range(pieces):
        h_start(n)
    for n in range(per, 2 * per):
        z_hop(2, n)
    stage_c(2)
    stage_b(3)

    flip_1 = tp + 1 - 2 * lax.rem(tp, 2)
    flip_2 = tp + 2 - 4 * lax.div(tp, 2)

    def doubling(held, send, recv, partners):
        def copy(n):
            return remote(held.at[2 * n], held.at[2 * n + 1], send.at[n], recv.at[n], partners[n])

        def start():
            copy(0).start()

        def step(n):
            copy(n).wait_recv()
            total = held[2 * n] + held[2 * n + 1]
            if n + 1 < len(partners):
                held[2 * n + 2] = total
                copy(n + 1).start()
            return total

        def drain():
            for n in range(len(partners)):
                copy(n).wait_send()

        return start, step, drain

    gain_start, gain_step, gain_drain = doubling(
        gains, as_, ar, ((pair, tp), (xn, tp), (yn, tp), (ep, flip_1), (ep, flip_2))
    )
    attn_start, attn_step, attn_drain = doubling(attn_gains, ns, nr, ((pair, tp), (xn, tp), (yn, tp)))
    gains[0] = jnp.zeros_like(gains[0])
    gains[0, 1:2, :] = jnp.sum(gain_part_ref[...], axis=0, keepdims=True)
    gains[0, 2:3, 0:rank] = gain_latent_part
    gain_start()

    loaded(10, 14)
    u_grad[...] = dot(latent_in[...], kv_grad[...], turned).astype(bf16)

    def w_store(b):
        slot = lax.rem(b, 2)
        return pltpu.make_async_copy(w_stage.at[slot], w_all.at[b], stage_sem.at[slot])

    def w_block(b, _):
        slot = lax.rem(b, 2)

        @pl.when(b >= 2)
        def _():
            w_store(b - 2).wait()

        at = pl.ds(pl.multiple_of(b * w_rows, 256), w_rows)
        own = hidden_ref[:, at]
        w_stage[slot, :, 0:q_cols] = dot(own, q_grad[...], turned).astype(bf16)
        found = dot(own, l_grad[...], turned)
        w_stage[slot, :, q_cols : q_cols + rank] = found[:, :rank].astype(bf16)
        w_stage[slot, :, q_cols + rank : o_start] = found[:, rank:].astype(bf16) + router_ref[at, :]
        cols = pl.ds(pl.multiple_of(b * o_cols, 256), o_cols)
        found = dot(attended[...], branch[:, :, cols].reshape(tokens, o_cols), turned)
        for n in range(o_rows // w_rows):
            w_stage[slot, :, o_start + n * o_cols : o_start + (n + 1) * o_cols] = (
                found[n * w_rows : (n + 1) * w_rows].astype(bf16)
            )
        u_at = pl.ds(pl.multiple_of(b * u_rows, u_rows), u_rows)
        for n in range(u_cols // u_wide):
            w_stage[slot, n * u_rows : (n + 1) * u_rows, u_start : u_start + u_wide] = (
                u_grad[u_at, n * u_wide : (n + 1) * u_wide]
            )
        w_store(b).start()
        return 0

    lax.fori_loop(0, count, w_block, 0)
    w_store(count - 2).wait()
    w_store(count - 1).wait()
    for slot in (3, 1, 2, 0):
        w_pair_copy(slot).start()
    for copy in shared_own():
        copy.start()
    for m in range(1, 8):
        for copy in shared_copies(m):
            copy.start()
    w_load(0).start()

    w_part = w_rows // depth

    def w_z_copy(k):
        to = lax.rem(tp + k, depth)
        src = w_pair.at[1, pl.ds(pl.multiple_of(to * w_part, w_part), w_part), pl.ds(q_cols, l_cols)]
        return remote(src, w_z.at[k - 1], wzs.at[k - 1], wzr.at[k - 1], (ep, to))

    def block_copy(n):
        return pltpu.make_async_copy(block_tile.at[n % 2], block_ref.at[pl.ds(n * piece, piece)], block_sem.at[n % 2])

    def block_rows(n):
        z_finish(n)
        if n >= 2:
            block_copy(n - 2).wait()

        def total(r, _):
            at = pl.ds(pl.multiple_of(r * 16, 16), 16)
            inside = pl.ds(pl.multiple_of(n % per * piece + r * 16, 16), 16)
            value = z_up[n, at, :].astype(f32) + z_down[n, at, :].astype(f32) - held_rows[n // per, 0, inside, :].astype(f32)
            block_tile[n % 2, at, :] = value.astype(bf16)
            return 0

        lax.fori_loop(0, piece // 16, total, 0)
        block_copy(n).start()

    def grad_copy(n):
        return pltpu.make_async_copy(grad_tile.at[n % 2], grad_in_ref.at[pl.ds(n * piece, piece)], grad_sem.at[n % 2])

    def grad_rows(n, gain_sum):
        h_finish(n)
        if n >= 2:
            grad_copy(n - 2).wait()
        resid_copy(n).wait()

        def total(r, gain_sum):
            at = pl.ds(pl.multiple_of(r * 16, 16), 16)
            inside = pl.ds(pl.multiple_of(n % per * piece + r * 16, 16), 16)
            u = h_up[n, at, :].astype(f32) + h_down[n, at, :].astype(f32) - hidden_part[n, at, :].astype(f32)
            v = resid[n % 2, at, :].astype(f32)
            inv = lax.rsqrt(jnp.mean(v * v, axis=-1, keepdims=True) + EPSILON)
            v_hat = v * inv
            gain_sum = gain_sum + (u * v_hat)[:8] + (u * v_hat)[8:]
            s = u * gain_attn[...]
            back = inv * (s - v_hat * jnp.mean(s * v_hat, axis=-1, keepdims=True))
            grad_tile[n % 2, at, :] = (branch[n // per, inside, :].astype(f32) + back).astype(bf16)
            return gain_sum

        gain_sum = lax.fori_loop(0, piece // 16, total, gain_sum)
        if n + 2 < pieces:
            resid_copy(n + 2).start()
        grad_copy(n).start()
        return gain_sum

    gain_sum = jnp.zeros((8, width), f32)
    for t in range(pieces + 2):
        if t < pieces:
            h_hop(1, t)
        if t >= 2:
            h_hop(2, t - 2)
        if t >= 4:
            gain_sum = grad_rows(t - 4, gain_sum)
        if t == 1:
            gain_step(0)
        if t == 2:
            w_stage_a()
        if t == 0:
            stage_c(3)
        if t == 3:
            gain_step(1)
        if t == 5:
            block_rows(0)
            block_rows(1)
            gain_step(2)
        if t == 6:
            gain_step(3)
        if t == 7:
            w_stage_b()
            block_rows(2)
            block_rows(3)
        if t == 8:
            gains_ref[...] = gain_step(4)
    for t in range(pieces // 2 + 2):
        if t < pieces // 2:
            z_hop(1, pieces // 2 + t)
        if t >= 2:
            z_hop(2, pieces // 2 + t - 2)
        if t < 2:
            gain_sum = grad_rows(pieces - 2 + t, gain_sum)
        if t == 1:
            attn_gains[0] = gain_sum
            attn_start()
        if t == 2:
            w_stage_c()
            w_first_copy(1).wait_send()
            w_pair[1, :, q_cols:o_start] = latent_part[...].astype(bf16)
            for k in range(1, depth):
                w_z_copy(k).start()
            attn_step(0)
            shared_place()
        if t == 4:
            attn_step(1)
    for n in range(pieces // 2, pieces):
        block_rows(n)
    for k in range(1, depth):
        w_z_copy(k).wait_recv()
    own = pl.ds(pl.multiple_of(tp * w_part, w_part), w_part)
    total = latent_part[own, :]
    for k in range(depth - 1):
        total = total + w_z[k].astype(f32)
    latent_ref[...] = total
    gains_ref[0:1, :] = jnp.sum(attn_step(2), axis=0, keepdims=True)

    for n in (pieces - 2, pieces - 1):
        block_copy(n).wait()
    for n in (pieces - 2, pieces - 1):
        grad_copy(n).wait()
    branch_drain()
    for i in range(depth):
        for slot in range(2):
            first_copy(i, slot).wait_send()
        second_copy(i).wait_send()
    z_drain()
    h_drain()
    for slot in range(4):
        w_pair_copy(slot).wait_send()
    w_first_copy(0).wait_send()
    w_second_copy().wait_send()
    for k in range(1, depth):
        w_z_copy(k).wait_send()
    gain_drain()
    attn_drain()
    for m in range(1, 8):
        for copy in shared_copies(m):
            copy.wait_send()


def tail_call(
    branch, middle, out_part, router, gain_part, inputs, s_in, s_out, w_output, w_query, w_latent, w_up,
    hidden, qn, qr, kv, kr, attended, latent_in, compressed, tables, gain_latent, gain_attn,
    heads, shared, cid,
):
    f32, bf16 = jnp.float32, jnp.bfloat16
    depth, _, rows, width = out_part.shape
    tokens = hidden.shape[0]
    blocks = s_in.shape[0]
    rank = compressed.shape[1]
    q_cols, l_cols = w_query.shape[1], rank + 128
    pieces = 2 * depth
    w_rows = width // blocks
    w_cols = q_cols + l_cols + w_output.shape[0] + rank * w_up.shape[1] // width
    dma = pltpu.SemaphoreType.DMA
    vmem, anywhere = pl.BlockSpec(memory_space=pltpu.VMEM), pl.BlockSpec(memory_space=pl.ANY)
    return pl.pallas_call(
        functools.partial(tail_kernel, depth, heads, shared),
        out_shape=(
            jax.ShapeDtypeStruct((tokens, width), bf16),
            jax.ShapeDtypeStruct((tokens, width), bf16),
            jax.ShapeDtypeStruct((8, width), f32),
            jax.ShapeDtypeStruct((w_rows, q_cols), f32),
            jax.ShapeDtypeStruct((w_output.shape[0], w_rows), f32),
            jax.ShapeDtypeStruct((rank // blocks, w_up.shape[1]), f32),
            jax.ShapeDtypeStruct((w_rows // depth, l_cols), f32),
            jax.ShapeDtypeStruct((2, w_rows, blocks * shared), f32),
            jax.ShapeDtypeStruct((blocks * shared, w_rows), f32),
            jax.ShapeDtypeStruct((blocks, w_rows, w_cols), bf16),
            jax.ShapeDtypeStruct((2, w_rows, w_cols), bf16),
        ),
        in_specs=[vmem, anywhere, anywhere, anywhere, vmem] + [anywhere] * 16 + [vmem, vmem],
        out_specs=(anywhere, anywhere) + (vmem,) * 7 + (anywhere, anywhere),
        scratch_shapes=[
            *(
                pltpu.VMEM(a.shape, a.dtype)
                for a in (
                    w_output, w_query, w_latent, w_up, hidden, qn, qr, kv, kr, attended, latent_in, compressed, tables, router,
                )
            ),
            dma((14,)),
            pltpu.VMEM((depth, rows, width), bf16),
            pltpu.VMEM((depth, 2, rows, width), bf16),
            pltpu.VMEM((depth, 2, rows, width), bf16),
            pltpu.VMEM((depth, rows, width), bf16),
            pltpu.VMEM((pieces, tokens // pieces, width), bf16),
            pltpu.VMEM((pieces, tokens // pieces, width), bf16),
            pltpu.VMEM((pieces, tokens // pieces, width), bf16),
            pltpu.VMEM((pieces, tokens // pieces, width), bf16),
            pltpu.VMEM((pieces, tokens // pieces, width), bf16),
            pltpu.VMEM((rows, width), f32),
            pltpu.VMEM((tokens, heads * VDIM), bf16),
            pltpu.VMEM((tokens, 128), f32),
            pltpu.VMEM((tokens, q_cols), bf16),
            pltpu.VMEM((tokens, heads * (NOPE + VDIM)), bf16),
            pltpu.VMEM((tokens, l_cols), bf16),
            pltpu.VMEM((rank, heads * (NOPE + VDIM)), bf16),
            pltpu.VMEM((2, w_rows, w_cols), bf16),
            pltpu.VMEM((4, w_rows, w_cols), bf16),
            pltpu.VMEM((w_rows, w_cols), bf16),
            pltpu.VMEM((depth - 1, w_rows // depth, l_cols), bf16),
            pltpu.VMEM((w_rows, l_cols), f32),
            pltpu.VMEM(s_in.shape, bf16),
            pltpu.VMEM(s_out.shape, bf16),
            pltpu.VMEM((2, tokens // pieces, width), bf16),
            pltpu.VMEM((2, tokens // pieces, width), bf16),
            pltpu.VMEM((2, tokens // pieces, width), bf16),
            pltpu.VMEM((10, 8, width), f32),
            pltpu.VMEM((6, 8, width), f32),
            dma((depth, 2)),
            dma((depth, 2)), dma((depth, 2)), dma((depth,)), dma((depth,)),
            dma((pieces,)), dma((pieces,)), dma((pieces,)), dma((pieces,)),
            dma((depth, 2)), dma((depth,)),
            dma((pieces,)), dma((pieces,)), dma((pieces,)), dma((pieces,)),
            dma((4,)), dma((4,)), dma((2,)), dma((2,)), dma, dma, dma((depth - 1,)), dma((depth - 1,)),
            dma((5,)), dma((5,)), dma((3,)), dma((3,)), dma((2,)), dma((2,)), dma((2,)), dma((2,)), dma((2,)), dma((8,)), dma((8,)), dma((8,)), dma((8,)),
        ],
        compiler_params=pltpu.CompilerParams(collective_id=cid, has_side_effects=True, vmem_limit_bytes=63 << 20),
    )(
        branch, middle, out_part, router, gain_part, inputs, s_in, s_out, w_output, w_query, w_latent, w_up,
        hidden, qn, qr, kv, kr, attended, latent_in, compressed, tables,
        gain_latent.reshape(1, rank), gain_attn.reshape(1, width),
    )


def rope_tables(length):
    half = ROPE // 2
    inverse = np.exp(np.arange(half) * (-math.log(10000.0) / half))
    angle = np.arange(length)[:, None] * inverse[None, :]
    cosine, sine = np.cos(angle), np.sin(angle)
    zero = np.zeros_like(sine)
    parts = ([cosine] * 4, [-sine, zero] * 2, [zero, sine] * 2)
    return jnp.asarray(np.stack([np.concatenate(p, axis=1) for p in parts]), jnp.float32)


def padded_hidden(routed, shared):
    return -(-(routed + shared + 24) // 128) * 128


def split_wide(values):
    high = values.astype(jnp.bfloat16)
    rest = values - high.astype(jnp.float32)
    mid = rest.astype(jnp.bfloat16)
    low = (rest - mid.astype(jnp.float32)).astype(jnp.bfloat16)
    return (high, mid, low)


def body_dense(
    inputs,
    gain_attn,
    w_query,
    w_latent,
    gain_latent,
    w_latent_up,
    w_output,
    gain_ffn,
    w_router,
    w_shared_in,
    w_shared_out,
    w_expert_in,
    w_expert_out,
    expert_ids,
    slot_ids,
    cotangent,
):
    f32, bf16 = jnp.float32, jnp.bfloat16
    tokens, model_width = inputs.shape
    ep_count, tp_count = lax.axis_size("ep"), lax.axis_size("tp")
    ep_index, tp_index = lax.axis_index("ep"), lax.axis_index("tp")
    heads_here = w_output.shape[0] // VDIM
    experts = w_router.shape[1]
    capacity = (9 * tokens * TOPK + 64 * experts - 1) // (64 * experts) * 8
    qk_width = NOPE + ROPE
    score_scale = qk_width ** (-0.5)
    rows_part = tokens // tp_count

    expert_range = jnp.arange(experts, dtype=jnp.int32)
    kept = jnp.any(
        (expert_ids[:, :, None] == expert_range) & (slot_ids < capacity)[:, :, None], axis=1
    ).astype(f32)
    kept_here = lax.all_to_all(kept, "ep", split_axis=1, concat_axis=0, tiled=True)
    rows_part = tokens // tp_count
    kept_lanes = jnp.broadcast_to(
        kept_here.reshape(ep_count, tp_count, rows_part, 1).swapaxes(0, 1),
        (tp_count, ep_count, rows_part, 128),
    ).astype(bf16)

    routed = w_expert_in.shape[3]
    shared = w_shared_in.shape[2] // ep_count
    hidden = padded_hidden(routed, shared)
    shared_start = ep_index * shared
    slab = routed // 128 * 128
    before, after = routed - slab, hidden - routed - shared
    router_parts = jnp.concatenate(split_wide(w_router), axis=1)
    beside = jnp.stack(
        [
            jnp.pad(router_parts, ((0, 0), (0, after - router_parts.shape[1]))),
            jnp.zeros((model_width, after), bf16),
        ]
    )
    shared_in = lax.dynamic_slice_in_dim(w_shared_in, shared_start, shared, 2)
    shared_in = jnp.concatenate([jnp.zeros((2, model_width, before), bf16), shared_in, beside], axis=2)
    shared_out = lax.dynamic_slice_in_dim(w_shared_out, shared_start, shared, 0)
    shared_out = jnp.pad(shared_out, ((0, after), (0, 0)))
    tables = rope_tables(tokens)
    (
        middle, hidden_all, cot_all, hidden_grads, gated, rows_grad,
        hidden_attn, query_nope, query_rope, key_value, key_pair, attended, latent_in, compressed, w_out,
    ) = experts_call(
        inputs, gain_attn, w_query, w_latent, gain_latent, w_latent_up, w_output, tables, gain_ffn, cotangent, kept_lanes,
        w_expert_in, w_expert_out, shared_in, shared_out, ep_count, tp_count, heads_here, shared, experts, 0,
    )
    branch, gain_ffn_part, grad_expert_in, grad_expert_out, shared_in_part, shared_out_part, router_part, layer_sum, _ = (
        sum_call(
            rows_grad, hidden_all, hidden_grads, gated, cot_all, middle, gain_ffn, w_out, routed, shared, experts, 1
        )
    )
    block_out, grad_inputs, gains, grad_query, grad_output, grad_latent_up, latent_sum, grad_shared_in, grad_shared_out, _, _ = (
        tail_call(
            branch, middle, layer_sum, router_part, gain_ffn_part, inputs, shared_in_part, shared_out_part,
            w_output, w_query, w_latent, w_latent_up, hidden_attn,
            query_nope, query_rope, key_value, key_pair,
            attended, latent_in, compressed, tables, gain_latent, gain_attn, heads_here, shared, 2,
        )
    )
    grad_latent = latent_sum[:, : KV_RANK + ROPE]
    grad_router = latent_sum[:, KV_RANK + ROPE : KV_RANK + ROPE + experts]
    flat = ep_index * tp_count + tp_index
    wide_part, rank_part = (n // (ep_count * tp_count) for n in (model_width, KV_RANK))
    grad_gain_attn = lax.dynamic_slice_in_dim(gains[0], flat * wide_part, wide_part, 0)
    grad_gain_ffn = lax.dynamic_slice_in_dim(gains[1], flat * wide_part, wide_part, 0)
    grad_gain_latent = lax.dynamic_slice_in_dim(gains[2], flat * rank_part, rank_part, 0)
    return (
        block_out,
        grad_inputs,
        grad_gain_attn,
        grad_query,
        grad_latent,
        grad_gain_latent,
        grad_latent_up,
        grad_output,
        grad_gain_ffn,
        grad_router,
        grad_shared_in,
        grad_shared_out,
        grad_expert_in,
        grad_expert_out,
    )


def solution(mesh):
    near = mesh.shape["ep"] == 8 and mesh.shape["tp"] == 4
    body = body_dense if near else body_slots
    placed = (
        P("ep", None),
        P(),
        P(None, "tp"),
        P(),
        P(),
        P(None, "tp"),
        P("tp", None),
        P(),
        P(),
        P(None, None, "tp"),
        P("tp", None),
        P("ep", None, None, "tp"),
        P("ep", "tp", None),
        P("ep", None),
        P("ep", None),
        P("ep", None),
    )
    return jax.shard_map(
        body,
        mesh=mesh,
        in_specs=placed,
        out_specs=(
            P("ep", None),
            P("ep", None),
            P(("ep", "tp")),
            P("ep", "tp"),
            P(("ep", "tp"), None),
            P(("ep", "tp")),
            P("ep", "tp"),
            P("tp", "ep"),
            P(("ep", "tp")),
            P(("ep", "tp"), None),
            P(None, "ep", "tp"),
            P("tp", "ep"),
            P("ep", None, None, "tp"),
            P("ep", "tp", None),
        ),
        check_vma=False,
    )
```

```python
import functools
import math

import jax
import jax.numpy as jnp
import numpy as np
from jax import lax
from jax.experimental import pallas as pl
from jax.experimental.pallas import tpu as pltpu
from jax.sharding import PartitionSpec as P

NOPE = 128
ROPE = 64
VDIM = 128
KV_RANK = 512
TOPK = 6
BLOCK = 256


EPSILON = 1e-06
HIGHEST = lax.Precision.HIGHEST


def angles(length, rope_width):
    half_width = rope_width // 2
    position = jnp.arange(length, dtype=jnp.float32)
    inverse = jnp.exp(jnp.arange(half_width, dtype=jnp.float32) * (-math.log(10000.0) / half_width))
    angle_table = position[:, None] * inverse[None, :]
    return (jnp.cos(angle_table), jnp.sin(angle_table))


def rotate(values, cosine, sine_table):
    half_width = values.shape[-1] // 2
    front_part = values[..., :half_width]
    second = values[..., half_width:]
    return jnp.concatenate(
        [front_part * cosine - second * sine_table, second * cosine + front_part * sine_table],
        axis=-1,
    )


def silu_parts(gate_val):
    sigmoid_val = jax.nn.sigmoid(gate_val)
    return (gate_val * sigmoid_val, sigmoid_val * (1.0 + gate_val * (1.0 - sigmoid_val)))


def norm_back(grad_norm, gain_vec, normed, inverse):
    scaled = grad_norm * gain_vec
    return inverse * (scaled - normed * jnp.mean(scaled * normed, axis=-1, keepdims=True))


def attention_scores(query_rot, key_nope, key_rope, score_scale, allowed):
    nope_scores = jnp.einsum(
        "qhd,khd->hqk", query_rot[..., :NOPE], key_nope, preferred_element_type=jnp.float32
    )
    rope_scores = jnp.einsum(
        "qhr,kr->hqk", query_rot[..., NOPE:], key_rope, preferred_element_type=jnp.float32
    )
    return jnp.where(allowed[None], (nope_scores + rope_scores) * score_scale, -1e30)


def expert_forward(received, w_expert_in, w_expert_out, sources):
    sectioned = received.reshape(sources, -1, received.shape[1], received.shape[2])
    gate_up = jnp.einsum(
        "secd,egdh->secgh", sectioned, w_expert_in, preferred_element_type=jnp.float32
    )
    gate_val, gate_slope = silu_parts(gate_up[..., 0, :])
    activated = (gate_val * gate_up[..., 1, :]).astype(jnp.bfloat16)
    produced = jnp.einsum(
        "sech,ehd->secd", activated, w_expert_out, preferred_element_type=jnp.float32
    )
    return (sectioned, gate_up, activated, produced.reshape(received.shape))


def body_slots(
    inputs,
    gain_attn,
    w_query,
    w_latent,
    gain_latent,
    w_latent_up,
    w_output,
    gain_ffn,
    w_router,
    w_shared_in,
    w_shared_out,
    w_expert_in,
    w_expert_out,
    expert_ids,
    slot_ids,
    cotangent,
):
    tokens, model_width = inputs.shape
    tp_count = lax.axis_size("tp")
    tp_index = lax.axis_index("tp")
    heads_here = w_output.shape[0] // VDIM
    experts = w_router.shape[1]
    local_experts = w_expert_in.shape[0]
    sources = experts // local_experts
    capacity = (9 * tokens * TOPK + 64 * experts - 1) // (64 * experts) * 8
    qk_width = NOPE + ROPE
    score_scale = qk_width ** (-0.5)
    rows_part = tokens // tp_count
    row_start = tp_index * rows_part
    resid = inputs.astype(jnp.float32)
    inv_first = lax.rsqrt(jnp.mean(resid * resid, axis=-1, keepdims=True) + EPSILON)
    normed_first = resid * inv_first
    hidden_attn = (normed_first * gain_attn).astype(jnp.bfloat16)
    cosine, sine_table = angles(tokens, ROPE)
    query_raw = jnp.dot(hidden_attn, w_query, preferred_element_type=jnp.float32).reshape(
        tokens, heads_here, qk_width
    )
    query_rot = jnp.concatenate(
        [
            query_raw[..., :NOPE],
            rotate(query_raw[..., NOPE:], cosine[:, None], sine_table[:, None]),
        ],
        axis=-1,
    ).astype(jnp.bfloat16)
    latent = jnp.dot(hidden_attn, w_latent, preferred_element_type=jnp.float32)
    compressed = latent[:, :KV_RANK]
    inv_latent = lax.rsqrt(jnp.mean(compressed * compressed, axis=-1, keepdims=True) + EPSILON)
    normed_latent = compressed * inv_latent
    latent_in = (normed_latent * gain_latent).astype(jnp.bfloat16)
    key_rope = rotate(latent[:, KV_RANK:], cosine, sine_table).astype(jnp.bfloat16)
    key_value = (
        jnp.dot(latent_in, w_latent_up, preferred_element_type=jnp.float32)
        .astype(jnp.bfloat16)
        .reshape(tokens, heads_here, NOPE + VDIM)
    )
    key_nope = key_value[..., :NOPE]
    values = key_value[..., NOPE:]
    block_ids = jnp.arange(tokens) // BLOCK
    allowed = block_ids[None, :] <= block_ids[:, None]
    scores = attention_scores(query_rot, key_nope, key_rope, score_scale, allowed)
    row_peak = jnp.max(scores, axis=-1, keepdims=True)
    exp_scores = jnp.exp(scores - row_peak)
    totals = jnp.sum(exp_scores, axis=-1, keepdims=True)
    attn_probs = exp_scores / totals
    log_total = row_peak + jnp.log(totals)
    attended = (
        jnp.einsum(
            "hqk,khd->qhd",
            attn_probs.astype(jnp.bfloat16),
            values,
            preferred_element_type=jnp.float32,
        )
        .astype(jnp.bfloat16)
        .reshape(tokens, heads_here * VDIM)
    )
    attn_full = lax.psum(
        jnp.dot(attended, w_output, preferred_element_type=jnp.float32).astype(jnp.bfloat16), "tp"
    ).astype(jnp.float32)
    middle = resid + attn_full
    inv_second = lax.rsqrt(jnp.mean(middle * middle, axis=-1, keepdims=True) + EPSILON)
    normed_second = middle * inv_second
    hidden_ffn = (normed_second * gain_ffn).astype(jnp.bfloat16)
    hidden_wide = hidden_ffn.astype(jnp.float32)
    logits = jnp.dot(hidden_wide, w_router, precision=HIGHEST, preferred_element_type=jnp.float32)
    logit_peak = jnp.max(logits, axis=-1, keepdims=True)
    exp_logits = jnp.exp(logits - logit_peak)
    router_probs = exp_logits / jnp.sum(exp_logits, axis=-1, keepdims=True)
    route_onehot = (
        expert_ids[:, :, None] == jnp.arange(experts, dtype=jnp.int32)[None, None, :]
    ).astype(jnp.float32)
    pair_gate = jnp.sum(route_onehot * router_probs[:, None, :], axis=-1)
    kept_pair = slot_ids < capacity
    flat_index = jnp.where(kept_pair, expert_ids * capacity + slot_ids, experts * capacity)
    row_numbers = jnp.broadcast_to(jnp.arange(tokens, dtype=jnp.int32)[:, None], (tokens, TOPK))
    owner_row = (
        jnp.full((experts * capacity,), tokens, jnp.int32)
        .at[flat_index.reshape(-1)]
        .set(row_numbers.reshape(-1), mode="drop")
    )
    outgoing = jnp.take(hidden_ffn, owner_row, axis=0, mode="fill", fill_value=0).reshape(
        experts, capacity, model_width
    )
    received = lax.all_to_all(outgoing, "ep", split_axis=0, concat_axis=0, tiled=True)
    sectioned, gate_up, activated, produced = expert_forward(
        received, w_expert_in, w_expert_out, sources
    )
    returned = lax.all_to_all(
        produced.astype(jnp.bfloat16), "ep", split_axis=0, concat_axis=0, tiled=True
    ).astype(produced.dtype)
    out_grad = cotangent.astype(jnp.float32)
    back_rows = returned.reshape(-1, model_width)
    combined = jnp.zeros((tokens, model_width), jnp.float32)
    gate_cols = []
    for pick_index in range(TOPK):
        taken_rows = jnp.take(
            back_rows, flat_index[:, pick_index], axis=0, mode="fill", fill_value=0.0
        )
        combined = combined + pair_gate[:, pick_index : pick_index + 1] * taken_rows
        gate_cols.append(jnp.sum(out_grad * taken_rows, axis=-1))
    gate_grad = jnp.stack(gate_cols, axis=1)
    shared_gate = jnp.dot(hidden_ffn, w_shared_in[0], preferred_element_type=jnp.float32)
    shared_up = jnp.dot(hidden_ffn, w_shared_in[1], preferred_element_type=jnp.float32)
    shared_val, shared_slope = silu_parts(shared_gate)
    shared_act = (shared_val * shared_up).astype(jnp.bfloat16)
    branch_part = jnp.dot(shared_act, w_shared_out, preferred_element_type=jnp.float32) + combined
    ffn_full = lax.psum(branch_part.astype(jnp.bfloat16), "tp").astype(jnp.float32)
    block_out = (middle + ffn_full).astype(jnp.bfloat16)
    slot_gate = (
        jnp.zeros((experts * capacity,), jnp.float32)
        .at[flat_index.reshape(-1)]
        .set(pair_gate.reshape(-1), mode="drop")
    )
    gathered_grad = jnp.take(cotangent, owner_row, axis=0, mode="fill", fill_value=0)
    slot_grad = (
        (slot_gate[:, None] * gathered_grad.astype(jnp.float32))
        .astype(jnp.bfloat16)
        .reshape(experts, capacity, model_width)
    )
    grad_arrived = lax.all_to_all(slot_grad, "ep", split_axis=0, concat_axis=0, tiled=True).reshape(
        sectioned.shape
    )
    act_grad = jnp.einsum(
        "secd,ehd->sech", grad_arrived, w_expert_out, preferred_element_type=jnp.float32
    )
    gate_val, gate_slope = silu_parts(gate_up[..., 0, :])
    up_val = gate_up[..., 1, :]
    gu_grad = jnp.stack([act_grad * up_val * gate_slope, act_grad * gate_val], axis=-2).astype(
        jnp.bfloat16
    )
    grad_expert_out = jnp.einsum(
        "sech,secd->ehd", activated, grad_arrived, preferred_element_type=jnp.float32
    )
    grad_expert_in = jnp.einsum(
        "secd,secgh->egdh", sectioned, gu_grad, preferred_element_type=jnp.float32
    )
    rows_grad = jnp.einsum(
        "secgh,egdh->secd", gu_grad, w_expert_in, preferred_element_type=jnp.float32
    ).reshape(received.shape)
    returned_grad = (
        lax.all_to_all(
            rows_grad.astype(jnp.bfloat16), "ep", split_axis=0, concat_axis=0, tiled=True
        )
        .astype(rows_grad.dtype)
        .reshape(-1, model_width)
    )
    routed_grad = jnp.zeros((tokens, model_width), jnp.float32)
    for pick_index in range(TOPK):
        routed_grad = routed_grad + jnp.take(
            returned_grad, flat_index[:, pick_index], axis=0, mode="fill", fill_value=0.0
        )
    shared_act_grad = jnp.einsum(
        "td,fd->tf", cotangent, w_shared_out, preferred_element_type=jnp.float32
    )
    shared_gate_grad = (shared_act_grad * shared_up * shared_slope).astype(jnp.bfloat16)
    shared_up_grad = (shared_act_grad * shared_val).astype(jnp.bfloat16)
    shared_out_grad = jnp.einsum(
        "tf,td->fd", shared_act, cotangent, preferred_element_type=jnp.float32
    )
    shared_in_grad = jnp.stack(
        [
            jnp.einsum(
                "td,tf->df", hidden_ffn, shared_gate_grad, preferred_element_type=jnp.float32
            ),
            jnp.einsum("td,tf->df", hidden_ffn, shared_up_grad, preferred_element_type=jnp.float32),
        ],
        axis=0,
    )
    shared_back = jnp.einsum(
        "tf,df->td", shared_gate_grad, w_shared_in[0], preferred_element_type=jnp.float32
    ) + jnp.einsum("tf,df->td", shared_up_grad, w_shared_in[1], preferred_element_type=jnp.float32)
    prob_grad = jnp.sum(route_onehot * gate_grad[:, :, None], axis=1)
    logit_grad = router_probs * (
        prob_grad - jnp.sum(router_probs * prob_grad, axis=-1, keepdims=True)
    )
    router_back = jnp.einsum(
        "te,de->td", logit_grad, w_router, precision=HIGHEST, preferred_element_type=jnp.float32
    )
    router_grad = jnp.einsum(
        "td,te->de", hidden_wide, logit_grad, precision=HIGHEST, preferred_element_type=jnp.float32
    )
    ffn_grad = lax.psum(
        (shared_back + routed_grad + router_back).astype(jnp.bfloat16), "tp"
    ).astype(jnp.float32)
    middle_grad = out_grad + norm_back(ffn_grad, gain_ffn, normed_second, inv_second)
    gain_ffn_grad = jnp.sum(
        lax.dynamic_slice_in_dim(ffn_grad * normed_second, row_start, rows_part, 0), axis=0
    )
    branch_grad = middle_grad.astype(jnp.bfloat16)
    output_w_grad = jnp.einsum(
        "tf,td->fd", attended, branch_grad, preferred_element_type=jnp.float32
    )
    attended_grad = (
        jnp.einsum("td,fd->tf", branch_grad, w_output, preferred_element_type=jnp.float32)
        .astype(jnp.bfloat16)
        .reshape(tokens, heads_here, VDIM)
    )
    scores_again = attention_scores(query_rot, key_nope, key_rope, score_scale, allowed)
    probs_again = jnp.exp(scores_again - log_total)
    values_grad = jnp.einsum(
        "hqk,qhd->khd",
        probs_again.astype(jnp.bfloat16),
        attended_grad,
        preferred_element_type=jnp.float32,
    )
    prob_part = jnp.einsum(
        "qhd,khd->hqk", attended_grad, values, preferred_element_type=jnp.float32
    )
    score_grad = (
        probs_again * (prob_part - jnp.sum(probs_again * prob_part, axis=-1, keepdims=True))
    ).astype(jnp.bfloat16)
    query_nope_grad = (
        jnp.einsum("hqk,khd->qhd", score_grad, key_nope, preferred_element_type=jnp.float32)
        * score_scale
    )
    query_rope_grad = (
        jnp.einsum("hqk,kr->qhr", score_grad, key_rope, preferred_element_type=jnp.float32)
        * score_scale
    )
    key_nope_grad = (
        jnp.einsum(
            "hqk,qhd->khd", score_grad, query_rot[..., :NOPE], preferred_element_type=jnp.float32
        )
        * score_scale
    )
    key_rope_grad = (
        jnp.einsum(
            "hqk,qhr->kr", score_grad, query_rot[..., NOPE:], preferred_element_type=jnp.float32
        )
        * score_scale
    )
    kv_grad = (
        jnp.concatenate([key_nope_grad, values_grad], axis=-1)
        .astype(jnp.bfloat16)
        .reshape(tokens, heads_here * (NOPE + VDIM))
    )
    latent_up_grad = jnp.einsum("tr,tf->rf", latent_in, kv_grad, preferred_element_type=jnp.float32)
    latent_in_grad = jnp.einsum(
        "tf,rf->tr", kv_grad, w_latent_up, preferred_element_type=jnp.float32
    )
    gain_latent_grad = jnp.sum(latent_in_grad * normed_latent, axis=0)
    latent_grad_part = jnp.concatenate(
        [
            norm_back(latent_in_grad, gain_latent, normed_latent, inv_latent),
            rotate(key_rope_grad, cosine, -sine_table),
        ],
        axis=-1,
    )
    query_grad = (
        jnp.concatenate(
            [query_nope_grad, rotate(query_rope_grad, cosine[:, None], -sine_table[:, None])],
            axis=-1,
        )
        .astype(jnp.bfloat16)
        .reshape(tokens, heads_here * qk_width)
    )
    query_w_grad = jnp.einsum(
        "td,tf->df", hidden_attn, query_grad, preferred_element_type=jnp.float32
    )
    hidden_part = jnp.einsum("tf,df->td", query_grad, w_query, preferred_element_type=jnp.float32)
    hidden_sum, latent_sum = (
        lax.psum(hidden_part.astype(jnp.bfloat16), "tp").astype(jnp.float32),
        lax.psum(latent_grad_part.astype(jnp.bfloat16), "tp").astype(jnp.float32),
    )
    latent_low = latent_sum.astype(jnp.bfloat16)
    attn_in_grad = hidden_sum + jnp.einsum(
        "tf,df->td", latent_low, w_latent, preferred_element_type=jnp.float32
    )
    latent_w_grad = jnp.einsum(
        "td,tf->df",
        lax.dynamic_slice_in_dim(hidden_attn, row_start, rows_part, 0),
        lax.dynamic_slice_in_dim(latent_low, row_start, rows_part, 0),
        preferred_element_type=jnp.float32,
    )
    gain_attn_grad = jnp.sum(
        lax.dynamic_slice_in_dim(attn_in_grad * normed_first, row_start, rows_part, 0), axis=0
    )
    grad_inputs = (
        middle_grad + norm_back(attn_in_grad, gain_attn, normed_first, inv_first)
    ).astype(jnp.bfloat16)
    grad_query, grad_latent_up, grad_output, grad_shared_in, grad_shared_out = (
        lax.psum_scatter(
            query_w_grad.astype(jnp.bfloat16), "ep", scatter_dimension=0, tiled=True
        ).astype(jnp.float32),
        lax.psum_scatter(
            latent_up_grad.astype(jnp.bfloat16), "ep", scatter_dimension=0, tiled=True
        ).astype(jnp.float32),
        lax.psum_scatter(
            output_w_grad.astype(jnp.bfloat16), "ep", scatter_dimension=1, tiled=True
        ).astype(jnp.float32),
        lax.psum_scatter(
            shared_in_grad.astype(jnp.bfloat16), "ep", scatter_dimension=1, tiled=True
        ).astype(jnp.float32),
        lax.psum_scatter(
            shared_out_grad.astype(jnp.bfloat16), "ep", scatter_dimension=1, tiled=True
        ).astype(jnp.float32),
    )
    grad_latent, grad_gain_latent, grad_gain_attn, grad_gain_ffn, grad_router = (
        lax.psum_scatter(latent_w_grad, ("ep", "tp"), scatter_dimension=0, tiled=True),
        lax.psum_scatter(gain_latent_grad, ("ep", "tp"), scatter_dimension=0, tiled=True),
        lax.psum_scatter(gain_attn_grad, ("ep", "tp"), scatter_dimension=0, tiled=True),
        lax.psum_scatter(gain_ffn_grad, ("ep", "tp"), scatter_dimension=0, tiled=True),
        lax.psum_scatter(router_grad, ("ep", "tp"), scatter_dimension=0, tiled=True),
    )
    return (
        block_out,
        grad_inputs,
        grad_gain_attn,
        grad_query,
        grad_latent,
        grad_gain_latent,
        grad_latent_up,
        grad_output,
        grad_gain_ffn,
        grad_router,
        grad_shared_in,
        grad_shared_out,
        grad_expert_in,
        grad_expert_out,
    )


MESH = pl.DeviceIdType.MESH


def plane_partners(ep):
    def flip(bit):
        return ep + bit - 2 * bit * lax.rem(lax.div(ep, bit), 2)

    return flip(1), flip(2), flip(4)


def line_order(tp):
    def pick(a, b, c, d):
        return jnp.where(tp == 0, a, jnp.where(tp == 1, b, jnp.where(tp == 2, c, d)))

    return (tp, pick(1, 0, 3, 2), pick(2, 2, 1, 1), pick(3, 3, 0, 0))


def greet(devices):
    barrier = pltpu.get_barrier_semaphore()
    for ep, tp in devices:
        pl.semaphore_signal(barrier, inc=1, device_id=(ep, tp), device_id_type=MESH)
    pl.semaphore_wait(barrier, len(devices))


def remote(src, dst, send, recv, device):
    return pltpu.make_async_remote_copy(
        src_ref=src, dst_ref=dst, send_sem=send, recv_sem=recv, device_id=device, device_id_type=MESH
    )


def add_rows(dst, a, b):
    def body(r, _):
        at = pl.ds(pl.multiple_of(r * 16, 16), 16)
        dst[at, :] = (a[at, :].astype(jnp.float32) + b[at, :].astype(jnp.float32)).astype(dst.dtype)
        return 0

    lax.fori_loop(0, dst.shape[0] // 16, body, 0)


def line_sum(own_of, got, send_sem, recv_sem, ep, tp, depth):
    far = line_order(tp)[::-1]
    between = (tp > 0) & (tp < depth - 1)
    near = jnp.where(tp > 0, tp - 1, tp + 1)

    def copy(n, src):
        chunk = far[n]
        to = jnp.where(chunk > tp, tp + 1, tp - 1)
        slot = jnp.where(chunk == tp - 1, depth, chunk)
        return remote(src, got.at[slot], send_sem.at[n], recv_sem.at[slot], (ep, to))

    def arrive(slot):
        remote(got.at[0], got.at[slot], send_sem.at[0], recv_sem.at[slot], (ep, near)).wait_recv()

    def start(n):
        @pl.when(jnp.logical_not(between))
        def _():
            copy(n, own_of(n)).start()

    def pass_on(n):
        @pl.when(between)
        def _():
            held = got.at[far[n]]
            arrive(far[n])
            add_rows(held, own_of(n), held)
            copy(n, held).start()

    def clear():
        @pl.when(tp == 0)
        def _():
            got[0] = jnp.zeros_like(got[0])

        @pl.when(tp == depth - 1)
        def _():
            got[depth] = jnp.zeros_like(got[depth])

    def finish():
        @pl.when(tp > 0)
        def _():
            arrive(tp)

        @pl.when(tp < depth - 1)
        def _():
            arrive(depth)

    def drain():
        for n in range(depth - 1):
            copy(n, got.at[0]).wait_send()

    return clear, start, pass_on, finish, drain


def line_total(own_of, pieces, up, down, up_send, up_recv, down_send, down_recv, ep, tp, depth):
    between = (tp > 0) & (tp < depth - 1)
    lowest, highest = tp == 0, tp == depth - 1
    above, below = jnp.minimum(tp + 1, depth - 1), jnp.maximum(tp - 1, 0)

    def up_copy(n, src):
        return remote(src, up.at[n], up_send.at[n], up_recv.at[n], (ep, above))

    def down_copy(n, src):
        return remote(src, down.at[n], down_send.at[n], down_recv.at[n], (ep, below))

    def start(n):
        @pl.when(lowest)
        def _():
            up_copy(n, own_of(n)).start()

        @pl.when(highest)
        def _():
            down_copy(n, own_of(n)).start()

    def hop(k, n):
        @pl.when(between & (tp == k))
        def _():
            up_copy(n, up.at[n]).wait_recv()
            add_rows(up.at[n], up.at[n], own_of(n))
            up_copy(n, up.at[n]).start()

        @pl.when(between & (tp == depth - 1 - k))
        def _():
            down_copy(n, down.at[n]).wait_recv()
            add_rows(down.at[n], down.at[n], own_of(n))
            down_copy(n, down.at[n]).start()

    def finish(n):
        @pl.when(lowest)
        def _():
            up[n] = own_of(n)[...]
            down_copy(n, down.at[n]).wait_recv()
            add_rows(down.at[n], down.at[n], own_of(n))

        @pl.when(highest)
        def _():
            down[n] = own_of(n)[...]
            up_copy(n, up.at[n]).wait_recv()
            add_rows(up.at[n], up.at[n], own_of(n))

    def drain():
        for n in range(pieces):

            @pl.when(jnp.logical_not(highest))
            def _():
                up_copy(n, up.at[n]).wait_send()

            @pl.when(jnp.logical_not(lowest))
            def _():
                down_copy(n, down.at[n]).wait_send()

    return start, hop, finish, drain


def turn(slab, table, sign):
    cosine, front, second = table
    return slab * cosine + sign * (pltpu.roll(slab, 96, 1) * front + pltpu.roll(slab, 32, 1) * second)


def experts_kernel(
    depth, blocks, heads, routed, shared, experts,
    inputs_ref, gain_attn, w_query, w_latent, gain_latent, w_up, w_output, tables,
    gain_ref, cot_ref, kept_hbm, e_in, e_out, s_in, s_out,
    middle_ref, h_out, cot_all, grads_out, gated_out, rows_out,
    hidden_out, qn_out, qr_out, kv_out, kr_out, attended_out, latent_in_out, compressed_out, w_out_out,
    part_ref, hidden, qn_ref, qr_ref, kv, kr_ref, attended, latent_in, compressed, rope_slab,
    kept_ref, w_in_ref, w_out_ref,
    h_all, got_z, cot_tile, gu, act_grad, prob_lanes, diff_lanes, pair_lanes,
    grads_tile, gated_tile, rows_tile,
    weight_sem, save_sem, local_sem, z_send, z_recv, line_send, line_recv, h_send, h_recv, c_send, c_recv, b_send, b_recv, tile_sem, store_sem,
):
    f32, bf16 = jnp.float32, jnp.bfloat16
    ep, tp = lax.axis_index("ep"), lax.axis_index("tp")
    pair, xn, yn = plane_partners(ep)
    parity = lax.rem(ep, 2)
    passed = jnp.where(parity == 0, xn, yn)
    onward = jnp.where(parity == 0, yn, xn)
    diag = xn + yn - ep
    rows = h_all.shape[2]
    width = h_all.shape[3]
    hidden_units = w_out_ref.shape[0]
    tokens = inputs_ref.shape[0]
    rank = compressed.shape[1]
    lanes = lax.broadcasted_iota(jnp.int32, (1, 128), 1)
    across = (((1,), (1,)), ((), ()))
    score_scale = (NOPE + ROPE) ** (-0.5)

    def dot(a, b, dims=(((1,), (0,)), ((), ()))):
        return lax.dot_general(a, b, dims, preferred_element_type=f32)

    half = blocks // 2
    tile = half * rows
    up, down = jnp.minimum(tp + 1, depth - 1), jnp.maximum(tp - 1, 0)

    def twin(block):
        return block + pair - ep

    greet([(pair, tp), (xn, tp), (yn, tp)] + [(ep, lax.rem(tp + k, depth)) for k in range(1, depth)])

    def part_rows(n):
        return part_ref.at[pl.ds(pl.multiple_of(line_order(tp)[depth - 1 - n] * rows, rows), rows)]

    z_clear, z_start, z_pass, z_finish, z_drain = line_sum(part_rows, got_z, z_send, z_recv, ep, tp, depth)
    z_clear()
    weight_loads = [
        pltpu.make_async_copy(kept_hbm, kept_ref, weight_sem.at[0]),
        pltpu.make_async_copy(e_out.at[0], w_out_ref.at[pl.ds(0, routed)], weight_sem.at[1]),
        pltpu.make_async_copy(s_out, w_out_ref.at[pl.ds(routed, hidden_units - routed)], weight_sem.at[2]),
    ]
    for g in range(2):
        own, beside = pl.ds(g * hidden_units, routed), pl.ds(g * hidden_units + routed, hidden_units - routed)
        weight_loads.append(pltpu.make_async_copy(e_in.at[0, g], w_in_ref.at[own], weight_sem.at[3 + 2 * g]))
        weight_loads.append(pltpu.make_async_copy(s_in.at[g], w_in_ref.at[beside], weight_sem.at[4 + 2 * g]))

    def h_copy(block, chunk, slot, to):
        ref = h_all.at[chunk, block]
        return remote(ref, ref, h_send.at[chunk, slot], h_recv.at[chunk, slot], (to, tp))

    def c_copy(block, chunk, slot, to):
        ref = cot_all.at[chunk, block]
        return remote(ref, ref, c_send.at[chunk, slot], c_recv.at[chunk, slot], (to, tp))

    def c_first(chunk, slot, to):
        src = cot_ref.at[pl.ds(pl.multiple_of(chunk * rows, rows), rows)]
        return remote(src, cot_all.at[chunk, ep], c_send.at[chunk, slot], c_recv.at[chunk, slot], (to, tp))

    buddy = tp + 1 - 2 * lax.rem(tp, 2)
    skipped, theirs = depth - 1 - tp, depth - 1 - buddy

    def buddy_copy(n, chunk):
        ref = cot_all.at[chunk, (xn, yn, diag)[n]]
        return remote(ref, ref, b_send.at[n], b_recv.at[n], (ep, buddy))

    def own_cot_in(chunk):
        src = cot_ref.at[pl.ds(pl.multiple_of(chunk * rows, rows), rows)]
        return pltpu.make_async_copy(src, rows_tile.at[0, chunk], local_sem.at[chunk])

    def own_cot_out(chunk):
        return pltpu.make_async_copy(rows_tile.at[0, chunk], cot_all.at[chunk, ep], local_sem.at[chunk])

    order = line_order(tp)

    def order_at(k):
        return jnp.where(k == 0, order[0], jnp.where(k == 1, order[1], jnp.where(k == 2, order[2], order[3])))

    for k in range(depth):

        @pl.when(order[k] != skipped)
        def _():
            c_first(order[k], 1, xn).start()
            c_first(order[k], 2, yn).start()

        c_first(order[k], 0, pair).start()
        own_cot_in(k).start()
    for copy in weight_loads:
        copy.start()

    def first_norm(r, _):
        at = pl.ds(pl.multiple_of(r * 16, 16), 16)
        v = inputs_ref[at, :].astype(f32)
        inverse = lax.rsqrt(jnp.mean(v * v, axis=-1, keepdims=True) + EPSILON)
        hidden[at, :] = (v * inverse * gain_attn[...]).astype(bf16)
        return 0

    lax.fori_loop(0, tokens // 16, first_norm, 0)
    table = tuple(tables[n] for n in range(3))
    latent = dot(hidden[...], w_latent[...], across)
    held = latent[:, :rank]
    compressed[...] = held
    inverse = lax.rsqrt(jnp.mean(held * held, axis=-1, keepdims=True) + EPSILON)
    latent_in[...] = (held * inverse * gain_latent[...]).astype(bf16)
    rope_slab[...] = jnp.zeros_like(rope_slab)
    rope_slab[:, 0:ROPE] = latent[:, rank:]
    key = turn(rope_slab[...], table, 1.0)
    kr_ref[0] = key.astype(bf16)
    kr_ref[1] = pltpu.roll(key, 64, 1).astype(bf16)
    kv[...] = dot(latent_in[...], w_up[...]).astype(bf16)
    wide = 2 * (NOPE + ROPE)
    for p in range(heads // 2):
        found = dot(hidden[...], w_query[:, p * wide : (p + 1) * wide])
        slabs = [found[:, n : n + 128] for n in (0, 128, 256)]
        qn_ref[:, 2 * p * NOPE : (2 * p + 1) * NOPE] = slabs[0].astype(bf16)
        odd = pltpu.roll(jnp.where(lanes < 64, slabs[2], slabs[1]), 64, 1)
        qn_ref[:, (2 * p + 1) * NOPE : (2 * p + 2) * NOPE] = odd.astype(bf16)
        qr_ref[:, p * 128 : (p + 1) * 128] = turn(jnp.where(lanes < 64, slabs[1], slabs[2]), table, 1.0).astype(bf16)
    for h in range(heads):
        for b in range(tokens // BLOCK):
            own = slice(b * BLOCK, (b + 1) * BLOCK)
            keys = slice(0, (b + 1) * BLOCK)
            slab = slice(h // 2 * 128, h // 2 * 128 + 128)
            at = slice(h * 128, h * 128 + 128)
            scores = dot(qn_ref[own, at], kv[keys, h * 256 : h * 256 + 128], across)
            scores = (scores + dot(qr_ref[own, slab], kr_ref[h % 2, keys, :], across)) * score_scale
            exps = jnp.exp(scores - jnp.max(scores, axis=-1, keepdims=True))
            probs = exps / jnp.sum(exps, axis=-1, keepdims=True)
            attended[own, at] = dot(probs.astype(bf16), kv[keys, h * 256 + 128 : h * 256 + 256]).astype(bf16)
    for n in range(0, width, 512):
        part_ref[:, n : n + 512] = dot(attended[...], w_output[:, n : n + 512]).astype(bf16)
    for n in range(depth - 1):
        z_start(n)
    saves = [
        pltpu.make_async_copy(src, dst, save_sem.at[n])
        for n, (src, dst) in enumerate(
            (
                (hidden, hidden_out), (qn_ref, qn_out), (qr_ref, qr_out), (kv, kv_out), (kr_ref, kr_out),
                (attended, attended_out), (latent_in, latent_in_out), (compressed, compressed_out),
            )
        )
    ]
    for copy in saves:
        copy.start()
    for k in range(depth):
        own_cot_in(k).wait()
        own_cot_out(k).start()

    for copy in weight_loads:
        copy.wait()
    w_out_save = pltpu.make_async_copy(w_out_ref, w_out_out, save_sem.at[8])
    w_out_save.start()
    z_pass(0)
    z_pass(1)
    z_pass(2)
    z_finish()

    def norm_rows(r, _):
        here = pl.ds(pl.multiple_of(r * 16, 16), 16)
        own = pl.ds(pl.multiple_of(tp * rows + r * 16, 16), 16)
        total = part_ref[own, :].astype(f32)
        total = total + got_z[tp, here, :].astype(f32) + got_z[depth, here, :].astype(f32)
        middle = inputs_ref[own, :].astype(f32) + total
        inverse = lax.rsqrt(jnp.mean(middle * middle, axis=-1, keepdims=True) + EPSILON)
        middle_ref[here, :] = middle
        h_all[tp, ep, here, :] = (middle * inverse * gain_ref[...]).astype(bf16)
        return 0

    lax.fori_loop(0, rows // 16, norm_rows, 0)
    for k in range(depth):
        own_cot_out(k).wait()

    def along(chunk, way, to):
        ref = h_all.at[chunk, ep]
        return remote(ref, ref, line_send.at[chunk, way], line_recv.at[chunk], (ep, to))

    def goes_up(chunk):
        return (chunk <= tp) & (tp < depth - 1)

    def goes_down(chunk):
        return (chunk >= tp) & (tp > 0)

    def send_chunk(k):
        chunk = order[k]
        if k > 0:
            along(chunk, 0, up).wait_recv()

        @pl.when(goes_up(chunk))
        def _():
            along(chunk, 0, up).start()

        @pl.when(goes_down(chunk))
        def _():
            along(chunk, 1, down).start()

        h_copy(ep, chunk, 1, xn).start()
        h_copy(ep, chunk, 2, yn).start()
        h_copy(ep, chunk, 0, pair).start()

    def forward_chunk(copy, chunk):
        copy(xn, chunk, 1, xn).wait_recv()
        copy(yn, chunk, 2, yn).wait_recv()
        copy(passed, chunk, 3, onward).start()
        copy(xn, chunk, 4, pair).start()
        copy(yn, chunk, 5, pair).start()

    def forward_diag(copy, chunk):
        copy(diag, chunk, 3, onward).wait_recv()
        copy(diag, chunk, 6, pair).start()

    def forward_skipped():
        for n, (block, slot) in enumerate(((xn, 4), (yn, 5), (diag, 6))):
            buddy_copy(n, skipped).wait_recv()
            c_copy(block, skipped, slot, pair).start()

    def await_pair(chunk, slots):
        for copy in (h_copy, c_copy):
            for slot, block in slots:
                copy(block, chunk, slot, pair).wait_recv()

    send_chunk(0)
    forward_chunk(c_copy, order[0])
    forward_chunk(h_copy, order[0])
    send_chunk(1)
    forward_chunk(c_copy, theirs)
    buddy_copy(0, theirs).start()
    buddy_copy(1, theirs).start()

    base = routed + shared
    slab = base // 128 * 128
    lane0 = base - slab
    near_half = lax.div(ep, half)

    def tile_copies(i):
        k, side = lax.div(i, 2), lax.rem(i, 2)
        chunk = order_at(k)
        start = jnp.where(side == 0, near_half, 1 - near_half) * half
        group = pl.ds(start, half)
        slot = lax.rem(i, 2)
        stores = [
            pltpu.make_async_copy(h_all.at[chunk, group], h_out.at[chunk, group], store_sem.at[slot, 0]),
            pltpu.make_async_copy(grads_tile.at[slot], grads_out.at[chunk, group], store_sem.at[slot, 1]),
            pltpu.make_async_copy(gated_tile.at[slot], gated_out.at[chunk, group], store_sem.at[slot, 2]),
            pltpu.make_async_copy(rows_tile.at[slot], rows_out.at[chunk, group], store_sem.at[slot, 3]),
        ]
        load = pltpu.make_async_copy(cot_all.at[chunk, group], cot_tile, tile_sem)
        return chunk, start, slot, load, stores

    def step(i, _):
        k, side = lax.div(i, 2), lax.rem(i, 2)
        chunk, start, slot, load, stores = tile_copies(i)

        @pl.when(side == 0)
        def _():
            await_pair(chunk, ((0, pair), (4, twin(xn))))

        @pl.when(i == 1)
        def _():
            forward_diag(c_copy, order[0])

        @pl.when(i == 2)
        def _():
            forward_diag(c_copy, theirs)
            buddy_copy(2, theirs).start()

        @pl.when(i == 3)
        def _():
            forward_diag(c_copy, order[1])

        @pl.when(side == 1)
        def _():
            forward_diag(h_copy, chunk)
            await_pair(chunk, ((5, twin(yn)), (6, twin(diag))))

        load.start()

        @pl.when(i >= 2)
        def _():
            for copy in tile_copies(i - 2)[4]:
                copy.wait()

        group = pl.ds(start, half)
        stores[0].start()
        for n in range(0, 2 * hidden_units, 512):
            gu[:, n : n + 512] = dot(h_all[chunk, group].reshape(tile, width), w_in_ref[n : n + 512, :], across)
        piece = gu[:, slab : slab + 128]
        logits = piece + pltpu.roll(piece, 128 - experts, 1) + pltpu.roll(piece, 128 - 2 * experts, 1)
        is_logit = (lanes >= lane0) & (lanes < lane0 + experts)
        logits = jnp.where(is_logit, logits, -1e30)
        exps = jnp.exp(logits - jnp.max(logits, axis=-1, keepdims=True))
        probs = exps / jnp.sum(exps, axis=-1, keepdims=True)
        here = (lanes == lane0 + ep).astype(f32)
        kept = kept_ref[chunk, group].reshape(tile, 128).astype(f32)
        prob_here = jnp.sum(probs * here * kept, axis=-1, keepdims=True)
        prob_lanes[...] = jnp.broadcast_to(prob_here, (tile, 128))
        diff_lanes[...] = here - probs

        @pl.when(i == 0)
        def _():
            forward_chunk(h_copy, order[1])
            send_chunk(2)

        @pl.when(i == 1)
        def _():
            forward_chunk(c_copy, order[1])
            send_chunk(3)

        @pl.when(i == 2)
        def _():
            forward_chunk(h_copy, order[2])

        @pl.when(i == 3)
        def _():
            forward_skipped()

        @pl.when(i == 4)
        def _():
            forward_chunk(h_copy, order[3])

        load.wait()
        act_grad[...] = lax.dot_general(
            cot_tile[...].reshape(tile, width), w_out_ref[...], (((1,), (1,)), ((), ())), preferred_element_type=f32
        )
        strip = 64

        def strips(r, _):
            at = pl.ds(pl.multiple_of(r * strip, strip), strip)
            gate_here = prob_lanes[at, :]
            pair_sum = jnp.zeros((strip, 128), f32)
            per = rows // strip
            block, inner = lax.div(r, per), pl.ds(pl.multiple_of(lax.rem(r, per) * strip, strip), strip)
            for n in range(0, hidden_units, 128):
                gate = gu[at, n : n + 128]
                up_val = gu[at, hidden_units + n : hidden_units + n + 128]
                grad = act_grad[at, n : n + 128]
                if n + 128 <= routed:
                    scale = gate_here
                elif n >= routed:
                    scale = None
                else:
                    scale = jnp.where(lanes < routed - n, gate_here, 1.0)
                sig = jax.nn.sigmoid(gate)
                silu = gate * sig
                act = silu * up_val
                if n < routed:
                    both = act * grad
                    if n + 128 > routed:
                        both = jnp.where(lanes < routed - n, both, 0.0)
                    pair_sum = pair_sum + both
                    act = act * scale
                    grad = grad * scale
                gated_tile[slot, block, inner, n : n + 128] = act.astype(bf16)
                grads_tile[slot, block, inner, n : n + 128] = (
                    grad * up_val * (sig * (1.0 + gate * (1.0 - sig)))
                ).astype(bf16)
                grads_tile[slot, block, inner, hidden_units + n : hidden_units + n + 128] = (grad * silu).astype(bf16)
            pair_lanes[at, :] = pair_sum
            return 0

        lax.fori_loop(0, tile // strip, strips, 0)
        pair_grad = jnp.sum(pair_lanes[...], axis=-1, keepdims=True)
        logit_grad = pair_grad * prob_lanes[...] * diff_lanes[...]
        logit_grad = logit_grad + pltpu.roll(logit_grad, experts, 1) + pltpu.roll(logit_grad, 2 * experts, 1)
        old = grads_tile[slot, :, :, slab : slab + 128].reshape(tile, 128)
        grads_tile[slot, :, :, slab : slab + 128] = (
            jnp.where(lanes >= lane0, logit_grad.astype(bf16), old).reshape(half, rows, 128)
        )
        for n in range(0, width, 512):
            rows_tile[slot, :, :, n : n + 512] = (
                dot(grads_tile[slot].reshape(tile, 2 * hidden_units), w_in_ref[:, n : n + 512]).astype(bf16).reshape(half, rows, 512)
            )
        for copy in stores[1:]:
            copy.start()
        return 0

    lax.fori_loop(0, 2 * depth, step, 0)
    for i in (2 * depth - 2, 2 * depth - 1):
        for copy in tile_copies(i)[4]:
            copy.wait()
    z_drain()
    for copy in saves:
        copy.wait()
    w_out_save.wait()

    def drain(k, _):
        chunk = order_at(k)

        @pl.when(goes_up(chunk))
        def _():
            along(chunk, 0, up).wait_send()

        @pl.when(goes_down(chunk))
        def _():
            along(chunk, 1, down).wait_send()

        for slot in range(7):
            h_copy(ep, chunk, slot, pair).wait_send()
        for slot in (0, 4, 5, 6):
            c_copy(ep, chunk, slot, pair).wait_send()

        @pl.when(chunk != skipped)
        def _():
            for slot in (1, 2, 3):
                c_copy(ep, chunk, slot, pair).wait_send()

        return 0

    lax.fori_loop(0, depth, drain, 0)
    for n in range(3):
        buddy_copy(n, theirs).wait_send()


def experts_call(
    inputs, gain_attn, w_query, w_latent, gain_latent, w_up, w_output, tables, gain, cotangent, kept, e_in, e_out, s_in, s_out,
    blocks, depth, heads, shared, experts, cid,
):
    f32, bf16 = jnp.float32, jnp.bfloat16
    tokens, width = inputs.shape
    rows = tokens // depth
    routed = e_out.shape[1]
    hidden = routed + s_out.shape[0]
    rank = w_up.shape[0]
    half = blocks // 2
    tile = half * rows
    dma = pltpu.SemaphoreType.DMA
    vmem, anywhere = pl.BlockSpec(memory_space=pltpu.VMEM), pl.BlockSpec(memory_space=pl.ANY)

    def units(size):
        return jax.ShapeDtypeStruct((depth, blocks, rows, size), bf16)

    kept_sizes = (
        ((tokens, width), bf16), ((tokens, heads * NOPE), bf16), ((tokens, heads * ROPE), bf16),
        ((tokens, heads * (NOPE + VDIM)), bf16), ((2, tokens, 128), bf16), ((tokens, heads * VDIM), bf16),
        ((tokens, rank), bf16), ((tokens, rank), f32),
    )

    return pl.pallas_call(
        functools.partial(experts_kernel, depth, blocks, heads, routed, shared, experts),
        out_shape=(
            jax.ShapeDtypeStruct((rows, width), f32),
            units(width), units(width), units(2 * hidden), units(hidden), units(width),
        )
        + tuple(jax.ShapeDtypeStruct(*size) for size in kept_sizes)
        + (jax.ShapeDtypeStruct((hidden, width), bf16),),
        in_specs=[vmem] * 9 + [anywhere] * 6,
        out_specs=(vmem,) + (anywhere,) * 14,
        scratch_shapes=[
            pltpu.VMEM((tokens, width), bf16),
            *(pltpu.VMEM(*size) for size in kept_sizes),
            pltpu.VMEM((tokens, 128), f32),
            pltpu.VMEM((depth, blocks, rows, 128), bf16),
            pltpu.VMEM((2 * hidden, width), bf16),
            pltpu.VMEM((hidden, width), bf16),
            pltpu.VMEM((depth, blocks, rows, width), bf16),
            pltpu.VMEM((depth + 1, rows, width), bf16),
            pltpu.VMEM((half, rows, width), bf16),
            pltpu.VMEM((tile, 2 * hidden), f32),
            pltpu.VMEM((tile, hidden), f32),
            pltpu.VMEM((tile, 128), f32),
            pltpu.VMEM((tile, 128), f32),
            pltpu.VMEM((tile, 128), f32),
            pltpu.VMEM((2, half, rows, 2 * hidden), bf16),
            pltpu.VMEM((2, half, rows, hidden), bf16),
            pltpu.VMEM((2, half, rows, width), bf16),
            dma((7,)), dma((9,)), dma((depth,)),
            dma((depth - 1,)), dma((depth + 1,)),
            dma((depth, 2)), dma((depth,)),
            dma((depth, 7)), dma((depth, 7)),
            dma((depth, 7)), dma((depth, 7)),
            dma((3,)), dma((3,)), dma, dma((2, 4)),
        ],
        compiler_params=pltpu.CompilerParams(collective_id=cid, has_side_effects=True, vmem_limit_bytes=63 << 20),
    )(
        inputs, gain_attn.reshape(1, width), w_query, w_latent, gain_latent.reshape(1, rank), w_up, w_output, tables,
        gain.reshape(1, width), cotangent, kept, e_in, e_out, s_in, s_out,
    )


def sum_kernel(
    depth, routed, shared, experts, part_ref, h_ref, grads_ref, gated_ref, cot_ref, middle_ref, gain_ref, w_out_ref,
    branch, gain_part, expert_in, expert_out, s_in, s_out, router, layer_sum, landed,
    in_grad, out_grad,
    load, store, layer, got_pair, got_first, got_second, got_z, keep, h_tile, grads_tile, gated_tile, cot_tile,
    own_cot, load_sem, store_sem, own_sem, lps, lpr, ps, pr, fs, fr, ss, sr, zs, zr, tile_sem, e_sem, o_sem,
):
    f32 = jnp.float32
    rows = part_ref.shape[2]
    count = h_tile.shape[0] * rows
    width = h_tile.shape[2]
    hidden = gated_tile.shape[2]
    ep, tp = lax.axis_index("ep"), lax.axis_index("tp")
    pair, xn, yn = plane_partners(ep)
    parity = lax.rem(ep, 2)
    first = jnp.where(parity == 0, xn, yn)
    second = jnp.where(parity == 0, yn, xn)
    diag = xn + yn - ep
    blocks = (first, diag, ep, second)
    pair_slot = (3, 1, 2, 0)
    greet([(pair, tp), (xn, tp), (yn, tp)] + [(ep, lax.rem(tp + k, depth)) for k in range(1, depth)])
    steps = [(k + 1) % depth for k in range(depth)]

    def chunk_of(i):
        return lax.rem(tp + steps[i], depth)

    def pair_copy(i, slot):
        src = part_ref.at[chunk_of(i), blocks[slot] + pair - ep]
        to = pair_slot[slot]
        return remote(src, got_pair.at[i, to], ps.at[i, slot], pr.at[i, to], (pair, tp))

    def pair_wait(i, slot):
        return remote(part_ref.at[0, 0], got_pair.at[i, slot], ps.at[i, slot], pr.at[i, slot], (pair, tp))

    def own_load(i, slot):
        return pltpu.make_async_copy(part_ref.at[chunk_of(i), blocks[slot]], load.at[slot], load_sem.at[slot])

    def first_copy(i, slot):
        return remote(got_pair.at[i, slot], got_first.at[i, slot], fs.at[i, slot], fr.at[i, slot], (first, tp))

    def second_copy(i):
        return remote(got_pair.at[i, 3], got_second.at[i], ss.at[i], sr.at[i], (second, tp))

    def z_copy(i):
        k = steps[i]
        return remote(got_pair.at[i, 2], got_z.at[k - 1], zs.at[k - 1], zr.at[k - 1], (ep, lax.rem(tp + k, depth)))

    def layer_pair(i, slot):
        src = layer.at[blocks[slot] + pair - ep]
        to = pair_slot[slot]
        return remote(src, landed.at[i, to], lps.at[i, slot], lpr.at[i, to], (pair, tp))

    def layer_load(i, slot):
        return pltpu.make_async_copy(landed.at[i, slot], load.at[slot], load_sem.at[slot])

    def layer_store(i, slot):
        return pltpu.make_async_copy(store.at[slot % 2], layer_sum.at[i, slot], store_sem.at[slot % 2])

    def layer_send(i):
        def columns(m, _):
            at = pl.ds(pl.multiple_of(m * 512, 512), 512)
            found = jnp.dot(gated_tile[...].reshape(count, hidden), w_out_ref[:, at], preferred_element_type=f32)
            layer[:, :, at] = found.astype(layer.dtype).reshape(layer.shape[0], rows, 512)
            return 0

        lax.fori_loop(0, width // 512, columns, 0)
        for slot in (3, 1, 2, 0):
            layer_pair(i, slot).start()

    def layer_add(i):
        for slot in range(4):
            layer_pair(i, pair_slot[slot]).wait_recv()
            layer_load(i, slot).start()
        for slot in range(4):
            layer_load(i, slot).wait()
            if slot >= 2:
                layer_store(i, slot - 2).wait()
            add_rows(store.at[slot % 2], load.at[slot], layer.at[blocks[slot]])
            layer_store(i, slot).start()
        layer_store(i, 2).wait()
        layer_store(i, 3).wait()
        for slot in range(4):
            layer_pair(i, slot).wait_send()

    for i in range(depth):
        for slot in (3, 1, 2, 0):
            pair_copy(i, slot).start()

    def tile_loads(c):
        return [
            pltpu.make_async_copy(src.at[c], dst, tile_sem.at[n])
            for n, (src, dst) in enumerate(
                ((h_ref, h_tile), (grads_ref, grads_tile), (gated_ref, gated_tile), (cot_ref, cot_tile))
            )
        ]

    def stage_a(i):
        for slot in range(4):
            own_load(i, slot).start()
        for slot in range(4):
            pair_wait(i, slot).wait_recv()
            own_load(i, slot).wait()
            add_rows(got_pair.at[i, slot], got_pair.at[i, slot], load.at[slot])
            if slot < 2:
                first_copy(i, slot).start()

    def stage_b(i):
        first_copy(i, 1).wait_recv()
        add_rows(got_pair.at[i, 3], got_pair.at[i, 3], got_first.at[i, 1])
        second_copy(i).start()
        first_copy(i, 0).wait_recv()
        add_rows(got_pair.at[i, 2], got_pair.at[i, 2], got_first.at[i, 0])

    def stage_c(i):
        second_copy(i).wait_recv()
        if i < depth - 1:
            add_rows(got_pair.at[i, 2], got_pair.at[i, 2], got_second.at[i])
            z_copy(i).start()
        else:
            add_rows(keep, got_pair.at[i, 2], got_second.at[i])


    blocks_all = h_tile.shape[0]
    def expert_out_copy():
        return pltpu.make_async_copy(out_grad.at[pl.ds(0, routed)], expert_out.at[0], o_sem)

    def expert_in_copy(g):
        return pltpu.make_async_copy(in_grad.at[pl.ds(g * hidden, routed)], expert_in.at[0, g], e_sem.at[g])

    def weights(c):
        for copy in tile_loads(c):
            copy.wait()
        turned = (((0,), (0,)), ((), ()))

        last = c == depth - 1

        def in_part(m, _):
            at = pl.ds(pl.multiple_of(m * 256, 256), 256)
            found = lax.dot_general(
                grads_tile[:, :, at].reshape(count, 256), h_tile[...].reshape(count, width), turned,
                preferred_element_type=f32,
            )
            in_grad[at, :] = found if c == 0 else in_grad[at, :] + found
            return 0

        lax.fori_loop(0, 2 * hidden // 256, in_part, 0)

        def out_part(m, _):
            at = pl.ds(pl.multiple_of(m * 512, 512), 512)
            found = lax.dot_general(
                gated_tile[...].reshape(count, hidden), cot_tile[:, :, at].reshape(count, 512), turned,
                preferred_element_type=f32,
            )
            out_grad[:, at] = found if c == 0 else out_grad[:, at] + found
            return 0

        lax.fori_loop(0, width // 512, out_part, 0)
        if last:
            expert_out_copy().start()
            expert_in_copy(0).start()
            expert_in_copy(1).start()
            router[...] = in_grad[routed + shared : routed + shared + experts, :]
            wide = width // blocks_all
            for b in range(blocks_all):
                at = slice(b * wide, (b + 1) * wide)
                s_out[b] = out_grad[routed : routed + s_out.shape[1], at].astype(s_out.dtype)
                for g in range(2):
                    top = g * hidden + routed
                    s_in[b, g] = in_grad[top : top + s_in.shape[2], at].astype(s_in.dtype)
        if c > 0:
            layer_add(c - 1)
        layer_send(c)
        if c + 1 < depth:
            for copy in tile_loads(c + 1):
                copy.start()

    own_copy = pltpu.make_async_copy(cot_ref.at[tp, ep], own_cot, own_sem)
    own_copy.start()
    for copy in tile_loads(0):
        copy.start()
    stage_a(0)
    stage_a(1)
    weights(0)
    stage_b(0)
    stage_a(2)
    weights(1)
    stage_b(1)
    stage_a(3)
    stage_c(0)
    weights(2)
    stage_b(2)
    stage_c(1)
    stage_b(3)
    weights(3)
    stage_c(2)
    stage_c(3)
    layer_add(depth - 1)
    for i in range(depth - 1):
        z_copy(i).wait_recv()
    own_copy.wait()

    def total(r, gain_sum):
        at = pl.ds(pl.multiple_of(r * 16, 16), 16)
        u = keep[at, :]
        for k in range(depth - 1):
            u = u + got_z[k, at, :].astype(f32)
        v = middle_ref[at, :]
        inverse = lax.rsqrt(jnp.mean(v * v, axis=-1, keepdims=True) + EPSILON)
        v_hat = v * inverse
        gain_sum = gain_sum + (u * v_hat)[:8] + (u * v_hat)[8:]
        s = u * gain_ref[...]
        back = inverse * (s - v_hat * jnp.mean(s * v_hat, axis=-1, keepdims=True))
        found = own_cot[at, :].astype(f32) + back
        branch[at, :] = found.astype(branch.dtype)
        return gain_sum

    gain_part[...] = lax.fori_loop(0, rows // 16, total, jnp.zeros((8, width), f32))
    expert_out_copy().wait()
    expert_in_copy(0).wait()
    expert_in_copy(1).wait()
    for i in range(depth):
        for slot in range(4):
            pair_copy(i, slot).wait_send()
        for slot in range(2):
            first_copy(i, slot).wait_send()
        second_copy(i).wait_send()
        if i < depth - 1:
            z_copy(i).wait_send()


def sum_call(part, h_all, grads, gated, cot_all, middle, gain, w_out, routed, shared, experts, cid):
    f32, bf16 = jnp.float32, jnp.bfloat16
    depth, blocks, rows, width = part.shape
    hidden = gated.shape[3]
    dma = pltpu.SemaphoreType.DMA
    vmem, anywhere = pl.BlockSpec(memory_space=pltpu.VMEM), pl.BlockSpec(memory_space=pl.ANY)
    return pl.pallas_call(
        functools.partial(sum_kernel, depth, routed, shared, experts),
        out_shape=(
            jax.ShapeDtypeStruct((rows, width), bf16),
            jax.ShapeDtypeStruct((8, width), f32),
            jax.ShapeDtypeStruct((1, 2, routed, width), f32),
            jax.ShapeDtypeStruct((1, routed, width), f32),
            jax.ShapeDtypeStruct((blocks, 2, -(-shared // 16) * 16, width // blocks), bf16),
            jax.ShapeDtypeStruct((blocks, -(-shared // 16) * 16, width // blocks), bf16),
            jax.ShapeDtypeStruct((experts, width), f32),
            jax.ShapeDtypeStruct((depth, 4, rows, width), bf16),
            jax.ShapeDtypeStruct((depth, 4, rows, width), bf16),
        ),
        in_specs=[anywhere] * 5 + [vmem] * 3,
        out_specs=(vmem,) * 2 + (anywhere,) * 2 + (vmem,) * 3 + (anywhere,) * 2,
        scratch_shapes=[
            pltpu.VMEM((2 * hidden, width), f32),
            pltpu.VMEM((hidden, width), f32),
            pltpu.VMEM((4, rows, width), bf16),
            pltpu.VMEM((2, rows, width), bf16),
            pltpu.VMEM((blocks, rows, width), bf16),
            pltpu.VMEM((depth, 4, rows, width), bf16),
            pltpu.VMEM((depth, 2, rows, width), bf16),
            pltpu.VMEM((depth, rows, width), bf16),
            pltpu.VMEM((depth - 1, rows, width), bf16),
            pltpu.VMEM((rows, width), f32),
            pltpu.VMEM((blocks, rows, width), bf16),
            pltpu.VMEM((blocks, rows, 2 * hidden), bf16),
            pltpu.VMEM((blocks, rows, hidden), bf16),
            pltpu.VMEM((blocks, rows, width), bf16),
            pltpu.VMEM((rows, width), bf16),
            dma((4,)), dma((2,)), dma, dma((depth, 4)), dma((depth, 4)), dma((depth, 4)), dma((depth, 4)), dma((depth, 2)), dma((depth, 2)),
            dma((depth,)), dma((depth,)), dma((depth - 1,)), dma((depth - 1,)), dma((4,)), dma((2,)), dma,
        ],
        compiler_params=pltpu.CompilerParams(collective_id=cid, has_side_effects=True, vmem_limit_bytes=62 << 20),
    )(part, h_all, grads, gated, cot_all, middle, gain.reshape(1, width), w_out)


def line_gather(ref, own, send_sem, recv_sem, ep, tp, depth):
    up, down = jnp.minimum(tp + 1, depth - 1), jnp.maximum(tp - 1, 0)
    order = line_order(tp)

    def along(k, way, to):
        chunk = order[k]
        src = own if k == 0 else ref.at[chunk]
        return remote(src, ref.at[chunk], send_sem.at[chunk, way], recv_sem.at[chunk], (ep, to))

    def each_way(k, act):
        @pl.when((order[k] <= tp) & (tp < depth - 1))
        def _():
            act(along(k, 0, up))

        @pl.when((order[k] >= tp) & (tp > 0))
        def _():
            act(along(k, 1, down))

    def pass_on(k):
        each_way(k, lambda copy: copy.start())

    def await_chunk(k):
        along(k, 0, up).wait_recv()

    def drain():
        for k in range(depth):
            each_way(k, lambda copy: copy.wait_send())

    return pass_on, await_chunk, drain


def tail_kernel(
    depth, heads, shared,
    branch_ref, middle_ref, part_ref, router_ref, gain_part_ref, inputs_ref, s_in, s_out,
    w_output_in, w_query_in, w_latent_in, w_up_in, hidden_in, qn_in, qr_in, kv_in, kr_in, attended_in, latent_in_in, compressed_in,
    tables_in, gain_latent, gain_attn,
    block_ref, grad_in_ref, gains_ref, query_ref, output_ref, up_ref, latent_ref, shared_in, shared_out, w_all, w_first,
    w_output, w_query, w_latent, w_up, hidden_ref, qn_ref, qr_ref, kv_ref, kr_ref, attended, latent_in, compressed,
    tables, load_in_sem,
    branch, held_rows, got_first, got_second, z_up, z_down, hidden_part, h_up, h_down, middle,
    d_out, d_kr, q_grad, kv_grad, l_grad, u_grad, w_stage, w_pair, w_second, w_z, latent_part, s_in_land, s_out_land, resid, grad_tile, block_tile, gains, attn_gains,
    load_sem, fs, fr, ss, sr, zus, zur, zds, zdr, bs, br, hus, hur, hds, hdr,
    wps, wpr, wfs, wfr, wss, wsr, wzs, wzr, as_, ar, ns, nr, misc_sem, resid_sem, grad_sem, block_sem, stage_sem, sis, sir, sos, sor,
):
    f32, bf16 = jnp.float32, jnp.bfloat16
    ep, tp = lax.axis_index("ep"), lax.axis_index("tp")
    pair, xn, yn = plane_partners(ep)
    parity = lax.rem(ep, 2)
    first = jnp.where(parity == 0, xn, yn)
    second = jnp.where(parity == 0, yn, xn)
    diag = xn + yn - ep
    blocks = (first, diag, ep, second)
    pair_slot = (3, 1, 2, 0)
    rows, width = middle.shape
    tokens = hidden_ref.shape[0]
    rank = compressed.shape[1]
    q_cols, l_cols = q_grad.shape[1], l_grad.shape[1]
    o_rows = attended.shape[1]
    count = w_all.shape[0]
    w_rows = w_all.shape[1]
    o_cols = width // count
    u_rows = rank // count
    u_cols = w_up.shape[1]
    o_start = q_cols + l_cols
    u_start = o_start + o_rows * o_cols // w_rows
    u_wide = u_rows * u_cols // w_rows
    order = line_order(tp)
    score_scale = (NOPE + ROPE) ** (-0.5)
    plane = [ep + sum(((pair, xn, yn)[n] - ep) * (m >> n & 1) for n in range(3)) for m in range(8)]
    greet([(to, tp) for to in plane[1:]] + [(ep, lax.rem(tp + k, depth)) for k in range(1, depth)])

    loads = [
        pltpu.make_async_copy(src, dst, load_in_sem.at[n])
        for n, (src, dst) in enumerate(
            (
                (w_output_in, w_output),
                (qn_in, qn_ref), (qr_in, qr_ref), (kv_in, kv_ref), (kr_in, kr_ref), (tables_in, tables),
                (w_up_in, w_up), (compressed_in, compressed), (w_query_in, w_query), (w_latent_in, w_latent),
                (hidden_in, hidden_ref), (attended_in, attended), (latent_in_in, latent_in),
            )
        )
    ]

    def loaded(first_load, last_load):
        for copy in loads[first_load:last_load]:
            copy.wait()

    branch_on, branch_wait, branch_drain = line_gather(branch, branch_ref, bs, br, ep, tp, depth)

    middle_copy = pltpu.make_async_copy(middle_ref, middle, misc_sem.at[1])

    def held_load(i, slot):
        return pltpu.make_async_copy(part_ref.at[i, slot], held_rows.at[i, slot - 2], load_sem.at[i, slot - 2])

    def first_copy(i, slot):
        return remote(part_ref.at[i, slot], got_first.at[i, slot], fs.at[i, slot], fr.at[i, slot], (first, tp))

    def second_copy(i):
        return remote(held_rows.at[i, 1], got_second.at[i], ss.at[i], sr.at[i], (second, tp))

    pieces, piece = h_up.shape[0], h_up.shape[1]
    per = rows // piece
    z_start, z_hop, z_finish, z_drain = line_total(
        lambda n: held_rows.at[n // per, 0, pl.ds(n % per * piece, piece)],
        pieces, z_up, z_down, zus, zur, zds, zdr, ep, tp, depth,
    )
    h_start, h_hop, h_finish, h_drain = line_total(
        lambda n: hidden_part.at[n], pieces, h_up, h_down, hus, hur, hds, hdr, ep, tp, depth
    )

    def stage_b(i):
        held_load(i, 3).wait()
        first_copy(i, 1).wait_recv()
        add_rows(held_rows.at[i, 1], held_rows.at[i, 1], got_first.at[i, 1])
        second_copy(i).start()
        held_load(i, 2).wait()
        first_copy(i, 0).wait_recv()
        add_rows(held_rows.at[i, 0], held_rows.at[i, 0], got_first.at[i, 0])

    def stage_c(i):
        second_copy(i).wait_recv()
        add_rows(held_rows.at[i, 0], held_rows.at[i, 0], got_second.at[i])

        @pl.when(tp == i)
        def _():
            middle_copy.wait()
            add_rows(held_rows.at[i, 0], held_rows.at[i, 0], middle)

        for n in range(per * i, per * i + per):
            z_start(n)

    def w_pair_copy(slot):
        to = pair_slot[slot]
        return remote(w_all.at[blocks[slot] + pair - ep], w_pair.at[to], wps.at[slot], wpr.at[to], (pair, tp))

    def w_pair_wait(slot):
        return remote(w_all.at[0], w_pair.at[slot], wps.at[slot], wpr.at[slot], (pair, tp))

    def w_first_copy(slot):
        return remote(w_pair.at[slot], w_first.at[slot], wfs.at[slot], wfr.at[slot], (first, tp))

    def w_second_copy():
        return remote(w_pair.at[3], w_second, wss, wsr, (second, tp))

    def w_load(slot):
        return pltpu.make_async_copy(w_all.at[blocks[slot]], w_stage.at[slot % 2], stage_sem.at[slot % 2])

    def w_stage_a():
        for slot in range(4):
            if slot < 3:
                w_load(slot + 1).start()
            w_pair_wait(slot).wait_recv()
            w_load(slot).wait()
            add_rows(w_pair.at[slot], w_pair.at[slot], w_stage.at[slot % 2])
            if slot < 2:
                w_first_copy(slot).start()

    def w_stage_b():
        def load(slot):
            return pltpu.make_async_copy(w_first.at[slot], w_stage.at[slot], stage_sem.at[slot])

        w_first_copy(1).wait_recv()
        load(1).start()
        w_first_copy(0).wait_recv()
        load(0).start()
        load(1).wait()
        add_rows(w_pair.at[3], w_pair.at[3], w_stage.at[1])
        w_second_copy().start()
        load(0).wait()
        add_rows(w_pair.at[2], w_pair.at[2], w_stage.at[0])

    def w_stage_c():
        w_second_copy().wait_recv()

        def total(cols, at=slice(None)):
            return w_pair[2, at, cols].astype(f32) + w_second[at, cols].astype(f32)

        query_ref[...] = total(slice(0, q_cols))
        latent_part[...] = total(slice(q_cols, o_start))
        for n in range(o_rows // w_rows):
            output_ref[n * w_rows : (n + 1) * w_rows, :] = total(slice(o_start + n * o_cols, o_start + (n + 1) * o_cols))
        for n in range(u_cols // u_wide):
            up_ref[:, n * u_wide : (n + 1) * u_wide] = total(
                slice(u_start, u_start + u_wide), slice(n * u_rows, (n + 1) * u_rows)
            )

    def shared_copies(m):
        to = plane[m]
        return (
            remote(s_in.at[to], s_in_land.at[ep], sis.at[m], sir.at[m], (to, tp)),
            remote(s_out.at[to], s_out_land.at[ep], sos.at[m], sor.at[m], (to, tp)),
        )

    def shared_own():
        return (
            pltpu.make_async_copy(s_in.at[ep], s_in_land.at[ep], sis.at[0]),
            pltpu.make_async_copy(s_out.at[ep], s_out_land.at[ep], sos.at[0]),
        )

    def shared_place():
        for m in range(1, 8):
            for copy in shared_copies(m):
                copy.wait_recv()
        for copy in shared_own():
            copy.wait()
        for n in range(s_in_land.shape[0]):
            at = slice(n * shared, (n + 1) * shared)
            for g in range(2):
                shared_in[g, at, :] = s_in_land[n, g].astype(f32)[:shared]
            shared_out[at, :] = s_out_land[n].astype(f32)[:shared]

    branch_on(0)
    branch[tp] = branch_ref[...]
    for i in range(depth):
        first_copy(i, 1).start()
        first_copy(i, 0).start()
        held_load(i, 3).start()
        held_load(i, 2).start()

    def resid_copy(n):
        return pltpu.make_async_copy(inputs_ref.at[pl.ds(n * piece, piece)], resid.at[n % 2], resid_sem.at[n % 2])

    for copy in loads:
        copy.start()
    resid_copy(0).start()
    resid_copy(1).start()
    middle_copy.start()

    turned, across = (((0,), (0,)), ((), ())), (((1,), (1,)), ((), ()))

    def dot(a, b, dims=(((1,), (0,)), ((), ()))):
        return lax.dot_general(a, b, dims, preferred_element_type=f32)

    def attended_grad(k):
        at = pl.ds(pl.multiple_of(order[k] * rows, rows), rows)
        d_out[at, :] = dot(branch[order[k]], w_output[...], across).astype(bf16)

    loaded(0, 1)
    attended_grad(0)
    branch_wait(1)
    branch_on(1)
    attended_grad(1)
    stage_b(0)
    branch_wait(2)
    branch_on(2)
    attended_grad(2)
    stage_c(0)
    stage_b(1)
    loaded(1, 6)
    branch_wait(3)
    branch_on(3)
    attended_grad(3)

    lanes = lax.broadcasted_iota(jnp.int32, (1, 128), 1)
    halves = tokens // BLOCK

    def head(h, even):
        mine = (lanes < 64) if even else (lanes >= 64)
        at_q = pl.ds(pl.multiple_of(h * NOPE, 128), 128)
        at_r = pl.ds(pl.multiple_of(lax.div(h, 2) * 128, 128), 128)
        at_k = pl.ds(pl.multiple_of(h * 256, 128), 128)
        at_v = pl.ds(pl.multiple_of(h * 256 + 128, 128), 128)
        kv_sum = [None, None]
        for b in reversed(range(halves)):
            own = slice(b * BLOCK, (b + 1) * BLOCK)
            keys = slice(0, (b + 1) * BLOCK)
            qn, qr = qn_ref[own, at_q], qr_ref[own, at_r]
            kn, kr = kv_ref[keys, at_k], kr_ref[0 if even else 1, keys, :]
            scores = (dot(qn, kn, across) + dot(qr, kr, across)) * score_scale
            exps = jnp.exp(scores - jnp.max(scores, axis=-1, keepdims=True))
            probs = exps / jnp.sum(exps, axis=-1, keepdims=True)
            grad = d_out[own, at_q]
            prob_part = dot(grad, kv_ref[keys, at_v], across)
            score_grad = (probs * (prob_part - jnp.sum(probs * prob_part, axis=-1, keepdims=True))).astype(bf16)
            found = (dot(score_grad, qn, turned) * score_scale, dot(probs.astype(bf16), grad, turned))
            r_grad = jnp.where(mine, dot(score_grad, qr, turned) * score_scale, 0.0)
            for n, at in enumerate((at_k, at_v)):
                if b < halves - 1:
                    kv_sum[n] = kv_sum[n] + found[n]
                else:
                    kv_sum[n] = found[n]
                kv_grad[own, at] = kv_sum[n][b * BLOCK :].astype(bf16)
                if b > 0:
                    kv_sum[n] = kv_sum[n][: b * BLOCK]
            d_kr[keys, :] = d_kr[keys, :] + r_grad
            yield own, dot(score_grad, kn) * score_scale, dot(score_grad, kr) * score_scale

    d_kr[...] = jnp.zeros_like(d_kr)

    def head_pair(p, _):
        evens = list(head(2 * p, True))
        odds = list(head(2 * p + 1, False))
        at = [pl.ds(pl.multiple_of(p * (2 * (NOPE + ROPE)) + n, 128), 128) for n in (0, 128, 256)]
        for (own, even, even_rope), (_, odd, odd_rope) in zip(evens, odds):
            table = tuple(tables[n, own, :] for n in range(3))
            rope = turn(even_rope + odd_rope, table, -1.0)
            odd = pltpu.roll(odd, 64, 1)
            q_grad[own, at[0]] = even.astype(bf16)
            q_grad[own, at[1]] = jnp.where(lanes < 64, rope, odd).astype(bf16)
            q_grad[own, at[2]] = jnp.where(lanes < 64, odd, rope).astype(bf16)
        return 0

    def head_pairs(p, _):
        head_pair(p, 0)

        @pl.when(p == 0)
        def _():
            stage_c(1)
            for n in range(per):
                z_hop(1, n)

        return 0

    lax.fori_loop(0, heads // 2, head_pairs, 0)
    for n in range(per):
        z_hop(2, n)
        z_hop(1, per + n)
    stage_b(2)

    loaded(6, 10)
    latent_back = dot(kv_grad[...], w_up[...], across)
    held = compressed[...]
    inverse = lax.rsqrt(jnp.mean(held * held, axis=-1, keepdims=True) + EPSILON)
    normed = held * inverse
    gain_latent_part = jnp.sum(latent_back * normed, axis=0, keepdims=True)
    scaled = latent_back * gain_latent[...]
    l_grad[:, :rank] = (inverse * (scaled - normed * jnp.mean(scaled * normed, axis=-1, keepdims=True))).astype(bf16)
    rope = d_kr[...] + pltpu.roll(d_kr[...], 64, 1)
    rope = turn(rope, tuple(tables[n] for n in range(3)), -1.0)
    l_grad[:, rank:] = jnp.where(lanes < 64, rope, 0.0).astype(bf16)

    for n in range(0, width, 512):
        part = dot(q_grad[...], w_query[n : n + 512, :], across) + dot(l_grad[:, : rank + ROPE], w_latent[:, n : n + 512])
        hidden_part[:, :, n : n + 512] = part.astype(bf16).reshape(pieces, piece, 512)
    for n in range(pieces):
        h_start(n)
    for n in range(per, 2 * per):
        z_hop(2, n)
    stage_c(2)
    stage_b(3)

    flip_1 = tp + 1 - 2 * lax.rem(tp, 2)
    flip_2 = tp + 2 - 4 * lax.div(tp, 2)

    def doubling(held, send, recv, partners):
        def copy(n):
            return remote(held.at[2 * n], held.at[2 * n + 1], send.at[n], recv.at[n], partners[n])

        def start():
            copy(0).start()

        def step(n):
            copy(n).wait_recv()
            total = held[2 * n] + held[2 * n + 1]
            if n + 1 < len(partners):
                held[2 * n + 2] = total
                copy(n + 1).start()
            return total

        def drain():
            for n in range(len(partners)):
                copy(n).wait_send()

        return start, step, drain

    gain_start, gain_step, gain_drain = doubling(
        gains, as_, ar, ((pair, tp), (xn, tp), (yn, tp), (ep, flip_1), (ep, flip_2))
    )
    attn_start, attn_step, attn_drain = doubling(attn_gains, ns, nr, ((pair, tp), (xn, tp), (yn, tp)))
    gains[0] = jnp.zeros_like(gains[0])
    gains[0, 1:2, :] = jnp.sum(gain_part_ref[...], axis=0, keepdims=True)
    gains[0, 2:3, 0:rank] = gain_latent_part
    gains[0, 8 : 8 + router_ref.shape[0], :] = router_ref[...]
    gain_start()

    loaded(10, 13)
    u_grad[...] = dot(latent_in[...], kv_grad[...], turned).astype(bf16)

    def w_store(b):
        slot = lax.rem(b, 2)
        return pltpu.make_async_copy(w_stage.at[slot], w_all.at[b], stage_sem.at[slot])

    def w_block(b, _):
        slot = lax.rem(b, 2)

        @pl.when(b >= 2)
        def _():
            w_store(b - 2).wait()

        at = pl.ds(pl.multiple_of(b * w_rows, 256), w_rows)
        own = hidden_ref[:, at]
        w_stage[slot, :, 0:q_cols] = dot(own, q_grad[...], turned).astype(bf16)
        found = dot(own, l_grad[...], turned)
        w_stage[slot, :, q_cols : q_cols + rank] = found[:, :rank].astype(bf16)
        w_stage[slot, :, q_cols + rank : o_start] = found[:, rank:].astype(bf16)
        cols = pl.ds(pl.multiple_of(b * o_cols, 256), o_cols)
        found = dot(attended[...], branch[:, :, cols].reshape(tokens, o_cols), turned)
        for n in range(o_rows // w_rows):
            w_stage[slot, :, o_start + n * o_cols : o_start + (n + 1) * o_cols] = (
                found[n * w_rows : (n + 1) * w_rows].astype(bf16)
            )
        u_at = pl.ds(pl.multiple_of(b * u_rows, u_rows), u_rows)
        for n in range(u_cols // u_wide):
            w_stage[slot, n * u_rows : (n + 1) * u_rows, u_start : u_start + u_wide] = (
                u_grad[u_at, n * u_wide : (n + 1) * u_wide]
            )
        w_store(b).start()
        return 0

    lax.fori_loop(0, count, w_block, 0)
    w_store(count - 2).wait()
    w_store(count - 1).wait()
    for slot in (3, 1, 2, 0):
        w_pair_copy(slot).start()
    for copy in shared_own():
        copy.start()
    for m in range(1, 8):
        for copy in shared_copies(m):
            copy.start()
    w_load(0).start()

    w_part = w_rows // depth

    def w_z_copy(k):
        to = lax.rem(tp + k, depth)
        src = w_pair.at[1, pl.ds(pl.multiple_of(to * w_part, w_part), w_part), pl.ds(q_cols, l_cols)]
        return remote(src, w_z.at[k - 1], wzs.at[k - 1], wzr.at[k - 1], (ep, to))

    def block_copy(n):
        return pltpu.make_async_copy(block_tile.at[n % 2], block_ref.at[pl.ds(n * piece, piece)], block_sem.at[n % 2])

    def block_rows(n):
        z_finish(n)
        if n >= 2:
            block_copy(n - 2).wait()

        def total(r, _):
            at = pl.ds(pl.multiple_of(r * 16, 16), 16)
            inside = pl.ds(pl.multiple_of(n % per * piece + r * 16, 16), 16)
            value = z_up[n, at, :].astype(f32) + z_down[n, at, :].astype(f32) - held_rows[n // per, 0, inside, :].astype(f32)
            block_tile[n % 2, at, :] = value.astype(bf16)
            return 0

        lax.fori_loop(0, piece // 16, total, 0)
        block_copy(n).start()

    def grad_copy(n):
        return pltpu.make_async_copy(grad_tile.at[n % 2], grad_in_ref.at[pl.ds(n * piece, piece)], grad_sem.at[n % 2])

    def grad_rows(n, gain_sum):
        h_finish(n)
        if n >= 2:
            grad_copy(n - 2).wait()
        resid_copy(n).wait()

        def total(r, gain_sum):
            at = pl.ds(pl.multiple_of(r * 16, 16), 16)
            inside = pl.ds(pl.multiple_of(n % per * piece + r * 16, 16), 16)
            u = h_up[n, at, :].astype(f32) + h_down[n, at, :].astype(f32) - hidden_part[n, at, :].astype(f32)
            v = resid[n % 2, at, :].astype(f32)
            inv = lax.rsqrt(jnp.mean(v * v, axis=-1, keepdims=True) + EPSILON)
            v_hat = v * inv
            gain_sum = gain_sum + (u * v_hat)[:8] + (u * v_hat)[8:]
            s = u * gain_attn[...]
            back = inv * (s - v_hat * jnp.mean(s * v_hat, axis=-1, keepdims=True))
            grad_tile[n % 2, at, :] = (branch[n // per, inside, :].astype(f32) + back).astype(bf16)
            return gain_sum

        gain_sum = lax.fori_loop(0, piece // 16, total, gain_sum)
        if n + 2 < pieces:
            resid_copy(n + 2).start()
        grad_copy(n).start()
        return gain_sum

    gain_sum = jnp.zeros((8, width), f32)
    for t in range(pieces + 2):
        if t < pieces:
            h_hop(1, t)
        if t >= 2:
            h_hop(2, t - 2)
        if t >= 4:
            gain_sum = grad_rows(t - 4, gain_sum)
        if t == 1:
            gain_step(0)
        if t == 2:
            w_stage_a()
        if t == 0:
            stage_c(3)
        if t == 3:
            gain_step(1)
        if t == 5:
            block_rows(0)
            block_rows(1)
            gain_step(2)
        if t == 6:
            gain_step(3)
        if t == 7:
            w_stage_b()
            block_rows(2)
            block_rows(3)
        if t == 8:
            gains_ref[...] = gain_step(4)
    for t in range(pieces // 2 + 2):
        if t < pieces // 2:
            z_hop(1, pieces // 2 + t)
        if t >= 2:
            z_hop(2, pieces // 2 + t - 2)
        if t < 2:
            gain_sum = grad_rows(pieces - 2 + t, gain_sum)
        if t == 1:
            attn_gains[0] = gain_sum
            attn_start()
        if t == 2:
            w_stage_c()
            w_first_copy(1).wait_send()
            w_pair[1, :, q_cols:o_start] = latent_part[...].astype(bf16)
            for k in range(1, depth):
                w_z_copy(k).start()
            attn_step(0)
            shared_place()
        if t == 4:
            attn_step(1)
    for n in range(pieces // 2, pieces):
        block_rows(n)
    for k in range(1, depth):
        w_z_copy(k).wait_recv()
    own = pl.ds(pl.multiple_of(tp * w_part, w_part), w_part)
    total = latent_part[own, :]
    for k in range(depth - 1):
        total = total + w_z[k].astype(f32)
    latent_ref[...] = total
    gains_ref[0:1, :] = jnp.sum(attn_step(2), axis=0, keepdims=True)

    for n in (pieces - 2, pieces - 1):
        block_copy(n).wait()
    for n in (pieces - 2, pieces - 1):
        grad_copy(n).wait()
    branch_drain()
    for i in range(depth):
        for slot in range(2):
            first_copy(i, slot).wait_send()
        second_copy(i).wait_send()
    z_drain()
    h_drain()
    for slot in range(4):
        w_pair_copy(slot).wait_send()
    w_first_copy(0).wait_send()
    w_second_copy().wait_send()
    for k in range(1, depth):
        w_z_copy(k).wait_send()
    gain_drain()
    attn_drain()
    for m in range(1, 8):
        for copy in shared_copies(m):
            copy.wait_send()


def tail_call(
    branch, middle, out_part, router, gain_part, inputs, s_in, s_out, w_output, w_query, w_latent, w_up,
    hidden, qn, qr, kv, kr, attended, latent_in, compressed, tables, gain_latent, gain_attn,
    heads, shared, cid,
):
    f32, bf16 = jnp.float32, jnp.bfloat16
    depth, _, rows, width = out_part.shape
    tokens = hidden.shape[0]
    blocks = s_in.shape[0]
    rank = compressed.shape[1]
    q_cols, l_cols = w_query.shape[1], rank + 128
    pieces = 2 * depth
    w_rows = width // blocks
    w_cols = q_cols + l_cols + w_output.shape[0] + rank * w_up.shape[1] // width
    dma = pltpu.SemaphoreType.DMA
    vmem, anywhere = pl.BlockSpec(memory_space=pltpu.VMEM), pl.BlockSpec(memory_space=pl.ANY)
    return pl.pallas_call(
        functools.partial(tail_kernel, depth, heads, shared),
        out_shape=(
            jax.ShapeDtypeStruct((tokens, width), bf16),
            jax.ShapeDtypeStruct((tokens, width), bf16),
            jax.ShapeDtypeStruct((8 + router.shape[0], width), f32),
            jax.ShapeDtypeStruct((w_rows, q_cols), f32),
            jax.ShapeDtypeStruct((w_output.shape[0], w_rows), f32),
            jax.ShapeDtypeStruct((rank // blocks, w_up.shape[1]), f32),
            jax.ShapeDtypeStruct((w_rows // depth, l_cols), f32),
            jax.ShapeDtypeStruct((2, blocks * shared, w_rows), f32),
            jax.ShapeDtypeStruct((blocks * shared, w_rows), f32),
            jax.ShapeDtypeStruct((blocks, w_rows, w_cols), bf16),
            jax.ShapeDtypeStruct((2, w_rows, w_cols), bf16),
        ),
        in_specs=[vmem, anywhere, anywhere, vmem, vmem] + [anywhere] * 16 + [vmem, vmem],
        out_specs=(anywhere, anywhere) + (vmem,) * 7 + (anywhere, anywhere),
        scratch_shapes=[
            *(
                pltpu.VMEM(a.shape, a.dtype)
                for a in (
                    w_output, w_query, w_latent, w_up, hidden, qn, qr, kv, kr, attended, latent_in, compressed, tables,
                )
            ),
            dma((13,)),
            pltpu.VMEM((depth, rows, width), bf16),
            pltpu.VMEM((depth, 2, rows, width), bf16),
            pltpu.VMEM((depth, 2, rows, width), bf16),
            pltpu.VMEM((depth, rows, width), bf16),
            pltpu.VMEM((pieces, tokens // pieces, width), bf16),
            pltpu.VMEM((pieces, tokens // pieces, width), bf16),
            pltpu.VMEM((pieces, tokens // pieces, width), bf16),
            pltpu.VMEM((pieces, tokens // pieces, width), bf16),
            pltpu.VMEM((pieces, tokens // pieces, width), bf16),
            pltpu.VMEM((rows, width), f32),
            pltpu.VMEM((tokens, heads * VDIM), bf16),
            pltpu.VMEM((tokens, 128), f32),
            pltpu.VMEM((tokens, q_cols), bf16),
            pltpu.VMEM((tokens, heads * (NOPE + VDIM)), bf16),
            pltpu.VMEM((tokens, l_cols), bf16),
            pltpu.VMEM((rank, heads * (NOPE + VDIM)), bf16),
            pltpu.VMEM((2, w_rows, w_cols), bf16),
            pltpu.VMEM((4, w_rows, w_cols), bf16),
            pltpu.VMEM((w_rows, w_cols), bf16),
            pltpu.VMEM((depth - 1, w_rows // depth, l_cols), bf16),
            pltpu.VMEM((w_rows, l_cols), f32),
            pltpu.VMEM(s_in.shape, bf16),
            pltpu.VMEM(s_out.shape, bf16),
            pltpu.VMEM((2, tokens // pieces, width), bf16),
            pltpu.VMEM((2, tokens // pieces, width), bf16),
            pltpu.VMEM((2, tokens // pieces, width), bf16),
            pltpu.VMEM((10, 8 + router.shape[0], width), f32),
            pltpu.VMEM((6, 8, width), f32),
            dma((depth, 2)),
            dma((depth, 2)), dma((depth, 2)), dma((depth,)), dma((depth,)),
            dma((pieces,)), dma((pieces,)), dma((pieces,)), dma((pieces,)),
            dma((depth, 2)), dma((depth,)),
            dma((pieces,)), dma((pieces,)), dma((pieces,)), dma((pieces,)),
            dma((4,)), dma((4,)), dma((2,)), dma((2,)), dma, dma, dma((depth - 1,)), dma((depth - 1,)),
            dma((5,)), dma((5,)), dma((3,)), dma((3,)), dma((2,)), dma((2,)), dma((2,)), dma((2,)), dma((2,)), dma((8,)), dma((8,)), dma((8,)), dma((8,)),
        ],
        compiler_params=pltpu.CompilerParams(collective_id=cid, has_side_effects=True, vmem_limit_bytes=63 << 20),
    )(
        branch, middle, out_part, router, gain_part, inputs, s_in, s_out, w_output, w_query, w_latent, w_up,
        hidden, qn, qr, kv, kr, attended, latent_in, compressed, tables,
        gain_latent.reshape(1, rank), gain_attn.reshape(1, width),
    )


def rope_tables(length):
    half = ROPE // 2
    inverse = np.exp(np.arange(half) * (-math.log(10000.0) / half))
    angle = np.arange(length)[:, None] * inverse[None, :]
    cosine, sine = np.cos(angle), np.sin(angle)
    zero = np.zeros_like(sine)
    parts = ([cosine] * 4, [-sine, zero] * 2, [zero, sine] * 2)
    return jnp.asarray(np.stack([np.concatenate(p, axis=1) for p in parts]), jnp.float32)


def padded_hidden(routed, shared):
    return -(-(routed + shared + 24) // 128) * 128


def split_wide(values):
    high = values.astype(jnp.bfloat16)
    rest = values - high.astype(jnp.float32)
    mid = rest.astype(jnp.bfloat16)
    low = (rest - mid.astype(jnp.float32)).astype(jnp.bfloat16)
    return (high, mid, low)


def body_dense(
    inputs,
    gain_attn,
    w_query,
    w_latent,
    gain_latent,
    w_latent_up,
    w_output,
    gain_ffn,
    w_router,
    w_shared_in,
    w_shared_out,
    w_expert_in,
    w_expert_out,
    expert_ids,
    slot_ids,
    cotangent,
):
    f32, bf16 = jnp.float32, jnp.bfloat16
    tokens, model_width = inputs.shape
    ep_count, tp_count = lax.axis_size("ep"), lax.axis_size("tp")
    ep_index, tp_index = lax.axis_index("ep"), lax.axis_index("tp")
    heads_here = w_output.shape[0] // VDIM
    experts = w_router.shape[1]
    capacity = (9 * tokens * TOPK + 64 * experts - 1) // (64 * experts) * 8
    qk_width = NOPE + ROPE
    score_scale = qk_width ** (-0.5)
    rows_part = tokens // tp_count

    expert_range = jnp.arange(experts, dtype=jnp.int32)
    kept = jnp.any(
        (expert_ids[:, :, None] == expert_range) & (slot_ids < capacity)[:, :, None], axis=1
    ).astype(f32)
    kept_here = lax.all_to_all(kept, "ep", split_axis=1, concat_axis=0, tiled=True)
    rows_part = tokens // tp_count
    kept_lanes = jnp.broadcast_to(
        kept_here.reshape(ep_count, tp_count, rows_part, 1).swapaxes(0, 1),
        (tp_count, ep_count, rows_part, 128),
    ).astype(bf16)

    routed = w_expert_in.shape[3]
    shared = w_shared_in.shape[2] // ep_count
    hidden = padded_hidden(routed, shared)
    shared_start = ep_index * shared
    after = hidden - routed - shared
    router_parts = jnp.concatenate(split_wide(w_router), axis=1).T
    beside = jnp.stack(
        [
            jnp.pad(router_parts, ((0, after - router_parts.shape[0]), (0, 0))),
            jnp.zeros((after, model_width), bf16),
        ]
    )
    shared_in = lax.dynamic_slice_in_dim(w_shared_in.swapaxes(1, 2), shared_start, shared, 1)
    shared_in = jnp.concatenate([shared_in, beside], axis=1)
    shared_out = lax.dynamic_slice_in_dim(w_shared_out, shared_start, shared, 0)
    shared_out = jnp.pad(shared_out, ((0, after), (0, 0)))
    tables = rope_tables(tokens)
    (
        middle, hidden_all, cot_all, hidden_grads, gated, rows_grad,
        hidden_attn, query_nope, query_rope, key_value, key_pair, attended, latent_in, compressed, w_out,
    ) = experts_call(
        inputs, gain_attn, w_query, w_latent.T, gain_latent, w_latent_up, w_output, tables, gain_ffn, cotangent, kept_lanes,
        w_expert_in.swapaxes(2, 3), w_expert_out, shared_in, shared_out, ep_count, tp_count, heads_here, shared, experts, 0,
    )
    branch, gain_ffn_part, grad_expert_in, grad_expert_out, shared_in_part, shared_out_part, router_part, layer_sum, _ = (
        sum_call(
            rows_grad, hidden_all, hidden_grads, gated, cot_all, middle, gain_ffn, w_out, routed, shared, experts, 1
        )
    )
    block_out, grad_inputs, gains, grad_query, grad_output, grad_latent_up, latent_sum, grad_shared_in, grad_shared_out, _, _ = (
        tail_call(
            branch, middle, layer_sum, router_part, gain_ffn_part, inputs, shared_in_part, shared_out_part,
            w_output, w_query, w_latent.T, w_latent_up, hidden_attn,
            query_nope, query_rope, key_value, key_pair,
            attended, latent_in, compressed, tables, gain_latent, gain_attn, heads_here, shared, 2,
        )
    )
    grad_latent = latent_sum[:, : KV_RANK + ROPE]
    flat = ep_index * tp_count + tp_index
    wide_part, rank_part = (n // (ep_count * tp_count) for n in (model_width, KV_RANK))
    grad_gain_attn = lax.dynamic_slice_in_dim(gains[0], flat * wide_part, wide_part, 0)
    grad_gain_ffn = lax.dynamic_slice_in_dim(gains[1], flat * wide_part, wide_part, 0)
    grad_gain_latent = lax.dynamic_slice_in_dim(gains[2], flat * rank_part, rank_part, 0)
    grad_router = lax.dynamic_slice_in_dim(gains[8:], flat * wide_part, wide_part, 1).T
    grad_expert_in = grad_expert_in.swapaxes(2, 3)
    grad_shared_in = grad_shared_in.swapaxes(1, 2)
    return (
        block_out,
        grad_inputs,
        grad_gain_attn,
        grad_query,
        grad_latent,
        grad_gain_latent,
        grad_latent_up,
        grad_output,
        grad_gain_ffn,
        grad_router,
        grad_shared_in,
        grad_shared_out,
        grad_expert_in,
        grad_expert_out,
    )


def solution(mesh):
    near = mesh.shape["ep"] == 8 and mesh.shape["tp"] == 4
    body = body_dense if near else body_slots
    placed = (
        P("ep", None),
        P(),
        P(None, "tp"),
        P(),
        P(),
        P(None, "tp"),
        P("tp", None),
        P(),
        P(),
        P(None, None, "tp"),
        P("tp", None),
        P("ep", None, None, "tp"),
        P("ep", "tp", None),
        P("ep", None),
        P("ep", None),
        P("ep", None),
    )
    return jax.shard_map(
        body,
        mesh=mesh,
        in_specs=placed,
        out_specs=(
            P("ep", None),
            P("ep", None),
            P(("ep", "tp")),
            P("ep", "tp"),
            P(("ep", "tp"), None),
            P(("ep", "tp")),
            P("ep", "tp"),
            P("tp", "ep"),
            P(("ep", "tp")),
            P(("ep", "tp"), None),
            P(None, "ep", "tp"),
            P("tp", "ep"),
            P("ep", None, None, "tp"),
            P("ep", "tp", None),
        ),
        check_vma=False,
    )
```

```python
import functools
import math

import jax
import jax.numpy as jnp
import numpy as np
from jax import lax
from jax.experimental import pallas as pl
from jax.experimental.pallas import tpu as pltpu
from jax.sharding import PartitionSpec as P

NOPE = 128
ROPE = 64
VDIM = 128
KV_RANK = 512
TOPK = 6
BLOCK = 256


EPSILON = 1e-06
HIGHEST = lax.Precision.HIGHEST


def angles(length, rope_width):
    half_width = rope_width // 2
    position = jnp.arange(length, dtype=jnp.float32)
    inverse = jnp.exp(jnp.arange(half_width, dtype=jnp.float32) * (-math.log(10000.0) / half_width))
    angle_table = position[:, None] * inverse[None, :]
    return (jnp.cos(angle_table), jnp.sin(angle_table))


def rotate(values, cosine, sine_table):
    half_width = values.shape[-1] // 2
    front_part = values[..., :half_width]
    second = values[..., half_width:]
    return jnp.concatenate(
        [front_part * cosine - second * sine_table, second * cosine + front_part * sine_table],
        axis=-1,
    )


def silu_parts(gate_val):
    sigmoid_val = jax.nn.sigmoid(gate_val)
    return (gate_val * sigmoid_val, sigmoid_val * (1.0 + gate_val * (1.0 - sigmoid_val)))


def norm_back(grad_norm, gain_vec, normed, inverse):
    scaled = grad_norm * gain_vec
    return inverse * (scaled - normed * jnp.mean(scaled * normed, axis=-1, keepdims=True))


def attention_scores(query_rot, key_nope, key_rope, score_scale, allowed):
    nope_scores = jnp.einsum(
        "qhd,khd->hqk", query_rot[..., :NOPE], key_nope, preferred_element_type=jnp.float32
    )
    rope_scores = jnp.einsum(
        "qhr,kr->hqk", query_rot[..., NOPE:], key_rope, preferred_element_type=jnp.float32
    )
    return jnp.where(allowed[None], (nope_scores + rope_scores) * score_scale, -1e30)


def expert_forward(received, w_expert_in, w_expert_out, sources):
    sectioned = received.reshape(sources, -1, received.shape[1], received.shape[2])
    gate_up = jnp.einsum(
        "secd,egdh->secgh", sectioned, w_expert_in, preferred_element_type=jnp.float32
    )
    gate_val, gate_slope = silu_parts(gate_up[..., 0, :])
    activated = (gate_val * gate_up[..., 1, :]).astype(jnp.bfloat16)
    produced = jnp.einsum(
        "sech,ehd->secd", activated, w_expert_out, preferred_element_type=jnp.float32
    )
    return (sectioned, gate_up, activated, produced.reshape(received.shape))


def body_slots(
    inputs,
    gain_attn,
    w_query,
    w_latent,
    gain_latent,
    w_latent_up,
    w_output,
    gain_ffn,
    w_router,
    w_shared_in,
    w_shared_out,
    w_expert_in,
    w_expert_out,
    expert_ids,
    slot_ids,
    cotangent,
):
    tokens, model_width = inputs.shape
    tp_count = lax.axis_size("tp")
    tp_index = lax.axis_index("tp")
    heads_here = w_output.shape[0] // VDIM
    experts = w_router.shape[1]
    local_experts = w_expert_in.shape[0]
    sources = experts // local_experts
    capacity = (9 * tokens * TOPK + 64 * experts - 1) // (64 * experts) * 8
    qk_width = NOPE + ROPE
    score_scale = qk_width ** (-0.5)
    rows_part = tokens // tp_count
    row_start = tp_index * rows_part
    resid = inputs.astype(jnp.float32)
    inv_first = lax.rsqrt(jnp.mean(resid * resid, axis=-1, keepdims=True) + EPSILON)
    normed_first = resid * inv_first
    hidden_attn = (normed_first * gain_attn).astype(jnp.bfloat16)
    cosine, sine_table = angles(tokens, ROPE)
    query_raw = jnp.dot(hidden_attn, w_query, preferred_element_type=jnp.float32).reshape(
        tokens, heads_here, qk_width
    )
    query_rot = jnp.concatenate(
        [
            query_raw[..., :NOPE],
            rotate(query_raw[..., NOPE:], cosine[:, None], sine_table[:, None]),
        ],
        axis=-1,
    ).astype(jnp.bfloat16)
    latent = jnp.dot(hidden_attn, w_latent, preferred_element_type=jnp.float32)
    compressed = latent[:, :KV_RANK]
    inv_latent = lax.rsqrt(jnp.mean(compressed * compressed, axis=-1, keepdims=True) + EPSILON)
    normed_latent = compressed * inv_latent
    latent_in = (normed_latent * gain_latent).astype(jnp.bfloat16)
    key_rope = rotate(latent[:, KV_RANK:], cosine, sine_table).astype(jnp.bfloat16)
    key_value = (
        jnp.dot(latent_in, w_latent_up, preferred_element_type=jnp.float32)
        .astype(jnp.bfloat16)
        .reshape(tokens, heads_here, NOPE + VDIM)
    )
    key_nope = key_value[..., :NOPE]
    values = key_value[..., NOPE:]
    block_ids = jnp.arange(tokens) // BLOCK
    allowed = block_ids[None, :] <= block_ids[:, None]
    scores = attention_scores(query_rot, key_nope, key_rope, score_scale, allowed)
    row_peak = jnp.max(scores, axis=-1, keepdims=True)
    exp_scores = jnp.exp(scores - row_peak)
    totals = jnp.sum(exp_scores, axis=-1, keepdims=True)
    attn_probs = exp_scores / totals
    log_total = row_peak + jnp.log(totals)
    attended = (
        jnp.einsum(
            "hqk,khd->qhd",
            attn_probs.astype(jnp.bfloat16),
            values,
            preferred_element_type=jnp.float32,
        )
        .astype(jnp.bfloat16)
        .reshape(tokens, heads_here * VDIM)
    )
    attn_full = lax.psum(
        jnp.dot(attended, w_output, preferred_element_type=jnp.float32).astype(jnp.bfloat16), "tp"
    ).astype(jnp.float32)
    middle = resid + attn_full
    inv_second = lax.rsqrt(jnp.mean(middle * middle, axis=-1, keepdims=True) + EPSILON)
    normed_second = middle * inv_second
    hidden_ffn = (normed_second * gain_ffn).astype(jnp.bfloat16)
    hidden_wide = hidden_ffn.astype(jnp.float32)
    logits = jnp.dot(hidden_wide, w_router, precision=HIGHEST, preferred_element_type=jnp.float32)
    logit_peak = jnp.max(logits, axis=-1, keepdims=True)
    exp_logits = jnp.exp(logits - logit_peak)
    router_probs = exp_logits / jnp.sum(exp_logits, axis=-1, keepdims=True)
    route_onehot = (
        expert_ids[:, :, None] == jnp.arange(experts, dtype=jnp.int32)[None, None, :]
    ).astype(jnp.float32)
    pair_gate = jnp.sum(route_onehot * router_probs[:, None, :], axis=-1)
    kept_pair = slot_ids < capacity
    flat_index = jnp.where(kept_pair, expert_ids * capacity + slot_ids, experts * capacity)
    row_numbers = jnp.broadcast_to(jnp.arange(tokens, dtype=jnp.int32)[:, None], (tokens, TOPK))
    owner_row = (
        jnp.full((experts * capacity,), tokens, jnp.int32)
        .at[flat_index.reshape(-1)]
        .set(row_numbers.reshape(-1), mode="drop")
    )
    outgoing = jnp.take(hidden_ffn, owner_row, axis=0, mode="fill", fill_value=0).reshape(
        experts, capacity, model_width
    )
    received = lax.all_to_all(outgoing, "ep", split_axis=0, concat_axis=0, tiled=True)
    sectioned, gate_up, activated, produced = expert_forward(
        received, w_expert_in, w_expert_out, sources
    )
    returned = lax.all_to_all(
        produced.astype(jnp.bfloat16), "ep", split_axis=0, concat_axis=0, tiled=True
    ).astype(produced.dtype)
    out_grad = cotangent.astype(jnp.float32)
    back_rows = returned.reshape(-1, model_width)
    combined = jnp.zeros((tokens, model_width), jnp.float32)
    gate_cols = []
    for pick_index in range(TOPK):
        taken_rows = jnp.take(
            back_rows, flat_index[:, pick_index], axis=0, mode="fill", fill_value=0.0
        )
        combined = combined + pair_gate[:, pick_index : pick_index + 1] * taken_rows
        gate_cols.append(jnp.sum(out_grad * taken_rows, axis=-1))
    gate_grad = jnp.stack(gate_cols, axis=1)
    shared_gate = jnp.dot(hidden_ffn, w_shared_in[0], preferred_element_type=jnp.float32)
    shared_up = jnp.dot(hidden_ffn, w_shared_in[1], preferred_element_type=jnp.float32)
    shared_val, shared_slope = silu_parts(shared_gate)
    shared_act = (shared_val * shared_up).astype(jnp.bfloat16)
    branch_part = jnp.dot(shared_act, w_shared_out, preferred_element_type=jnp.float32) + combined
    ffn_full = lax.psum(branch_part.astype(jnp.bfloat16), "tp").astype(jnp.float32)
    block_out = (middle + ffn_full).astype(jnp.bfloat16)
    slot_gate = (
        jnp.zeros((experts * capacity,), jnp.float32)
        .at[flat_index.reshape(-1)]
        .set(pair_gate.reshape(-1), mode="drop")
    )
    gathered_grad = jnp.take(cotangent, owner_row, axis=0, mode="fill", fill_value=0)
    slot_grad = (
        (slot_gate[:, None] * gathered_grad.astype(jnp.float32))
        .astype(jnp.bfloat16)
        .reshape(experts, capacity, model_width)
    )
    grad_arrived = lax.all_to_all(slot_grad, "ep", split_axis=0, concat_axis=0, tiled=True).reshape(
        sectioned.shape
    )
    act_grad = jnp.einsum(
        "secd,ehd->sech", grad_arrived, w_expert_out, preferred_element_type=jnp.float32
    )
    gate_val, gate_slope = silu_parts(gate_up[..., 0, :])
    up_val = gate_up[..., 1, :]
    gu_grad = jnp.stack([act_grad * up_val * gate_slope, act_grad * gate_val], axis=-2).astype(
        jnp.bfloat16
    )
    grad_expert_out = jnp.einsum(
        "sech,secd->ehd", activated, grad_arrived, preferred_element_type=jnp.float32
    )
    grad_expert_in = jnp.einsum(
        "secd,secgh->egdh", sectioned, gu_grad, preferred_element_type=jnp.float32
    )
    rows_grad = jnp.einsum(
        "secgh,egdh->secd", gu_grad, w_expert_in, preferred_element_type=jnp.float32
    ).reshape(received.shape)
    returned_grad = (
        lax.all_to_all(
            rows_grad.astype(jnp.bfloat16), "ep", split_axis=0, concat_axis=0, tiled=True
        )
        .astype(rows_grad.dtype)
        .reshape(-1, model_width)
    )
    routed_grad = jnp.zeros((tokens, model_width), jnp.float32)
    for pick_index in range(TOPK):
        routed_grad = routed_grad + jnp.take(
            returned_grad, flat_index[:, pick_index], axis=0, mode="fill", fill_value=0.0
        )
    shared_act_grad = jnp.einsum(
        "td,fd->tf", cotangent, w_shared_out, preferred_element_type=jnp.float32
    )
    shared_gate_grad = (shared_act_grad * shared_up * shared_slope).astype(jnp.bfloat16)
    shared_up_grad = (shared_act_grad * shared_val).astype(jnp.bfloat16)
    shared_out_grad = jnp.einsum(
        "tf,td->fd", shared_act, cotangent, preferred_element_type=jnp.float32
    )
    shared_in_grad = jnp.stack(
        [
            jnp.einsum(
                "td,tf->df", hidden_ffn, shared_gate_grad, preferred_element_type=jnp.float32
            ),
            jnp.einsum("td,tf->df", hidden_ffn, shared_up_grad, preferred_element_type=jnp.float32),
        ],
        axis=0,
    )
    shared_back = jnp.einsum(
        "tf,df->td", shared_gate_grad, w_shared_in[0], preferred_element_type=jnp.float32
    ) + jnp.einsum("tf,df->td", shared_up_grad, w_shared_in[1], preferred_element_type=jnp.float32)
    prob_grad = jnp.sum(route_onehot * gate_grad[:, :, None], axis=1)
    logit_grad = router_probs * (
        prob_grad - jnp.sum(router_probs * prob_grad, axis=-1, keepdims=True)
    )
    router_back = jnp.einsum(
        "te,de->td", logit_grad, w_router, precision=HIGHEST, preferred_element_type=jnp.float32
    )
    router_grad = jnp.einsum(
        "td,te->de", hidden_wide, logit_grad, precision=HIGHEST, preferred_element_type=jnp.float32
    )
    ffn_grad = lax.psum(
        (shared_back + routed_grad + router_back).astype(jnp.bfloat16), "tp"
    ).astype(jnp.float32)
    middle_grad = out_grad + norm_back(ffn_grad, gain_ffn, normed_second, inv_second)
    gain_ffn_grad = jnp.sum(
        lax.dynamic_slice_in_dim(ffn_grad * normed_second, row_start, rows_part, 0), axis=0
    )
    branch_grad = middle_grad.astype(jnp.bfloat16)
    output_w_grad = jnp.einsum(
        "tf,td->fd", attended, branch_grad, preferred_element_type=jnp.float32
    )
    attended_grad = (
        jnp.einsum("td,fd->tf", branch_grad, w_output, preferred_element_type=jnp.float32)
        .astype(jnp.bfloat16)
        .reshape(tokens, heads_here, VDIM)
    )
    scores_again = attention_scores(query_rot, key_nope, key_rope, score_scale, allowed)
    probs_again = jnp.exp(scores_again - log_total)
    values_grad = jnp.einsum(
        "hqk,qhd->khd",
        probs_again.astype(jnp.bfloat16),
        attended_grad,
        preferred_element_type=jnp.float32,
    )
    prob_part = jnp.einsum(
        "qhd,khd->hqk", attended_grad, values, preferred_element_type=jnp.float32
    )
    score_grad = (
        probs_again * (prob_part - jnp.sum(probs_again * prob_part, axis=-1, keepdims=True))
    ).astype(jnp.bfloat16)
    query_nope_grad = (
        jnp.einsum("hqk,khd->qhd", score_grad, key_nope, preferred_element_type=jnp.float32)
        * score_scale
    )
    query_rope_grad = (
        jnp.einsum("hqk,kr->qhr", score_grad, key_rope, preferred_element_type=jnp.float32)
        * score_scale
    )
    key_nope_grad = (
        jnp.einsum(
            "hqk,qhd->khd", score_grad, query_rot[..., :NOPE], preferred_element_type=jnp.float32
        )
        * score_scale
    )
    key_rope_grad = (
        jnp.einsum(
            "hqk,qhr->kr", score_grad, query_rot[..., NOPE:], preferred_element_type=jnp.float32
        )
        * score_scale
    )
    kv_grad = (
        jnp.concatenate([key_nope_grad, values_grad], axis=-1)
        .astype(jnp.bfloat16)
        .reshape(tokens, heads_here * (NOPE + VDIM))
    )
    latent_up_grad = jnp.einsum("tr,tf->rf", latent_in, kv_grad, preferred_element_type=jnp.float32)
    latent_in_grad = jnp.einsum(
        "tf,rf->tr", kv_grad, w_latent_up, preferred_element_type=jnp.float32
    )
    gain_latent_grad = jnp.sum(latent_in_grad * normed_latent, axis=0)
    latent_grad_part = jnp.concatenate(
        [
            norm_back(latent_in_grad, gain_latent, normed_latent, inv_latent),
            rotate(key_rope_grad, cosine, -sine_table),
        ],
        axis=-1,
    )
    query_grad = (
        jnp.concatenate(
            [query_nope_grad, rotate(query_rope_grad, cosine[:, None], -sine_table[:, None])],
            axis=-1,
        )
        .astype(jnp.bfloat16)
        .reshape(tokens, heads_here * qk_width)
    )
    query_w_grad = jnp.einsum(
        "td,tf->df", hidden_attn, query_grad, preferred_element_type=jnp.float32
    )
    hidden_part = jnp.einsum("tf,df->td", query_grad, w_query, preferred_element_type=jnp.float32)
    hidden_sum, latent_sum = (
        lax.psum(hidden_part.astype(jnp.bfloat16), "tp").astype(jnp.float32),
        lax.psum(latent_grad_part.astype(jnp.bfloat16), "tp").astype(jnp.float32),
    )
    latent_low = latent_sum.astype(jnp.bfloat16)
    attn_in_grad = hidden_sum + jnp.einsum(
        "tf,df->td", latent_low, w_latent, preferred_element_type=jnp.float32
    )
    latent_w_grad = jnp.einsum(
        "td,tf->df",
        lax.dynamic_slice_in_dim(hidden_attn, row_start, rows_part, 0),
        lax.dynamic_slice_in_dim(latent_low, row_start, rows_part, 0),
        preferred_element_type=jnp.float32,
    )
    gain_attn_grad = jnp.sum(
        lax.dynamic_slice_in_dim(attn_in_grad * normed_first, row_start, rows_part, 0), axis=0
    )
    grad_inputs = (
        middle_grad + norm_back(attn_in_grad, gain_attn, normed_first, inv_first)
    ).astype(jnp.bfloat16)
    grad_query, grad_latent_up, grad_output, grad_shared_in, grad_shared_out = (
        lax.psum_scatter(
            query_w_grad.astype(jnp.bfloat16), "ep", scatter_dimension=0, tiled=True
        ).astype(jnp.float32),
        lax.psum_scatter(
            latent_up_grad.astype(jnp.bfloat16), "ep", scatter_dimension=0, tiled=True
        ).astype(jnp.float32),
        lax.psum_scatter(
            output_w_grad.astype(jnp.bfloat16), "ep", scatter_dimension=1, tiled=True
        ).astype(jnp.float32),
        lax.psum_scatter(
            shared_in_grad.astype(jnp.bfloat16), "ep", scatter_dimension=1, tiled=True
        ).astype(jnp.float32),
        lax.psum_scatter(
            shared_out_grad.astype(jnp.bfloat16), "ep", scatter_dimension=1, tiled=True
        ).astype(jnp.float32),
    )
    grad_latent, grad_gain_latent, grad_gain_attn, grad_gain_ffn, grad_router = (
        lax.psum_scatter(latent_w_grad, ("ep", "tp"), scatter_dimension=0, tiled=True),
        lax.psum_scatter(gain_latent_grad, ("ep", "tp"), scatter_dimension=0, tiled=True),
        lax.psum_scatter(gain_attn_grad, ("ep", "tp"), scatter_dimension=0, tiled=True),
        lax.psum_scatter(gain_ffn_grad, ("ep", "tp"), scatter_dimension=0, tiled=True),
        lax.psum_scatter(router_grad, ("ep", "tp"), scatter_dimension=0, tiled=True),
    )
    return (
        block_out,
        grad_inputs,
        grad_gain_attn,
        grad_query,
        grad_latent,
        grad_gain_latent,
        grad_latent_up,
        grad_output,
        grad_gain_ffn,
        grad_router,
        grad_shared_in,
        grad_shared_out,
        grad_expert_in,
        grad_expert_out,
    )


MESH = pl.DeviceIdType.MESH


def plane_partners(ep):
    def flip(bit):
        return ep + bit - 2 * bit * lax.rem(lax.div(ep, bit), 2)

    return flip(1), flip(2), flip(4)


def line_order(tp):
    def pick(a, b, c, d):
        return jnp.where(tp == 0, a, jnp.where(tp == 1, b, jnp.where(tp == 2, c, d)))

    return (tp, pick(1, 0, 3, 2), pick(2, 2, 1, 1), pick(3, 3, 0, 0))


def greet(devices):
    barrier = pltpu.get_barrier_semaphore()
    for ep, tp in devices:
        pl.semaphore_signal(barrier, inc=1, device_id=(ep, tp), device_id_type=MESH)
    pl.semaphore_wait(barrier, len(devices))


def remote(src, dst, send, recv, device):
    return pltpu.make_async_remote_copy(
        src_ref=src, dst_ref=dst, send_sem=send, recv_sem=recv, device_id=device, device_id_type=MESH
    )


def add_rows(dst, a, b):
    def body(r, _):
        at = pl.ds(pl.multiple_of(r * 16, 16), 16)
        dst[at, :] = (a[at, :].astype(jnp.float32) + b[at, :].astype(jnp.float32)).astype(dst.dtype)
        return 0

    lax.fori_loop(0, dst.shape[0] // 16, body, 0)


def line_sum(own_of, got, send_sem, recv_sem, ep, tp, depth):
    far = line_order(tp)[::-1]
    between = (tp > 0) & (tp < depth - 1)
    near = jnp.where(tp > 0, tp - 1, tp + 1)

    def copy(n, src):
        chunk = far[n]
        to = jnp.where(chunk > tp, tp + 1, tp - 1)
        slot = jnp.where(chunk == tp - 1, depth, chunk)
        return remote(src, got.at[slot], send_sem.at[n], recv_sem.at[slot], (ep, to))

    def arrive(slot):
        remote(got.at[0], got.at[slot], send_sem.at[0], recv_sem.at[slot], (ep, near)).wait_recv()

    def start(n):
        @pl.when(jnp.logical_not(between))
        def _():
            copy(n, own_of(n)).start()

    def pass_on(n):
        @pl.when(between)
        def _():
            held = got.at[far[n]]
            arrive(far[n])
            add_rows(held, own_of(n), held)
            copy(n, held).start()

    def clear():
        @pl.when(tp == 0)
        def _():
            got[0] = jnp.zeros_like(got[0])

        @pl.when(tp == depth - 1)
        def _():
            got[depth] = jnp.zeros_like(got[depth])

    def finish():
        @pl.when(tp > 0)
        def _():
            arrive(tp)

        @pl.when(tp < depth - 1)
        def _():
            arrive(depth)

    def drain():
        for n in range(depth - 1):
            copy(n, got.at[0]).wait_send()

    return clear, start, pass_on, finish, drain


def line_total(own_of, pieces, up, down, up_send, up_recv, down_send, down_recv, ep, tp, depth):
    between = (tp > 0) & (tp < depth - 1)
    lowest, highest = tp == 0, tp == depth - 1
    above, below = jnp.minimum(tp + 1, depth - 1), jnp.maximum(tp - 1, 0)

    def up_copy(n, src):
        return remote(src, up.at[n], up_send.at[n], up_recv.at[n], (ep, above))

    def down_copy(n, src):
        return remote(src, down.at[n], down_send.at[n], down_recv.at[n], (ep, below))

    def start(n):
        @pl.when(lowest)
        def _():
            up_copy(n, own_of(n)).start()

        @pl.when(highest)
        def _():
            down_copy(n, own_of(n)).start()

    def hop(k, n):
        @pl.when(between & (tp == k))
        def _():
            up_copy(n, up.at[n]).wait_recv()
            add_rows(up.at[n], up.at[n], own_of(n))
            up_copy(n, up.at[n]).start()

        @pl.when(between & (tp == depth - 1 - k))
        def _():
            down_copy(n, down.at[n]).wait_recv()
            add_rows(down.at[n], down.at[n], own_of(n))
            down_copy(n, down.at[n]).start()

    def finish(n):
        @pl.when(lowest)
        def _():
            up[n] = own_of(n)[...]
            down_copy(n, down.at[n]).wait_recv()
            add_rows(down.at[n], down.at[n], own_of(n))

        @pl.when(highest)
        def _():
            down[n] = own_of(n)[...]
            up_copy(n, up.at[n]).wait_recv()
            add_rows(up.at[n], up.at[n], own_of(n))

    def drain():
        for n in range(pieces):

            @pl.when(jnp.logical_not(highest))
            def _():
                up_copy(n, up.at[n]).wait_send()

            @pl.when(jnp.logical_not(lowest))
            def _():
                down_copy(n, down.at[n]).wait_send()

    return start, hop, finish, drain


def turn(slab, table, sign):
    cosine, front, second = table
    return slab * cosine + sign * (pltpu.roll(slab, 96, 1) * front + pltpu.roll(slab, 32, 1) * second)


def experts_kernel(
    depth, blocks, heads, routed, shared, experts,
    inputs_in, gain_attn, w_query_in, w_latent_in, gain_latent, w_up_in, w_output_in, tables_in,
    gain_ref, cot_ref, kept_hbm, e_in, e_out, s_in, s_out,
    middle_ref, h_out, cot_all, grads_out, gated_out, rows_out,
    hidden_out, qn_out, qr_out, kv_out, kr_out, attended_out, latent_in_out, compressed_out, w_out_out,
    inputs_ref, w_query, w_latent, w_up, w_output, tables, in_sem,
    part_ref, hidden, qn_ref, qr_ref, kv, kr_ref, attended, latent_in, compressed, rope_slab,
    kept_ref, w_in_ref, w_out_ref,
    h_all, got_z, cot_tile, gu, act_grad, prob_lanes, diff_lanes, pair_lanes,
    grads_tile, gated_tile, rows_tile,
    weight_sem, save_sem, local_sem, z_send, z_recv, line_send, line_recv, h_send, h_recv, c_send, c_recv, b_send, b_recv, tile_sem, store_sem,
):
    f32, bf16 = jnp.float32, jnp.bfloat16
    ep, tp = lax.axis_index("ep"), lax.axis_index("tp")
    pair, xn, yn = plane_partners(ep)
    parity = lax.rem(ep, 2)
    passed = jnp.where(parity == 0, xn, yn)
    onward = jnp.where(parity == 0, yn, xn)
    diag = xn + yn - ep
    rows = h_all.shape[2]
    width = h_all.shape[3]
    hidden_units = w_out_ref.shape[0]
    tokens = inputs_ref.shape[0]
    rank = compressed.shape[1]
    lanes = lax.broadcasted_iota(jnp.int32, (1, 128), 1)
    across = (((1,), (1,)), ((), ()))
    score_scale = (NOPE + ROPE) ** (-0.5)

    def dot(a, b, dims=(((1,), (0,)), ((), ()))):
        return lax.dot_general(a, b, dims, preferred_element_type=f32)

    half = blocks // 2
    tile = half * rows
    up, down = jnp.minimum(tp + 1, depth - 1), jnp.maximum(tp - 1, 0)

    def twin(block):
        return block + pair - ep

    loads = [
        pltpu.make_async_copy(src, dst, in_sem.at[n])
        for n, (src, dst) in enumerate(
            (
                (inputs_in, inputs_ref), (w_latent_in, w_latent), (tables_in, tables), (w_up_in, w_up),
                (w_query_in, w_query), (w_output_in, w_output),
            )
        )
    ]
    for copy in loads:
        copy.start()
    greet([(pair, tp), (xn, tp), (yn, tp)] + [(ep, lax.rem(tp + k, depth)) for k in range(1, depth)])

    def part_rows(n):
        return part_ref.at[pl.ds(pl.multiple_of(line_order(tp)[depth - 1 - n] * rows, rows), rows)]

    z_clear, z_start, z_pass, z_finish, z_drain = line_sum(part_rows, got_z, z_send, z_recv, ep, tp, depth)
    z_clear()
    weight_loads = [
        pltpu.make_async_copy(kept_hbm, kept_ref, weight_sem.at[0]),
        pltpu.make_async_copy(e_out.at[0], w_out_ref.at[pl.ds(0, routed)], weight_sem.at[1]),
        pltpu.make_async_copy(s_out, w_out_ref.at[pl.ds(routed, hidden_units - routed)], weight_sem.at[2]),
    ]
    for g in range(2):
        own, beside = pl.ds(g * hidden_units, routed), pl.ds(g * hidden_units + routed, hidden_units - routed)
        weight_loads.append(pltpu.make_async_copy(e_in.at[0, g], w_in_ref.at[own], weight_sem.at[3 + 2 * g]))
        weight_loads.append(pltpu.make_async_copy(s_in.at[g], w_in_ref.at[beside], weight_sem.at[4 + 2 * g]))

    def h_copy(block, chunk, slot, to):
        ref = h_all.at[chunk, block]
        return remote(ref, ref, h_send.at[chunk, slot], h_recv.at[chunk, slot], (to, tp))

    def c_copy(block, chunk, slot, to):
        ref = cot_all.at[chunk, block]
        return remote(ref, ref, c_send.at[chunk, slot], c_recv.at[chunk, slot], (to, tp))

    def c_first(chunk, slot, to):
        src = cot_ref.at[pl.ds(pl.multiple_of(chunk * rows, rows), rows)]
        return remote(src, cot_all.at[chunk, ep], c_send.at[chunk, slot], c_recv.at[chunk, slot], (to, tp))

    buddy = tp + 1 - 2 * lax.rem(tp, 2)
    skipped, theirs = depth - 1 - tp, depth - 1 - buddy

    def buddy_copy(n, chunk):
        ref = cot_all.at[chunk, (xn, yn, diag)[n]]
        return remote(ref, ref, b_send.at[n], b_recv.at[n], (ep, buddy))

    def own_cot_in(chunk):
        src = cot_ref.at[pl.ds(pl.multiple_of(chunk * rows, rows), rows)]
        return pltpu.make_async_copy(src, rows_tile.at[0, chunk], local_sem.at[chunk])

    def own_cot_out(chunk):
        return pltpu.make_async_copy(rows_tile.at[0, chunk], cot_all.at[chunk, ep], local_sem.at[chunk])

    order = line_order(tp)

    def order_at(k):
        return jnp.where(k == 0, order[0], jnp.where(k == 1, order[1], jnp.where(k == 2, order[2], order[3])))

    for k in range(depth):

        @pl.when(order[k] != skipped)
        def _():
            c_first(order[k], 1, xn).start()
            c_first(order[k], 2, yn).start()

        c_first(order[k], 0, pair).start()
        own_cot_in(k).start()
    for copy in weight_loads:
        copy.start()

    def first_norm(r, _):
        at = pl.ds(pl.multiple_of(r * 16, 16), 16)
        v = inputs_ref[at, :].astype(f32)
        inverse = lax.rsqrt(jnp.mean(v * v, axis=-1, keepdims=True) + EPSILON)
        hidden[at, :] = (v * inverse * gain_attn[...]).astype(bf16)
        return 0

    loads[0].wait()
    lax.fori_loop(0, tokens // 16, first_norm, 0)
    for copy in loads[1:]:
        copy.wait()
    table = tuple(tables[n] for n in range(3))
    latent = dot(hidden[...], w_latent[...], across)
    held = latent[:, :rank]
    compressed[...] = held
    inverse = lax.rsqrt(jnp.mean(held * held, axis=-1, keepdims=True) + EPSILON)
    latent_in[...] = (held * inverse * gain_latent[...]).astype(bf16)
    rope_slab[...] = jnp.zeros_like(rope_slab)
    rope_slab[:, 0:ROPE] = latent[:, rank:]
    key = turn(rope_slab[...], table, 1.0)
    kr_ref[0] = key.astype(bf16)
    kr_ref[1] = pltpu.roll(key, 64, 1).astype(bf16)
    kv[...] = dot(latent_in[...], w_up[...]).astype(bf16)
    wide = 2 * (NOPE + ROPE)
    for p in range(heads // 2):
        found = dot(hidden[...], w_query[:, p * wide : (p + 1) * wide])
        slabs = [found[:, n : n + 128] for n in (0, 128, 256)]
        qn_ref[:, 2 * p * NOPE : (2 * p + 1) * NOPE] = slabs[0].astype(bf16)
        odd = pltpu.roll(jnp.where(lanes < 64, slabs[2], slabs[1]), 64, 1)
        qn_ref[:, (2 * p + 1) * NOPE : (2 * p + 2) * NOPE] = odd.astype(bf16)
        qr_ref[:, p * 128 : (p + 1) * 128] = turn(jnp.where(lanes < 64, slabs[1], slabs[2]), table, 1.0).astype(bf16)
    for h in range(heads):
        for b in range(tokens // BLOCK):
            own = slice(b * BLOCK, (b + 1) * BLOCK)
            keys = slice(0, (b + 1) * BLOCK)
            slab = slice(h // 2 * 128, h // 2 * 128 + 128)
            at = slice(h * 128, h * 128 + 128)
            scores = dot(qn_ref[own, at], kv[keys, h * 256 : h * 256 + 128], across)
            scores = (scores + dot(qr_ref[own, slab], kr_ref[h % 2, keys, :], across)) * score_scale
            exps = jnp.exp(scores - jnp.max(scores, axis=-1, keepdims=True))
            probs = exps / jnp.sum(exps, axis=-1, keepdims=True)
            attended[own, at] = dot(probs.astype(bf16), kv[keys, h * 256 + 128 : h * 256 + 256]).astype(bf16)
    for n in range(0, width, 512):
        part_ref[:, n : n + 512] = dot(attended[...], w_output[:, n : n + 512]).astype(bf16)
    for n in range(depth - 1):
        z_start(n)
    saves = [
        pltpu.make_async_copy(src, dst, save_sem.at[n])
        for n, (src, dst) in enumerate(
            (
                (hidden, hidden_out), (qn_ref, qn_out), (qr_ref, qr_out), (kv, kv_out), (kr_ref, kr_out),
                (attended, attended_out), (latent_in, latent_in_out), (compressed, compressed_out),
            )
        )
    ]
    for copy in saves:
        copy.start()
    for k in range(depth):
        own_cot_in(k).wait()
        own_cot_out(k).start()

    for copy in weight_loads:
        copy.wait()
    w_out_save = pltpu.make_async_copy(w_out_ref, w_out_out, save_sem.at[8])
    w_out_save.start()
    z_pass(0)
    z_pass(1)
    z_pass(2)
    z_finish()

    def norm_rows(r, _):
        here = pl.ds(pl.multiple_of(r * 16, 16), 16)
        own = pl.ds(pl.multiple_of(tp * rows + r * 16, 16), 16)
        total = part_ref[own, :].astype(f32)
        total = total + got_z[tp, here, :].astype(f32) + got_z[depth, here, :].astype(f32)
        middle = inputs_ref[own, :].astype(f32) + total
        inverse = lax.rsqrt(jnp.mean(middle * middle, axis=-1, keepdims=True) + EPSILON)
        middle_ref[here, :] = middle
        h_all[tp, ep, here, :] = (middle * inverse * gain_ref[...]).astype(bf16)
        return 0

    lax.fori_loop(0, rows // 16, norm_rows, 0)
    for k in range(depth):
        own_cot_out(k).wait()

    def along(chunk, way, to):
        ref = h_all.at[chunk, ep]
        return remote(ref, ref, line_send.at[chunk, way], line_recv.at[chunk], (ep, to))

    def goes_up(chunk):
        return (chunk <= tp) & (tp < depth - 1)

    def goes_down(chunk):
        return (chunk >= tp) & (tp > 0)

    def send_chunk(k):
        chunk = order[k]
        if k > 0:
            along(chunk, 0, up).wait_recv()

        @pl.when(goes_up(chunk))
        def _():
            along(chunk, 0, up).start()

        @pl.when(goes_down(chunk))
        def _():
            along(chunk, 1, down).start()

        h_copy(ep, chunk, 1, xn).start()
        h_copy(ep, chunk, 2, yn).start()
        h_copy(ep, chunk, 0, pair).start()

    def forward_chunk(copy, chunk):
        copy(xn, chunk, 1, xn).wait_recv()
        copy(yn, chunk, 2, yn).wait_recv()
        copy(passed, chunk, 3, onward).start()
        copy(xn, chunk, 4, pair).start()
        copy(yn, chunk, 5, pair).start()

    def forward_diag(copy, chunk):
        copy(diag, chunk, 3, onward).wait_recv()
        copy(diag, chunk, 6, pair).start()

    def forward_skipped():
        for n, (block, slot) in enumerate(((xn, 4), (yn, 5), (diag, 6))):
            buddy_copy(n, skipped).wait_recv()
            c_copy(block, skipped, slot, pair).start()

    def await_pair(chunk, slots):
        for copy in (h_copy, c_copy):
            for slot, block in slots:
                copy(block, chunk, slot, pair).wait_recv()

    send_chunk(0)
    forward_chunk(c_copy, order[0])
    forward_chunk(h_copy, order[0])
    send_chunk(1)
    forward_chunk(c_copy, theirs)
    buddy_copy(0, theirs).start()
    buddy_copy(1, theirs).start()

    base = routed + shared
    slab = base // 128 * 128
    lane0 = base - slab
    near_half = lax.div(ep, half)

    def tile_copies(i):
        k, side = lax.div(i, 2), lax.rem(i, 2)
        chunk = order_at(k)
        start = jnp.where(side == 0, near_half, 1 - near_half) * half
        group = pl.ds(start, half)
        slot = lax.rem(i, 2)
        stores = [
            pltpu.make_async_copy(h_all.at[chunk, group], h_out.at[chunk, group], store_sem.at[slot, 0]),
            pltpu.make_async_copy(grads_tile.at[slot], grads_out.at[chunk, group], store_sem.at[slot, 1]),
            pltpu.make_async_copy(gated_tile.at[slot], gated_out.at[chunk, group], store_sem.at[slot, 2]),
            pltpu.make_async_copy(rows_tile.at[slot], rows_out.at[chunk, group], store_sem.at[slot, 3]),
        ]
        load = pltpu.make_async_copy(cot_all.at[chunk, group], cot_tile, tile_sem)
        return chunk, start, slot, load, stores

    def step(i, _):
        k, side = lax.div(i, 2), lax.rem(i, 2)
        chunk, start, slot, load, stores = tile_copies(i)

        @pl.when(side == 0)
        def _():
            await_pair(chunk, ((0, pair), (4, twin(xn))))

        @pl.when(i == 1)
        def _():
            forward_diag(c_copy, order[0])

        @pl.when(i == 2)
        def _():
            forward_diag(c_copy, theirs)
            buddy_copy(2, theirs).start()

        @pl.when(i == 3)
        def _():
            forward_diag(c_copy, order[1])

        @pl.when(side == 1)
        def _():
            forward_diag(h_copy, chunk)
            await_pair(chunk, ((5, twin(yn)), (6, twin(diag))))

        load.start()

        @pl.when(i >= 2)
        def _():
            for copy in tile_copies(i - 2)[4]:
                copy.wait()

        group = pl.ds(start, half)
        stores[0].start()
        for n in range(0, 2 * hidden_units, 512):
            gu[:, n : n + 512] = dot(h_all[chunk, group].reshape(tile, width), w_in_ref[n : n + 512, :], across)
        piece = gu[:, slab : slab + 128]
        logits = piece + pltpu.roll(piece, 128 - experts, 1) + pltpu.roll(piece, 128 - 2 * experts, 1)
        is_logit = (lanes >= lane0) & (lanes < lane0 + experts)
        logits = jnp.where(is_logit, logits, -1e30)
        exps = jnp.exp(logits - jnp.max(logits, axis=-1, keepdims=True))
        probs = exps / jnp.sum(exps, axis=-1, keepdims=True)
        here = (lanes == lane0 + ep).astype(f32)
        kept = kept_ref[chunk, group].reshape(tile, 128).astype(f32)
        prob_here = jnp.sum(probs * here * kept, axis=-1, keepdims=True)
        prob_lanes[...] = jnp.broadcast_to(prob_here, (tile, 128))
        diff_lanes[...] = here - probs

        @pl.when(i == 0)
        def _():
            forward_chunk(h_copy, order[1])
            send_chunk(2)

        @pl.when(i == 1)
        def _():
            forward_chunk(c_copy, order[1])
            send_chunk(3)

        @pl.when(i == 2)
        def _():
            forward_chunk(h_copy, order[2])

        @pl.when(i == 3)
        def _():
            forward_skipped()

        @pl.when(i == 4)
        def _():
            forward_chunk(h_copy, order[3])

        load.wait()
        act_grad[...] = lax.dot_general(
            cot_tile[...].reshape(tile, width), w_out_ref[...], (((1,), (1,)), ((), ())), preferred_element_type=f32
        )
        strip = 64

        def strips(r, _):
            at = pl.ds(pl.multiple_of(r * strip, strip), strip)
            gate_here = prob_lanes[at, :]
            pair_sum = jnp.zeros((strip, 128), f32)
            per = rows // strip
            block, inner = lax.div(r, per), pl.ds(pl.multiple_of(lax.rem(r, per) * strip, strip), strip)
            for n in range(0, hidden_units, 128):
                gate = gu[at, n : n + 128]
                up_val = gu[at, hidden_units + n : hidden_units + n + 128]
                grad = act_grad[at, n : n + 128]
                if n + 128 <= routed:
                    scale = gate_here
                elif n >= routed:
                    scale = None
                else:
                    scale = jnp.where(lanes < routed - n, gate_here, 1.0)
                sig = jax.nn.sigmoid(gate)
                silu = gate * sig
                act = silu * up_val
                if n < routed:
                    both = act * grad
                    if n + 128 > routed:
                        both = jnp.where(lanes < routed - n, both, 0.0)
                    pair_sum = pair_sum + both
                    act = act * scale
                    grad = grad * scale
                gated_tile[slot, block, inner, n : n + 128] = act.astype(bf16)
                grads_tile[slot, block, inner, n : n + 128] = (
                    grad * up_val * (sig * (1.0 + gate * (1.0 - sig)))
                ).astype(bf16)
                grads_tile[slot, block, inner, hidden_units + n : hidden_units + n + 128] = (grad * silu).astype(bf16)
            pair_lanes[at, :] = pair_sum
            return 0

        lax.fori_loop(0, tile // strip, strips, 0)
        pair_grad = jnp.sum(pair_lanes[...], axis=-1, keepdims=True)
        logit_grad = pair_grad * prob_lanes[...] * diff_lanes[...]
        logit_grad = logit_grad + pltpu.roll(logit_grad, experts, 1) + pltpu.roll(logit_grad, 2 * experts, 1)
        old = grads_tile[slot, :, :, slab : slab + 128].reshape(tile, 128)
        grads_tile[slot, :, :, slab : slab + 128] = (
            jnp.where(lanes >= lane0, logit_grad.astype(bf16), old).reshape(half, rows, 128)
        )
        for n in range(0, width, 512):
            rows_tile[slot, :, :, n : n + 512] = (
                dot(grads_tile[slot].reshape(tile, 2 * hidden_units), w_in_ref[:, n : n + 512]).astype(bf16).reshape(half, rows, 512)
            )
        for copy in stores[1:]:
            copy.start()
        return 0

    lax.fori_loop(0, 2 * depth, step, 0)
    for i in (2 * depth - 2, 2 * depth - 1):
        for copy in tile_copies(i)[4]:
            copy.wait()
    z_drain()
    for copy in saves:
        copy.wait()
    w_out_save.wait()

    def drain(k, _):
        chunk = order_at(k)

        @pl.when(goes_up(chunk))
        def _():
            along(chunk, 0, up).wait_send()

        @pl.when(goes_down(chunk))
        def _():
            along(chunk, 1, down).wait_send()

        for slot in range(7):
            h_copy(ep, chunk, slot, pair).wait_send()
        for slot in (0, 4, 5, 6):
            c_copy(ep, chunk, slot, pair).wait_send()

        @pl.when(chunk != skipped)
        def _():
            for slot in (1, 2, 3):
                c_copy(ep, chunk, slot, pair).wait_send()

        return 0

    lax.fori_loop(0, depth, drain, 0)
    for n in range(3):
        buddy_copy(n, theirs).wait_send()


def experts_call(
    inputs, gain_attn, w_query, w_latent, gain_latent, w_up, w_output, tables, gain, cotangent, kept, e_in, e_out, s_in, s_out,
    blocks, depth, heads, shared, experts, cid,
):
    f32, bf16 = jnp.float32, jnp.bfloat16
    tokens, width = inputs.shape
    rows = tokens // depth
    routed = e_out.shape[1]
    hidden = routed + s_out.shape[0]
    rank = w_up.shape[0]
    half = blocks // 2
    tile = half * rows
    dma = pltpu.SemaphoreType.DMA
    vmem, anywhere = pl.BlockSpec(memory_space=pltpu.VMEM), pl.BlockSpec(memory_space=pl.ANY)

    def units(size):
        return jax.ShapeDtypeStruct((depth, blocks, rows, size), bf16)

    kept_sizes = (
        ((tokens, width), bf16), ((tokens, heads * NOPE), bf16), ((tokens, heads * ROPE), bf16),
        ((tokens, heads * (NOPE + VDIM)), bf16), ((2, tokens, 128), bf16), ((tokens, heads * VDIM), bf16),
        ((tokens, rank), bf16), ((tokens, rank), f32),
    )

    return pl.pallas_call(
        functools.partial(experts_kernel, depth, blocks, heads, routed, shared, experts),
        out_shape=(
            jax.ShapeDtypeStruct((rows, width), f32),
            units(width), units(width), units(2 * hidden), units(hidden), units(width),
        )
        + tuple(jax.ShapeDtypeStruct(*size) for size in kept_sizes)
        + (jax.ShapeDtypeStruct((hidden, width), bf16),),
        in_specs=[anywhere, vmem, anywhere, anywhere, vmem, anywhere, anywhere, anywhere, vmem] + [anywhere] * 6,
        out_specs=(vmem,) + (anywhere,) * 14,
        scratch_shapes=[
            *(pltpu.VMEM(a.shape, a.dtype) for a in (inputs, w_query, w_latent, w_up, w_output, tables)),
            dma((6,)),
            pltpu.VMEM((tokens, width), bf16),
            *(pltpu.VMEM(*size) for size in kept_sizes),
            pltpu.VMEM((tokens, 128), f32),
            pltpu.VMEM((depth, blocks, rows, 128), bf16),
            pltpu.VMEM((2 * hidden, width), bf16),
            pltpu.VMEM((hidden, width), bf16),
            pltpu.VMEM((depth, blocks, rows, width), bf16),
            pltpu.VMEM((depth + 1, rows, width), bf16),
            pltpu.VMEM((half, rows, width), bf16),
            pltpu.VMEM((tile, 2 * hidden), f32),
            pltpu.VMEM((tile, hidden), f32),
            pltpu.VMEM((tile, 128), f32),
            pltpu.VMEM((tile, 128), f32),
            pltpu.VMEM((tile, 128), f32),
            pltpu.VMEM((2, half, rows, 2 * hidden), bf16),
            pltpu.VMEM((2, half, rows, hidden), bf16),
            pltpu.VMEM((2, half, rows, width), bf16),
            dma((7,)), dma((9,)), dma((depth,)),
            dma((depth - 1,)), dma((depth + 1,)),
            dma((depth, 2)), dma((depth,)),
            dma((depth, 7)), dma((depth, 7)),
            dma((depth, 7)), dma((depth, 7)),
            dma((3,)), dma((3,)), dma, dma((2, 4)),
        ],
        compiler_params=pltpu.CompilerParams(collective_id=cid, has_side_effects=True, vmem_limit_bytes=63 << 20),
    )(
        inputs, gain_attn.reshape(1, width), w_query, w_latent, gain_latent.reshape(1, rank), w_up, w_output, tables,
        gain.reshape(1, width), cotangent, kept, e_in, e_out, s_in, s_out,
    )


def sum_kernel(
    depth, routed, shared, experts, part_ref, h_ref, grads_ref, gated_ref, cot_ref, middle_ref, gain_ref, w_out_ref,
    branch, gain_part, expert_in, expert_out, s_in, s_out, router, layer_sum, landed,
    in_grad, out_grad,
    load, store, layer, got_pair, got_first, got_second, got_z, keep, h_tile, grads_tile, gated_tile, cot_tile,
    own_cot, load_sem, store_sem, own_sem, lps, lpr, ps, pr, fs, fr, ss, sr, zs, zr, tile_sem, e_sem, o_sem,
):
    f32 = jnp.float32
    rows = part_ref.shape[2]
    count = h_tile.shape[0] * rows
    width = h_tile.shape[2]
    hidden = gated_tile.shape[2]
    ep, tp = lax.axis_index("ep"), lax.axis_index("tp")
    pair, xn, yn = plane_partners(ep)
    parity = lax.rem(ep, 2)
    first = jnp.where(parity == 0, xn, yn)
    second = jnp.where(parity == 0, yn, xn)
    diag = xn + yn - ep
    blocks = (first, diag, ep, second)
    pair_slot = (3, 1, 2, 0)
    greet([(pair, tp), (xn, tp), (yn, tp)] + [(ep, lax.rem(tp + k, depth)) for k in range(1, depth)])
    steps = [(k + 1) % depth for k in range(depth)]

    def chunk_of(i):
        return lax.rem(tp + steps[i], depth)

    def pair_copy(i, slot):
        src = part_ref.at[chunk_of(i), blocks[slot] + pair - ep]
        to = pair_slot[slot]
        return remote(src, got_pair.at[i, to], ps.at[i, slot], pr.at[i, to], (pair, tp))

    def pair_wait(i, slot):
        return remote(part_ref.at[0, 0], got_pair.at[i, slot], ps.at[i, slot], pr.at[i, slot], (pair, tp))

    def own_load(i, slot):
        return pltpu.make_async_copy(part_ref.at[chunk_of(i), blocks[slot]], load.at[slot], load_sem.at[slot])

    def first_copy(i, slot):
        return remote(got_pair.at[i, slot], got_first.at[i, slot], fs.at[i, slot], fr.at[i, slot], (first, tp))

    def second_copy(i):
        return remote(got_pair.at[i, 3], got_second.at[i], ss.at[i], sr.at[i], (second, tp))

    def z_copy(i):
        k = steps[i]
        return remote(got_pair.at[i, 2], got_z.at[k - 1], zs.at[k - 1], zr.at[k - 1], (ep, lax.rem(tp + k, depth)))

    def layer_pair(i, slot):
        src = layer.at[blocks[slot] + pair - ep]
        to = pair_slot[slot]
        return remote(src, landed.at[i, to], lps.at[i, slot], lpr.at[i, to], (pair, tp))

    def layer_load(i, slot):
        return pltpu.make_async_copy(landed.at[i, slot], load.at[slot], load_sem.at[slot])

    def layer_store(i, slot):
        return pltpu.make_async_copy(store.at[slot % 2], layer_sum.at[i, slot], store_sem.at[slot % 2])

    def layer_send(i):
        def columns(m, _):
            at = pl.ds(pl.multiple_of(m * 512, 512), 512)
            found = jnp.dot(gated_tile[...].reshape(count, hidden), w_out_ref[:, at], preferred_element_type=f32)
            layer[:, :, at] = found.astype(layer.dtype).reshape(layer.shape[0], rows, 512)
            return 0

        lax.fori_loop(0, width // 512, columns, 0)
        for slot in (3, 1, 2, 0):
            layer_pair(i, slot).start()

    def layer_add(i):
        for slot in range(4):
            layer_pair(i, pair_slot[slot]).wait_recv()
            layer_load(i, slot).start()
        for slot in range(4):
            layer_load(i, slot).wait()
            if slot >= 2:
                layer_store(i, slot - 2).wait()
            add_rows(store.at[slot % 2], load.at[slot], layer.at[blocks[slot]])
            layer_store(i, slot).start()
        layer_store(i, 2).wait()
        layer_store(i, 3).wait()
        for slot in range(4):
            layer_pair(i, slot).wait_send()

    for i in range(depth):
        for slot in (3, 1, 2, 0):
            pair_copy(i, slot).start()

    def tile_loads(c):
        return [
            pltpu.make_async_copy(src.at[c], dst, tile_sem.at[n])
            for n, (src, dst) in enumerate(
                ((h_ref, h_tile), (grads_ref, grads_tile), (gated_ref, gated_tile), (cot_ref, cot_tile))
            )
        ]

    def stage_a(i):
        for slot in range(4):
            own_load(i, slot).start()
        for slot in range(4):
            pair_wait(i, slot).wait_recv()
            own_load(i, slot).wait()
            add_rows(got_pair.at[i, slot], got_pair.at[i, slot], load.at[slot])
            if slot < 2:
                first_copy(i, slot).start()

    def stage_b(i):
        first_copy(i, 1).wait_recv()
        add_rows(got_pair.at[i, 3], got_pair.at[i, 3], got_first.at[i, 1])
        second_copy(i).start()
        first_copy(i, 0).wait_recv()
        add_rows(got_pair.at[i, 2], got_pair.at[i, 2], got_first.at[i, 0])

    def stage_c(i):
        second_copy(i).wait_recv()
        if i < depth - 1:
            add_rows(got_pair.at[i, 2], got_pair.at[i, 2], got_second.at[i])
            z_copy(i).start()
        else:
            add_rows(keep, got_pair.at[i, 2], got_second.at[i])


    blocks_all = h_tile.shape[0]
    def expert_out_copy():
        return pltpu.make_async_copy(out_grad.at[pl.ds(0, routed)], expert_out.at[0], o_sem)

    def expert_in_copy(g):
        return pltpu.make_async_copy(in_grad.at[pl.ds(g * hidden, routed)], expert_in.at[0, g], e_sem.at[g])

    def weights(c):
        for copy in tile_loads(c):
            copy.wait()
        turned = (((0,), (0,)), ((), ()))

        last = c == depth - 1

        def in_part(m, _):
            at = pl.ds(pl.multiple_of(m * 256, 256), 256)
            found = lax.dot_general(
                grads_tile[:, :, at].reshape(count, 256), h_tile[...].reshape(count, width), turned,
                preferred_element_type=f32,
            )
            in_grad[at, :] = found if c == 0 else in_grad[at, :] + found
            return 0

        lax.fori_loop(0, 2 * hidden // 256, in_part, 0)

        def out_part(m, _):
            at = pl.ds(pl.multiple_of(m * 512, 512), 512)
            found = lax.dot_general(
                gated_tile[...].reshape(count, hidden), cot_tile[:, :, at].reshape(count, 512), turned,
                preferred_element_type=f32,
            )
            out_grad[:, at] = found if c == 0 else out_grad[:, at] + found
            return 0

        lax.fori_loop(0, width // 512, out_part, 0)
        if last:
            expert_out_copy().start()
            expert_in_copy(0).start()
            expert_in_copy(1).start()
            router[...] = in_grad[routed + shared : routed + shared + experts, :]
            wide = width // blocks_all
            for b in range(blocks_all):
                at = slice(b * wide, (b + 1) * wide)
                s_out[b] = out_grad[routed : routed + s_out.shape[1], at].astype(s_out.dtype)
                for g in range(2):
                    top = g * hidden + routed
                    s_in[b, g] = in_grad[top : top + s_in.shape[2], at].astype(s_in.dtype)
        if c > 0:
            layer_add(c - 1)
        layer_send(c)
        if c + 1 < depth:
            for copy in tile_loads(c + 1):
                copy.start()

    own_copy = pltpu.make_async_copy(cot_ref.at[tp, ep], own_cot, own_sem)
    own_copy.start()
    for copy in tile_loads(0):
        copy.start()
    stage_a(0)
    stage_a(1)
    weights(0)
    stage_b(0)
    stage_a(2)
    weights(1)
    stage_b(1)
    stage_a(3)
    stage_c(0)
    weights(2)
    stage_b(2)
    stage_c(1)
    stage_b(3)
    weights(3)
    stage_c(2)
    stage_c(3)
    layer_add(depth - 1)
    for i in range(depth - 1):
        z_copy(i).wait_recv()
    own_copy.wait()

    def total(r, gain_sum):
        at = pl.ds(pl.multiple_of(r * 16, 16), 16)
        u = keep[at, :]
        for k in range(depth - 1):
            u = u + got_z[k, at, :].astype(f32)
        v = middle_ref[at, :]
        inverse = lax.rsqrt(jnp.mean(v * v, axis=-1, keepdims=True) + EPSILON)
        v_hat = v * inverse
        gain_sum = gain_sum + (u * v_hat)[:8] + (u * v_hat)[8:]
        s = u * gain_ref[...]
        back = inverse * (s - v_hat * jnp.mean(s * v_hat, axis=-1, keepdims=True))
        found = own_cot[at, :].astype(f32) + back
        branch[at, :] = found.astype(branch.dtype)
        return gain_sum

    gain_part[...] = lax.fori_loop(0, rows // 16, total, jnp.zeros((8, width), f32))
    expert_out_copy().wait()
    expert_in_copy(0).wait()
    expert_in_copy(1).wait()
    for i in range(depth):
        for slot in range(4):
            pair_copy(i, slot).wait_send()
        for slot in range(2):
            first_copy(i, slot).wait_send()
        second_copy(i).wait_send()
        if i < depth - 1:
            z_copy(i).wait_send()


def sum_call(part, h_all, grads, gated, cot_all, middle, gain, w_out, routed, shared, experts, cid):
    f32, bf16 = jnp.float32, jnp.bfloat16
    depth, blocks, rows, width = part.shape
    hidden = gated.shape[3]
    dma = pltpu.SemaphoreType.DMA
    vmem, anywhere = pl.BlockSpec(memory_space=pltpu.VMEM), pl.BlockSpec(memory_space=pl.ANY)
    return pl.pallas_call(
        functools.partial(sum_kernel, depth, routed, shared, experts),
        out_shape=(
            jax.ShapeDtypeStruct((rows, width), bf16),
            jax.ShapeDtypeStruct((8, width), f32),
            jax.ShapeDtypeStruct((1, 2, routed, width), f32),
            jax.ShapeDtypeStruct((1, routed, width), f32),
            jax.ShapeDtypeStruct((blocks, 2, -(-shared // 16) * 16, width // blocks), bf16),
            jax.ShapeDtypeStruct((blocks, -(-shared // 16) * 16, width // blocks), bf16),
            jax.ShapeDtypeStruct((experts, width), f32),
            jax.ShapeDtypeStruct((depth, 4, rows, width), bf16),
            jax.ShapeDtypeStruct((depth, 4, rows, width), bf16),
        ),
        in_specs=[anywhere] * 5 + [vmem] * 3,
        out_specs=(vmem,) * 2 + (anywhere,) * 2 + (vmem,) * 3 + (anywhere,) * 2,
        scratch_shapes=[
            pltpu.VMEM((2 * hidden, width), f32),
            pltpu.VMEM((hidden, width), f32),
            pltpu.VMEM((4, rows, width), bf16),
            pltpu.VMEM((2, rows, width), bf16),
            pltpu.VMEM((blocks, rows, width), bf16),
            pltpu.VMEM((depth, 4, rows, width), bf16),
            pltpu.VMEM((depth, 2, rows, width), bf16),
            pltpu.VMEM((depth, rows, width), bf16),
            pltpu.VMEM((depth - 1, rows, width), bf16),
            pltpu.VMEM((rows, width), f32),
            pltpu.VMEM((blocks, rows, width), bf16),
            pltpu.VMEM((blocks, rows, 2 * hidden), bf16),
            pltpu.VMEM((blocks, rows, hidden), bf16),
            pltpu.VMEM((blocks, rows, width), bf16),
            pltpu.VMEM((rows, width), bf16),
            dma((4,)), dma((2,)), dma, dma((depth, 4)), dma((depth, 4)), dma((depth, 4)), dma((depth, 4)), dma((depth, 2)), dma((depth, 2)),
            dma((depth,)), dma((depth,)), dma((depth - 1,)), dma((depth - 1,)), dma((4,)), dma((2,)), dma,
        ],
        compiler_params=pltpu.CompilerParams(collective_id=cid, has_side_effects=True, vmem_limit_bytes=62 << 20),
    )(part, h_all, grads, gated, cot_all, middle, gain.reshape(1, width), w_out)


def line_gather(ref, own, send_sem, recv_sem, ep, tp, depth):
    up, down = jnp.minimum(tp + 1, depth - 1), jnp.maximum(tp - 1, 0)
    order = line_order(tp)

    def along(k, way, to):
        chunk = order[k]
        src = own if k == 0 else ref.at[chunk]
        return remote(src, ref.at[chunk], send_sem.at[chunk, way], recv_sem.at[chunk], (ep, to))

    def each_way(k, act):
        @pl.when((order[k] <= tp) & (tp < depth - 1))
        def _():
            act(along(k, 0, up))

        @pl.when((order[k] >= tp) & (tp > 0))
        def _():
            act(along(k, 1, down))

    def pass_on(k):
        each_way(k, lambda copy: copy.start())

    def await_chunk(k):
        along(k, 0, up).wait_recv()

    def drain():
        for k in range(depth):
            each_way(k, lambda copy: copy.wait_send())

    return pass_on, await_chunk, drain


def tail_kernel(
    depth, heads, shared,
    branch_ref, middle_ref, part_ref, router_ref, gain_part_ref, inputs_ref, s_in, s_out,
    w_output_in, w_query_in, w_latent_in, w_up_in, hidden_in, qn_in, qr_in, kv_in, kr_in, attended_in, latent_in_in, compressed_in,
    tables_in, gain_latent, gain_attn,
    block_ref, grad_in_ref, gains_ref, query_ref, output_ref, up_ref, latent_ref, shared_in, shared_out, w_all, w_first,
    w_output, w_query, w_latent, w_up, hidden_ref, qn_ref, qr_ref, kv_ref, kr_ref, attended, latent_in, compressed,
    tables, load_in_sem,
    branch, held_rows, got_first, got_second, z_up, z_down, hidden_part, h_up, h_down, middle,
    d_out, d_kr, q_grad, kv_grad, l_grad, u_grad, w_stage, w_pair, w_second, w_z, latent_part, s_in_land, s_out_land, resid, grad_tile, block_tile, gains, attn_gains,
    load_sem, fs, fr, ss, sr, zus, zur, zds, zdr, bs, br, hus, hur, hds, hdr,
    wps, wpr, wfs, wfr, wss, wsr, wzs, wzr, as_, ar, ns, nr, misc_sem, resid_sem, grad_sem, block_sem, stage_sem, sis, sir, sos, sor,
):
    f32, bf16 = jnp.float32, jnp.bfloat16
    ep, tp = lax.axis_index("ep"), lax.axis_index("tp")
    pair, xn, yn = plane_partners(ep)
    parity = lax.rem(ep, 2)
    first = jnp.where(parity == 0, xn, yn)
    second = jnp.where(parity == 0, yn, xn)
    diag = xn + yn - ep
    blocks = (first, diag, ep, second)
    pair_slot = (3, 1, 2, 0)
    rows, width = middle.shape
    tokens = hidden_ref.shape[0]
    rank = compressed.shape[1]
    q_cols, l_cols = q_grad.shape[1], l_grad.shape[1]
    o_rows = attended.shape[1]
    count = w_all.shape[0]
    w_rows = w_all.shape[1]
    o_cols = width // count
    u_rows = rank // count
    u_cols = w_up.shape[1]
    o_start = q_cols + l_cols
    u_start = o_start + o_rows * o_cols // w_rows
    u_wide = u_rows * u_cols // w_rows
    order = line_order(tp)
    score_scale = (NOPE + ROPE) ** (-0.5)
    plane = [ep + sum(((pair, xn, yn)[n] - ep) * (m >> n & 1) for n in range(3)) for m in range(8)]
    greet([(to, tp) for to in plane[1:]] + [(ep, lax.rem(tp + k, depth)) for k in range(1, depth)])

    loads = [
        pltpu.make_async_copy(src, dst, load_in_sem.at[n])
        for n, (src, dst) in enumerate(
            (
                (w_output_in, w_output),
                (qn_in, qn_ref), (qr_in, qr_ref), (kv_in, kv_ref), (kr_in, kr_ref), (tables_in, tables),
                (w_up_in, w_up), (compressed_in, compressed), (w_query_in, w_query), (w_latent_in, w_latent),
                (hidden_in, hidden_ref), (attended_in, attended), (latent_in_in, latent_in),
            )
        )
    ]

    def loaded(first_load, last_load):
        for copy in loads[first_load:last_load]:
            copy.wait()

    branch_on, branch_wait, branch_drain = line_gather(branch, branch_ref, bs, br, ep, tp, depth)

    middle_copy = pltpu.make_async_copy(middle_ref, middle, misc_sem.at[1])

    def held_load(i, slot):
        return pltpu.make_async_copy(part_ref.at[i, slot], held_rows.at[i, slot - 2], load_sem.at[i, slot - 2])

    def first_copy(i, slot):
        return remote(part_ref.at[i, slot], got_first.at[i, slot], fs.at[i, slot], fr.at[i, slot], (first, tp))

    def second_copy(i):
        return remote(held_rows.at[i, 1], got_second.at[i], ss.at[i], sr.at[i], (second, tp))

    pieces, piece = h_up.shape[0], h_up.shape[1]
    per = rows // piece
    z_start, z_hop, z_finish, z_drain = line_total(
        lambda n: held_rows.at[n // per, 0, pl.ds(n % per * piece, piece)],
        pieces, z_up, z_down, zus, zur, zds, zdr, ep, tp, depth,
    )
    h_start, h_hop, h_finish, h_drain = line_total(
        lambda n: hidden_part.at[n], pieces, h_up, h_down, hus, hur, hds, hdr, ep, tp, depth
    )

    def stage_b(i):
        held_load(i, 3).wait()
        first_copy(i, 1).wait_recv()
        add_rows(held_rows.at[i, 1], held_rows.at[i, 1], got_first.at[i, 1])
        second_copy(i).start()
        held_load(i, 2).wait()
        first_copy(i, 0).wait_recv()
        add_rows(held_rows.at[i, 0], held_rows.at[i, 0], got_first.at[i, 0])

    def stage_c(i):
        second_copy(i).wait_recv()
        add_rows(held_rows.at[i, 0], held_rows.at[i, 0], got_second.at[i])

        @pl.when(tp == i)
        def _():
            middle_copy.wait()
            add_rows(held_rows.at[i, 0], held_rows.at[i, 0], middle)

        for n in range(per * i, per * i + per):
            z_start(n)

    def w_pair_copy(slot):
        to = pair_slot[slot]
        return remote(w_all.at[blocks[slot] + pair - ep], w_pair.at[to], wps.at[slot], wpr.at[to], (pair, tp))

    def w_pair_wait(slot):
        return remote(w_all.at[0], w_pair.at[slot], wps.at[slot], wpr.at[slot], (pair, tp))

    def w_first_copy(slot):
        return remote(w_pair.at[slot], w_first.at[slot], wfs.at[slot], wfr.at[slot], (first, tp))

    def w_second_copy():
        return remote(w_pair.at[3], w_second, wss, wsr, (second, tp))

    def w_load(slot):
        return pltpu.make_async_copy(w_all.at[blocks[slot]], w_stage.at[slot % 2], stage_sem.at[slot % 2])

    def w_stage_a():
        for slot in range(4):
            if slot < 3:
                w_load(slot + 1).start()
            w_pair_wait(slot).wait_recv()
            w_load(slot).wait()
            add_rows(w_pair.at[slot], w_pair.at[slot], w_stage.at[slot % 2])
            if slot < 2:
                w_first_copy(slot).start()

    def w_stage_b():
        def load(slot):
            return pltpu.make_async_copy(w_first.at[slot], w_stage.at[slot], stage_sem.at[slot])

        w_first_copy(1).wait_recv()
        load(1).start()
        w_first_copy(0).wait_recv()
        load(0).start()
        load(1).wait()
        add_rows(w_pair.at[3], w_pair.at[3], w_stage.at[1])
        w_second_copy().start()
        load(0).wait()
        add_rows(w_pair.at[2], w_pair.at[2], w_stage.at[0])

    def w_stage_c():
        w_second_copy().wait_recv()

        def total(cols, at=slice(None)):
            return w_pair[2, at, cols].astype(f32) + w_second[at, cols].astype(f32)

        query_ref[...] = total(slice(0, q_cols))
        latent_part[...] = total(slice(q_cols, o_start))
        for n in range(o_rows // w_rows):
            output_ref[n * w_rows : (n + 1) * w_rows, :] = total(slice(o_start + n * o_cols, o_start + (n + 1) * o_cols))
        for n in range(u_cols // u_wide):
            up_ref[:, n * u_wide : (n + 1) * u_wide] = total(
                slice(u_start, u_start + u_wide), slice(n * u_rows, (n + 1) * u_rows)
            )

    def shared_copies(m):
        to = plane[m]
        return (
            remote(s_in.at[to], s_in_land.at[ep], sis.at[m], sir.at[m], (to, tp)),
            remote(s_out.at[to], s_out_land.at[ep], sos.at[m], sor.at[m], (to, tp)),
        )

    def shared_own():
        return (
            pltpu.make_async_copy(s_in.at[ep], s_in_land.at[ep], sis.at[0]),
            pltpu.make_async_copy(s_out.at[ep], s_out_land.at[ep], sos.at[0]),
        )

    def shared_place():
        for m in range(1, 8):
            for copy in shared_copies(m):
                copy.wait_recv()
        for copy in shared_own():
            copy.wait()
        for n in range(s_in_land.shape[0]):
            at = slice(n * shared, (n + 1) * shared)
            for g in range(2):
                shared_in[g, at, :] = s_in_land[n, g].astype(f32)[:shared]
            shared_out[at, :] = s_out_land[n].astype(f32)[:shared]

    branch_on(0)
    branch[tp] = branch_ref[...]
    for i in range(depth):
        first_copy(i, 1).start()
        first_copy(i, 0).start()
        held_load(i, 3).start()
        held_load(i, 2).start()

    def resid_copy(n):
        return pltpu.make_async_copy(inputs_ref.at[pl.ds(n * piece, piece)], resid.at[n % 2], resid_sem.at[n % 2])

    for copy in loads:
        copy.start()
    resid_copy(0).start()
    resid_copy(1).start()
    middle_copy.start()

    turned, across = (((0,), (0,)), ((), ())), (((1,), (1,)), ((), ()))

    def dot(a, b, dims=(((1,), (0,)), ((), ()))):
        return lax.dot_general(a, b, dims, preferred_element_type=f32)

    def attended_grad(k):
        at = pl.ds(pl.multiple_of(order[k] * rows, rows), rows)
        d_out[at, :] = dot(branch[order[k]], w_output[...], across).astype(bf16)

    loaded(0, 1)
    attended_grad(0)
    branch_wait(1)
    branch_on(1)
    attended_grad(1)
    stage_b(0)
    branch_wait(2)
    branch_on(2)
    attended_grad(2)
    stage_c(0)
    stage_b(1)
    loaded(1, 6)
    branch_wait(3)
    branch_on(3)
    attended_grad(3)

    lanes = lax.broadcasted_iota(jnp.int32, (1, 128), 1)
    halves = tokens // BLOCK

    def head(h, even):
        mine = (lanes < 64) if even else (lanes >= 64)
        at_q = pl.ds(pl.multiple_of(h * NOPE, 128), 128)
        at_r = pl.ds(pl.multiple_of(lax.div(h, 2) * 128, 128), 128)
        at_k = pl.ds(pl.multiple_of(h * 256, 128), 128)
        at_v = pl.ds(pl.multiple_of(h * 256 + 128, 128), 128)
        kv_sum = [None, None]
        for b in reversed(range(halves)):
            own = slice(b * BLOCK, (b + 1) * BLOCK)
            keys = slice(0, (b + 1) * BLOCK)
            qn, qr = qn_ref[own, at_q], qr_ref[own, at_r]
            kn, kr = kv_ref[keys, at_k], kr_ref[0 if even else 1, keys, :]
            scores = (dot(qn, kn, across) + dot(qr, kr, across)) * score_scale
            exps = jnp.exp(scores - jnp.max(scores, axis=-1, keepdims=True))
            probs = exps / jnp.sum(exps, axis=-1, keepdims=True)
            grad = d_out[own, at_q]
            prob_part = dot(grad, kv_ref[keys, at_v], across)
            score_grad = (probs * (prob_part - jnp.sum(probs * prob_part, axis=-1, keepdims=True))).astype(bf16)
            found = (dot(score_grad, qn, turned) * score_scale, dot(probs.astype(bf16), grad, turned))
            r_grad = jnp.where(mine, dot(score_grad, qr, turned) * score_scale, 0.0)
            for n, at in enumerate((at_k, at_v)):
                if b < halves - 1:
                    kv_sum[n] = kv_sum[n] + found[n]
                else:
                    kv_sum[n] = found[n]
                kv_grad[own, at] = kv_sum[n][b * BLOCK :].astype(bf16)
                if b > 0:
                    kv_sum[n] = kv_sum[n][: b * BLOCK]
            d_kr[keys, :] = d_kr[keys, :] + r_grad
            yield own, dot(score_grad, kn) * score_scale, dot(score_grad, kr) * score_scale

    d_kr[...] = jnp.zeros_like(d_kr)

    def head_pair(p, _):
        evens = list(head(2 * p, True))
        odds = list(head(2 * p + 1, False))
        at = [pl.ds(pl.multiple_of(p * (2 * (NOPE + ROPE)) + n, 128), 128) for n in (0, 128, 256)]
        for (own, even, even_rope), (_, odd, odd_rope) in zip(evens, odds):
            table = tuple(tables[n, own, :] for n in range(3))
            rope = turn(even_rope + odd_rope, table, -1.0)
            odd = pltpu.roll(odd, 64, 1)
            q_grad[own, at[0]] = even.astype(bf16)
            q_grad[own, at[1]] = jnp.where(lanes < 64, rope, odd).astype(bf16)
            q_grad[own, at[2]] = jnp.where(lanes < 64, odd, rope).astype(bf16)
        return 0

    def head_pairs(p, _):
        head_pair(p, 0)

        @pl.when(p == 0)
        def _():
            stage_c(1)
            for n in range(per):
                z_hop(1, n)

        return 0

    lax.fori_loop(0, heads // 2, head_pairs, 0)
    for n in range(per):
        z_hop(2, n)
        z_hop(1, per + n)
    stage_b(2)

    loaded(6, 10)
    latent_back = dot(kv_grad[...], w_up[...], across)
    held = compressed[...]
    inverse = lax.rsqrt(jnp.mean(held * held, axis=-1, keepdims=True) + EPSILON)
    normed = held * inverse
    gain_latent_part = jnp.sum(latent_back * normed, axis=0, keepdims=True)
    scaled = latent_back * gain_latent[...]
    l_grad[:, :rank] = (inverse * (scaled - normed * jnp.mean(scaled * normed, axis=-1, keepdims=True))).astype(bf16)
    rope = d_kr[...] + pltpu.roll(d_kr[...], 64, 1)
    rope = turn(rope, tuple(tables[n] for n in range(3)), -1.0)
    l_grad[:, rank:] = jnp.where(lanes < 64, rope, 0.0).astype(bf16)

    for n in range(0, width, 512):
        part = dot(q_grad[...], w_query[n : n + 512, :], across) + dot(l_grad[:, : rank + ROPE], w_latent[:, n : n + 512])
        hidden_part[:, :, n : n + 512] = part.astype(bf16).reshape(pieces, piece, 512)
    for n in range(pieces):
        h_start(n)
    for n in range(per, 2 * per):
        z_hop(2, n)
    stage_c(2)
    stage_b(3)

    flip_1 = tp + 1 - 2 * lax.rem(tp, 2)
    flip_2 = tp + 2 - 4 * lax.div(tp, 2)

    def doubling(held, send, recv, partners):
        def copy(n):
            return remote(held.at[2 * n], held.at[2 * n + 1], send.at[n], recv.at[n], partners[n])

        def start():
            copy(0).start()

        def step(n):
            copy(n).wait_recv()
            total = held[2 * n] + held[2 * n + 1]
            if n + 1 < len(partners):
                held[2 * n + 2] = total
                copy(n + 1).start()
            return total

        def drain():
            for n in range(len(partners)):
                copy(n).wait_send()

        return start, step, drain

    gain_start, gain_step, gain_drain = doubling(
        gains, as_, ar, ((pair, tp), (xn, tp), (yn, tp), (ep, flip_1), (ep, flip_2))
    )
    attn_start, attn_step, attn_drain = doubling(attn_gains, ns, nr, ((pair, tp), (xn, tp), (yn, tp)))
    gains[0] = jnp.zeros_like(gains[0])
    gains[0, 1:2, :] = jnp.sum(gain_part_ref[...], axis=0, keepdims=True)
    gains[0, 2:3, 0:rank] = gain_latent_part
    gains[0, 8 : 8 + router_ref.shape[0], :] = router_ref[...]
    gain_start()

    loaded(10, 13)
    u_grad[...] = dot(latent_in[...], kv_grad[...], turned).astype(bf16)

    def w_store(b):
        slot = lax.rem(b, 2)
        return pltpu.make_async_copy(w_stage.at[slot], w_all.at[b], stage_sem.at[slot])

    def w_block(b, _):
        slot = lax.rem(b, 2)

        @pl.when(b >= 2)
        def _():
            w_store(b - 2).wait()

        at = pl.ds(pl.multiple_of(b * w_rows, 256), w_rows)
        own = hidden_ref[:, at]
        w_stage[slot, :, 0:q_cols] = dot(own, q_grad[...], turned).astype(bf16)
        found = dot(own, l_grad[...], turned)
        w_stage[slot, :, q_cols : q_cols + rank] = found[:, :rank].astype(bf16)
        w_stage[slot, :, q_cols + rank : o_start] = found[:, rank:].astype(bf16)
        cols = pl.ds(pl.multiple_of(b * o_cols, 256), o_cols)
        found = dot(attended[...], branch[:, :, cols].reshape(tokens, o_cols), turned)
        for n in range(o_rows // w_rows):
            w_stage[slot, :, o_start + n * o_cols : o_start + (n + 1) * o_cols] = (
                found[n * w_rows : (n + 1) * w_rows].astype(bf16)
            )
        u_at = pl.ds(pl.multiple_of(b * u_rows, u_rows), u_rows)
        for n in range(u_cols // u_wide):
            w_stage[slot, n * u_rows : (n + 1) * u_rows, u_start : u_start + u_wide] = (
                u_grad[u_at, n * u_wide : (n + 1) * u_wide]
            )
        w_store(b).start()
        return 0

    lax.fori_loop(0, count, w_block, 0)
    w_store(count - 2).wait()
    w_store(count - 1).wait()
    for slot in (3, 1, 2, 0):
        w_pair_copy(slot).start()
    for copy in shared_own():
        copy.start()
    for m in range(1, 8):
        for copy in shared_copies(m):
            copy.start()
    w_load(0).start()

    w_part = w_rows // depth

    def w_z_copy(k):
        to = lax.rem(tp + k, depth)
        src = w_pair.at[1, pl.ds(pl.multiple_of(to * w_part, w_part), w_part), pl.ds(q_cols, l_cols)]
        return remote(src, w_z.at[k - 1], wzs.at[k - 1], wzr.at[k - 1], (ep, to))

    def block_copy(n):
        return pltpu.make_async_copy(block_tile.at[n % 2], block_ref.at[pl.ds(n * piece, piece)], block_sem.at[n % 2])

    def block_rows(n):
        z_finish(n)
        if n >= 2:
            block_copy(n - 2).wait()

        def total(r, _):
            at = pl.ds(pl.multiple_of(r * 16, 16), 16)
            inside = pl.ds(pl.multiple_of(n % per * piece + r * 16, 16), 16)
            value = z_up[n, at, :].astype(f32) + z_down[n, at, :].astype(f32) - held_rows[n // per, 0, inside, :].astype(f32)
            block_tile[n % 2, at, :] = value.astype(bf16)
            return 0

        lax.fori_loop(0, piece // 16, total, 0)
        block_copy(n).start()

    def grad_copy(n):
        return pltpu.make_async_copy(grad_tile.at[n % 2], grad_in_ref.at[pl.ds(n * piece, piece)], grad_sem.at[n % 2])

    def grad_rows(n, gain_sum):
        h_finish(n)
        if n >= 2:
            grad_copy(n - 2).wait()
        resid_copy(n).wait()

        def total(r, gain_sum):
            at = pl.ds(pl.multiple_of(r * 16, 16), 16)
            inside = pl.ds(pl.multiple_of(n % per * piece + r * 16, 16), 16)
            u = h_up[n, at, :].astype(f32) + h_down[n, at, :].astype(f32) - hidden_part[n, at, :].astype(f32)
            v = resid[n % 2, at, :].astype(f32)
            inv = lax.rsqrt(jnp.mean(v * v, axis=-1, keepdims=True) + EPSILON)
            v_hat = v * inv
            gain_sum = gain_sum + (u * v_hat)[:8] + (u * v_hat)[8:]
            s = u * gain_attn[...]
            back = inv * (s - v_hat * jnp.mean(s * v_hat, axis=-1, keepdims=True))
            grad_tile[n % 2, at, :] = (branch[n // per, inside, :].astype(f32) + back).astype(bf16)
            return gain_sum

        gain_sum = lax.fori_loop(0, piece // 16, total, gain_sum)
        if n + 2 < pieces:
            resid_copy(n + 2).start()
        grad_copy(n).start()
        return gain_sum

    gain_sum = jnp.zeros((8, width), f32)
    for t in range(pieces + 2):
        if t < pieces:
            h_hop(1, t)
        if t >= 2:
            h_hop(2, t - 2)
        if t >= 4:
            gain_sum = grad_rows(t - 4, gain_sum)
        if t == 1:
            gain_step(0)
        if t == 2:
            w_stage_a()
        if t == 0:
            stage_c(3)
        if t == 3:
            gain_step(1)
        if t == 5:
            block_rows(0)
            block_rows(1)
            gain_step(2)
        if t == 6:
            gain_step(3)
        if t == 7:
            w_stage_b()
            block_rows(2)
            block_rows(3)
        if t == 8:
            gains_ref[...] = gain_step(4)
    for t in range(pieces // 2 + 2):
        if t < pieces // 2:
            z_hop(1, pieces // 2 + t)
        if t >= 2:
            z_hop(2, pieces // 2 + t - 2)
        if t < 2:
            gain_sum = grad_rows(pieces - 2 + t, gain_sum)
        if t == 1:
            attn_gains[0] = gain_sum
            attn_start()
        if t == 2:
            w_stage_c()
            w_first_copy(1).wait_send()
            w_pair[1, :, q_cols:o_start] = latent_part[...].astype(bf16)
            for k in range(1, depth):
                w_z_copy(k).start()
            attn_step(0)
            shared_place()
        if t == 4:
            attn_step(1)
    for n in range(pieces // 2, pieces):
        block_rows(n)
    for k in range(1, depth):
        w_z_copy(k).wait_recv()
    own = pl.ds(pl.multiple_of(tp * w_part, w_part), w_part)
    total = latent_part[own, :]
    for k in range(depth - 1):
        total = total + w_z[k].astype(f32)
    latent_ref[...] = total
    gains_ref[0:1, :] = jnp.sum(attn_step(2), axis=0, keepdims=True)

    for n in (pieces - 2, pieces - 1):
        block_copy(n).wait()
    for n in (pieces - 2, pieces - 1):
        grad_copy(n).wait()
    branch_drain()
    for i in range(depth):
        for slot in range(2):
            first_copy(i, slot).wait_send()
        second_copy(i).wait_send()
    z_drain()
    h_drain()
    for slot in range(4):
        w_pair_copy(slot).wait_send()
    w_first_copy(0).wait_send()
    w_second_copy().wait_send()
    for k in range(1, depth):
        w_z_copy(k).wait_send()
    gain_drain()
    attn_drain()
    for m in range(1, 8):
        for copy in shared_copies(m):
            copy.wait_send()


def tail_call(
    branch, middle, out_part, router, gain_part, inputs, s_in, s_out, w_output, w_query, w_latent, w_up,
    hidden, qn, qr, kv, kr, attended, latent_in, compressed, tables, gain_latent, gain_attn,
    heads, shared, cid,
):
    f32, bf16 = jnp.float32, jnp.bfloat16
    depth, _, rows, width = out_part.shape
    tokens = hidden.shape[0]
    blocks = s_in.shape[0]
    rank = compressed.shape[1]
    q_cols, l_cols = w_query.shape[1], rank + 128
    pieces = 2 * depth
    w_rows = width // blocks
    w_cols = q_cols + l_cols + w_output.shape[0] + rank * w_up.shape[1] // width
    dma = pltpu.SemaphoreType.DMA
    vmem, anywhere = pl.BlockSpec(memory_space=pltpu.VMEM), pl.BlockSpec(memory_space=pl.ANY)
    return pl.pallas_call(
        functools.partial(tail_kernel, depth, heads, shared),
        out_shape=(
            jax.ShapeDtypeStruct((tokens, width), bf16),
            jax.ShapeDtypeStruct((tokens, width), bf16),
            jax.ShapeDtypeStruct((8 + router.shape[0], width), f32),
            jax.ShapeDtypeStruct((w_rows, q_cols), f32),
            jax.ShapeDtypeStruct((w_output.shape[0], w_rows), f32),
            jax.ShapeDtypeStruct((rank // blocks, w_up.shape[1]), f32),
            jax.ShapeDtypeStruct((w_rows // depth, l_cols), f32),
            jax.ShapeDtypeStruct((2, blocks * shared, w_rows), f32),
            jax.ShapeDtypeStruct((blocks * shared, w_rows), f32),
            jax.ShapeDtypeStruct((blocks, w_rows, w_cols), bf16),
            jax.ShapeDtypeStruct((2, w_rows, w_cols), bf16),
        ),
        in_specs=[vmem, anywhere, anywhere, vmem, vmem] + [anywhere] * 16 + [vmem, vmem],
        out_specs=(anywhere, anywhere) + (vmem,) * 7 + (anywhere, anywhere),
        scratch_shapes=[
            *(
                pltpu.VMEM(a.shape, a.dtype)
                for a in (
                    w_output, w_query, w_latent, w_up, hidden, qn, qr, kv, kr, attended, latent_in, compressed, tables,
                )
            ),
            dma((13,)),
            pltpu.VMEM((depth, rows, width), bf16),
            pltpu.VMEM((depth, 2, rows, width), bf16),
            pltpu.VMEM((depth, 2, rows, width), bf16),
            pltpu.VMEM((depth, rows, width), bf16),
            pltpu.VMEM((pieces, tokens // pieces, width), bf16),
            pltpu.VMEM((pieces, tokens // pieces, width), bf16),
            pltpu.VMEM((pieces, tokens // pieces, width), bf16),
            pltpu.VMEM((pieces, tokens // pieces, width), bf16),
            pltpu.VMEM((pieces, tokens // pieces, width), bf16),
            pltpu.VMEM((rows, width), f32),
            pltpu.VMEM((tokens, heads * VDIM), bf16),
            pltpu.VMEM((tokens, 128), f32),
            pltpu.VMEM((tokens, q_cols), bf16),
            pltpu.VMEM((tokens, heads * (NOPE + VDIM)), bf16),
            pltpu.VMEM((tokens, l_cols), bf16),
            pltpu.VMEM((rank, heads * (NOPE + VDIM)), bf16),
            pltpu.VMEM((2, w_rows, w_cols), bf16),
            pltpu.VMEM((4, w_rows, w_cols), bf16),
            pltpu.VMEM((w_rows, w_cols), bf16),
            pltpu.VMEM((depth - 1, w_rows // depth, l_cols), bf16),
            pltpu.VMEM((w_rows, l_cols), f32),
            pltpu.VMEM(s_in.shape, bf16),
            pltpu.VMEM(s_out.shape, bf16),
            pltpu.VMEM((2, tokens // pieces, width), bf16),
            pltpu.VMEM((2, tokens // pieces, width), bf16),
            pltpu.VMEM((2, tokens // pieces, width), bf16),
            pltpu.VMEM((10, 8 + router.shape[0], width), f32),
            pltpu.VMEM((6, 8, width), f32),
            dma((depth, 2)),
            dma((depth, 2)), dma((depth, 2)), dma((depth,)), dma((depth,)),
            dma((pieces,)), dma((pieces,)), dma((pieces,)), dma((pieces,)),
            dma((depth, 2)), dma((depth,)),
            dma((pieces,)), dma((pieces,)), dma((pieces,)), dma((pieces,)),
            dma((4,)), dma((4,)), dma((2,)), dma((2,)), dma, dma, dma((depth - 1,)), dma((depth - 1,)),
            dma((5,)), dma((5,)), dma((3,)), dma((3,)), dma((2,)), dma((2,)), dma((2,)), dma((2,)), dma((2,)), dma((8,)), dma((8,)), dma((8,)), dma((8,)),
        ],
        compiler_params=pltpu.CompilerParams(collective_id=cid, has_side_effects=True, vmem_limit_bytes=63 << 20),
    )(
        branch, middle, out_part, router, gain_part, inputs, s_in, s_out, w_output, w_query, w_latent, w_up,
        hidden, qn, qr, kv, kr, attended, latent_in, compressed, tables,
        gain_latent.reshape(1, rank), gain_attn.reshape(1, width),
    )


def rope_tables(length):
    half = ROPE // 2
    inverse = np.exp(np.arange(half) * (-math.log(10000.0) / half))
    angle = np.arange(length)[:, None] * inverse[None, :]
    cosine, sine = np.cos(angle), np.sin(angle)
    zero = np.zeros_like(sine)
    parts = ([cosine] * 4, [-sine, zero] * 2, [zero, sine] * 2)
    return jnp.asarray(np.stack([np.concatenate(p, axis=1) for p in parts]), jnp.float32)


def padded_hidden(routed, shared):
    return -(-(routed + shared + 24) // 128) * 128


def split_wide(values):
    high = values.astype(jnp.bfloat16)
    rest = values - high.astype(jnp.float32)
    mid = rest.astype(jnp.bfloat16)
    low = (rest - mid.astype(jnp.float32)).astype(jnp.bfloat16)
    return (high, mid, low)


def body_dense(
    inputs,
    gain_attn,
    w_query,
    w_latent,
    gain_latent,
    w_latent_up,
    w_output,
    gain_ffn,
    w_router,
    w_shared_in,
    w_shared_out,
    w_expert_in,
    w_expert_out,
    expert_ids,
    slot_ids,
    cotangent,
):
    f32, bf16 = jnp.float32, jnp.bfloat16
    tokens, model_width = inputs.shape
    ep_count, tp_count = lax.axis_size("ep"), lax.axis_size("tp")
    ep_index, tp_index = lax.axis_index("ep"), lax.axis_index("tp")
    heads_here = w_output.shape[0] // VDIM
    experts = w_router.shape[1]
    capacity = (9 * tokens * TOPK + 64 * experts - 1) // (64 * experts) * 8
    qk_width = NOPE + ROPE
    score_scale = qk_width ** (-0.5)
    rows_part = tokens // tp_count

    expert_range = jnp.arange(experts, dtype=jnp.int32)
    kept = jnp.any(
        (expert_ids[:, :, None] == expert_range) & (slot_ids < capacity)[:, :, None], axis=1
    ).astype(f32)
    kept_here = lax.all_to_all(kept, "ep", split_axis=1, concat_axis=0, tiled=True)
    rows_part = tokens // tp_count
    kept_lanes = jnp.broadcast_to(
        kept_here.reshape(ep_count, tp_count, rows_part, 1).swapaxes(0, 1),
        (tp_count, ep_count, rows_part, 128),
    ).astype(bf16)

    routed = w_expert_in.shape[3]
    shared = w_shared_in.shape[2] // ep_count
    hidden = padded_hidden(routed, shared)
    shared_start = ep_index * shared
    after = hidden - routed - shared
    router_parts = jnp.concatenate(split_wide(w_router), axis=1).T
    beside = jnp.stack(
        [
            jnp.pad(router_parts, ((0, after - router_parts.shape[0]), (0, 0))),
            jnp.zeros((after, model_width), bf16),
        ]
    )
    shared_in = lax.dynamic_slice_in_dim(w_shared_in.swapaxes(1, 2), shared_start, shared, 1)
    shared_in = jnp.concatenate([shared_in, beside], axis=1)
    shared_out = lax.dynamic_slice_in_dim(w_shared_out, shared_start, shared, 0)
    shared_out = jnp.pad(shared_out, ((0, after), (0, 0)))
    tables = rope_tables(tokens)
    (
        middle, hidden_all, cot_all, hidden_grads, gated, rows_grad,
        hidden_attn, query_nope, query_rope, key_value, key_pair, attended, latent_in, compressed, w_out,
    ) = experts_call(
        inputs, gain_attn, w_query, w_latent.T, gain_latent, w_latent_up, w_output, tables, gain_ffn, cotangent, kept_lanes,
        w_expert_in.swapaxes(2, 3), w_expert_out, shared_in, shared_out, ep_count, tp_count, heads_here, shared, experts, 0,
    )
    branch, gain_ffn_part, grad_expert_in, grad_expert_out, shared_in_part, shared_out_part, router_part, layer_sum, _ = (
        sum_call(
            rows_grad, hidden_all, hidden_grads, gated, cot_all, middle, gain_ffn, w_out, routed, shared, experts, 1
        )
    )
    block_out, grad_inputs, gains, grad_query, grad_output, grad_latent_up, latent_sum, grad_shared_in, grad_shared_out, _, _ = (
        tail_call(
            branch, middle, layer_sum, router_part, gain_ffn_part, inputs, shared_in_part, shared_out_part,
            w_output, w_query, w_latent.T, w_latent_up, hidden_attn,
            query_nope, query_rope, key_value, key_pair,
            attended, latent_in, compressed, tables, gain_latent, gain_attn, heads_here, shared, 2,
        )
    )
    grad_latent = latent_sum[:, : KV_RANK + ROPE]
    flat = ep_index * tp_count + tp_index
    wide_part, rank_part = (n // (ep_count * tp_count) for n in (model_width, KV_RANK))
    grad_gain_attn = lax.dynamic_slice_in_dim(gains[0], flat * wide_part, wide_part, 0)
    grad_gain_ffn = lax.dynamic_slice_in_dim(gains[1], flat * wide_part, wide_part, 0)
    grad_gain_latent = lax.dynamic_slice_in_dim(gains[2], flat * rank_part, rank_part, 0)
    grad_router = lax.dynamic_slice_in_dim(gains[8:], flat * wide_part, wide_part, 1).T
    grad_expert_in = grad_expert_in.swapaxes(2, 3)
    grad_shared_in = grad_shared_in.swapaxes(1, 2)
    return (
        block_out,
        grad_inputs,
        grad_gain_attn,
        grad_query,
        grad_latent,
        grad_gain_latent,
        grad_latent_up,
        grad_output,
        grad_gain_ffn,
        grad_router,
        grad_shared_in,
        grad_shared_out,
        grad_expert_in,
        grad_expert_out,
    )


def solution(mesh):
    near = mesh.shape["ep"] == 8 and mesh.shape["tp"] == 4
    body = body_dense if near else body_slots
    placed = (
        P("ep", None),
        P(),
        P(None, "tp"),
        P(),
        P(),
        P(None, "tp"),
        P("tp", None),
        P(),
        P(),
        P(None, None, "tp"),
        P("tp", None),
        P("ep", None, None, "tp"),
        P("ep", "tp", None),
        P("ep", None),
        P("ep", None),
        P("ep", None),
    )
    return jax.shard_map(
        body,
        mesh=mesh,
        in_specs=placed,
        out_specs=(
            P("ep", None),
            P("ep", None),
            P(("ep", "tp")),
            P("ep", "tp"),
            P(("ep", "tp"), None),
            P(("ep", "tp")),
            P("ep", "tp"),
            P("tp", "ep"),
            P(("ep", "tp")),
            P(("ep", "tp"), None),
            P(None, "ep", "tp"),
            P("tp", "ep"),
            P("ep", None, None, "tp"),
            P("ep", "tp", None),
        ),
        check_vma=False,
    )
```
